32 devices in a mesh: wide: 8 (over z, y), narrow: 4 (over x, core).
Axes of the slice: x: 2, y: 2, z: 4, core: 2. Of those that a mesh axis runs over, the one named last changes fastest.
Arguments:
- patches: bfloat16 [768, 196, 768], P(('wide', 'narrow')), may hold values from -6 to 6
- keep_order: int32 [768, 196], P(('wide', 'narrow')), may hold values from 0 to 195, each once within a row
- cotangent: bfloat16 [768, 49, 768], P(('wide', 'narrow')), may hold values from -6 to 6
- first_gain: bfloat16 [768], P(('wide', 'narrow')), may hold values from 0.5 to 1.5
- first_shift: bfloat16 [768], P(('wide', 'narrow')), may hold values from -3 to 3
- project_in: bfloat16 [768, 2304], P(('wide', 'narrow')), may hold values from -0.21875 to 0.21875
- query_bias: bfloat16 [768], P(('wide', 'narrow')), may hold values from -3 to 3
- value_bias: bfloat16 [768], P(('wide', 'narrow')), may hold values from -3 to 3
- project_out: bfloat16 [768, 768], P(('wide', 'narrow')), may hold values from -0.625 to 0.625
- output_bias: bfloat16 [768], P(('wide', 'narrow')), may hold values from -3 to 3
- second_gain: bfloat16 [768], P(('wide', 'narrow')), may hold values from 0.5 to 1.5
- second_shift: bfloat16 [768], P(('wide', 'narrow')), may hold values from -3 to 3
- up_weight: bfloat16 [3072, 768], P('wide', 'narrow'), may hold values from -0.21875 to 0.21875
- up_bias: bfloat16 [3072], P(('wide', 'narrow')), may hold values from -3 to 3
- down_weight: bfloat16 [3072, 768], P('wide', 'narrow'), may hold values from -0.109375 to 0.109375
- down_bias: bfloat16 [768], P(('wide', 'narrow')), may hold values from -3 to 3
Outputs:
- result: bfloat16 [768, 49, 768], P(('wide', 'narrow'))
- patch_grad: float32 [768, 196, 768], P(('wide', 'narrow'))
- first_gain_grad: float32 [768], P(('wide', 'narrow'))
- first_shift_grad: float32 [768], P(('wide', 'narrow'))
- project_in_grad: float32 [768, 2304], P(('wide', 'narrow'))
- query_bias_grad: float32 [768], P(('wide', 'narrow'))
- value_bias_grad: float32 [768], P(('wide', 'narrow'))
- project_out_grad: float32 [768, 768], P(('wide', 'narrow'))
- output_bias_grad: float32 [768], P(('wide', 'narrow'))
- second_gain_grad: float32 [768], P(('wide', 'narrow'))
- second_shift_grad: float32 [768], P(('wide', 'narrow'))
- up_weight_grad: float32 [3072, 768], P('wide', 'narrow')
- up_bias_grad: float32 [3072], P(('wide', 'narrow'))
- down_weight_grad: float32 [3072, 768], P('wide', 'narrow')
- down_bias_grad: float32 [768], P(('wide', 'narrow'))
The draws below stay inside these ranges and needn't reach their ends.
Inputs may be any that keep to these rules, and one draw needn't show every extreme that they name: `keep_order`: each row is a permutation of the patch numbers; its first 49 entries name the image's visible patches.
All inputs are finite; a program needn't handle non-finite values.
Results may differ from the reference program's by a relative error of at most 0.012.
Values may be sent and summed in bfloat16 or wider, within the bound.
A program may use at most 192 MiB of HBM per device.

```python
import jax
import jax.numpy as jnp
from jax import lax

D = 768
HEADS = 12
HEAD_DIM = 64
FF = 3072
PATCHES = 196
VIS = 49
IMG_DEV = 24
IMAGES = 768
N_NARROW = 4


def level_of(rng, dims, split, least, high):
    def one(dim, parts):
        heights = jax.random.uniform(jax.random.fold_in(jax.random.fold_in(rng, 6), dim), (parts,), jnp.float32, least / len(split), high / len(split))
        return jnp.repeat(jnp.exp(heights), dims[dim] // parts).reshape((-1,) + (1,) * (len(dims) - dim - 1))

    factor_of = one(*split[0])
    for cut in split[1:]:
        factor_of = factor_of * one(*cut)
    return factor_of


def noise(stream_key, shape, scale, reach, pieces=(), kind=jnp.bfloat16):
    array = scale * jax.random.normal(stream_key, shape, jnp.float32)
    if pieces:
        array = array * level_of(stream_key, shape, pieces, -0.22, 0.18)
    return jnp.clip(array, -reach, reach).astype(kind)


def setup_inputs(seed: int = 0) -> dict:
    key_list = jax.random.split(jax.random.key(seed), 17)
    patches = noise(key_list[0], (IMAGES, PATCHES, D), 1.0, 6.0, ((0, 32),))
    keep_order = jax.vmap(lambda own: jax.random.permutation(own, PATCHES))(jax.random.split(key_list[1], IMAGES)).reshape((IMAGES, PATCHES)).astype(jnp.int32)
    cotangent = noise(key_list[2], (IMAGES, VIS, D), 1.0, 6.0, ((0, 32),))
    first_gain = jnp.clip(1.0 + 0.1 * jax.random.normal(key_list[3], (D,), jnp.float32), 0.5, 1.5).astype(jnp.bfloat16)
    first_shift = noise(key_list[4], (D,), 0.3, 3.0, ((0, 32),))
    project_in = noise(key_list[5], (D, 3 * D), D ** -0.5, 0.21875, ((0, 32),))
    query_bias = noise(key_list[6], (D,), 0.3, 3.0, ((0, 32),))
    value_bias = noise(key_list[7], (D,), 0.3, 3.0, ((0, 32),))
    project_out = noise(key_list[8], (D, D), (D // 8) ** -0.5, 0.625, ((0, 32),))
    output_bias = noise(key_list[9], (D,), 0.3, 3.0, ((0, 32),))
    second_gain = jnp.clip(1.0 + 0.1 * jax.random.normal(key_list[10], (D,), jnp.float32), 0.5, 1.5).astype(jnp.bfloat16)
    second_shift = noise(key_list[11], (D,), 0.3, 3.0, ((0, 32),))
    up_weight = noise(key_list[12], (FF, D), D ** -0.5, 0.21875, ((0, 8), (1, 4)))
    up_bias = noise(key_list[13], (FF,), 0.3, 3.0, ((0, 32),))
    down_weight = noise(key_list[14], (FF, D), FF ** -0.5, 0.109375, ((0, 8), (1, 4)))
    down_bias = noise(key_list[15], (D,), 0.3, 3.0, ((0, 32),))
    return dict(patches=patches, keep_order=keep_order, cotangent=cotangent, first_gain=first_gain, first_shift=first_shift, project_in=project_in, query_bias=query_bias, value_bias=value_bias, project_out=project_out, output_bias=output_bias, second_gain=second_gain, second_shift=second_shift, up_weight=up_weight, up_bias=up_bias, down_weight=down_weight, down_bias=down_bias)


@jax.custom_vjp
def low(v):
    return lax.optimization_barrier(v.astype(jnp.bfloat16)).astype(jnp.float32)

@jax.custom_vjp
def low_back(v):
    return v

def low_keep(v):
    return (low(v), None)

def low_pass(kept, grad):
    return (grad,)

def back_keep(v):
    return (v, None)

def back_low(kept, grad):
    return (low(grad),)
low.defvjp(low_keep, low_pass)
low_back.defvjp(back_keep, back_low)
EPSILON = 1e-06
HIGH = lax.Precision.HIGHEST

def layer_norm(values, gain, shift):
    mean = lax.optimization_barrier(jnp.mean(values, axis=-1, keepdims=True))
    centred = values - mean
    spread = lax.optimization_barrier(jnp.mean(centred * centred, axis=-1, keepdims=True))
    return centred * lax.rsqrt(spread + EPSILON) * gain + shift

def block_forward(params, patches, picks):
    first_gain, first_shift, project_in, query_bias, value_bias, project_out, output_bias, second_gain, second_shift, up_weight, up_bias, down_weight, down_bias = params
    count = patches.shape[0]
    inputs = jnp.take_along_axis(patches, picks[:, :, None], axis=1)
    normed_one = low(layer_norm(inputs, first_gain, first_shift))
    joint_shift = jnp.concatenate([query_bias, jnp.zeros_like(query_bias), value_bias])
    mixed = jnp.einsum('bnd,de->bne', normed_one, project_in, precision=HIGH) + joint_shift
    mixed = low(low_back(mixed)).reshape(count, VIS, 3, HEADS, HEAD_DIM)
    query = mixed[:, :, 0]
    keys = mixed[:, :, 1]
    values = mixed[:, :, 2]
    scores = low_back(jnp.einsum('bqhe,bkhe->bhqk', query, keys, precision=HIGH) * HEAD_DIM ** (-0.5))
    probs = jax.nn.softmax(scores, axis=-1)
    attended = jnp.einsum('bhqk,bkhe->bqhe', low(probs), values, precision=HIGH).reshape(count, VIS, D)
    attended = low_back(low(attended))
    branch = jnp.einsum('bnd,de->bne', attended, project_out, precision=HIGH) + output_bias
    middle = inputs + low_back(branch)
    normed_two = low(layer_norm(middle, second_gain, second_shift))
    before = low_back(jnp.einsum('bnd,fd->bnf', normed_two, up_weight, precision=HIGH) + up_bias)
    activated = low(jax.nn.gelu(before, approximate=False))
    feed = jnp.einsum('bnf,fd->bnd', activated, down_weight, precision=HIGH) + down_bias
    return middle + feed

def reference(patches, keep_order, cotangent, first_gain, first_shift, project_in, query_bias, value_bias, project_out, output_bias, second_gain, second_shift, up_weight, up_bias, down_weight, down_bias):
    params = tuple((piece.astype(jnp.float32) for piece in (first_gain, first_shift, project_in, query_bias, value_bias, project_out, output_bias, second_gain, second_shift, up_weight, up_bias, down_weight, down_bias)))
    block = IMG_DEV * N_NARROW
    steps = patches.shape[0] // block

    def one_block(totals, index):
        start = (index * block).astype(jnp.int32)
        patch_block = lax.dynamic_slice_in_dim(patches, start, block, 0).astype(jnp.float32)
        pick_block = lax.dynamic_slice_in_dim(keep_order, start, block, 0)[:, :VIS].astype(jnp.int32)
        grad_block = lax.dynamic_slice_in_dim(cotangent, start, block, 0).astype(jnp.float32)

        def forward(param_list, patch_values):
            return block_forward(param_list, patch_values, pick_block)
        output, pull = jax.vjp(forward, params, patch_block)
        param_grads, patch_grads = pull(grad_block)
        totals = jax.tree.map(jnp.add, totals, param_grads)
        return (totals, (output.astype(jnp.bfloat16), patch_grads))
    zeros = jax.tree.map(jnp.zeros_like, params)
    totals, (outputs, patch_grads) = lax.scan(one_block, zeros, jnp.arange(steps, dtype=jnp.int32))
    result = outputs.reshape(patches.shape[0], VIS, D)
    patch_grad = patch_grads.reshape(patches.shape[0], PATCHES, D)
    return (result, patch_grad, totals[0], totals[1], totals[2], totals[3], totals[4], totals[5], totals[6], totals[7], totals[8], totals[9], totals[10], totals[11], totals[12])
```

```python
import functools

import jax
import jax.numpy as jnp
from jax import lax
from jax.experimental import pallas as pl
from jax.experimental.pallas import tpu as pltpu
from jax.sharding import PartitionSpec as P

D = 768
HEADS = 12
HEAD_DIM = 64
PATCHES = 196
VIS = 49
PAD = 64
SIDE = 4
WIDTH = SIDE * HEAD_DIM
GROUPS = HEADS // SIDE
TOGETHER = 8
HIDDEN = 512
EPSILON = 1e-06
SCALE = HEAD_DIM ** (-0.5)
F32 = jnp.float32
BF16 = jnp.bfloat16
AXES = ("wide", "narrow")
G1, B1, QB, VB, OB, G2, B2, DB = range(8)


def params(**more):
    return pltpu.CompilerParams(vmem_limit_bytes=60 * 1024 * 1024, **more)


def mm(left, right):
    return jnp.dot(left, right, preferred_element_type=F32)


def mm_t(left, right):
    return lax.dot_general(left, right, (((1,), (1,)), ((), ())), preferred_element_type=F32)


def t_mm(left, right):
    return lax.dot_general(left, right, (((0,), (0,)), ((), ())), preferred_element_type=F32)


def norm_parts(values):
    mean = jnp.mean(values, axis=-1, keepdims=True)
    centred = values - mean
    spread = jnp.mean(centred * centred, axis=-1, keepdims=True)
    scale = lax.rsqrt(spread + EPSILON)
    return centred * scale, scale


def norm_back(grad, gain, normed, scale):
    pulled = grad * gain
    inner = jnp.mean(pulled * normed, axis=-1, keepdims=True)
    return scale * (pulled - jnp.mean(pulled, axis=-1, keepdims=True) - normed * inner)


def sum_rows(values):
    return jnp.sum(values, axis=0, keepdims=True)


def load_wide(ref, rows=slice(None)):
    return jnp.concatenate([ref[k, rows, :] for k in range(D // 128)], axis=1)


def store_wide(ref, rows, values):
    for k in range(D // 128):
        ref[k, rows, :] = values[:, k * 128 : (k + 1) * 128]


def heads_apart(block):
    lane = lax.broadcasted_iota(jnp.int32, block.shape, 1) // HEAD_DIM
    zero = jnp.zeros_like(block)
    return jnp.concatenate([jnp.where(lane == h, block, zero) for h in range(SIDE)], axis=0)


def heads_together(product):
    lane = lax.broadcasted_iota(jnp.int32, (HEAD_DIM, WIDTH), 1) // HEAD_DIM
    out = jnp.zeros((HEAD_DIM, WIDTH), F32)
    for h in range(SIDE):
        out = jnp.where(lane == h, product[h * HEAD_DIM : (h + 1) * HEAD_DIM], out)
    return out


def picked(order):
    lane = lax.broadcasted_iota(jnp.int32, (1, PAD), 1)
    order = jnp.where(lane < VIS, order, -1)
    row = lax.broadcasted_iota(jnp.int32, (PATCHES, PAD), 0)
    return jnp.where(row == order, 1.0, 0.0).astype(BF16)


LINE = 4
BLOCK = 128
MESH = pl.DeviceIdType.MESH


def place():
    wide, narrow = lax.axis_index("wide"), lax.axis_index("narrow")
    return wide // 2, wide % 2, narrow // 2, narrow % 2


def device(z, y, x, c):
    return (2 * z + y, 2 * x + c)


def greet():
    z, y, x, c = place()
    barrier = pltpu.get_barrier_semaphore()
    peers = [device((z + k) % LINE, y, x, c) for k in range(1, LINE)]
    peers += [device(z, 1 - y, x, c), device(z, y, 1 - x, c), device(z, y, x, 1 - c)]
    for peer in peers:
        pl.semaphore_signal(barrier, inc=1, device_id=peer, device_id_type=MESH)
    pl.semaphore_wait(barrier, len(peers))


def remote(src, dst, send, recv, peer):
    return pltpu.make_async_remote_copy(
        src_ref=src, dst_ref=dst, send_sem=send, recv_sem=recv, device_id=peer, device_id_type=MESH
    )


class Gather:
    COPIES = 17

    def __init__(self, src, slot, x_first, halves, send, recv, own):
        self.src, self.slot, self.x_first, self.halves = src, slot, x_first, halves
        self.send, self.recv, self.own = send, recv, own
        self.z, self.y, self.x, self.c = place()

    def flip(self, z, first, second):
        y, x = self.y, self.x
        if first if self.x_first else second:
            x = 1 - x
        if second if self.x_first else first:
            y = 1 - y
        return z, y, x

    def line(self, k):
        return (self.z - k) % LINE

    def copy(self, at, src, dst, peer):
        return remote(src, dst, self.send.at[at], self.recv.at[at], peer)

    def to_z(self, k):
        peer = device((self.z + k) % LINE, self.y, self.x, self.c)
        return self.copy(k - 1, self.src, self.slot(self.z, self.y, self.x), peer)

    def to_first(self, k):
        slot = self.slot(self.line(k), self.y, self.x)
        peer = device(*self.flip(self.z, True, False), self.c)
        return self.copy(3 + k, self.src if k == 0 else slot, slot, peer)

    def to_second(self, k):
        slot = self.slot(self.line(k), self.y, self.x)
        peer = device(*self.flip(self.z, False, True), self.c)
        return self.copy(7 + k, self.src if k == 0 else slot, slot, peer)

    def on_to_second(self, k):
        slot = self.slot(*self.flip(self.line(k), True, False))
        peer = device(*self.flip(self.z, False, True), self.c)
        return self.copy(11 + k, slot, slot, peer)

    def to_core(self, j, c=None):
        part = self.halves(self.c if c is None else c)[j]
        return self.copy(15 + j, part, part, device(self.z, self.y, self.x, 1 - self.c))

    def keep(self):
        return pltpu.make_async_copy(self.src, self.slot(self.z, self.y, self.x), self.own)

    def arrived(self, at, z, first, second):
        slot = self.slot(*self.flip(z, first, second))
        self.copy(at, slot, slot, device(self.z, self.y, self.x, 1 - self.c)).wait_recv()

    def start(self):
        self.keep().start()
        for k in range(1, LINE):
            self.to_z(k).start()
        self.to_first(0).start()
        self.to_second(0).start()

    def first(self):
        for k in range(1, LINE):
            self.arrived(k - 1, self.line(k), False, False)
            self.to_first(k).start()
            self.to_second(k).start()

    def second(self):
        for k in range(LINE):
            self.arrived(3 + k, self.line(k), True, False)
            self.on_to_second(k).start()

    def core(self):
        for k in range(LINE):
            self.arrived(7 + k, self.line(k), False, True)
            self.arrived(11 + k, self.line(k), True, True)
        self.keep().wait()
        for j in range(len(self.halves(self.c))):
            self.to_core(j).start()

    def finish(self):
        for j in range(len(self.halves(self.c))):
            self.to_core(j, 1 - self.c).wait_recv()
        for k in range(1, LINE):
            self.to_z(k).wait_send()
        for k in range(LINE):
            self.to_first(k).wait_send()
            self.to_second(k).wait_send()
            self.on_to_second(k).wait_send()
        for j in range(len(self.halves(self.c))):
            self.to_core(j).wait_send()


def rows_of(start, size):
    return pl.ds(pl.multiple_of(start, size), size)


def pick_step(order_ref, patches_ref, out_ref, wide_ref):
    values = patches_ref[...].astype(F32).reshape(PATCHES * TOGETHER, D)
    store_wide(wide_ref, slice(None), values)
    for j in range(TOGETHER):
        hot = picked(order_ref[j, :, :PAD])
        own = load_wide(wide_ref, pl.ds(j, PATCHES, stride=TOGETHER)).astype(BF16)
        out_ref[j * PAD : (j + 1) * PAD, :] = t_mm(hot, own).astype(BF16)


PICK_IN = [
    pl.BlockSpec((TOGETHER, 1, 128), lambda i: (i, 0, 0)),
    pl.BlockSpec((PATCHES, TOGETHER, D), lambda i: (0, i, 0)),
]
PICK_OUT = pl.BlockSpec((TOGETHER * PAD, D), lambda i: (i, 0))
PICK_WIDE = pltpu.VMEM((D // 128, PATCHES * TOGETHER, 128), F32)


def pick(order, patches):
    images = order.shape[0]
    return pl.pallas_call(
        pick_step,
        grid=(images // TOGETHER,),
        in_specs=PICK_IN,
        out_specs=PICK_OUT,
        out_shape=jax.ShapeDtypeStruct((images * PAD, D), BF16),
        scratch_shapes=[PICK_WIDE],
        compiler_params=params(),
        name="pick",
    )(order, patches)


IN_HALF = 1280
OUT_HALF = 384
LANES = IN_HALF // 2


def pick_gather_kernel(order_ref, patches_ref, share_ref, x_ref, all_ref, piece_ref, wide_ref, other, own, send, recv, near):
    step = pl.program_id(0)
    z, y, x, c = place()
    rows = 24
    swap = remote(share_ref.at[1 - c], other, near.at[0], near.at[1], device(z, y, x, 1 - c))

    def item(j):
        def slot(z, y, x):
            at = rows_of(((2 * z + y) * 2 + x) * 2 * rows, 2 * rows)
            return all_ref.at[at, rows_of(c * IN_HALF + j * LANES, LANES)]

        def halves(c):
            return [all_ref.at[:, rows_of(c * IN_HALF + j * LANES, LANES)]]

        return Gather(own.at[j], slot, j == 0, halves, send.at[j], recv.at[j], near.at[2 + j])

    items = [item(0), item(1)]

    @pl.when(step == 0)
    def _():
        greet()
        swap.start()

    pick_step(order_ref, patches_ref, x_ref, wide_ref)

    @pl.when(step == 0)
    def _():
        swap.wait()
        mine = share_ref[c].astype(F32)[:rows]
        theirs = other[...].astype(F32)[:rows]
        top = jnp.where(c == 0, mine, theirs)
        low = jnp.where(c == 0, theirs, mine)
        piece = jnp.concatenate([top, low], axis=0).astype(BF16)
        own[0] = piece[:, :LANES]
        own[1] = piece[:, LANES:IN_HALF]
        piece_ref[...] = piece[:, IN_HALF:]
        for one in items:
            one.start()

    @pl.when(step == pl.num_programs(0) - 1)
    def _():
        for one in items:
            one.first()
        for one in items:
            one.second()
        for one in items:
            one.core()
        for one in items:
            one.finish()


def pick_gather(order, patches, share):
    images = order.shape[0]
    rows = 24
    return pl.pallas_call(
        pick_gather_kernel,
        grid=(images // TOGETHER,),
        in_specs=PICK_IN + [pl.BlockSpec(share.shape, lambda i: (0, 0, 0))],
        out_specs=[PICK_OUT, pl.BlockSpec(memory_space=pl.ANY), pl.BlockSpec((2 * rows, OUT_HALF), lambda i: (0, 0))],
        out_shape=[
            jax.ShapeDtypeStruct((images * PAD, D), BF16),
            jax.ShapeDtypeStruct((D, 2 * IN_HALF), BF16),
            jax.ShapeDtypeStruct((2 * rows, OUT_HALF), BF16),
        ],
        scratch_shapes=[
            PICK_WIDE,
            pltpu.VMEM(share.shape[1:], BF16),
            pltpu.VMEM((2, 2 * rows, LANES), BF16),
            pltpu.SemaphoreType.DMA((2, Gather.COPIES)),
            pltpu.SemaphoreType.DMA((2, Gather.COPIES)),
            pltpu.SemaphoreType.DMA((4,)),
        ],
        compiler_params=params(collective_id=1, has_side_effects=True),
        name="pick_gather",
    )(order, patches, share)


def scores_of(k4, q_apart):
    return mm_t(k4, q_apart) * SCALE


def attend_kernel(x_ref, wi_ref, vec_ref, mixed_ref, att_ref, total_ref):
    attend_step(x_ref[...], wi_ref, vec_ref, mixed_ref, att_ref, total_ref)


def attend_step(x, wi_ref, vec_ref, mixed_ref, att_ref, total_ref):
    normed, _ = norm_parts(x.astype(F32))
    low = (normed * vec_ref[G1 : G1 + 1, :] + vec_ref[B1 : B1 + 1, :]).astype(BF16)
    for part in range(3):
        cols = slice(part * D, (part + 1) * D)
        product = mm(low, wi_ref[:, cols])
        if part == 0:
            product = product + vec_ref[QB : QB + 1, :]
        if part == 2:
            product = product + vec_ref[VB : VB + 1, :]
        mixed_ref[:, cols] = product.astype(BF16)
    key_row = lax.broadcasted_iota(jnp.int32, (PAD, WIDTH), 0)
    for img in range(SIDE):
        rows = slice(img * PAD, (img + 1) * PAD)
        for g in range(GROUPS):
            q4 = mixed_ref[rows, g * WIDTH : (g + 1) * WIDTH]
            k4 = mixed_ref[rows, D + g * WIDTH : D + (g + 1) * WIDTH]
            v4 = mixed_ref[rows, 2 * D + g * WIDTH : 2 * D + (g + 1) * WIDTH]
            scores = jnp.where(key_row < VIS, scores_of(k4, heads_apart(q4)), -1e30)
            top = jnp.max(scores, axis=0, keepdims=True)
            raised = jnp.exp(scores - top)
            total = sum_rows(raised)
            weights = (raised * (1.0 / total)).astype(BF16)
            at = img * GROUPS + g
            total_ref[0, at : at + 1, :] = top + jnp.log(total)
            att = heads_together(t_mm(weights, v4))
            att_ref[rows, g * WIDTH : (g + 1) * WIDTH] = att.astype(BF16)


def attend(x, wi, vec):
    rows = x.shape[0]
    steps = rows // (SIDE * PAD)
    block = SIDE * PAD
    return pl.pallas_call(
        attend_kernel,
        grid=(steps,),
        in_specs=[
            pl.BlockSpec((block, D), lambda i: (i, 0)),
            pl.BlockSpec((D, 3 * D), lambda i: (0, 0)),
            pl.BlockSpec(vec.shape, lambda i: (0, 0)),
        ],
        out_specs=[
            pl.BlockSpec((block, 3 * D), lambda i: (i, 0)),
            pl.BlockSpec((block, D), lambda i: (i, 0)),
            pl.BlockSpec((1, 16, WIDTH), lambda i: (i, 0, 0)),
        ],
        out_shape=[
            jax.ShapeDtypeStruct((rows, 3 * D), BF16),
            jax.ShapeDtypeStruct((rows, D), BF16),
            jax.ShapeDtypeStruct((steps, 16, WIDTH), F32),
        ],
        compiler_params=params(),
        name="attend",
    )(x, wi, vec)


def gelu_both(x):
    bell = jnp.exp(-0.5 * x * x) * 0.3989422804014327
    below = 0.5 * (1.0 + lax.erf(x * 0.7071067811865476))
    return x * below, below + x * bell


def feed_start(x_ref, att_ref, cot_ref, wo_ref, vec_ref, sums_ref, middle, low, grad, low_t, grad_t, feed, back, act, inner):
    rows = cot_ref.shape[0]
    images = rows // VIS
    held = middle.shape[1]
    feed[...] = jnp.zeros_like(feed)
    back[...] = jnp.zeros_like(back)
    act[held:, :] = jnp.zeros((act.shape[0] - held, HIDDEN), BF16)
    inner[held:, :] = jnp.zeros((act.shape[0] - held, HIDDEN), BF16)
    middle[:, rows:, :] = jnp.zeros((D // 128, held - rows, 128), F32)
    for g in range(images // TOGETHER):
        at = slice(g * TOGETHER * PAD, (g + 1) * TOGETHER * PAD)
        branch = mm(att_ref[at, :], wo_ref[...]) + vec_ref[OB : OB + 1, :]
        mid = x_ref[at, :].astype(F32) + branch
        for j in range(TOGETHER):
            token = pl.ds(g * TOGETHER + j, VIS, stride=images)
            store_wide(middle, token, mid[j * PAD : j * PAD + VIS])
    grad[:rows, :] = cot_ref[...]
    grad[rows:, :] = jnp.zeros((held - rows, D), BF16)
    sums_ref[DB : DB + 1, :] = sum_rows(cot_ref[...].astype(F32))
    normed, _ = norm_parts(load_wide(middle))
    low[...] = (normed * vec_ref[G2 : G2 + 1, :] + vec_ref[B2 : B2 + 1, :]).astype(BF16)
    low_t[:, held:] = jnp.zeros((D, low_t.shape[1] - held), BF16)
    grad_t[:, held:] = jnp.zeros((D, low_t.shape[1] - held), BF16)
    low_t[:, :held] = low[...].T
    grad_t[:, :held] = grad[...].T


def feed_step(up, upb, down, upg_ref, downg_ref, upbg_ref, middle, low, grad, low_t, grad_t, feed, back, act, inner):
    half = low.shape[0] // 2
    upbg = jnp.zeros((1, HIDDEN), F32)
    for part in range(2):
        at = slice(part * half, (part + 1) * half)
        before = mm(low[at, :], up[...]) + upb
        hidden_grad = mm(grad[at, :], down[...])
        value, slope = gelu_both(before)
        act[at, :] = value.astype(BF16)
        before_grad = (hidden_grad * slope).astype(BF16)
        inner[at, :] = before_grad
        upbg = upbg + sum_rows(before_grad.astype(F32))
        feed[at, :] += mm_t(act[at, :], down[...])
        back[at, :] += mm_t(before_grad, up[...])
    upbg_ref[...] = upbg
    downg_ref[...] = mm(grad_t[...], act[...]).astype(BF16)
    upg_ref[...] = mm(low_t[...], inner[...]).astype(BF16)


def feed_end(vec_ref, result_ref, mg_ref, sums_ref, middle, low, grad, low_t, grad_t, feed, back, act, inner):
    rows = result_ref.shape[0]
    images = rows // VIS
    held = low.shape[0]
    mid = load_wide(middle)
    result = feed[...] + mid + vec_ref[DB : DB + 1, :]
    result_ref[...] = result[:rows].astype(BF16)
    normed, scale = norm_parts(mid)
    pull = back[...]
    sums_ref[G2 : G2 + 1, :] = sum_rows(pull * normed)
    sums_ref[B2 : B2 + 1, :] = sum_rows(pull)
    mid_grad = grad[...].astype(F32) + norm_back(pull, vec_ref[G2 : G2 + 1, :], normed, scale)
    real = lax.broadcasted_iota(jnp.int32, (held, 1), 0) < rows
    mid_grad = jnp.where(real, mid_grad, 0.0)
    sums_ref[OB : OB + 1, :] = sum_rows(mid_grad.astype(BF16).astype(F32))
    store_wide(middle, slice(None), mid_grad)
    for j in range(images):
        out = j * PAD
        token = pl.ds(j, VIS, stride=images)
        mg_ref[out : out + PAD, :] = jnp.zeros((PAD, D), F32)
        mg_ref[out : out + VIS, :] = load_wide(middle, token)


def feed_scratch(rows):
    held = -(-rows // 32) * 32
    deep = -(-rows // 256) * 256
    return [
        pltpu.VMEM((D // 128, held, 128), F32),
        pltpu.VMEM((held, D), BF16),
        pltpu.VMEM((held, D), BF16),
        pltpu.VMEM((D, deep), BF16),
        pltpu.VMEM((D, deep), BF16),
        pltpu.VMEM((held, D), F32),
        pltpu.VMEM((held, D), F32),
        pltpu.VMEM((deep, HIDDEN), BF16),
        pltpu.VMEM((deep, HIDDEN), BF16),
    ]


def feed_kernel(
    x_ref, att_ref, cot_ref, wo_ref, vec_ref, up_ref, upb_ref, down_ref,
    result_ref, mg_ref, upg_ref, downg_ref, upbg_ref, sums_ref, *scratch,
):
    step = pl.program_id(0)

    @pl.when(step == 0)
    def _():
        feed_start(x_ref, att_ref, cot_ref, wo_ref, vec_ref, sums_ref, *scratch)

    feed_step(up_ref, upb_ref[...], down_ref, upg_ref, downg_ref, upbg_ref, *scratch)

    @pl.when(step == pl.num_programs(0) - 1)
    def _():
        feed_end(vec_ref, result_ref, mg_ref, sums_ref, *scratch)


def feed_forward(x, att, cot, wo, vec, up, upb, down):
    rows = cot.shape[0]
    whole = lambda a: pl.BlockSpec(a.shape, lambda i, n=a.ndim: (0,) * n)
    ff = up.shape[1]
    hid = lambda r: pl.BlockSpec((r, HIDDEN), lambda i: (0, i))
    full = lambda s: pl.BlockSpec(s, lambda i, n=len(s): (0,) * n)
    return pl.pallas_call(
        feed_kernel,
        grid=(ff // HIDDEN,),
        in_specs=[whole(x), whole(att), whole(cot), whole(wo), whole(vec), hid(D), hid(1), hid(D)],
        out_specs=[full(cot.shape), full((x.shape[0], D)), hid(D), hid(D), hid(1), full((8, D))],
        out_shape=[
            jax.ShapeDtypeStruct(cot.shape, BF16),
            jax.ShapeDtypeStruct((x.shape[0], D), F32),
            jax.ShapeDtypeStruct((D, ff), BF16),
            jax.ShapeDtypeStruct((D, ff), BF16),
            jax.ShapeDtypeStruct((1, ff), F32),
            jax.ShapeDtypeStruct((8, D), F32),
        ],
        scratch_shapes=feed_scratch(rows),
        compiler_params=params(),
        name="feed_forward",
    )(x, att, cot, wo, vec, up, upb, down)


CHUNK = 1024
CHUNKS = 3


def forward_kernel(
    x_ref, wi_ref, cot_ref, upb_ref, piece_ref, up_own, down_own,
    mixed_ref, att_ref, total_ref, result_ref, mg_ref, upg_ref, downg_ref, upbg_ref, sums_ref, vec_ref, wo_ref,
    att_all, wo_all, up_all, down_all, send, recv, own, *scratch,
):
    step = pl.program_id(0)
    early = x_ref.shape[0] // (SIDE * PAD)
    z, y, x, c = place()
    features = D // 4

    def weight(j, src, dst, s, x_first):
        lanes = BLOCK
        def slot(z, y, x):
            rows = rows_of((2 * x + c) * features, features)
            return dst.at[rows, rows_of(s * CHUNK + y * HIDDEN + z * lanes, lanes)]

        def halves(c):
            return [dst.at[rows_of((2 * k + c) * features, features), pl.ds(s * CHUNK, CHUNK)] for k in range(2)]

        block = src.at[:, pl.ds(s * lanes, lanes)]
        return Gather(block, slot, x_first, halves, send.at[j], recv.at[j], own.at[j])

    def outward(j):
        def slot(z, y, x):
            return wo_all.at[rows_of(((2 * z + y) * 2 + x) * 48, 48), rows_of(c * OUT_HALF, OUT_HALF)]

        def halves(c):
            return [wo_all.at[:, rows_of(c * OUT_HALF, OUT_HALF)]]

        return Gather(piece_ref, slot, True, halves, send.at[j], recv.at[j], own.at[j])

    chunks = [
        [weight(2 * s, up_own, up_all, s, True), weight(2 * s + 1, down_own, down_all, s, False)]
        for s in range(CHUNKS)
    ]
    chunks.append([outward(2 * CHUNKS)])
    plan = {
        0: [("start", 0)],
        1: [("start", 3)],
        2: [("first", 0), ("start", 1)],
        3: [("second", 0), ("first", 3)],
        4: [("second", 3), ("first", 1), ("start", 2)],
        5: [("core", 0), ("core", 3), ("second", 1)],
        6: [("finish", 0), ("finish", 3)],
        7: [("first", 2), ("core", 1)],
        8: [("finish", 1), ("second", 2)],
        9: [("core", 2)],
        10: [("finish", 2)],
    }
    for at, acts in plan.items():

        @pl.when(step == at)
        def _(at=at, acts=acts):
            if at == 0:
                greet()
            for act, which in acts:
                for one in chunks[which]:
                    getattr(one, act)()

    @pl.when(step == 0)
    def _():
        vec_ref[...] = wi_ref[:, 3 * D : 3 * D + BLOCK].astype(F32).T[:16]

    @pl.when(step < early)
    def _():
        at = rows_of(step * SIDE * PAD, SIDE * PAD)
        attend_step(x_ref[at, :], wi_ref, vec_ref, mixed_ref, att_ref, total_ref)
        att_all[at, :] = att_ref[...]

    @pl.when(step == early)
    def _():
        wo_ref[...] = wo_all[...]
        feed_start(x_ref, att_all, cot_ref, wo_all, vec_ref, sums_ref, *scratch)

    @pl.when(step >= early)
    def _():
        at = rows_of((step - early) * HIDDEN, HIDDEN)
        feed_step(up_all.at[:, at], upb_ref[:, at], down_all.at[:, at], upg_ref, downg_ref, upbg_ref, *scratch)

    @pl.when(step == pl.num_programs(0) - 1)
    def _():
        feed_end(vec_ref, result_ref, mg_ref, sums_ref, *scratch)


def forward(x, wi, cot, upb, piece, up, down):
    rows = x.shape[0]
    block = SIDE * PAD
    early = rows // block
    ff = upb.shape[1]
    late = ff // HIDDEN
    whole = lambda a: pl.BlockSpec(a.shape, lambda i, n=a.ndim: (0,) * n)
    full = lambda s: pl.BlockSpec(s, lambda i, n=len(s): (0,) * n)
    before = lambda w: pl.BlockSpec((block, w), lambda i: (jnp.minimum(i, early - 1), 0))
    hid = lambda r: pl.BlockSpec((r, HIDDEN), lambda i: (0, jnp.maximum(i - early, 0)))
    here = pl.BlockSpec(memory_space=pl.ANY)
    shape = jax.ShapeDtypeStruct
    count = 2 * CHUNKS + 1
    return pl.pallas_call(
        forward_kernel,
        grid=(early + late,),
        in_specs=[whole(x), whole(wi), whole(cot), whole(upb), here, here, here],
        out_specs=[
            before(3 * D), before(D),
            pl.BlockSpec((1, 16, WIDTH), lambda i: (jnp.minimum(i, early - 1), 0, 0)),
            full(cot.shape), full((rows, D)), hid(D), hid(D), hid(1), full((8, D)), full((16, D)), full((D, D)),
        ],
        out_shape=[
            shape((rows, 3 * D), BF16), shape((rows, D), BF16), shape((early, 16, WIDTH), F32),
            shape(cot.shape, BF16), shape((rows, D), F32), shape((D, ff), BF16), shape((D, ff), BF16),
            shape((1, ff), F32), shape((8, D), F32), shape((16, D), F32), shape((D, D), BF16),
        ],
        scratch_shapes=[
            pltpu.VMEM((rows, D), BF16),
            pltpu.VMEM((D, D), BF16),
            pltpu.VMEM((D, ff), BF16),
            pltpu.VMEM((D, ff), BF16),
            pltpu.SemaphoreType.DMA((count, Gather.COPIES)),
            pltpu.SemaphoreType.DMA((count, Gather.COPIES)),
            pltpu.SemaphoreType.DMA((count,)),
        ] + feed_scratch(cot.shape[0]),
        compiler_params=params(collective_id=2, has_side_effects=True),
        name="forward",
    )(x, wi, cot, upb, piece, up, down)


def unattend_kernel(
    x_ref, mg_ref, mixed_ref, att_ref, total_ref, wi_ref, wo_ref, vec_ref,
    ig_ref, wig_ref, wog_ref, sums_ref, low_t, att_t, branch, mixed_grad,
):
    step = pl.program_id(0)
    block = SIDE * PAD

    @pl.when(step == 0)
    def _():
        sums_ref[...] = jnp.zeros_like(sums_ref)

    at_step = pl.ds(pl.multiple_of(step * block, block), block)
    gain = vec_ref[G1 : G1 + 1, :]
    normed, scale = norm_parts(x_ref[...].astype(F32))
    low = (normed * gain + vec_ref[B1 : B1 + 1, :]).astype(BF16)
    low_t[:, at_step] = low.T
    att_t[:, at_step] = att_ref[...].T
    low_mg = mg_ref[...].astype(BF16)
    branch[at_step, :] = low_mg
    att_grad = mm_t(low_mg, wo_ref[...]).astype(BF16)
    key_row = lax.broadcasted_iota(jnp.int32, (PAD, WIDTH), 0)
    for img in range(SIDE):
        rows = slice(img * PAD, (img + 1) * PAD)
        out_rows = pl.ds(pl.multiple_of(step * block + img * PAD, PAD), PAD)
        for g in range(GROUPS):
            cols = slice(g * WIDTH, (g + 1) * WIDTH)
            k_cols = slice(D + g * WIDTH, D + (g + 1) * WIDTH)
            v_cols = slice(2 * D + g * WIDTH, 2 * D + (g + 1) * WIDTH)
            k4 = mixed_ref[rows, k_cols]
            v4 = mixed_ref[rows, v_cols]
            q_apart = heads_apart(mixed_ref[rows, cols])
            a_apart = heads_apart(att_grad[rows, cols])
            at = img * GROUPS + g
            exact = jnp.exp(scores_of(k4, q_apart) - total_ref[0, at : at + 1, :])
            exact = jnp.where(key_row < VIS, exact, 0.0)
            pulled = mm_t(v4, a_apart)
            centre = sum_rows(exact * pulled)
            score_grad = (exact * (pulled - centre)).astype(BF16)
            q_grad = heads_together(t_mm(score_grad, k4)) * SCALE
            k_grad = mm(score_grad, q_apart) * SCALE
            v_grad = mm(exact.astype(BF16), a_apart)
            mixed_grad[out_rows, cols] = q_grad.astype(BF16)
            mixed_grad[out_rows, k_cols] = k_grad.astype(BF16)
            mixed_grad[out_rows, v_cols] = v_grad.astype(BF16)
    own = mixed_grad[at_step, :]
    sums_ref[QB : QB + 1, :] += sum_rows(own[:, :D].astype(F32))
    sums_ref[VB : VB + 1, :] += sum_rows(own[:, 2 * D :].astype(F32))
    pull = mm_t(own, wi_ref[...])
    sums_ref[G1 : G1 + 1, :] += sum_rows(pull * normed)
    sums_ref[B1 : B1 + 1, :] += sum_rows(pull)
    ig_ref[...] = mg_ref[...] + norm_back(pull, gain, normed, scale)

    @pl.when(step == pl.num_programs(0) - 1)
    def _():
        for part in range(3):
            cols = slice(part * D, (part + 1) * D)
            wig_ref[:, cols] = mm(low_t[...], mixed_grad[:, cols]).astype(BF16)
        wog_ref[...] = mm(att_t[...], branch[...]).astype(BF16)


def unattend(x, mg, mixed, att, totals, wi, wo, vec):
    rows = x.shape[0]
    block = SIDE * PAD
    row = lambda a: pl.BlockSpec((block, a.shape[1]), lambda i: (i, 0))
    whole = lambda s: pl.BlockSpec(s, lambda i: (0, 0))
    return pl.pallas_call(
        unattend_kernel,
        grid=(rows // block,),
        in_specs=[
            row(x), row(mg), row(mixed), row(att),
            pl.BlockSpec((1, 16, WIDTH), lambda i: (i, 0, 0)),
            whole(wi.shape), whole(wo.shape), whole(vec.shape),
        ],
        out_specs=[row(x), whole(wi.shape), whole(wo.shape), whole((8, D))],
        out_shape=[
            jax.ShapeDtypeStruct((rows, D), F32),
            jax.ShapeDtypeStruct(wi.shape, BF16),
            jax.ShapeDtypeStruct(wo.shape, BF16),
            jax.ShapeDtypeStruct((8, D), F32),
        ],
        scratch_shapes=[
            pltpu.VMEM((D, rows), BF16),
            pltpu.VMEM((D, rows), BF16),
            pltpu.VMEM((rows, D), BF16),
            pltpu.VMEM((rows, 3 * D), BF16),
        ],
        compiler_params=params(),
        name="unattend",
    )(x, mg, mixed, att, totals, wi, wo, vec)


def spread_kernel(order_ref, ig_ref, out_ref):
    blocks = D // 128
    rows = out_ref.reshape(PATCHES * blocks * TOGETHER, 128)
    for j in range(TOGETHER):
        hot = picked(order_ref[j, :, :PAD])
        ig = ig_ref[j * PAD : (j + 1) * PAD, :]
        high = ig.astype(BF16)
        rest = (ig - high.astype(F32)).astype(BF16)
        both = jnp.concatenate([high, rest], axis=0)
        own = mm(jnp.concatenate([hot, hot], axis=1), both)
        for k in range(blocks):
            at = pl.ds(k * TOGETHER + j, PATCHES, stride=blocks * TOGETHER)
            rows[at, :] = own[:, k * 128 : (k + 1) * 128]


def spread(order, ig):
    images = order.shape[0]
    return pl.pallas_call(
        spread_kernel,
        grid=(images // TOGETHER,),
        in_specs=[
            pl.BlockSpec((TOGETHER, 1, 128), lambda i: (i, 0, 0)),
            pl.BlockSpec((TOGETHER * PAD, D), lambda i: (i, 0)),
        ],
        out_specs=pl.BlockSpec((PATCHES, 1, D // 128, TOGETHER, 128), lambda i: (0, i, 0, 0, 0)),
        out_shape=jax.ShapeDtypeStruct((PATCHES, images // TOGETHER, D // 128, TOGETHER, 128), F32),
        compiler_params=params(),
        name="spread",
    )(order, ig)


def local(
    patches, keep_order, cotangent, first_gain, first_shift, project_in, query_bias, value_bias,
    project_out, output_bias, second_gain, second_shift, up_weight, up_bias, down_weight, down_bias,
):
    rows_own = project_in.shape[0]
    hidden_own = up_bias.shape[0]
    images = patches.shape[0]
    wide, narrow = lax.axis_size("wide"), lax.axis_size("narrow")
    vectors = [first_gain, first_shift, query_bias, value_bias, output_bias, second_gain, second_shift, down_bias]
    order = keep_order[:, None, :128]
    patches = patches.transpose(1, 0, 2)
    cot = cotangent.transpose(1, 0, 2).reshape(VIS * images, D)
    if (wide, narrow) == (8, 4):
        columns = [v[:, None] for v in vectors] + [up_bias.reshape(4, rows_own).T]
        held = 3 * D + 12
        share = jnp.concatenate([project_in] + columns + [jnp.zeros((rows_own, 2 * IN_HALF - held), BF16)], axis=1)
        share = jnp.stack(
            [
                jnp.concatenate([share[:, c * IN_HALF :][:, :IN_HALF], project_out[:, c * OUT_HALF :][:, :OUT_HALF]], axis=1)
                for c in range(2)
            ]
        )
        share = jnp.pad(share, ((0, 0), (0, 32 - rows_own), (0, 0)))
        x, wi, piece = pick_gather(order, patches, share)
        upb = wi[:, 3 * D + 8 : 3 * D + 12].reshape(4, 2, 4, rows_own, 4)
        upb = upb.transpose(0, 1, 2, 4, 3).reshape(4, 2, CHUNKS, BLOCK).transpose(2, 1, 0, 3)
        upb = upb.reshape(1, -1).astype(F32)
        mixed, att, totals, result, mg, upg, downg, upbg, sums_two, vec, wo = forward(
            x, wi, cot, upb, piece, up_weight.T, down_weight.T
        )
        mend = lambda g: g.reshape(-1, CHUNKS, 2, 4, BLOCK).transpose(0, 3, 2, 1, 4).reshape(-1, CHUNKS * CHUNK)
        upg, downg, upbg = mend(upg), mend(downg), mend(upbg)
        wi = wi[:, : 3 * D]
    else:
        share = jnp.concatenate([jnp.stack(vectors).reshape(1, -1), up_bias.reshape(1, -1)], axis=1)
        shares = lax.all_gather(share, AXES, axis=0, tiled=True)
        vec = shares[:, : 8 * rows_own].reshape(-1, 8, rows_own).transpose(1, 0, 2).reshape(8, D)
        vec = jnp.pad(vec.astype(F32), ((0, 8), (0, 0)))
        upb = shares[:, 8 * rows_own :].reshape(1, -1).astype(F32)
        wi = lax.all_gather(project_in, AXES, axis=0, tiled=True)
        wo = lax.all_gather(project_out, AXES, axis=0, tiled=True)
        ffw = jnp.stack([up_weight.T, down_weight.T])
        ffw = lax.all_gather(ffw, "narrow", axis=1, tiled=True)
        ffw = lax.all_gather(ffw, "wide", axis=2, tiled=True)
        x = pick(order, patches)
        mixed, att, totals = attend(x, wi, vec)
        result, mg, upg, downg, upbg, sums_two = feed_forward(x, att, cot, wo, vec, ffw[0], upb, ffw[1])
    ig, wig, wog, sums_one = unattend(x, mg, mixed, att, totals, wi, wo, vec)
    patch_grad = spread(order, ig).transpose(1, 3, 0, 2, 4).reshape(images, PATCHES, D)
    result = result.reshape(VIS, images, D).transpose(1, 0, 2)

    ffg = jnp.stack([upg, downg])
    ffg = lax.psum_scatter(ffg, "wide", scatter_dimension=2, tiled=True)
    ffg = lax.psum_scatter(ffg, "narrow", scatter_dimension=1, tiled=True).astype(F32)
    wig = lax.psum_scatter(wig, AXES, scatter_dimension=0, tiled=True).astype(F32)
    wog = lax.psum_scatter(wog, AXES, scatter_dimension=0, tiled=True).astype(F32)
    picks = [sums_one[G1], sums_one[B1], sums_one[QB], sums_one[VB]]
    picks += [sums_two[OB], sums_two[G2], sums_two[B2], sums_two[DB]]
    parts = jnp.stack(picks).reshape(8, -1, rows_own).transpose(1, 0, 2).reshape(-1, 8 * rows_own)
    parts = jnp.concatenate([parts, upbg.reshape(-1, hidden_own)], axis=1)
    own = lax.psum_scatter(parts, AXES, scatter_dimension=0, tiled=True)[0]
    s = [own[k * rows_own : (k + 1) * rows_own] for k in range(8)]
    return (
        result, patch_grad, s[0], s[1], wig, s[2], s[3], wog, s[4], s[5], s[6],
        ffg[0].T, own[8 * rows_own :], ffg[1].T, s[7],
    )


def solution(mesh):
    both = P(AXES)
    rows = P(AXES, None)
    cube = P(AXES, None, None)
    tile = P("wide", "narrow")
    return jax.shard_map(
        local,
        mesh=mesh,
        in_specs=(
            cube, rows, cube, both, both, rows, both, both, rows, both, both, both, tile, both, tile, both,
        ),
        out_specs=(
            cube, cube, both, both, rows, both, both, rows, both, both, both, tile, both, tile, both,
        ),
        check_vma=False,
    )
```

```python
import functools

import jax
import jax.numpy as jnp
from jax import lax
from jax.experimental import pallas as pl
from jax.experimental.pallas import tpu as pltpu
from jax.sharding import PartitionSpec as P

D = 768
HEADS = 12
HEAD_DIM = 64
PATCHES = 196
VIS = 49
PAD = 64
SIDE = 4
WIDTH = SIDE * HEAD_DIM
GROUPS = HEADS // SIDE
TOGETHER = 8
HIDDEN = 512
EPSILON = 1e-06
SCALE = HEAD_DIM ** (-0.5)
F32 = jnp.float32
BF16 = jnp.bfloat16
AXES = ("wide", "narrow")
G1, B1, QB, VB, OB, G2, B2, DB = range(8)


def params(**more):
    return pltpu.CompilerParams(vmem_limit_bytes=60 * 1024 * 1024, **more)


def mm(left, right):
    return jnp.dot(left, right, preferred_element_type=F32)


def mm_t(left, right):
    return lax.dot_general(left, right, (((1,), (1,)), ((), ())), preferred_element_type=F32)


def t_mm(left, right):
    return lax.dot_general(left, right, (((0,), (0,)), ((), ())), preferred_element_type=F32)


def norm_parts(values):
    mean = jnp.mean(values, axis=-1, keepdims=True)
    centred = values - mean
    spread = jnp.mean(centred * centred, axis=-1, keepdims=True)
    scale = lax.rsqrt(spread + EPSILON)
    return centred * scale, scale


def norm_back(grad, gain, normed, scale):
    pulled = grad * gain
    inner = jnp.mean(pulled * normed, axis=-1, keepdims=True)
    return scale * (pulled - jnp.mean(pulled, axis=-1, keepdims=True) - normed * inner)


def sum_rows(values):
    return jnp.sum(values, axis=0, keepdims=True)


def load_wide(ref, rows=slice(None)):
    return jnp.concatenate([ref[k, rows, :] for k in range(D // 128)], axis=1)


def store_wide(ref, rows, values):
    for k in range(D // 128):
        ref[k, rows, :] = values[:, k * 128 : (k + 1) * 128]


def heads_apart(block):
    lane = lax.broadcasted_iota(jnp.int32, block.shape, 1) // HEAD_DIM
    zero = jnp.zeros_like(block)
    return jnp.concatenate([jnp.where(lane == h, block, zero) for h in range(SIDE)], axis=0)


def heads_together(product):
    lane = lax.broadcasted_iota(jnp.int32, (HEAD_DIM, WIDTH), 1) // HEAD_DIM
    out = jnp.zeros((HEAD_DIM, WIDTH), F32)
    for h in range(SIDE):
        out = jnp.where(lane == h, product[h * HEAD_DIM : (h + 1) * HEAD_DIM], out)
    return out


def picked(order):
    lane = lax.broadcasted_iota(jnp.int32, (1, PAD), 1)
    order = jnp.where(lane < VIS, order, -1)
    row = lax.broadcasted_iota(jnp.int32, (PATCHES, PAD), 0)
    return jnp.where(row == order, 1.0, 0.0).astype(BF16)


LINE = 4
BLOCK = 128
MESH = pl.DeviceIdType.MESH


def place():
    wide, narrow = lax.axis_index("wide"), lax.axis_index("narrow")
    return wide // 2, wide % 2, narrow // 2, narrow % 2


def device(z, y, x, c):
    return (2 * z + y, 2 * x + c)


def greet():
    z, y, x, c = place()
    barrier = pltpu.get_barrier_semaphore()
    peers = [device((z + k) % LINE, y, x, c) for k in range(1, LINE)]
    peers += [device(z, 1 - y, x, c), device(z, y, 1 - x, c), device(z, y, x, 1 - c)]
    for peer in peers:
        pl.semaphore_signal(barrier, inc=1, device_id=peer, device_id_type=MESH)
    pl.semaphore_wait(barrier, len(peers))


def remote(src, dst, send, recv, peer):
    return pltpu.make_async_remote_copy(
        src_ref=src, dst_ref=dst, send_sem=send, recv_sem=recv, device_id=peer, device_id_type=MESH
    )


class Gather:
    COPIES = 17

    def __init__(self, src, slot, x_first, halves, send, recv, own):
        self.src, self.slot, self.x_first, self.halves = src, slot, x_first, halves
        self.send, self.recv, self.own = send, recv, own
        self.z, self.y, self.x, self.c = place()

    def flip(self, z, first, second):
        y, x = self.y, self.x
        if first if self.x_first else second:
            x = 1 - x
        if second if self.x_first else first:
            y = 1 - y
        return z, y, x

    def line(self, k):
        return (self.z - k) % LINE

    def copy(self, at, src, dst, peer):
        return remote(src, dst, self.send.at[at], self.recv.at[at], peer)

    def to_z(self, k):
        peer = device((self.z + k) % LINE, self.y, self.x, self.c)
        return self.copy(k - 1, self.src, self.slot(self.z, self.y, self.x), peer)

    def to_first(self, k):
        slot = self.slot(self.line(k), self.y, self.x)
        peer = device(*self.flip(self.z, True, False), self.c)
        return self.copy(3 + k, self.src if k == 0 else slot, slot, peer)

    def to_second(self, k):
        slot = self.slot(self.line(k), self.y, self.x)
        peer = device(*self.flip(self.z, False, True), self.c)
        return self.copy(7 + k, self.src if k == 0 else slot, slot, peer)

    def on_to_second(self, k):
        slot = self.slot(*self.flip(self.line(k), True, False))
        peer = device(*self.flip(self.z, False, True), self.c)
        return self.copy(11 + k, slot, slot, peer)

    def to_core(self, j, c=None):
        part = self.halves(self.c if c is None else c)[j]
        return self.copy(15 + j, part, part, device(self.z, self.y, self.x, 1 - self.c))

    def keep(self):
        return pltpu.make_async_copy(self.src, self.slot(self.z, self.y, self.x), self.own)

    def arrived(self, at, z, first, second):
        slot = self.slot(*self.flip(z, first, second))
        self.copy(at, slot, slot, device(self.z, self.y, self.x, 1 - self.c)).wait_recv()

    def start(self):
        self.keep().start()
        for k in range(1, LINE):
            self.to_z(k).start()
        self.to_first(0).start()
        self.to_second(0).start()

    def first(self):
        for k in range(1, LINE):
            self.arrived(k - 1, self.line(k), False, False)
            self.to_first(k).start()
            self.to_second(k).start()

    def second(self):
        for k in range(LINE):
            self.arrived(3 + k, self.line(k), True, False)
            self.on_to_second(k).start()

    def core(self):
        for k in range(LINE):
            self.arrived(7 + k, self.line(k), False, True)
            self.arrived(11 + k, self.line(k), True, True)
        self.keep().wait()
        for j in range(len(self.halves(self.c))):
            self.to_core(j).start()

    def finish(self):
        for j in range(len(self.halves(self.c))):
            self.to_core(j, 1 - self.c).wait_recv()
        for k in range(1, LINE):
            self.to_z(k).wait_send()
        for k in range(LINE):
            self.to_first(k).wait_send()
            self.to_second(k).wait_send()
            self.on_to_second(k).wait_send()
        for j in range(len(self.halves(self.c))):
            self.to_core(j).wait_send()


class Sum:
    COPIES = 8

    def __init__(self, take, own, theirs, ways, line, boxes, send, recv, near):
        self.take, self.own, self.theirs, self.ways, self.line, self.boxes = take, own, theirs, ways, line, boxes
        self.send, self.recv, self.near = send, recv, near
        self.z, self.y, self.x, self.c = place()

    def copy(self, at, src, dst, peer):
        return remote(src, dst, self.send.at[at], self.recv.at[at], device(*peer))

    def loads(self):
        return [pltpu.make_async_copy(src, dst, self.near.at[j]) for j, (src, dst) in enumerate(self.take(self.c, self.own))]

    def to_core(self):
        peer = (self.z, self.y, self.x, 1 - self.c)
        return [self.copy(6 + j, src, dst, peer) for j, (src, dst) in enumerate(self.take(1 - self.c, self.theirs))]

    def out(self, turn):
        goes, _, x_way = self.ways[turn]
        peer = (self.z, self.y, 1 - self.x, self.c) if x_way else (self.z, 1 - self.y, self.x, self.c)
        return self.copy(turn, goes, self.boxes[turn], peer)

    def to_z(self, k):
        to = (self.z + k) % LINE
        return self.copy(1 + k, self.line(to), self.boxes[2].at[k - 1], (to, self.y, self.x, self.c))

    def load(self):
        for one in self.loads() + self.to_core():
            one.start()

    def first(self):
        for one in self.loads():
            one.wait()
        for one in self.to_core():
            one.wait_recv()
        self.own[...] = self.own[...] + self.theirs[...]
        self.out(0).start()

    def second(self):
        self.out(0).wait_recv()
        stays = self.ways[0][1]
        stays[...] = stays[...] + self.boxes[0][...]
        self.out(1).start()

    def third(self):
        self.out(1).wait_recv()
        stays = self.ways[1][1]
        stays[...] = stays[...] + self.boxes[1][...]
        for k in range(1, LINE):
            self.to_z(k).start()

    def total(self):
        for k in range(1, LINE):
            self.to_z(k).wait_recv()
        out = self.line(self.z)[...].astype(F32)
        for k in range(LINE - 1):
            out = out + self.boxes[2][k].astype(F32)
        for one in self.to_core() + [self.out(0), self.out(1)] + [self.to_z(k) for k in range(1, LINE)]:
            one.wait_send()
        return out


def rows_of(start, size):
    return pl.ds(pl.multiple_of(start, size), size)


def pick_step(order_ref, patches_ref, out_ref, wide_ref):
    values = patches_ref[...].astype(F32).reshape(PATCHES * TOGETHER, D)
    store_wide(wide_ref, slice(None), values)
    for j in range(TOGETHER):
        hot = picked(order_ref[j : j + 1, :PAD])
        own = load_wide(wide_ref, pl.ds(j, PATCHES, stride=TOGETHER)).astype(BF16)
        out_ref[j * PAD : (j + 1) * PAD, :] = t_mm(hot, own).astype(BF16)


PICK_IN = [
    pl.BlockSpec((TOGETHER, PATCHES), lambda i: (i, 0)),
    pl.BlockSpec((PATCHES, TOGETHER, D), lambda i: (0, i, 0)),
]
PICK_OUT = pl.BlockSpec((TOGETHER * PAD, D), lambda i: (i, 0))
PICK_WIDE = pltpu.VMEM((D // 128, PATCHES * TOGETHER, 128), F32)


def pick(order, patches):
    images = order.shape[0]
    return pl.pallas_call(
        pick_step,
        grid=(images // TOGETHER,),
        in_specs=PICK_IN,
        out_specs=PICK_OUT,
        out_shape=jax.ShapeDtypeStruct((images * PAD, D), BF16),
        scratch_shapes=[PICK_WIDE],
        compiler_params=params(),
        name="pick",
    )(order, patches)


IN_HALF = 1280
OUT_HALF = 384
LANES = IN_HALF // 2


def pick_gather_kernel(
    order_ref, patches_ref, in_ref, out_ref, vectors_ref, x_ref, all_ref, piece_ref,
    wide_ref, share_ref, other, own, send, recv, near,
):
    step = pl.program_id(0)
    z, y, x, c = place()
    rows = 24
    swap = remote(share_ref.at[1 - c], other, near.at[0], near.at[1], device(z, y, x, 1 - c))

    def item(j):
        def slot(z, y, x):
            at = rows_of(((2 * z + y) * 2 + x) * 2 * rows, 2 * rows)
            return all_ref.at[at, rows_of(c * IN_HALF + j * LANES, LANES)]

        def halves(c):
            return [all_ref.at[:, rows_of(c * IN_HALF + j * LANES, LANES)]]

        return Gather(own.at[j], slot, j == 0, halves, send.at[j], recv.at[j], near.at[2 + j])

    items = [item(0), item(1)]

    @pl.when(step == 0)
    def _():
        vectors = vectors_ref[...].astype(F32)
        row = lax.broadcasted_iota(jnp.int32, (vectors.shape[0], BLOCK), 0)
        lane = lax.broadcasted_iota(jnp.int32, (vectors.shape[0], BLOCK), 1)
        columns = t_mm(vectors.astype(BF16), jnp.where(row == lane, 1.0, 0.0).astype(BF16)).astype(BF16)
        share_ref[...] = jnp.zeros_like(share_ref)
        share_ref[0, :rows, :IN_HALF] = in_ref[:, :IN_HALF]
        share_ref[0, :rows, IN_HALF:] = out_ref[:, :OUT_HALF]
        share_ref[1, :rows, : 3 * D - IN_HALF] = in_ref[:, IN_HALF:]
        share_ref[1, :rows, 3 * D - IN_HALF : 3 * D - IN_HALF + BLOCK] = columns
        share_ref[1, :rows, IN_HALF:] = out_ref[:, OUT_HALF:]
        greet()
        swap.start()

    pick_step(order_ref, patches_ref, x_ref, wide_ref)

    @pl.when(step == 0)
    def _():
        swap.wait()
        mine = share_ref[c].astype(F32)[:rows]
        theirs = other[...].astype(F32)[:rows]
        top = jnp.where(c == 0, mine, theirs)
        low = jnp.where(c == 0, theirs, mine)
        piece = jnp.concatenate([top, low], axis=0).astype(BF16)
        own[0] = piece[:, :LANES]
        own[1] = piece[:, LANES:IN_HALF]
        piece_ref[...] = piece[:, IN_HALF:]
        for one in items:
            one.start()

    @pl.when(step == pl.num_programs(0) - 1)
    def _():
        for one in items:
            one.first()
        for one in items:
            one.second()
        for one in items:
            one.core()
        for one in items:
            one.finish()


def pick_gather(order, patches, project_in, project_out, vectors):
    images = order.shape[0]
    rows = 24
    return pl.pallas_call(
        pick_gather_kernel,
        grid=(images // TOGETHER,),
        in_specs=PICK_IN + [pl.BlockSpec(a.shape, lambda i: (0, 0)) for a in (project_in, project_out, vectors)],
        out_specs=[PICK_OUT, pl.BlockSpec(memory_space=pl.ANY), pl.BlockSpec((2 * rows, OUT_HALF), lambda i: (0, 0))],
        out_shape=[
            jax.ShapeDtypeStruct((images * PAD, D), BF16),
            jax.ShapeDtypeStruct((D, 2 * IN_HALF), BF16),
            jax.ShapeDtypeStruct((2 * rows, OUT_HALF), BF16),
        ],
        scratch_shapes=[
            PICK_WIDE,
            pltpu.VMEM((2, 32, IN_HALF + OUT_HALF), BF16),
            pltpu.VMEM((32, IN_HALF + OUT_HALF), BF16),
            pltpu.VMEM((2, 2 * rows, LANES), BF16),
            pltpu.SemaphoreType.DMA((2, Gather.COPIES)),
            pltpu.SemaphoreType.DMA((2, Gather.COPIES)),
            pltpu.SemaphoreType.DMA((4,)),
        ],
        compiler_params=params(collective_id=1, has_side_effects=True),
        name="pick_gather",
    )(order, patches, project_in, project_out, vectors)


def scores_of(k4, q_apart):
    return mm_t(k4, q_apart) * SCALE


def attend_kernel(x_ref, wi_ref, vec_ref, mixed_ref, att_ref, total_ref):
    attend_step(x_ref[...], wi_ref, vec_ref, mixed_ref, att_ref, total_ref)


def attend_step(x, wi_ref, vec_ref, mixed_ref, att_ref, total_ref):
    normed, _ = norm_parts(x.astype(F32))
    low = (normed * vec_ref[G1 : G1 + 1, :] + vec_ref[B1 : B1 + 1, :]).astype(BF16)
    for part in range(3):
        cols = slice(part * D, (part + 1) * D)
        product = mm(low, wi_ref[:, cols])
        if part == 0:
            product = product + vec_ref[QB : QB + 1, :]
        if part == 2:
            product = product + vec_ref[VB : VB + 1, :]
        mixed_ref[:, cols] = product.astype(BF16)
    key_row = lax.broadcasted_iota(jnp.int32, (PAD, WIDTH), 0)
    for img in range(SIDE):
        rows = slice(img * PAD, (img + 1) * PAD)
        for g in range(GROUPS):
            q4 = mixed_ref[rows, g * WIDTH : (g + 1) * WIDTH]
            k4 = mixed_ref[rows, D + g * WIDTH : D + (g + 1) * WIDTH]
            v4 = mixed_ref[rows, 2 * D + g * WIDTH : 2 * D + (g + 1) * WIDTH]
            scores = jnp.where(key_row < VIS, scores_of(k4, heads_apart(q4)), -1e30)
            top = jnp.max(scores, axis=0, keepdims=True)
            raised = jnp.exp(scores - top)
            total = sum_rows(raised)
            weights = (raised * (1.0 / total)).astype(BF16)
            at = img * GROUPS + g
            total_ref[0, at : at + 1, :] = top + jnp.log(total)
            att = heads_together(t_mm(weights, v4))
            att_ref[rows, g * WIDTH : (g + 1) * WIDTH] = att.astype(BF16)


def attend(x, wi, vec):
    rows = x.shape[0]
    steps = rows // (SIDE * PAD)
    block = SIDE * PAD
    return pl.pallas_call(
        attend_kernel,
        grid=(steps,),
        in_specs=[
            pl.BlockSpec((block, D), lambda i: (i, 0)),
            pl.BlockSpec((D, 3 * D), lambda i: (0, 0)),
            pl.BlockSpec(vec.shape, lambda i: (0, 0)),
        ],
        out_specs=[
            pl.BlockSpec((block, 3 * D), lambda i: (i, 0)),
            pl.BlockSpec((block, D), lambda i: (i, 0)),
            pl.BlockSpec((1, 16, WIDTH), lambda i: (i, 0, 0)),
        ],
        out_shape=[
            jax.ShapeDtypeStruct((rows, 3 * D), BF16),
            jax.ShapeDtypeStruct((rows, D), BF16),
            jax.ShapeDtypeStruct((steps, 16, WIDTH), F32),
        ],
        compiler_params=params(),
        name="attend",
    )(x, wi, vec)


def gelu_both(x):
    bell = jnp.exp(-0.5 * x * x) * 0.3989422804014327
    below = 0.5 * (1.0 + lax.erf(x * 0.7071067811865476))
    return x * below, below + x * bell


def feed_start(x_ref, att_ref, cot_ref, wo_ref, vec_ref, sums_ref, middle, low, grad, low_t, grad_t, feed, back, act, inner):
    rows = cot_ref.shape[0]
    images = rows // VIS
    held = middle.shape[1]
    feed[...] = jnp.zeros_like(feed)
    back[...] = jnp.zeros_like(back)
    act[held:, :] = jnp.zeros((act.shape[0] - held, HIDDEN), BF16)
    inner[held:, :] = jnp.zeros((act.shape[0] - held, HIDDEN), BF16)
    middle[:, rows:, :] = jnp.zeros((D // 128, held - rows, 128), F32)
    for g in range(images // TOGETHER):
        at = slice(g * TOGETHER * PAD, (g + 1) * TOGETHER * PAD)
        branch = mm(att_ref[at, :], wo_ref[...]) + vec_ref[OB : OB + 1, :]
        mid = x_ref[at, :].astype(F32) + branch
        for j in range(TOGETHER):
            token = pl.ds(g * TOGETHER + j, VIS, stride=images)
            store_wide(middle, token, mid[j * PAD : j * PAD + VIS])
    grad[:rows, :] = cot_ref[...]
    grad[rows:, :] = jnp.zeros((held - rows, D), BF16)
    sums_ref[DB : DB + 1, :] = sum_rows(cot_ref[...].astype(F32))
    normed, _ = norm_parts(load_wide(middle))
    low[...] = (normed * vec_ref[G2 : G2 + 1, :] + vec_ref[B2 : B2 + 1, :]).astype(BF16)
    low_t[:, held:] = jnp.zeros((D, low_t.shape[1] - held), BF16)
    grad_t[:, held:] = jnp.zeros((D, low_t.shape[1] - held), BF16)
    low_t[:, :held] = low[...].T
    grad_t[:, :held] = grad[...].T


def feed_step(up, upb, down, upg_ref, downg_ref, upbg_ref, middle, low, grad, low_t, grad_t, feed, back, act, inner):
    half = low.shape[0] // 2
    upbg = jnp.zeros((1, HIDDEN), F32)
    for part in range(2):
        at = slice(part * half, (part + 1) * half)
        before = mm(low[at, :], up[...]) + upb
        hidden_grad = mm(grad[at, :], down[...])
        value, slope = gelu_both(before)
        act[at, :] = value.astype(BF16)
        before_grad = (hidden_grad * slope).astype(BF16)
        inner[at, :] = before_grad
        upbg = upbg + sum_rows(before_grad.astype(F32))
        feed[at, :] += mm_t(act[at, :], down[...])
        back[at, :] += mm_t(before_grad, up[...])
    upbg_ref[...] = upbg
    downg_ref[...] = mm(grad_t[...], act[...]).astype(BF16)
    upg_ref[...] = mm(low_t[...], inner[...]).astype(BF16)


def feed_end(vec_ref, result_ref, mg_ref, sums_ref, middle, low, grad, low_t, grad_t, feed, back, act, inner):
    rows = result_ref.shape[0]
    images = rows // VIS
    held = low.shape[0]
    mid = load_wide(middle)
    result = feed[...] + mid + vec_ref[DB : DB + 1, :]
    result_ref[...] = result[:rows].astype(BF16)
    normed, scale = norm_parts(mid)
    pull = back[...]
    sums_ref[G2 : G2 + 1, :] = sum_rows(pull * normed)
    sums_ref[B2 : B2 + 1, :] = sum_rows(pull)
    mid_grad = grad[...].astype(F32) + norm_back(pull, vec_ref[G2 : G2 + 1, :], normed, scale)
    real = lax.broadcasted_iota(jnp.int32, (held, 1), 0) < rows
    mid_grad = jnp.where(real, mid_grad, 0.0)
    sums_ref[OB : OB + 1, :] = sum_rows(mid_grad.astype(BF16).astype(F32))
    store_wide(middle, slice(None), mid_grad)
    for j in range(images):
        out = j * PAD
        token = pl.ds(j, VIS, stride=images)
        mg_ref[out : out + PAD, :] = jnp.zeros((PAD, D), F32)
        mg_ref[out : out + VIS, :] = load_wide(middle, token)


def feed_scratch(rows):
    held = -(-rows // 32) * 32
    deep = -(-rows // 256) * 256
    return [
        pltpu.VMEM((D // 128, held, 128), F32),
        pltpu.VMEM((held, D), BF16),
        pltpu.VMEM((held, D), BF16),
        pltpu.VMEM((D, deep), BF16),
        pltpu.VMEM((D, deep), BF16),
        pltpu.VMEM((held, D), F32),
        pltpu.VMEM((held, D), F32),
        pltpu.VMEM((deep, HIDDEN), BF16),
        pltpu.VMEM((deep, HIDDEN), BF16),
    ]


def feed_kernel(
    x_ref, att_ref, cot_ref, wo_ref, vec_ref, up_ref, upb_ref, down_ref,
    result_ref, mg_ref, upg_ref, downg_ref, upbg_ref, sums_ref, *scratch,
):
    step = pl.program_id(0)

    @pl.when(step == 0)
    def _():
        feed_start(x_ref, att_ref, cot_ref, wo_ref, vec_ref, sums_ref, *scratch)

    feed_step(up_ref, upb_ref[...], down_ref, upg_ref, downg_ref, upbg_ref, *scratch)

    @pl.when(step == pl.num_programs(0) - 1)
    def _():
        feed_end(vec_ref, result_ref, mg_ref, sums_ref, *scratch)


def feed_forward(x, att, cot, wo, vec, up, upb, down):
    rows = cot.shape[0]
    whole = lambda a: pl.BlockSpec(a.shape, lambda i, n=a.ndim: (0,) * n)
    ff = up.shape[1]
    hid = lambda r: pl.BlockSpec((r, HIDDEN), lambda i: (0, i))
    full = lambda s: pl.BlockSpec(s, lambda i, n=len(s): (0,) * n)
    return pl.pallas_call(
        feed_kernel,
        grid=(ff // HIDDEN,),
        in_specs=[whole(x), whole(att), whole(cot), whole(wo), whole(vec), hid(D), hid(1), hid(D)],
        out_specs=[full(cot.shape), full((x.shape[0], D)), hid(D), hid(D), hid(1), full((8, D))],
        out_shape=[
            jax.ShapeDtypeStruct(cot.shape, BF16),
            jax.ShapeDtypeStruct((x.shape[0], D), F32),
            jax.ShapeDtypeStruct((D, ff), BF16),
            jax.ShapeDtypeStruct((D, ff), BF16),
            jax.ShapeDtypeStruct((1, ff), F32),
            jax.ShapeDtypeStruct((8, D), F32),
        ],
        scratch_shapes=feed_scratch(rows),
        compiler_params=params(),
        name="feed_forward",
    )(x, att, cot, wo, vec, up, upb, down)


CHUNK = 1024
CHUNKS = 3


def forward_kernel(
    x_ref, wi_ref, cot_ref, upb_ref, piece_ref, up_own, down_own,
    mixed_ref, att_ref, total_ref, result_ref, mg_ref, upg_ref, downg_ref, upbg_ref, sums_ref, vec_ref, wo_ref,
    att_all, wo_all, up_all, down_all, send, recv, own, *scratch,
):
    step = pl.program_id(0)
    early = x_ref.shape[0] // (SIDE * PAD)
    z, y, x, c = place()
    features = D // 4

    def weight(j, src, dst, s, x_first):
        lanes = BLOCK
        def slot(z, y, x):
            rows = rows_of((2 * x + c) * features, features)
            return dst.at[rows, rows_of(s * CHUNK + y * HIDDEN + z * lanes, lanes)]

        def halves(c):
            return [dst.at[rows_of((2 * k + c) * features, features), pl.ds(s * CHUNK, CHUNK)] for k in range(2)]

        block = src.at[:, pl.ds(s * lanes, lanes)]
        return Gather(block, slot, x_first, halves, send.at[j], recv.at[j], own.at[j])

    def outward(j):
        def slot(z, y, x):
            return wo_all.at[rows_of(((2 * z + y) * 2 + x) * 48, 48), rows_of(c * OUT_HALF, OUT_HALF)]

        def halves(c):
            return [wo_all.at[:, rows_of(c * OUT_HALF, OUT_HALF)]]

        return Gather(piece_ref, slot, True, halves, send.at[j], recv.at[j], own.at[j])

    chunks = [
        [weight(2 * s, up_own, up_all, s, True), weight(2 * s + 1, down_own, down_all, s, False)]
        for s in range(CHUNKS)
    ]
    chunks.append([outward(2 * CHUNKS)])
    plan = {
        0: [("start", 0)],
        1: [("start", 3)],
        2: [("first", 0), ("start", 1)],
        3: [("second", 0), ("first", 3)],
        4: [("second", 3), ("first", 1), ("start", 2)],
        5: [("core", 0), ("core", 3), ("second", 1)],
        6: [("finish", 0), ("finish", 3)],
        7: [("first", 2), ("core", 1)],
        8: [("finish", 1), ("second", 2)],
        9: [("core", 2)],
        10: [("finish", 2)],
    }
    for at, acts in plan.items():

        @pl.when(step == at)
        def _(at=at, acts=acts):
            if at == 0:
                greet()
            for act, which in acts:
                for one in chunks[which]:
                    getattr(one, act)()

    @pl.when(step == 0)
    def _():
        vec_ref[...] = wi_ref[:, 3 * D : 3 * D + BLOCK].astype(F32).T[:16]

    @pl.when(step < early)
    def _():
        at = rows_of(step * SIDE * PAD, SIDE * PAD)
        attend_step(x_ref[at, :], wi_ref, vec_ref, mixed_ref, att_ref, total_ref)
        att_all[at, :] = att_ref[...]

    @pl.when(step == early)
    def _():
        wo_ref[...] = wo_all[...]
        feed_start(x_ref, att_all, cot_ref, wo_all, vec_ref, sums_ref, *scratch)

    @pl.when(step >= early)
    def _():
        at = rows_of((step - early) * HIDDEN, HIDDEN)
        feed_step(up_all.at[:, at], upb_ref[:, at], down_all.at[:, at], upg_ref, downg_ref, upbg_ref, *scratch)

    @pl.when(step == pl.num_programs(0) - 1)
    def _():
        feed_end(vec_ref, result_ref, mg_ref, sums_ref, *scratch)


def forward(x, wi, cot, upb, piece, up, down):
    rows = x.shape[0]
    block = SIDE * PAD
    early = rows // block
    ff = upb.shape[1]
    late = ff // HIDDEN
    whole = lambda a: pl.BlockSpec(a.shape, lambda i, n=a.ndim: (0,) * n)
    full = lambda s: pl.BlockSpec(s, lambda i, n=len(s): (0,) * n)
    before = lambda w: pl.BlockSpec((block, w), lambda i: (jnp.minimum(i, early - 1), 0))
    hid = lambda r: pl.BlockSpec((r, HIDDEN), lambda i: (0, jnp.maximum(i - early, 0)))
    here = pl.BlockSpec(memory_space=pl.ANY)
    shape = jax.ShapeDtypeStruct
    count = 2 * CHUNKS + 1
    return pl.pallas_call(
        forward_kernel,
        grid=(early + late,),
        in_specs=[whole(x), whole(wi), whole(cot), whole(upb), here, here, here],
        out_specs=[
            before(3 * D), before(D),
            pl.BlockSpec((1, 16, WIDTH), lambda i: (jnp.minimum(i, early - 1), 0, 0)),
            full(cot.shape), full((rows, D)), hid(D), hid(D), hid(1), full((8, D)), full((16, D)), full((D, D)),
        ],
        out_shape=[
            shape((rows, 3 * D), BF16), shape((rows, D), BF16), shape((early, 16, WIDTH), F32),
            shape(cot.shape, BF16), shape((rows, D), F32), shape((D, ff), BF16), shape((D, ff), BF16),
            shape((1, ff), F32), shape((8, D), F32), shape((16, D), F32), shape((D, D), BF16),
        ],
        scratch_shapes=[
            pltpu.VMEM((rows, D), BF16),
            pltpu.VMEM((D, D), BF16),
            pltpu.VMEM((D, ff), BF16),
            pltpu.VMEM((D, ff), BF16),
            pltpu.SemaphoreType.DMA((count, Gather.COPIES)),
            pltpu.SemaphoreType.DMA((count, Gather.COPIES)),
            pltpu.SemaphoreType.DMA((count,)),
        ] + feed_scratch(cot.shape[0]),
        compiler_params=params(collective_id=2, has_side_effects=True),
        name="forward",
    )(x, wi, cot, upb, piece, up, down)


def unattend_kernel(
    x_ref, mg_ref, mixed_ref, att_ref, total_ref, wo_ref, vec_ref, *refs
):
    step = pl.program_id(0)
    remote_sums = len(refs) > 8
    if remote_sums:
        upg_ref, downg_ref, mixed_grad, wig_ref, wog_ref, sums_ref, upf_ref, downf_ref, low_t, att_t, branch, *boxes = refs
        sums = feed_sums(upg_ref, downg_ref, *boxes)
        plan = {
            0: [("load", 0), ("load", 1), ("load", 2)],
            1: [("first", 0)],
            2: [("second", 0), ("first", 1)],
            3: [("third", 0), ("second", 1), ("first", 2)],
            4: [("total", 0), ("third", 1), ("second", 2)],
            5: [("total", 1), ("third", 2)],
        }

        def act(name, which):
            for one, out in zip(sums[which], (upf_ref, downf_ref)):
                value = getattr(one, name)()
                if name == "total":
                    out[:, which * BLOCK : (which + 1) * BLOCK] = value

        for at, acts in plan.items():

            @pl.when(step == at)
            def _(at=at, acts=acts):
                if at == 0:
                    greet()
                for name, which in acts:
                    act(name, which)
    else:
        mixed_grad, wig_ref, wog_ref, sums_ref, low_t, att_t, branch = refs
    block = SIDE * PAD

    @pl.when(step == 0)
    def _():
        sums_ref[...] = jnp.zeros_like(sums_ref)

    at_step = pl.ds(pl.multiple_of(step * block, block), block)
    gain = vec_ref[G1 : G1 + 1, :]
    normed, _ = norm_parts(x_ref[...].astype(F32))
    low = (normed * gain + vec_ref[B1 : B1 + 1, :]).astype(BF16)
    low_t[:, at_step] = low.T
    att_t[:, at_step] = att_ref[...].T
    low_mg = mg_ref[...].astype(BF16)
    branch[at_step, :] = low_mg
    att_grad = mm_t(low_mg, wo_ref[...]).astype(BF16)
    key_row = lax.broadcasted_iota(jnp.int32, (PAD, WIDTH), 0)
    for img in range(SIDE):
        rows = slice(img * PAD, (img + 1) * PAD)
        out_rows = pl.ds(pl.multiple_of(step * block + img * PAD, PAD), PAD)
        for g in range(GROUPS):
            cols = slice(g * WIDTH, (g + 1) * WIDTH)
            k_cols = slice(D + g * WIDTH, D + (g + 1) * WIDTH)
            v_cols = slice(2 * D + g * WIDTH, 2 * D + (g + 1) * WIDTH)
            k4 = mixed_ref[rows, k_cols]
            v4 = mixed_ref[rows, v_cols]
            q_apart = heads_apart(mixed_ref[rows, cols])
            a_apart = heads_apart(att_grad[rows, cols])
            at = img * GROUPS + g
            exact = jnp.exp(scores_of(k4, q_apart) - total_ref[0, at : at + 1, :])
            exact = jnp.where(key_row < VIS, exact, 0.0)
            pulled = mm_t(v4, a_apart)
            centre = sum_rows(exact * pulled)
            score_grad = (exact * (pulled - centre)).astype(BF16)
            q_grad = heads_together(t_mm(score_grad, k4)) * SCALE
            k_grad = mm(score_grad, q_apart) * SCALE
            v_grad = mm(exact.astype(BF16), a_apart)
            mixed_grad[out_rows, cols] = q_grad.astype(BF16)
            mixed_grad[out_rows, k_cols] = k_grad.astype(BF16)
            mixed_grad[out_rows, v_cols] = v_grad.astype(BF16)
    own = mixed_grad[at_step, :]
    sums_ref[QB : QB + 1, :] += sum_rows(own[:, :D].astype(F32))
    sums_ref[VB : VB + 1, :] += sum_rows(own[:, 2 * D :].astype(F32))

    @pl.when(step == pl.num_programs(0) - 1)
    def _():
        for part in range(3):
            cols = slice(part * D, (part + 1) * D)
            wig_ref[:, cols] = mm(low_t[...], mixed_grad[:, cols]).astype(BF16)
        wog_ref[...] = mm(att_t[...], branch[...]).astype(BF16)
        if remote_sums:
            act("total", CHUNKS - 1)


def feed_sums(upg_ref, downg_ref, own, theirs, box_y, box_x, box_two, box_z, send, recv, near):
    z, y, x, c = place()
    features = D // 4

    def one(s, which):
        grads = (upg_ref, downg_ref)[which]
        j = 2 * s + which

        def take(c, into):
            return [
                (grads.at[rows_of((2 * k + c) * features, features), pl.ds(s * CHUNK, CHUNK)], into.at[k])
                for k in range(2)
            ]

        mine = own.at[j]
        keep, give = rows_of(y * HIDDEN, HIDDEN), rows_of((1 - y) * HIDDEN, HIDDEN)
        if which == 0:
            ways = [
                (mine.at[:, :, give], mine.at[:, :, keep], False),
                (mine.at[1 - x, :, keep], mine.at[x, :, keep], True),
            ]
            box_one = box_y.at[s]
        else:
            ways = [(mine.at[1 - x], mine.at[x], True), (mine.at[x, :, give], mine.at[x, :, keep], False)]
            box_one = box_x.at[s]
        line = lambda to: mine.at[x, :, rows_of(y * HIDDEN + to * BLOCK, BLOCK)]
        boxes = (box_one, box_two.at[j], box_z.at[j])
        return Sum(lambda c, into: take(c, into), mine, theirs.at[j], ways, line, boxes, send.at[j], recv.at[j], near.at[j])

    return [[one(s, 0), one(s, 1)] for s in range(CHUNKS)]


def feed_sum_scratch():
    features = D // 4
    count = 2 * CHUNKS
    return [
        pltpu.VMEM((count, 2, features, CHUNK), BF16),
        pltpu.VMEM((count, 2, features, CHUNK), BF16),
        pltpu.VMEM((CHUNKS, 2, features, HIDDEN), BF16),
        pltpu.VMEM((CHUNKS, features, CHUNK), BF16),
        pltpu.VMEM((count, features, HIDDEN), BF16),
        pltpu.VMEM((count, LINE - 1, features, BLOCK), BF16),
        pltpu.SemaphoreType.DMA((count, Sum.COPIES)),
        pltpu.SemaphoreType.DMA((count, Sum.COPIES)),
        pltpu.SemaphoreType.DMA((count, 2)),
    ]


def unattend(x, mg, mixed, att, totals, wo, vec, grads=()):
    rows = x.shape[0]
    block = SIDE * PAD
    row = lambda a: pl.BlockSpec((block, a.shape[1]), lambda i: (i, 0))
    whole = lambda s: pl.BlockSpec(s, lambda i: (0, 0))
    shape = jax.ShapeDtypeStruct
    wi = (D, 3 * D)
    more = [shape((D // 4, CHUNKS * BLOCK), F32)] * 2 if grads else []
    return pl.pallas_call(
        unattend_kernel,
        grid=(rows // block,),
        in_specs=[
            row(x), row(mg), row(mixed), row(att),
            pl.BlockSpec((1, 16, WIDTH), lambda i: (i, 0, 0)),
            whole(wo.shape), whole(vec.shape),
        ] + [pl.BlockSpec(memory_space=pl.ANY)] * len(grads),
        out_specs=[whole(mixed.shape), whole(wi), whole(wo.shape), whole((8, D))] + [whole(m.shape) for m in more],
        out_shape=[shape(mixed.shape, BF16), shape(wi, BF16), shape(wo.shape, BF16), shape((8, D), F32)] + more,
        scratch_shapes=[
            pltpu.VMEM((D, rows), BF16),
            pltpu.VMEM((D, rows), BF16),
            pltpu.VMEM((rows, D), BF16),
        ] + (feed_sum_scratch() if grads else []),
        compiler_params=params(collective_id=3, has_side_effects=True) if grads else params(),
        name="unattend",
    )(x, mg, mixed, att, totals, wo, vec, *grads)


def unnorm_step(x, mg, mixed_grad, wi_ref, vec_ref, ig_ref, sums_ref):
    normed, scale = norm_parts(x.astype(F32))
    pull = mm_t(mixed_grad, wi_ref[...])
    sums_ref[G1 : G1 + 1, :] += sum_rows(pull * normed)
    sums_ref[B1 : B1 + 1, :] += sum_rows(pull)
    ig_ref[...] = mg + norm_back(pull, vec_ref[G1 : G1 + 1, :], normed, scale)


def unnorm_kernel(x_ref, mg_ref, mixed_grad_ref, wi_ref, vec_ref, ig_ref, sums_ref):
    @pl.when(pl.program_id(0) == 0)
    def _():
        sums_ref[...] = jnp.zeros_like(sums_ref)

    unnorm_step(x_ref[...], mg_ref[...], mixed_grad_ref[...], wi_ref, vec_ref, ig_ref, sums_ref)


ITEM = 384
ITEMS = 4


def unnorm_sum_kernel(
    x_ref, mg_ref, mixed_grad_ref, wi_ref, vec_ref, wig_ref, wog_ref, sums_one_ref, sums_two_ref, upbg_ref,
    ig_ref, wi_out, wo_out, vec_out, sums_ref, own, theirs, box_one, box_two, box_z, end, other_end,
    vec_own, vec_theirs, vec_one, vec_two, vec_z, send, recv, near,
):
    step = pl.program_id(0)
    z, y, x, c = place()
    rows = 24

    def ways(mine, x_first):
        if x_first:
            return [(mine.at[:, :, 1 - x], mine.at[:, :, x], True), (mine.at[:, 1 - y, x], mine.at[:, y, x], False)]
        return [(mine.at[:, 1 - y], mine.at[:, y], False), (mine.at[:, y, 1 - x], mine.at[:, y, x], True)]

    def item(j):
        def take(c, into):
            if j < ITEMS - 1:
                return [(wig_ref.at[:, :, :, :, rows_of(c * (3 * ITEM) + j * ITEM, ITEM)], into)]
            return [(wog_ref.at[:, :, :, :, rows_of(c * ITEM, ITEM)], into)]

        mine = own.at[j]
        boxes = (box_one.at[j], box_two.at[j], box_z.at[j])
        line = lambda to: mine.at[to, y, x]
        return Sum(take, mine, theirs.at[j], ways(mine, j % 2 == 1), line, boxes, send.at[j], recv.at[j], near.at[j])

    items = [item(j) for j in range(ITEMS)]
    line = lambda to: vec_own.at[to, y, x]
    boxes = (vec_one, vec_two, vec_z)
    vector = Sum(
        lambda c, into: [(vec_own, into)], vec_own, vec_theirs, ways(vec_own, False), line, boxes,
        send.at[ITEMS], recv.at[ITEMS], near.at[ITEMS],
    )

    def swap(j):
        give = end.at[j, pl.ds(pl.multiple_of((1 - c) * rows, 8), rows)]
        return remote(give, other_end.at[j], send.at[ITEMS + 1, j], recv.at[ITEMS + 1, j], device(z, y, x, 1 - c))

    @pl.when(step == 0)
    def _():
        greet()
        for one in items:
            one.load()
        sums_ref[...] = jnp.zeros_like(sums_ref)

    @pl.when(step == 1)
    def _():
        for one in items:
            one.first()

    unnorm_step(x_ref[...], mg_ref[...], mixed_grad_ref[...], wi_ref, vec_ref, ig_ref, sums_ref)

    @pl.when(step == pl.num_programs(0) - 1)
    def _():
        own_sums = [sums_ref[G1 : G1 + 1, :], sums_ref[B1 : B1 + 1, :]]
        own_sums += [sums_one_ref[QB : QB + 1, :], sums_one_ref[VB : VB + 1, :]]
        own_sums += [sums_two_ref[k : k + 1, :] for k in (OB, G2, B2, DB)]
        own_sums += [upbg_ref[...], jnp.zeros((BLOCK - 12, D), F32)]
        stacked = jnp.concatenate(own_sums, axis=0).T.reshape(vec_own.shape)
        vec_own[...] = stacked
        for one in vector.to_core():
            one.start()
        for one in items:
            one.second()
        for one in vector.to_core():
            one.wait_recv()
        for one in vector.to_core():
            one.wait_send()
        vec_own[...] = vec_own[...] + vec_theirs[...]
        vector.out(0).start()
        for one in items:
            one.third()
        vector.second()
        for j, one in enumerate(items[:2]):
            end[j] = one.total()
            swap(j).start()
        vector.third()
        for j, one in enumerate(items[2:]):
            end[j + 2] = one.total()
            swap(j + 2).start()
        for k in range(1, LINE):
            vector.to_z(k).wait_recv()
        total = vec_own[z, y, x]
        for k in range(LINE - 1):
            total = total + vec_z[k]
        vec_one[0, 0] = total
        vec_out[...] = jnp.zeros_like(vec_out)
        turned = vec_one[0, 0, pl.ds(pl.multiple_of(c * rows, 8), rows), :]
        row = lax.broadcasted_iota(jnp.int32, (rows, BLOCK), 0)
        lane = lax.broadcasted_iota(jnp.int32, (rows, BLOCK), 1)
        eye = jnp.where(row == lane, 1.0, 0.0)
        vec_out[...] = lax.dot_general(
            turned, eye, (((0,), (0,)), ((), ())), preferred_element_type=F32, precision=lax.Precision.HIGHEST
        )[:16]
        for one in [vector.out(0), vector.out(1)] + [vector.to_z(k) for k in range(1, LINE)]:
            one.wait_send()
        for j in range(ITEMS):
            swap(j).wait()
            mine = end[j, pl.ds(pl.multiple_of(c * rows, 8), rows)]
            if j < ITEMS - 1:
                wi_out[:, rows_of(c * (3 * ITEM) + j * ITEM, ITEM)] = mine
                wi_out[:, rows_of((1 - c) * (3 * ITEM) + j * ITEM, ITEM)] = other_end[j]
            else:
                wo_out[:, rows_of(c * ITEM, ITEM)] = mine
                wo_out[:, rows_of((1 - c) * ITEM, ITEM)] = other_end[j]


def unnorm(x, mg, mixed_grad, wi, vec, *more):
    rows = x.shape[0]
    block = SIDE * PAD
    row = lambda a: pl.BlockSpec((block, a.shape[1]), lambda i: (i, 0))
    whole = lambda s: pl.BlockSpec(s, lambda i: (0, 0))
    shape = jax.ShapeDtypeStruct
    in_specs = [row(x), row(mg), row(mixed_grad), whole((D, 3 * D)), whole(vec.shape)]
    if not more:
        return pl.pallas_call(
            unnorm_kernel,
            grid=(rows // block,),
            in_specs=in_specs,
            out_specs=[row(x), whole((8, D))],
            out_shape=[shape((rows, D), F32), shape((8, D), F32)],
            compiler_params=params(),
            name="unnorm",
        )(x, mg, mixed_grad, wi, vec)
    wig, wog, sums_one, sums_two, upbg = more
    chips = (LINE, 2, 2, 48)
    here = pl.BlockSpec(memory_space=pl.ANY)
    boxes = lambda lead, lanes, dtype: [
        pltpu.VMEM(lead + chips + (lanes,), dtype), pltpu.VMEM(lead + chips + (lanes,), dtype),
        pltpu.VMEM(lead + (LINE, 2, 48, lanes), dtype), pltpu.VMEM(lead + (LINE, 48, lanes), dtype),
        pltpu.VMEM(lead + (LINE - 1, 48, lanes), dtype),
    ]
    return pl.pallas_call(
        unnorm_sum_kernel,
        grid=(rows // block,),
        in_specs=in_specs + [here, here, whole((8, D)), whole((8, D)), whole(upbg.shape)],
        out_specs=[row(x), whole((24, 3 * D)), whole((24, D)), whole((16, BLOCK))],
        out_shape=[shape((rows, D), F32), shape((24, 3 * D), F32), shape((24, D), F32), shape((16, BLOCK), F32)],
        scratch_shapes=[pltpu.VMEM((8, D), F32)] + boxes((ITEMS,), ITEM, BF16) + [
            pltpu.VMEM((ITEMS, 48, ITEM), F32),
            pltpu.VMEM((ITEMS, 24, ITEM), F32),
        ] + boxes((), BLOCK, F32) + [
            pltpu.SemaphoreType.DMA((ITEMS + 2, Sum.COPIES)),
            pltpu.SemaphoreType.DMA((ITEMS + 2, Sum.COPIES)),
            pltpu.SemaphoreType.DMA((ITEMS + 1, 2)),
        ],
        compiler_params=params(collective_id=4, has_side_effects=True),
        name="unnorm",
    )(x, mg, mixed_grad, wi, vec, wig.reshape(chips + (3 * D,)), wog.reshape(chips + (D,)), sums_one, sums_two, upbg)


def spread_kernel(order_ref, ig_ref, out_ref):
    blocks = D // 128
    rows = out_ref.reshape(PATCHES * blocks * TOGETHER, 128)
    for j in range(TOGETHER):
        hot = picked(order_ref[j : j + 1, :PAD])
        ig = ig_ref[j * PAD : (j + 1) * PAD, :]
        high = ig.astype(BF16)
        rest = (ig - high.astype(F32)).astype(BF16)
        both = jnp.concatenate([high, rest], axis=0)
        own = mm(jnp.concatenate([hot, hot], axis=1), both)
        for k in range(blocks):
            at = pl.ds(k * TOGETHER + j, PATCHES, stride=blocks * TOGETHER)
            rows[at, :] = own[:, k * 128 : (k + 1) * 128]


def spread(order, ig):
    images = order.shape[0]
    return pl.pallas_call(
        spread_kernel,
        grid=(images // TOGETHER,),
        in_specs=[
            pl.BlockSpec((TOGETHER, PATCHES), lambda i: (i, 0)),
            pl.BlockSpec((TOGETHER * PAD, D), lambda i: (i, 0)),
        ],
        out_specs=pl.BlockSpec((PATCHES, 1, D // 128, TOGETHER, 128), lambda i: (0, i, 0, 0, 0)),
        out_shape=jax.ShapeDtypeStruct((PATCHES, images // TOGETHER, D // 128, TOGETHER, 128), F32),
        compiler_params=params(),
        name="spread",
    )(order, ig)


def local(
    patches, keep_order, cotangent, first_gain, first_shift, project_in, query_bias, value_bias,
    project_out, output_bias, second_gain, second_shift, up_weight, up_bias, down_weight, down_bias,
):
    rows_own = project_in.shape[0]
    hidden_own = up_bias.shape[0]
    images = patches.shape[0]
    wide, narrow = lax.axis_size("wide"), lax.axis_size("narrow")
    vectors = [first_gain, first_shift, query_bias, value_bias, output_bias, second_gain, second_shift, down_bias]
    order = keep_order
    patches = patches.transpose(1, 0, 2)
    cot = cotangent.transpose(1, 0, 2).reshape(VIS * images, D)
    if (wide, narrow) == (8, 4):
        flat = jnp.concatenate(vectors + [up_bias]).reshape(12, rows_own)
        x, wi, piece = pick_gather(order, patches, project_in, project_out, flat)
        upb = wi[:, 3 * D + 8 : 3 * D + 12].reshape(4, 2, 4, rows_own, 4)
        upb = upb.transpose(0, 1, 2, 4, 3).reshape(4, 2, CHUNKS, BLOCK).transpose(2, 1, 0, 3)
        upb = upb.reshape(1, -1).astype(F32)
        mixed, att, totals, result, mg, upg, downg, upbg, sums_two, vec, wo = forward(
            x, wi, cot, upb, piece, up_weight.T, down_weight.T
        )
        mixed_grad, wig, wog, sums_one, upf, downf = unattend(x, mg, mixed, att, totals, wo, vec, (upg, downg))
        upbg = upbg.reshape(CHUNKS, 2, 4, BLOCK).transpose(2, 1, 0, 3).reshape(8, 4, 4, rows_own)
        upbg = upbg.transpose(2, 0, 1, 3).reshape(4, D)
        ig, wig, wog, s = unnorm(x, mg, mixed_grad, wi, vec, wig, wog, sums_one, sums_two, upbg)
        s = s[:, :rows_own]
        upf, downf, upbf = upf.T, downf.T, s[8:12].reshape(-1)
    else:
        share = jnp.concatenate([jnp.stack(vectors).reshape(1, -1), up_bias.reshape(1, -1)], axis=1)
        shares = lax.all_gather(share, AXES, axis=0, tiled=True)
        vec = shares[:, : 8 * rows_own].reshape(-1, 8, rows_own).transpose(1, 0, 2).reshape(8, D)
        vec = jnp.pad(vec.astype(F32), ((0, 8), (0, 0)))
        upb = shares[:, 8 * rows_own :].reshape(1, -1).astype(F32)
        wi = lax.all_gather(project_in, AXES, axis=0, tiled=True)
        wo = lax.all_gather(project_out, AXES, axis=0, tiled=True)
        ffw = jnp.stack([up_weight.T, down_weight.T])
        ffw = lax.all_gather(ffw, "narrow", axis=1, tiled=True)
        ffw = lax.all_gather(ffw, "wide", axis=2, tiled=True)
        x = pick(order, patches)
        mixed, att, totals = attend(x, wi, vec)
        result, mg, upg, downg, upbg, sums_two = feed_forward(x, att, cot, wo, vec, ffw[0], upb, ffw[1])
        mixed_grad, wig, wog, sums_one = unattend(x, mg, mixed, att, totals, wo, vec)
        ig, sums_norm = unnorm(x, mg, mixed_grad, wi, vec)
        ffg = jnp.stack([upg, downg])
        ffg = lax.psum_scatter(ffg, "wide", scatter_dimension=2, tiled=True)
        ffg = lax.psum_scatter(ffg, "narrow", scatter_dimension=1, tiled=True).astype(F32)
        wig = lax.psum_scatter(wig, AXES, scatter_dimension=0, tiled=True).astype(F32)
        wog = lax.psum_scatter(wog, AXES, scatter_dimension=0, tiled=True).astype(F32)
        picks = [sums_norm[G1], sums_norm[B1], sums_one[QB], sums_one[VB]]
        picks += [sums_two[OB], sums_two[G2], sums_two[B2], sums_two[DB]]
        parts = jnp.stack(picks).reshape(8, -1, rows_own).transpose(1, 0, 2).reshape(-1, 8 * rows_own)
        parts = jnp.concatenate([parts, upbg.reshape(-1, hidden_own)], axis=1)
        own = lax.psum_scatter(parts, AXES, scatter_dimension=0, tiled=True)[0]
        s = [own[k * rows_own : (k + 1) * rows_own] for k in range(8)]
        upf, downf, upbf = ffg[0].T, ffg[1].T, own[8 * rows_own :]
    patch_grad = spread(order, ig).transpose(1, 3, 0, 2, 4).reshape(images, PATCHES, D)
    result = result.reshape(VIS, images, D).transpose(1, 0, 2)
    return (
        result, patch_grad, s[0], s[1], wig, s[2], s[3], wog, s[4], s[5], s[6], upf, upbf, downf, s[7],
    )


def solution(mesh):
    both = P(AXES)
    rows = P(AXES, None)
    cube = P(AXES, None, None)
    tile = P("wide", "narrow")
    return jax.shard_map(
        local,
        mesh=mesh,
        in_specs=(
            cube, rows, cube, both, both, rows, both, both, rows, both, both, both, tile, both, tile, both,
        ),
        out_specs=(
            cube, cube, both, both, rows, both, both, rows, both, both, both, tile, both, tile, both,
        ),
        check_vma=False,
    )
```

```python
import functools

import jax
import jax.numpy as jnp
from jax import lax
from jax.experimental import pallas as pl
from jax.experimental.pallas import tpu as pltpu
from jax.sharding import PartitionSpec as P

D = 768
HEADS = 12
HEAD_DIM = 64
PATCHES = 196
VIS = 49
PAD = 64
SIDE = 4
WIDTH = SIDE * HEAD_DIM
GROUPS = HEADS // SIDE
TOGETHER = 8
HIDDEN = 512
EPSILON = 1e-06
SCALE = HEAD_DIM ** (-0.5)
F32 = jnp.float32
BF16 = jnp.bfloat16
AXES = ("wide", "narrow")
G1, B1, QB, VB, OB, G2, B2, DB = range(8)


def params(**more):
    return pltpu.CompilerParams(vmem_limit_bytes=60 * 1024 * 1024, **more)


def mm(left, right):
    return jnp.dot(left, right, preferred_element_type=F32)


def mm_t(left, right):
    return lax.dot_general(left, right, (((1,), (1,)), ((), ())), preferred_element_type=F32)


def t_mm(left, right):
    return lax.dot_general(left, right, (((0,), (0,)), ((), ())), preferred_element_type=F32)


def norm_parts(values):
    mean = jnp.mean(values, axis=-1, keepdims=True)
    centred = values - mean
    spread = jnp.mean(centred * centred, axis=-1, keepdims=True)
    scale = lax.rsqrt(spread + EPSILON)
    return centred * scale, scale


def norm_back(grad, gain, normed, scale):
    pulled = grad * gain
    inner = jnp.mean(pulled * normed, axis=-1, keepdims=True)
    return scale * (pulled - jnp.mean(pulled, axis=-1, keepdims=True) - normed * inner)


def sum_rows(values):
    return jnp.sum(values, axis=0, keepdims=True)


def load_wide(ref, rows=slice(None)):
    return jnp.concatenate([ref[k, rows, :] for k in range(D // 128)], axis=1)


def store_wide(ref, rows, values):
    for k in range(D // 128):
        ref[k, rows, :] = values[:, k * 128 : (k + 1) * 128]


def heads_apart(block):
    lane = lax.broadcasted_iota(jnp.int32, block.shape, 1) // HEAD_DIM
    zero = jnp.zeros_like(block)
    return jnp.concatenate([jnp.where(lane == h, block, zero) for h in range(SIDE)], axis=0)


def heads_together(product):
    lane = lax.broadcasted_iota(jnp.int32, (HEAD_DIM, WIDTH), 1) // HEAD_DIM
    out = jnp.zeros((HEAD_DIM, WIDTH), F32)
    for h in range(SIDE):
        out = jnp.where(lane == h, product[h * HEAD_DIM : (h + 1) * HEAD_DIM], out)
    return out


def picked(order, first=0, count=PATCHES):
    lane = lax.broadcasted_iota(jnp.int32, (1, PAD), 1)
    order = jnp.where(lane < VIS, order, -1)
    row = lax.broadcasted_iota(jnp.int32, (count, PAD), 0) + first
    return jnp.where(row == order, 1.0, 0.0).astype(BF16)


LINE = 4
BLOCK = 128
CHUNK = 1024
CHUNKS = 3
MESH = pl.DeviceIdType.MESH


def place():
    wide, narrow = lax.axis_index("wide"), lax.axis_index("narrow")
    return wide // 2, wide % 2, narrow // 2, narrow % 2


def device(z, y, x, c):
    return (2 * z + y, 2 * x + c)


def greet():
    z, y, x, c = place()
    barrier = pltpu.get_barrier_semaphore()
    peers = [device((z + k) % LINE, y, x, c) for k in range(1, LINE)]
    peers += [device(z, 1 - y, x, c), device(z, y, 1 - x, c), device(z, y, x, 1 - c)]
    for peer in peers:
        pl.semaphore_signal(barrier, inc=1, device_id=peer, device_id_type=MESH)
    pl.semaphore_wait(barrier, len(peers))


def remote(src, dst, send, recv, peer):
    return pltpu.make_async_remote_copy(
        src_ref=src, dst_ref=dst, send_sem=send, recv_sem=recv, device_id=peer, device_id_type=MESH
    )


class Gather:
    COPIES = 17

    def __init__(self, src, slot, x_first, halves, send, recv, own):
        self.src, self.slot, self.x_first, self.halves = src, slot, x_first, halves
        self.send, self.recv, self.own = send, recv, own
        self.z, self.y, self.x, self.c = place()

    def flip(self, z, first, second):
        y, x = self.y, self.x
        if first if self.x_first else second:
            x = 1 - x
        if second if self.x_first else first:
            y = 1 - y
        return z, y, x

    def line(self, k):
        return (self.z - k) % LINE

    def copy(self, at, src, dst, peer):
        return remote(src, dst, self.send.at[at], self.recv.at[at], peer)

    def to_z(self, k):
        peer = device((self.z + k) % LINE, self.y, self.x, self.c)
        return self.copy(k - 1, self.src, self.slot(self.z, self.y, self.x), peer)

    def to_first(self, k):
        slot = self.slot(self.line(k), self.y, self.x)
        peer = device(*self.flip(self.z, True, False), self.c)
        return self.copy(3 + k, self.src if k == 0 else slot, slot, peer)

    def to_second(self, k):
        slot = self.slot(self.line(k), self.y, self.x)
        peer = device(*self.flip(self.z, False, True), self.c)
        return self.copy(7 + k, self.src if k == 0 else slot, slot, peer)

    def on_to_second(self, k):
        slot = self.slot(*self.flip(self.line(k), True, False))
        peer = device(*self.flip(self.z, False, True), self.c)
        return self.copy(11 + k, slot, slot, peer)

    def to_core(self, j, c=None):
        part = self.halves(self.c if c is None else c)[j]
        return self.copy(15 + j, part, part, device(self.z, self.y, self.x, 1 - self.c))

    def keep(self):
        return pltpu.make_async_copy(self.src, self.slot(self.z, self.y, self.x), self.own)

    def arrived(self, at, z, first, second):
        slot = self.slot(*self.flip(z, first, second))
        self.copy(at, slot, slot, device(self.z, self.y, self.x, 1 - self.c)).wait_recv()

    def start(self):
        self.keep().start()
        for k in range(1, LINE):
            self.to_z(k).start()
        self.to_first(0).start()
        self.to_second(0).start()

    def first(self):
        for k in range(1, LINE):
            self.arrived(k - 1, self.line(k), False, False)
            self.to_first(k).start()
            self.to_second(k).start()

    def second(self):
        for k in range(LINE):
            self.arrived(3 + k, self.line(k), True, False)
            self.on_to_second(k).start()

    def core(self):
        for k in range(LINE):
            self.arrived(7 + k, self.line(k), False, True)
            self.arrived(11 + k, self.line(k), True, True)
        self.keep().wait()
        for j in range(len(self.halves(self.c))):
            self.to_core(j).start()

    def finish(self):
        for j in range(len(self.halves(self.c))):
            self.to_core(j, 1 - self.c).wait_recv()
        for k in range(1, LINE):
            self.to_z(k).wait_send()
        for k in range(LINE):
            self.to_first(k).wait_send()
            self.to_second(k).wait_send()
            self.on_to_second(k).wait_send()
        for j in range(len(self.halves(self.c))):
            self.to_core(j).wait_send()


class Sum:
    COPIES = 8

    def __init__(self, take, own, theirs, ways, line, boxes, send, recv, near):
        self.take, self.own, self.theirs, self.ways, self.line, self.boxes = take, own, theirs, ways, line, boxes
        self.send, self.recv, self.near = send, recv, near
        self.z, self.y, self.x, self.c = place()

    def copy(self, at, src, dst, peer):
        return remote(src, dst, self.send.at[at], self.recv.at[at], device(*peer))

    def loads(self):
        return [pltpu.make_async_copy(src, dst, self.near.at[j]) for j, (src, dst) in enumerate(self.take(self.c, self.own))]

    def to_core(self):
        peer = (self.z, self.y, self.x, 1 - self.c)
        return [self.copy(6 + j, src, dst, peer) for j, (src, dst) in enumerate(self.take(1 - self.c, self.theirs))]

    def out(self, turn):
        goes, _, x_way = self.ways[turn]
        peer = (self.z, self.y, 1 - self.x, self.c) if x_way else (self.z, 1 - self.y, self.x, self.c)
        return self.copy(turn, goes, self.boxes[turn], peer)

    def to_z(self, k):
        to = (self.z + k) % LINE
        return self.copy(1 + k, self.line(to), self.boxes[2].at[k - 1], (to, self.y, self.x, self.c))

    def load(self):
        for one in self.loads() + self.to_core():
            one.start()

    def first(self):
        for one in self.loads():
            one.wait()
        for one in self.to_core():
            one.wait_recv()
        self.own[...] = self.own[...] + self.theirs[...]
        self.out(0).start()

    def second(self):
        self.out(0).wait_recv()
        stays = self.ways[0][1]
        stays[...] = stays[...] + self.boxes[0][...]
        self.out(1).start()

    def third(self):
        self.out(1).wait_recv()
        stays = self.ways[1][1]
        stays[...] = stays[...] + self.boxes[1][...]
        for k in range(1, LINE):
            self.to_z(k).start()

    def total(self):
        for k in range(1, LINE):
            self.to_z(k).wait_recv()
        out = self.line(self.z)[...].astype(F32)
        for k in range(LINE - 1):
            out = out + self.boxes[2][k].astype(F32)
        for one in self.to_core() + [self.out(0), self.out(1)] + [self.to_z(k) for k in range(1, LINE)]:
            one.wait_send()
        return out


def rows_of(start, size, extent=None):
    return pl.ds(pl.multiple_of(start, size), size if extent is None else extent)


PICK_PARTS = 2
PICK_ROWS = PATCHES // PICK_PARTS


def pick_step(part, order_ref, patches_ref, out_ref, at, wide_ref):
    values = patches_ref[...].astype(F32).reshape(PICK_ROWS * TOGETHER, D)
    store_wide(wide_ref, slice(0, PICK_ROWS * TOGETHER), values)
    for j in range(TOGETHER):
        hot = picked(order_ref[j : j + 1, :PAD], part * PICK_ROWS, PICK_ROWS)
        own = load_wide(wide_ref, pl.ds(j, PICK_ROWS, stride=TOGETHER)).astype(BF16)
        rows = pl.ds(pl.multiple_of(at + j * PAD, PAD), PAD)
        value = t_mm(hot, own)
        out_ref[rows, :] = jnp.where(part == 0, value, value + out_ref[rows, :].astype(F32)).astype(BF16)


def pick_in(images):
    blocks = images // TOGETHER
    index = lambda i: (jnp.minimum(i // PICK_PARTS, blocks - 1), 0)
    place_of = lambda i: (jnp.where(i < PICK_PARTS * blocks, i % PICK_PARTS, PICK_PARTS - 1), index(i)[0], 0)
    return [pl.BlockSpec((TOGETHER, PATCHES), index), pl.BlockSpec((PICK_ROWS, TOGETHER, D), place_of)]


def pick_kernel(order_ref, patches_ref, out_ref, wide_ref):
    pick_step(pl.program_id(0) % PICK_PARTS, order_ref, patches_ref, out_ref, 0, wide_ref)


def pick(order, patches):
    images = order.shape[0]
    return pl.pallas_call(
        pick_kernel,
        grid=(images // TOGETHER * PICK_PARTS,),
        in_specs=pick_in(images),
        out_specs=pl.BlockSpec((TOGETHER * PAD, D), lambda i: (i // PICK_PARTS, 0)),
        out_shape=jax.ShapeDtypeStruct((images * PAD, D), BF16),
        scratch_shapes=[pltpu.VMEM((D // 128, PICK_ROWS * TOGETHER, 128), F32)],
        compiler_params=params(),
        name="pick",
    )(order, patches)


HALF = 384
OWN = 24
PIECES = 3
SHARE = 4 * HALF + BLOCK


def parts_of_groups(block, g):
    return [block[:, k * D + g * WIDTH : k * D + (g + 1) * WIDTH] for k in range(3)]


def chip_row(z, y, x):
    return rows_of(((2 * z + y) * 2 + x) * 2 * OWN, 2 * OWN)


def share_out(in_ref, out_ref, vectors_ref, share_ref):
    vectors = vectors_ref[...]
    row = lax.broadcasted_iota(jnp.int32, (vectors.shape[0], BLOCK), 0)
    lane = lax.broadcasted_iota(jnp.int32, (vectors.shape[0], BLOCK), 1)
    columns = t_mm(vectors, jnp.where(row == lane, 1.0, 0.0).astype(BF16)).astype(BF16)
    share_ref[...] = jnp.zeros_like(share_ref)
    for g in range(GROUPS):
        both = jnp.concatenate(parts_of_groups(in_ref, g), axis=1)
        for h in range(2):
            share_ref[h, :OWN, g * HALF : (g + 1) * HALF] = both[:, h * HALF : (h + 1) * HALF]
    for h in range(2):
        share_ref[h, :OWN, 3 * HALF : 4 * HALF] = out_ref[:, h * HALF : (h + 1) * HALF]
        share_ref[h, :OWN, 4 * HALF :] = columns


def both_rows(mine, theirs):
    c = lax.axis_index("narrow") % 2
    mine, theirs = mine.astype(F32)[:OWN], theirs.astype(F32)[:OWN]
    top, low = jnp.where(c == 0, mine, theirs), jnp.where(c == 0, theirs, mine)
    return jnp.concatenate([top, low], axis=0).astype(BF16)


def hidden_bias(columns, out_ref):
    rows = 4 * OWN
    row = lax.broadcasted_iota(jnp.int32, (rows, 4 * rows * 4), 0)
    lane = lax.broadcasted_iota(jnp.int32, (rows, 4 * rows * 4), 1)
    which, hidden = lane // (4 * rows), lane % (4 * rows)
    hot = jnp.where(hidden == (row // OWN) * (4 * OWN) + which * OWN + row % OWN, 1.0, 0.0).astype(BF16)
    take = lax.broadcasted_iota(jnp.int32, (16, 4 * rows * 4), 0) == 8 + lane[:1] // (4 * rows)
    for w in range(2 * LINE):
        spread = t_mm(columns[w * rows : (w + 1) * rows, :16], hot)
        line = sum_rows(jnp.where(take, spread, 0.0))
        own = sum(line[:, k * 4 * rows : (k + 1) * 4 * rows] for k in range(4))
        for s in range(CHUNKS):
            at = s * CHUNK + (w % 2) * HIDDEN + (w // 2) * BLOCK
            out_ref[:, at : at + BLOCK] = own[:, s * BLOCK : (s + 1) * BLOCK]


def scores_of(k4, q_apart):
    return mm_t(k4, q_apart) * SCALE


BLOCKS = 3


def low_one(x, vec_ref):
    normed, _ = norm_parts(x.astype(F32))
    return (normed * vec_ref[G1 : G1 + 1, :] + vec_ref[B1 : B1 + 1, :]).astype(BF16)


def attend_step(g, low, wi, vec_ref, mixed_ref, total_ref, att, at):
    cols = rows_of(g * WIDTH, WIDTH)
    product = mm(low, wi[...])
    mixed_ref[:, :WIDTH] = (product[:, :WIDTH] + vec_ref[QB : QB + 1, cols]).astype(BF16)
    mixed_ref[:, WIDTH : 2 * WIDTH] = product[:, WIDTH : 2 * WIDTH].astype(BF16)
    mixed_ref[:, 2 * WIDTH :] = (product[:, 2 * WIDTH :] + vec_ref[VB : VB + 1, cols]).astype(BF16)
    key_row = lax.broadcasted_iota(jnp.int32, (PAD, WIDTH), 0)
    for img in range(TOGETHER):
        rows = slice(img * PAD, (img + 1) * PAD)
        q4, k4, v4 = [mixed_ref[rows, k * WIDTH : (k + 1) * WIDTH] for k in range(3)]
        scores = jnp.where(key_row < VIS, scores_of(k4, heads_apart(q4)), -1e30)
        top = jnp.max(scores, axis=0, keepdims=True)
        raised = jnp.exp(scores - top)
        total = sum_rows(raised)
        weights = (raised * (1.0 / total)).astype(BF16)
        total_ref[0, img // SIDE, img % SIDE : img % SIDE + 1, :] = top + jnp.log(total)
        att[pl.ds(pl.multiple_of(at + img * PAD, PAD), PAD), cols] = heads_together(t_mm(weights, v4)).astype(BF16)


def attend_kernel(x_ref, wi_ref, vec_ref, mixed_ref, att_ref, total_ref, low):
    step = pl.program_id(0)
    g, b = step // BLOCKS, step % BLOCKS
    at = b * (TOGETHER * PAD)
    rows = rows_of(at, TOGETHER * PAD)

    @pl.when(g == 0)
    def _():
        low[rows, :] = low_one(x_ref[rows, :], vec_ref)

    attend_step(g, low[rows, :], wi_ref.at[0], vec_ref, mixed_ref, total_ref, att_ref, at)


def full(*shape):
    return pl.BlockSpec(shape, lambda i: (0,) * len(shape))


def whole(a):
    return full(*a.shape)


def by_group(*block, lead=0, blocks=BLOCKS):
    def index(i):
        i = jnp.clip(i - lead, 0, GROUPS * blocks - 1)
        g, b = i // blocks, i % blocks
        return (g, b, 0, 0) if len(block) == 4 else (b, g)

    return pl.BlockSpec(block, index)


def TOTALS(lead):
    return by_group(1, TOGETHER // SIDE, 8, WIDTH, lead=lead)


def totals_shape(rows):
    return jax.ShapeDtypeStruct((GROUPS, rows // (SIDE * PAD), 8, WIDTH), F32)


def attend(x, wi, vec):
    rows = x.shape[0]
    block = TOGETHER * PAD
    shape = jax.ShapeDtypeStruct
    return pl.pallas_call(
        attend_kernel,
        grid=(GROUPS * BLOCKS,),
        in_specs=[whole(x), pl.BlockSpec((1, D, D), lambda i: (i // BLOCKS, 0, 0)), whole(vec)],
        out_specs=[by_group(block, D), full(rows, D), TOTALS(0)],
        out_shape=[
            shape((rows, 3 * D), BF16), shape((rows, D), BF16), totals_shape(rows),
        ],
        scratch_shapes=[pltpu.VMEM((rows, D), BF16)],
        compiler_params=params(),
        name="attend",
    )(x, wi, vec)


def gelu_both(x):
    bell = jnp.exp(-0.5 * x * x) * 0.3989422804014327
    below = 0.5 * (1.0 + lax.erf(x * 0.7071067811865476))
    return x * below, below + x * bell


def feed_start(x_ref, att_ref, cot_ref, wo_ref, vec_ref, sums_ref, middle, low, grad, low_t, grad_t, feed, back, act, inner):
    rows = cot_ref.shape[0]
    images = rows // VIS
    held = middle.shape[1]
    feed[...] = jnp.zeros_like(feed)
    back[...] = jnp.zeros_like(back)
    act[held:, :] = jnp.zeros((act.shape[0] - held, HIDDEN), BF16)
    inner[held:, :] = jnp.zeros((act.shape[0] - held, HIDDEN), BF16)
    middle[:, rows:, :] = jnp.zeros((D // 128, held - rows, 128), F32)
    for g in range(images // TOGETHER):
        at = slice(g * TOGETHER * PAD, (g + 1) * TOGETHER * PAD)
        branch = mm(att_ref[at, :], wo_ref[...]) + vec_ref[OB : OB + 1, :]
        mid = x_ref[at, :].astype(F32) + branch
        for j in range(TOGETHER):
            token = pl.ds(g * TOGETHER + j, VIS, stride=images)
            store_wide(middle, token, mid[j * PAD : j * PAD + VIS])
    grad[:rows, :] = cot_ref[...]
    grad[rows:, :] = jnp.zeros((held - rows, D), BF16)
    sums_ref[DB : DB + 1, :] = sum_rows(cot_ref[...].astype(F32))
    normed, _ = norm_parts(load_wide(middle))
    low[...] = (normed * vec_ref[G2 : G2 + 1, :] + vec_ref[B2 : B2 + 1, :]).astype(BF16)
    low_t[:, held:] = jnp.zeros((D, low_t.shape[1] - held), BF16)
    grad_t[:, held:] = jnp.zeros((D, low_t.shape[1] - held), BF16)
    low_t[:, :held] = low[...].T
    grad_t[:, :held] = grad[...].T


def feed_step(up, upb, down, upbg_ref, middle, low, grad, low_t, grad_t, feed, back, act, inner):
    half = low.shape[0] // 2
    upbg = jnp.zeros((1, HIDDEN), F32)
    for part in range(2):
        at = slice(part * half, (part + 1) * half)
        before = mm(low[at, :], up[...]) + upb
        hidden_grad = mm(grad[at, :], down[...])
        value, slope = gelu_both(before)
        act[at, :] = value.astype(BF16)
        before_grad = (hidden_grad * slope).astype(BF16)
        inner[at, :] = before_grad
        upbg = upbg + sum_rows(before_grad.astype(F32))
        feed[at, :] += mm_t(act[at, :], down[...])
        back[at, :] += mm_t(before_grad, up[...])
    upbg_ref[...] = upbg


def feed_grads(upg_ref, downg_ref, middle, low, grad, low_t, grad_t, feed, back, act, inner):
    downg_ref[...] = mm(grad_t[...], act[...]).astype(BF16)
    upg_ref[...] = mm(low_t[...], inner[...]).astype(BF16)


def feed_end(vec_ref, result_ref, mg_ref, sums_ref, middle, low, grad, low_t, grad_t, feed, back, act, inner):
    rows = result_ref.shape[0]
    images = rows // VIS
    held = low.shape[0]
    mid = load_wide(middle)
    result = feed[...] + mid + vec_ref[DB : DB + 1, :]
    result_ref[...] = result[:rows].astype(BF16)
    normed, scale = norm_parts(mid)
    pull = back[...]
    sums_ref[G2 : G2 + 1, :] = sum_rows(pull * normed)
    sums_ref[B2 : B2 + 1, :] = sum_rows(pull)
    mid_grad = grad[...].astype(F32) + norm_back(pull, vec_ref[G2 : G2 + 1, :], normed, scale)
    real = lax.broadcasted_iota(jnp.int32, (held, 1), 0) < rows
    mid_grad = jnp.where(real, mid_grad, 0.0)
    sums_ref[OB : OB + 1, :] = sum_rows(mid_grad.astype(BF16).astype(F32))
    store_wide(middle, slice(None), mid_grad)
    for j in range(images):
        out = j * PAD
        token = pl.ds(j, VIS, stride=images)
        own = jnp.concatenate([load_wide(middle, token), jnp.zeros((PAD - VIS, D), F32)], axis=0)
        mg_ref[out : out + PAD, :] = own.astype(BF16)


def feed_scratch(rows):
    held = -(-rows // 32) * 32
    deep = -(-rows // 256) * 256
    return [
        pltpu.VMEM((D // 128, held, 128), F32),
        pltpu.VMEM((held, D), BF16),
        pltpu.VMEM((held, D), BF16),
        pltpu.VMEM((D, deep), BF16),
        pltpu.VMEM((D, deep), BF16),
        pltpu.VMEM((held, D), F32),
        pltpu.VMEM((held, D), F32),
        pltpu.VMEM((deep, HIDDEN), BF16),
        pltpu.VMEM((deep, HIDDEN), BF16),
    ]


def feed_kernel(
    x_ref, att_ref, cot_ref, wo_ref, vec_ref, up_ref, upb_ref, down_ref,
    result_ref, mg_ref, upg_ref, downg_ref, upbg_ref, sums_ref, *scratch,
):
    step = pl.program_id(0)

    @pl.when(step == 0)
    def _():
        feed_start(x_ref, att_ref, cot_ref, wo_ref, vec_ref, sums_ref, *scratch)

    feed_step(up_ref, upb_ref[...], down_ref, upbg_ref, *scratch)
    feed_grads(upg_ref, downg_ref, *scratch)

    @pl.when(step == pl.num_programs(0) - 1)
    def _():
        feed_end(vec_ref, result_ref, mg_ref, sums_ref, *scratch)


def feed_forward(x, att, cot, wo, vec, up, upb, down):
    rows = cot.shape[0]
    ff = up.shape[1]
    hid = lambda r: pl.BlockSpec((r, HIDDEN), lambda i: (0, i))
    return pl.pallas_call(
        feed_kernel,
        grid=(ff // HIDDEN,),
        in_specs=[whole(x), whole(att), whole(cot), whole(wo), whole(vec), hid(D), hid(1), hid(D)],
        out_specs=[whole(cot), full(x.shape[0], D), hid(D), hid(D), hid(1), full(8, D)],
        out_shape=[
            jax.ShapeDtypeStruct(cot.shape, BF16),
            jax.ShapeDtypeStruct((x.shape[0], D), BF16),
            jax.ShapeDtypeStruct((D, ff), BF16),
            jax.ShapeDtypeStruct((D, ff), BF16),
            jax.ShapeDtypeStruct((1, ff), F32),
            jax.ShapeDtypeStruct((8, D), F32),
        ],
        scratch_shapes=feed_scratch(rows),
        compiler_params=params(),
        name="feed_forward",
    )(x, att, cot, wo, vec, up, upb, down)


FORWARD = {
    1: [("start", "v"), ("start", "g0"), ("start", "g1")],
    2: [("start", "g2")],
    3: [("first", "v"), ("start", 0)],
    4: [("first", "g0")],
    5: [("second", "v"), ("start", "out")],
    6: [("first", "g1"), ("second", "g0"), ("core", "v"), ("first", "g2"), ("finish", "v"), ("core", "g0"), ("second", "g1"), ("finish", "g0"), ("second", "g2")],
    7: [("first", 0)],
    8: [("core", "g1"), ("core", "g2"), ("first", "out"), ("start", 1)],
    9: [("finish", "g1"), ("finish", "g2")],
    10: [("second", 0)],
    11: [("second", "out")],
    12: [("first", 1), ("start", 2)],
    13: [("core", 0)],
    14: [("core", "out")],
    15: [("finish", 0), ("finish", "out")],
    16: [("second", 1), ("first", 2)],
    18: [("core", 1)],
    19: [("load", "sum"), ("finish", 1)],
    20: [("second", 2), ("first", "sum")],
    22: [("core", 2)],
    23: [("finish", 2)],
    24: [("second", "sum")],
    26: [("third", "sum")],
}


def forward_kernel(
    order_ref, patches_ref, in_ref, out_ref, vectors_ref, cot_ref, up_own, down_own,
    x_ref, mixed_ref, total_ref, att_ref, result_ref, mg_ref, upg_ref, downg_ref, upbg_ref, sums_ref, vec_ref, wi_ref, wo_ref,
    upf_ref, downf_ref, share_ref, other, piece, columns, upb, wi_all, wo_all, up_all, down_all, send, recv, own, near, *scratch,
):
    step = pl.program_id(0)
    picks = x_ref.shape[0] // (TOGETHER * PAD) * PICK_PARTS
    early = picks + GROUPS * BLOCKS
    last = pl.num_programs(0) - 1
    z, y, x, c = place()
    features = D // 4
    feed_parts, sum_parts = scratch[:9], scratch[9:]
    middle = feed_parts[0]
    low_all = mg_ref
    swap = remote(share_ref.at[1 - c], other, near.at[0], near.at[1], device(z, y, x, 1 - c))

    def weight(j, src, dst, s, x_first):
        def slot(z, y, x):
            rows = rows_of((2 * x + c) * features, features)
            return dst.at[rows, rows_of(s * CHUNK + y * HIDDEN + z * BLOCK, BLOCK)]

        def halves(c):
            return [dst.at[rows_of((2 * k + c) * features, features), pl.ds(s * CHUNK, CHUNK)] for k in range(2)]

        block = src.at[:, pl.ds(s * BLOCK, BLOCK)]
        return Gather(block, slot, x_first, halves, send.at[j], recv.at[j], own.at[j])

    def square(j, k, dst, x_first, start=0, width=HALF):
        lanes = lambda c: rows_of(c * HALF + start, BLOCK, width)
        slot = lambda z, y, x: dst.at[chip_row(z, y, x), lanes(c)]
        halves = lambda c: [dst.at[:, lanes(c)]]
        block = piece.at[:, pl.ds(k * HALF + start, width)]
        return Gather(block, slot, x_first, halves, send.at[j], recv.at[j], own.at[j])

    items = {
        s: [weight(2 * s, up_own, up_all, s, True), weight(2 * s + 1, down_own, down_all, s, False)]
        for s in range(CHUNKS)
    }
    j = 2 * CHUNKS
    slot = lambda z, y, x: columns.at[chip_row(z, y, x)]
    items["v"] = [Gather(piece.at[:, pl.ds(4 * HALF, BLOCK)], slot, True, lambda c: [], send.at[j], recv.at[j], own.at[j])]
    items["g0"] = [square(j + 1, 0, wi_all.at[0], False, 0, 2 * BLOCK), square(j + 2, 0, wi_all.at[0], True, 2 * BLOCK, BLOCK)]
    items["g1"] = [square(j + 3, 1, wi_all.at[1], True)]
    items["g2"] = [square(j + 4, 2, wi_all.at[2], False)]
    items["out"] = [square(j + 5, 3, wo_all, True)]
    items["sum"] = feed_sums((up_all, down_all), [0], *sum_parts)[0]
    copies = [
        pltpu.make_async_copy(wi_all, wi_ref, near.at[2]),
        pltpu.make_async_copy(wo_all, wo_ref, near.at[3]),
    ]
    for k in range(1, CHUNKS):
        lanes, dst = pl.ds(k * CHUNK, CHUNK), pl.ds((k - 1) * CHUNK, CHUNK)
        copies.append(pltpu.make_async_copy(up_all.at[:, lanes], upg_ref.at[:, dst], near.at[2 + 2 * k]))
        copies.append(pltpu.make_async_copy(down_all.at[:, lanes], downg_ref.at[:, dst], near.at[3 + 2 * k]))

    @pl.when(step == 0)
    def _():
        share_out(in_ref, out_ref, vectors_ref, share_ref)
        greet()
        swap.start()

    @pl.when(step == 1)
    def _():
        swap.wait()
        piece[...] = both_rows(share_ref[c], other[...])

    for at, acts in FORWARD.items():

        @pl.when(step == at)
        def _(acts=acts):
            for act, which in acts:
                for one in items[which]:
                    getattr(one, act)()

    @pl.when(step < picks)
    def _():
        pick_step(step % PICK_PARTS, order_ref, patches_ref, x_ref, step // PICK_PARTS * (TOGETHER * PAD), middle)

    @pl.when(step == picks)
    def _():
        vec_ref[...] = columns[...].astype(F32).T[:16]
        hidden_bias(columns[...], upb)

    g, b = (step - picks) // BLOCKS, (step - picks) % BLOCKS
    at = b * (TOGETHER * PAD)
    rows = rows_of(at, TOGETHER * PAD)

    @pl.when((step >= picks) & (g == 0))
    def _():
        low_all[rows, :] = low_one(x_ref[rows, :], vec_ref)

    @pl.when((step >= picks) & (step < early))
    def _():
        attend_step(g, low_all[rows, :], wi_all.at[g], vec_ref, mixed_ref, total_ref, att_ref, at)

    @pl.when(step == early)
    def _():
        copies[0].start()
        copies[1].start()
        feed_start(x_ref, att_ref, cot_ref, wo_all, vec_ref, sums_ref, *feed_parts)

    lanes = rows_of((step - early) // 2 * HIDDEN, HIDDEN)

    @pl.when((step >= early) & ((step - early) % 2 == 0))
    def _():
        feed_step(up_all.at[:, lanes], upb[:, lanes], down_all.at[:, lanes], upbg_ref, *feed_parts)

    @pl.when((step >= early) & ((step - early) % 2 == 1))
    def _():
        feed_grads(up_all.at[:, lanes], down_all.at[:, lanes], *feed_parts)

    for k in range(1, CHUNKS):

        @pl.when(step == early + 2 * (k + 1) * (CHUNK // HIDDEN) - 1)
        def _(k=k):
            copies[2 * k].start()
            copies[2 * k + 1].start()

    @pl.when(step == last)
    def _():
        feed_end(vec_ref, result_ref, mg_ref, sums_ref, *feed_parts)
        upf_ref[...], downf_ref[...] = [one.total() for one in items["sum"]]
        for one in copies:
            one.wait()


def forward(order, patches, project_in, project_out, vectors, cot, up, down):
    images = order.shape[0]
    rows = images * PAD
    block = TOGETHER * PAD
    picks = images // TOGETHER * PICK_PARTS
    early = picks + GROUPS * BLOCKS
    ff = CHUNKS * CHUNK
    late = 2 * ff // HIDDEN
    here = pl.BlockSpec(memory_space=pl.ANY)
    shape = jax.ShapeDtypeStruct
    count = 2 * CHUNKS + 6
    done = (D // 4, BLOCK)
    return pl.pallas_call(
        forward_kernel,
        grid=(early + late,),
        in_specs=pick_in(images) + [whole(project_in), whole(project_out), whole(vectors), whole(cot), here, here],
        out_specs=[
            full(rows, D), by_group(block, D, lead=picks), TOTALS(picks), full(rows, D),
            whole(cot), full(rows, D), here, here,
            pl.BlockSpec((1, HIDDEN), lambda i: (0, jnp.maximum(i - early, 0) // 2)),
            full(8, D), full(16, D), here, here, full(*done), full(*done),
        ],
        out_shape=[
            shape((rows, D), BF16), shape((rows, 3 * D), BF16), totals_shape(rows), shape((rows, D), BF16),
            shape(cot.shape, BF16), shape((rows, D), BF16), shape((D, ff - CHUNK), BF16), shape((D, ff - CHUNK), BF16),
            shape((1, ff), F32), shape((8, D), F32), shape((16, D), F32),
            shape((GROUPS, D, D), BF16), shape((D, D), BF16), shape(done, F32), shape(done, F32),
        ],
        scratch_shapes=[
            pltpu.VMEM((2, 32, SHARE), BF16),
            pltpu.VMEM((32, SHARE), BF16),
            pltpu.VMEM((2 * OWN, SHARE), BF16),
            pltpu.VMEM((D, BLOCK), BF16),
            pltpu.VMEM((1, ff), F32),
            pltpu.VMEM((GROUPS, D, D), BF16),
            pltpu.VMEM((D, D), BF16),
            pltpu.VMEM((D, ff), BF16),
            pltpu.VMEM((D, ff), BF16),
            pltpu.SemaphoreType.DMA((count, Gather.COPIES)),
            pltpu.SemaphoreType.DMA((count, Gather.COPIES)),
            pltpu.SemaphoreType.DMA((count,)),
            pltpu.SemaphoreType.DMA((2 + 2 * CHUNKS,)),
        ] + feed_scratch(cot.shape[0]) + feed_sum_scratch(1),
        compiler_params=params(collective_id=2, has_side_effects=True),
        name="forward",
    )(order, patches, project_in, project_out, vectors, cot, up, down)


BACKWARD = {
    0: [("load", 1)],
    2: [("first", 1)],
    3: [("load", 2)],
    5: [("first", 2)],
    6: [("load", "out"), ("load", "g0"), ("second", 1)],
    7: [("first", "out"), ("first", "g0")],
    9: [("second", 2)],
    11: [("third", 1)],
    12: [("load", "g1")],
    13: [("second", "out"), ("second", "g0"), ("first", "g1")],
    15: [("total", 1), ("third", 2)],
    16: [("third", "out"), ("third", "g0")],
    18: [("second", "g1"), ("load", "g2"), ("load", "v")],
    19: [("first", "g2"), ("total", 2)],
    20: [("total", "out"), ("third", "g1"), ("first", "v")],
    21: [("total", "g0"), ("second", "g2")],
    22: [("total", "g1"), ("second", "v")],
    23: [("third", "g2")],
}
BACK = 6


def unattend_step(mixed_ref, att_grad, totals, grads, g, at):
    key_row = lax.broadcasted_iota(jnp.int32, (PAD, WIDTH), 0)
    for img in range(SIDE):
        rows = slice(img * PAD, (img + 1) * PAD)
        q4, k4, v4 = [mixed_ref[rows, k * WIDTH : (k + 1) * WIDTH] for k in range(3)]
        q_apart = heads_apart(q4)
        a_apart = heads_apart(att_grad[rows, :])
        exact = jnp.exp(scores_of(k4, q_apart) - totals[0, 0, img : img + 1, :])
        exact = jnp.where(key_row < VIS, exact, 0.0)
        pulled = mm_t(v4, a_apart)
        centre = sum_rows(exact * pulled)
        score_grad = (exact * (pulled - centre)).astype(BF16)
        q_grad = heads_together(t_mm(score_grad, k4)) * SCALE
        k_grad = mm(score_grad, q_apart) * SCALE
        v_grad = mm(exact.astype(BF16), a_apart)
        out = pl.ds(pl.multiple_of(at + img * PAD, PAD), PAD)
        grads[g, out, :WIDTH] = q_grad.astype(BF16)
        grads[g, out, WIDTH : 2 * WIDTH] = k_grad.astype(BF16)
        grads[g, out, 2 * WIDTH :] = v_grad.astype(BF16)


def unnorm_step(x, mg, grads, rows, wi_ref, vec_ref, ig_ref, sums_ref):
    normed, scale = norm_parts(x.astype(F32))
    pull = sum(mm_t(grads[g, rows, :], wi_ref[g]) for g in range(GROUPS))
    sums_ref[G1 : G1 + 1, :] += sum_rows(pull * normed)
    sums_ref[B1 : B1 + 1, :] += sum_rows(pull)
    ig_ref[...] = mg.astype(F32) + norm_back(pull, vec_ref[G1 : G1 + 1, :], normed, scale)


def backward_kernel(x_ref, mg_ref, mixed_ref, att_ref, total_ref, wi_ref, wo_ref, vec_ref, *refs):
    step = pl.program_id(0)
    walk = GROUPS * BACK
    last = pl.num_programs(0) - 1
    g, b = step // BACK, step % BACK
    at = b * (SIDE * PAD)
    rows = rows_of(at, SIDE * PAD)
    remote_sums = len(refs) > 9
    if remote_sums:
        upg_ref, downg_ref, sums_two_ref, upbg_ref = refs[:4]
        ig_ref, wi_out, wo_out, vec_out, upf_ref, downf_ref = refs[4:10]
        low_t, att_t, grads, sums_ref, wig_ref, wog_ref, end, other_end, end_send, end_recv = refs[10:20]
        feed_parts, square_parts, early_parts, late_parts = refs[20:29], refs[29:37], refs[37:45], refs[45:]
        z, y, x, c = place()
        items = dict(enumerate(feed_sums((upg_ref, downg_ref), range(1, CHUNKS), *feed_parts), 1))
        for j, name in enumerate(("g0", "g1", "out")):
            src = wog_ref if name == "out" else wig_ref.at[j]
            items[name] = [square_sum(j, j, src, slice(0, HALF), j == 1, *square_parts)]
        cuts = [slice(0, 2 * BLOCK), slice(2 * BLOCK, HALF)]
        items["g2"] = [square_sum(3, 3 + j, wig_ref.at[2], cut, j == 1, *square_parts) for j, cut in enumerate(cuts)]
        items["v"] = [vector_sum(*early_parts)]
        items["late"] = [vector_sum(*late_parts)]
        places = {"g0": 0, "g1": 1, "g2": 2, "out": 3}

        def swap(j):
            give = end.at[j, pl.ds(pl.multiple_of((1 - c) * OWN, 8), OWN)]
            return remote(give, other_end.at[j], end_send.at[j], end_recv.at[j], device(z, y, x, 1 - c))

        def act(name, which):
            values = [getattr(one, name)() for one in items[which]]
            if name != "total":
                return
            if which in (1, 2):
                lanes = slice((which - 1) * BLOCK, which * BLOCK)
                upf_ref[:, lanes], downf_ref[:, lanes] = values
            elif which in places:
                end[places[which]] = jnp.concatenate(values, axis=1)
                swap(places[which]).start()
            else:
                early = which == "v"
                value = jnp.where(c == 0, values[0][:, :OWN], values[0][:, OWN : 2 * OWN])
                at = slice(0, 16) if early else slice(16, 24)
                vec_out[at, :OWN] = value

        for when, acts in BACKWARD.items():

            @pl.when(step == when)
            def _(when=when, acts=acts):
                if when == 0:
                    greet()
                for name, which in acts:
                    if (name, which) == ("load", "v"):
                        own = [sums_ref[k : k + 1, :] for k in (QB, VB)]
                        own += [sums_two_ref[k : k + 1, :] for k in (OB, G2, B2, DB)]
                        own += [upbg_ref[...], jnp.zeros((6, D), F32)]
                        items["v"][0].fill(jnp.concatenate(own, axis=0))
                    act(name, which)
    else:
        ig_ref, wi_out, wo_out, sums_ref, low_t, att_t, grads, wig_ref, wog_ref = refs

    @pl.when(step == 0)
    def _():
        sums_ref[...] = jnp.zeros_like(sums_ref)

    @pl.when(g == 0)
    def _():
        low_t[:, rows] = low_one(x_ref[rows, :], vec_ref).T
        att_t[:, rows] = att_ref[...].T

    @pl.when(step < walk)
    def _():
        cols = rows_of(g * WIDTH, WIDTH)
        att_grad = mm_t(mg_ref[rows, :], wo_ref[cols, :]).astype(BF16)
        unattend_step(mixed_ref, att_grad, total_ref, grads, g, at)
        own = grads[g, rows, :]
        sums_ref[QB : QB + 1, cols] += sum_rows(own[:, :WIDTH].astype(F32))
        sums_ref[VB : VB + 1, cols] += sum_rows(own[:, 2 * WIDTH :].astype(F32))

    @pl.when(step == BACK - 1)
    def _():
        wog_ref[...] = mm(att_t[...], mg_ref[...]).astype(BF16).reshape(wog_ref.shape)

    @pl.when((b == BACK - 1) & (step < walk))
    def _():
        wig_ref[g] = mm(low_t[...], grads[g]).astype(BF16).reshape(wig_ref.shape[1:])

    @pl.when(step >= walk)
    def _():
        unnorm_step(x_ref[rows, :], mg_ref[rows, :], grads, rows, wi_ref, vec_ref, ig_ref, sums_ref)

    @pl.when(step == last)
    def _():
        if not remote_sums:
            wi_out[...] = wig_ref[...].reshape(wi_out.shape)
            wo_out[...] = wog_ref[...].reshape(wo_out.shape)
            return
        vec_out[...] = jnp.zeros_like(vec_out)
        items["late"][0].fill(jnp.concatenate([sums_ref[G1 : B1 + 1, :], jnp.zeros((6, D), F32)], axis=0))
        for name, which in (
            ("load", "late"), ("first", "late"), ("third", "v"), ("second", "late"), ("total", "g2"),
            ("third", "late"), ("total", "v"), ("total", "late"),
        ):
            act(name, which)
        for j in range(PIECES + 1):
            swap(j).wait()
            mine, theirs = end[j, pl.ds(pl.multiple_of(c * OWN, 8), OWN), :], other_end[j]
            both = jnp.concatenate([jnp.where(c == 0, mine, theirs), jnp.where(c == 0, theirs, mine)], axis=1)
            if j < GROUPS:
                for k in range(3):
                    wi_out[:, k * D + j * WIDTH : k * D + (j + 1) * WIDTH] = both[:, k * WIDTH : (k + 1) * WIDTH]
            else:
                wo_out[...] = both


CHIPS = (LINE, 2, 2, 2 * OWN)


def ways_of(mine, x_first):
    z, y, x, c = place()
    if x_first:
        return [(mine.at[:, :, 1 - x], mine.at[:, :, x], True), (mine.at[:, 1 - y, x], mine.at[:, y, x], False)]
    return [(mine.at[:, 1 - y], mine.at[:, y], False), (mine.at[:, y, 1 - x], mine.at[:, y, x], True)]


def square_sum(j, at, src, lanes, x_first, own, theirs, box_one, box_two, box_z, send, recv, near):
    z, y, x, c = place()
    width = lanes.stop - lanes.start

    def take(c, into):
        return [(src.at[:, :, :, :, rows_of(c * HALF + lanes.start, BLOCK, width)], into)]

    lanes = pl.ds(lanes.start, width)
    mine = own.at[j, :, :, :, :, lanes]
    line = lambda to: mine.at[to, y, x]
    boxes = (box_one.at[j, :, :, :, lanes], box_two.at[j, :, :, lanes], box_z.at[j, :, :, lanes])
    return Sum(
        take, mine, theirs.at[j, :, :, :, :, lanes], ways_of(mine, x_first), line, boxes, send.at[at], recv.at[at], near.at[at]
    )


class VectorSum(Sum):
    def fill(self, vectors):
        self.own[...] = jnp.zeros(self.own.shape, F32)
        for k in range(2 * LINE * 2):
            z, y, x = k // 4, k // 2 % 2, k % 2
            part = vectors[:, k * 2 * OWN : (k + 1) * 2 * OWN]
            self.own[z, y, x, :, : 2 * OWN] = part

    def loads(self):
        return []

    def first(self):
        for one in self.to_core():
            one.wait_recv()
        for one in self.to_core():
            one.wait_send()
        self.own[...] = self.own[...] + self.theirs[...]
        self.out(0).start()

    def total(self):
        for k in range(1, LINE):
            self.to_z(k).wait_recv()
        out = self.line(self.z)[...]
        for k in range(LINE - 1):
            out = out + self.boxes[2][k]
        for one in [self.out(0), self.out(1)] + [self.to_z(k) for k in range(1, LINE)]:
            one.wait_send()
        return out


def vector_sum(own, theirs, box_one, box_two, box_z, send, recv, near):
    z, y, x, c = place()
    mine = own.at[0]
    line = lambda to: mine.at[to, y, x]
    boxes = (box_one.at[0], box_two.at[0], box_z.at[0])
    return VectorSum(
        lambda c, into: [(mine, into)], mine, theirs.at[0], ways_of(mine, False), line, boxes, send.at[0], recv.at[0], near.at[0]
    )


def square_sum_scratch(count, lanes=HALF, dtype=BF16, rows=2 * OWN, copies=None):
    chips = CHIPS[:3] + (rows,)
    copies = count if copies is None else copies
    return [
        pltpu.VMEM((count,) + chips + (lanes,), dtype),
        pltpu.VMEM((count,) + chips + (lanes,), dtype),
        pltpu.VMEM((count, LINE, 2, rows, lanes), dtype),
        pltpu.VMEM((count, LINE, rows, lanes), dtype),
        pltpu.VMEM((count, LINE - 1, rows, lanes), dtype),
        pltpu.SemaphoreType.DMA((copies, Sum.COPIES)),
        pltpu.SemaphoreType.DMA((copies, Sum.COPIES)),
        pltpu.SemaphoreType.DMA((copies, 2)),
    ]


def feed_sums(grads_refs, which_chunks, own, theirs, box_y, box_x, box_two, box_z, send, recv, near):
    z, y, x, c = place()
    features = D // 4

    def one(s, which):
        grads = grads_refs[which]
        j = 2 * s + which

        def take(c, into):
            return [
                (grads.at[rows_of((2 * k + c) * features, features), pl.ds(s * CHUNK, CHUNK)], into.at[k])
                for k in range(2)
            ]

        mine = own.at[j]
        keep, give = rows_of(y * HIDDEN, HIDDEN), rows_of((1 - y) * HIDDEN, HIDDEN)
        if which == 0:
            ways = [
                (mine.at[:, :, give], mine.at[:, :, keep], False),
                (mine.at[1 - x, :, keep], mine.at[x, :, keep], True),
            ]
            box_one = box_y.at[s]
        else:
            ways = [(mine.at[1 - x], mine.at[x], True), (mine.at[x, :, give], mine.at[x, :, keep], False)]
            box_one = box_x.at[s]
        line = lambda to: mine.at[x, :, rows_of(y * HIDDEN + to * BLOCK, BLOCK)]
        boxes = (box_one, box_two.at[j], box_z.at[j])
        return Sum(lambda c, into: take(c, into), mine, theirs.at[j], ways, line, boxes, send.at[j], recv.at[j], near.at[j])

    return [[one(s, 0), one(s, 1)] for s in range(len(which_chunks))]


def feed_sum_scratch(chunks):
    features = D // 4
    count = 2 * chunks
    return [
        pltpu.VMEM((count, 2, features, CHUNK), BF16),
        pltpu.VMEM((count, 2, features, CHUNK), BF16),
        pltpu.VMEM((chunks, 2, features, HIDDEN), BF16),
        pltpu.VMEM((chunks, features, CHUNK), BF16),
        pltpu.VMEM((count, features, HIDDEN), BF16),
        pltpu.VMEM((count, LINE - 1, features, BLOCK), BF16),
        pltpu.SemaphoreType.DMA((count, Sum.COPIES)),
        pltpu.SemaphoreType.DMA((count, Sum.COPIES)),
        pltpu.SemaphoreType.DMA((count, 2)),
    ]


def backward(x, mg, mixed, att, totals, wi, wo, vec, *more):
    rows = x.shape[0]
    block = SIDE * PAD
    walk = GROUPS * BACK
    shape = jax.ShapeDtypeStruct
    scratch = [pltpu.VMEM((D, rows), BF16), pltpu.VMEM((D, rows), BF16), pltpu.VMEM((GROUPS, rows, D), BF16)]
    sums = [pltpu.VMEM((8, D), F32)]
    weights = [pltpu.VMEM((GROUPS,) + CHIPS + (D,), BF16), pltpu.VMEM(CHIPS + (D,), BF16)]
    specs = []
    if more:
        here = pl.BlockSpec(memory_space=pl.ANY)
        specs = [here, here, whole(more[2]), whole(more[3])]
        own = (D // 4, (CHUNKS - 1) * BLOCK)
        out = [(OWN, 3 * D), (OWN, D), (24, BLOCK), own, own]
        scratch += sums + weights + [
            pltpu.VMEM((PIECES + 1, 2 * OWN, HALF), F32),
            pltpu.VMEM((PIECES + 1, OWN, HALF), F32),
            pltpu.SemaphoreType.DMA((PIECES + 1,)),
            pltpu.SemaphoreType.DMA((PIECES + 1,)),
        ] + feed_sum_scratch(CHUNKS - 1) + square_sum_scratch(PIECES + 1, copies=PIECES + 2)
        scratch += square_sum_scratch(1, BLOCK, F32, 16) + square_sum_scratch(1, BLOCK, F32, 8)
        out_shape = [shape(s, F32) for s in out]
    else:
        out = [(GROUPS, D, D), (D, D), (8, D)]
        out_shape = [shape(s, F32 if s[0] == 8 else BF16) for s in out]
        scratch += weights
    return pl.pallas_call(
        backward_kernel,
        grid=(walk + BACK,),
        in_specs=[
            whole(x), whole(mg), by_group(block, D, blocks=BACK),
            pl.BlockSpec((block, D), lambda i: (jnp.minimum(i, BACK - 1), 0)),
            by_group(1, 1, 8, WIDTH, blocks=BACK), whole(wi), whole(wo), whole(vec),
        ] + specs,
        out_specs=[pl.BlockSpec((block, D), lambda i: (jnp.maximum(i - walk, 0), 0))] + [full(*s) for s in out],
        out_shape=[shape((rows, D), F32)] + out_shape,
        scratch_shapes=scratch,
        compiler_params=params(collective_id=3, has_side_effects=True) if more else params(),
        name="backward",
    )(x, mg, mixed, att, totals, wi, wo, vec, *more)


def spread_kernel(order_ref, ig_ref, out_ref):
    blocks = D // 128
    rows = out_ref.reshape(PATCHES * blocks * TOGETHER, 128)
    for j in range(TOGETHER):
        hot = picked(order_ref[j : j + 1, :PAD])
        ig = ig_ref[j * PAD : (j + 1) * PAD, :]
        high = ig.astype(BF16)
        rest = (ig - high.astype(F32)).astype(BF16)
        both = jnp.concatenate([high, rest], axis=0)
        own = mm(jnp.concatenate([hot, hot], axis=1), both)
        for k in range(blocks):
            at = pl.ds(k * TOGETHER + j, PATCHES, stride=blocks * TOGETHER)
            rows[at, :] = own[:, k * 128 : (k + 1) * 128]


def spread(order, ig):
    images = order.shape[0]
    return pl.pallas_call(
        spread_kernel,
        grid=(images // TOGETHER,),
        in_specs=[
            pl.BlockSpec((TOGETHER, PATCHES), lambda i: (i, 0)),
            pl.BlockSpec((TOGETHER * PAD, D), lambda i: (i, 0)),
        ],
        out_specs=pl.BlockSpec((PATCHES, 1, D // 128, TOGETHER, 128), lambda i: (0, i, 0, 0, 0)),
        out_shape=jax.ShapeDtypeStruct((PATCHES, images // TOGETHER, D // 128, TOGETHER, 128), F32),
        compiler_params=params(),
        name="spread",
    )(order, ig)


def local(
    patches, keep_order, cotangent, first_gain, first_shift, project_in, query_bias, value_bias,
    project_out, output_bias, second_gain, second_shift, up_weight, up_bias, down_weight, down_bias,
):
    rows_own = project_in.shape[0]
    hidden_own = up_bias.shape[0]
    images = patches.shape[0]
    wide, narrow = lax.axis_size("wide"), lax.axis_size("narrow")
    vectors = [first_gain, first_shift, query_bias, value_bias, output_bias, second_gain, second_shift, down_bias]
    order = keep_order
    patches = patches.transpose(1, 0, 2)
    cot = cotangent.transpose(1, 0, 2).reshape(VIS * images, D)
    if (wide, narrow) == (8, 4):
        flat = jnp.concatenate([jnp.stack(vectors), up_bias.reshape(4, rows_own)], axis=0)
        x, mixed, totals, att, result, mg, upg, downg, upbg, sums_two, vec, wi, wo, up_zero, down_zero = forward(
            order, patches, project_in, project_out, flat, cot, up_weight.T, down_weight.T
        )
        upbg = upbg.reshape(CHUNKS, 2, 4, BLOCK).transpose(2, 1, 0, 3).reshape(8, 4, 4, rows_own)
        upbg = upbg.transpose(2, 0, 1, 3).reshape(4, D)
        ig, wig, wog, s, upf, downf = backward(
            x, mg, mixed, att, totals, wi, wo, vec, upg, downg, sums_two, upbg
        )
        upf = jnp.concatenate([up_zero, upf], axis=1).T
        downf = jnp.concatenate([down_zero, downf], axis=1).T
        upbf = s[6:10, :rows_own].reshape(-1)
        s = [s[k, :rows_own] for k in (16, 17, 0, 1, 2, 3, 4, 5)]
    else:
        share = jnp.concatenate([jnp.stack(vectors).reshape(1, -1), up_bias.reshape(1, -1)], axis=1)
        shares = lax.all_gather(share, AXES, axis=0, tiled=True)
        vec = shares[:, : 8 * rows_own].reshape(-1, 8, rows_own).transpose(1, 0, 2).reshape(8, D)
        vec = jnp.pad(vec.astype(F32), ((0, 8), (0, 0)))
        upb = shares[:, 8 * rows_own :].reshape(1, -1).astype(F32)
        wi = lax.all_gather(project_in, AXES, axis=0, tiled=True)
        wo = lax.all_gather(project_out, AXES, axis=0, tiled=True)
        ffw = jnp.stack([up_weight.T, down_weight.T])
        ffw = lax.all_gather(ffw, "narrow", axis=1, tiled=True)
        ffw = lax.all_gather(ffw, "wide", axis=2, tiled=True)
        wi = wi.reshape(D, 3, GROUPS, WIDTH).transpose(2, 0, 1, 3).reshape(GROUPS, D, D)
        x = pick(order, patches)
        mixed, att, totals = attend(x, wi, vec)
        result, mg, upg, downg, upbg, sums_two = feed_forward(x, att, cot, wo, vec, ffw[0], upb, ffw[1])
        ig, wig, wog, sums_one = backward(x, mg, mixed, att, totals, wi, wo, vec)
        wig = wig.reshape(GROUPS, D, 3, WIDTH).transpose(1, 2, 0, 3).reshape(D, 3 * D)
        ffg = jnp.stack([upg, downg])
        ffg = lax.psum_scatter(ffg, "wide", scatter_dimension=2, tiled=True)
        ffg = lax.psum_scatter(ffg, "narrow", scatter_dimension=1, tiled=True).astype(F32)
        wig = lax.psum_scatter(wig, AXES, scatter_dimension=0, tiled=True).astype(F32)
        wog = lax.psum_scatter(wog, AXES, scatter_dimension=0, tiled=True).astype(F32)
        picks = [sums_one[G1], sums_one[B1], sums_one[QB], sums_one[VB]]
        picks += [sums_two[OB], sums_two[G2], sums_two[B2], sums_two[DB]]
        parts = jnp.stack(picks).reshape(8, -1, rows_own).transpose(1, 0, 2).reshape(-1, 8 * rows_own)
        parts = jnp.concatenate([parts, upbg.reshape(-1, hidden_own)], axis=1)
        own = lax.psum_scatter(parts, AXES, scatter_dimension=0, tiled=True)[0]
        s = [own[k * rows_own : (k + 1) * rows_own] for k in range(8)]
        upf, downf, upbf = ffg[0].T, ffg[1].T, own[8 * rows_own :]
    patch_grad = spread(order, ig).transpose(1, 3, 0, 2, 4).reshape(images, PATCHES, D)
    result = result.reshape(VIS, images, D).transpose(1, 0, 2)
    return (
        result, patch_grad, s[0], s[1], wig, s[2], s[3], wog, s[4], s[5], s[6], upf, upbf, downf, s[7],
    )


def solution(mesh):
    both = P(AXES)
    rows = P(AXES, None)
    cube = P(AXES, None, None)
    tile = P("wide", "narrow")
    return jax.shard_map(
        local,
        mesh=mesh,
        in_specs=(
            cube, rows, cube, both, both, rows, both, both, rows, both, both, both, tile, both, tile, both,
        ),
        out_specs=(
            cube, cube, both, both, rows, both, both, rows, both, both, both, tile, both, tile, both,
        ),
        check_vma=False,
    )
```

```python
import functools

import jax
import jax.numpy as jnp
from jax import lax
from jax.experimental import pallas as pl
from jax.experimental.pallas import tpu as pltpu
from jax.sharding import PartitionSpec as P

D = 768
HEADS = 12
HEAD_DIM = 64
PATCHES = 196
VIS = 49
PAD = 64
SIDE = 4
WIDTH = SIDE * HEAD_DIM
GROUPS = HEADS // SIDE
TOGETHER = 8
HIDDEN = 512
EPSILON = 1e-06
SCALE = HEAD_DIM ** (-0.5)
F32 = jnp.float32
BF16 = jnp.bfloat16
AXES = ("wide", "narrow")
G1, B1, QB, VB, OB, G2, B2, DB = range(8)


def params(**more):
    return pltpu.CompilerParams(vmem_limit_bytes=60 * 1024 * 1024, **more)


def mm(left, right):
    return jnp.dot(left, right, preferred_element_type=F32)


def mm_t(left, right):
    return lax.dot_general(left, right, (((1,), (1,)), ((), ())), preferred_element_type=F32)


def t_mm(left, right):
    return lax.dot_general(left, right, (((0,), (0,)), ((), ())), preferred_element_type=F32)


def norm_parts(values):
    mean = jnp.mean(values, axis=-1, keepdims=True)
    centred = values - mean
    spread = jnp.mean(centred * centred, axis=-1, keepdims=True)
    scale = lax.rsqrt(spread + EPSILON)
    return centred * scale, scale


def norm_back(grad, gain, normed, scale):
    pulled = grad * gain
    inner = jnp.mean(pulled * normed, axis=-1, keepdims=True)
    return scale * (pulled - jnp.mean(pulled, axis=-1, keepdims=True) - normed * inner)


def sum_rows(values):
    return jnp.sum(values, axis=0, keepdims=True)


def load_wide(ref, rows=slice(None)):
    return jnp.concatenate([ref[k, rows, :] for k in range(D // 128)], axis=1)


def store_wide(ref, rows, values):
    for k in range(D // 128):
        ref[k, rows, :] = values[:, k * 128 : (k + 1) * 128]


def heads_apart(block):
    lane = lax.broadcasted_iota(jnp.int32, block.shape, 1) // HEAD_DIM
    zero = jnp.zeros_like(block)
    return jnp.concatenate([jnp.where(lane == h, block, zero) for h in range(SIDE)], axis=0)


def heads_together(product):
    lane = lax.broadcasted_iota(jnp.int32, (HEAD_DIM, WIDTH), 1) // HEAD_DIM
    out = jnp.zeros((HEAD_DIM, WIDTH), F32)
    for h in range(SIDE):
        out = jnp.where(lane == h, product[h * HEAD_DIM : (h + 1) * HEAD_DIM], out)
    return out


def picked(order, first=0, count=PATCHES):
    lane = lax.broadcasted_iota(jnp.int32, (1, PAD), 1)
    order = jnp.where(lane < VIS, order, -1)
    row = lax.broadcasted_iota(jnp.int32, (count, PAD), 0) + first
    return jnp.where(row == order, 1.0, 0.0).astype(BF16)


LINE = 4
BLOCK = 128
CHUNK = 1024
CHUNKS = 3
MESH = pl.DeviceIdType.MESH


def place():
    wide, narrow = lax.axis_index("wide"), lax.axis_index("narrow")
    return lax.shift_right_logical(wide, 1), wide & 1, lax.shift_right_logical(narrow, 1), narrow & 1


def device(z, y, x, c):
    return (2 * z + y, 2 * x + c)


def at_step(step, plan, run):
    keys = sorted(plan)
    if len(keys) <= 2:
        for key in keys:
            pl.when(step == key)(functools.partial(run, plan[key]))
        return
    middle = keys[len(keys) // 2]
    low = {key: plan[key] for key in keys if key < middle}
    high = {key: plan[key] for key in keys if key >= middle}
    pl.when(step < middle)(lambda: at_step(step, low, run))
    pl.when(step >= middle)(lambda: at_step(step, high, run))


def of_three(i, size):
    group = (i >= size).astype(jnp.int32) + (i >= 2 * size).astype(jnp.int32)
    return group, i - group * size


def greet():
    z, y, x, c = place()
    barrier = pltpu.get_barrier_semaphore()
    peers = [device((z + k) & (LINE - 1), y, x, c) for k in range(1, LINE)]
    peers += [device(z, 1 - y, x, c), device(z, y, 1 - x, c), device(z, y, x, 1 - c), device(z, 1 - y, 1 - x, c)]
    for peer in peers:
        pl.semaphore_signal(barrier, inc=1, device_id=peer, device_id_type=MESH)
    pl.semaphore_wait(barrier, len(peers))


def remote(src, dst, send, recv, peer):
    return pltpu.make_async_remote_copy(
        src_ref=src, dst_ref=dst, send_sem=send, recv_sem=recv, device_id=peer, device_id_type=MESH
    )


class Gather:
    COPIES = 4

    def __init__(self, src, slot, x_first, halves, span, send, recv, own, direct=False):
        self.direct, self.span = direct, span
        self.src, self.slot, self.x_first, self.halves = src, slot, x_first, halves
        self.send, self.recv, self.own = send, recv, own
        self.z, self.y, self.x, self.c = place()

    def flip(self, z, first, second):
        y, x = self.y, self.x
        if first if self.x_first else second:
            x = 1 - x
        if second if self.x_first else first:
            y = 1 - y
        return z, y, x

    def line(self, k):
        return (self.z - k) & (LINE - 1)

    def copy(self, at, src, dst, peer):
        return remote(src, dst, self.send.at[at], self.recv.at[at], peer)

    def to_z(self, k):
        peer = device((self.z + k) & (LINE - 1), self.y, self.x, self.c)
        return self.copy(0, self.src, self.slot(self.z, self.y, self.x), peer)

    def to_first(self, k):
        slot = self.slot(self.line(k), self.y, self.x)
        peer = device(*self.flip(self.z, True, False), self.c)
        return self.copy(1, self.src if k == 0 else slot, slot, peer)

    def to_second(self, k):
        slot = self.slot(self.line(k), self.y, self.x)
        peer = device(*self.flip(self.z, False, True), self.c)
        return self.copy(2, self.src if k == 0 else slot, slot, peer)

    def on_to_second(self, k):
        slot = self.slot(*self.flip(self.line(k), True, False))
        peer = device(*self.flip(self.z, False, True), self.c)
        return self.copy(2, slot, slot, peer)

    def to_both(self, k):
        slot = self.slot(self.line(k), self.y, self.x)
        peer = device(*self.flip(self.z, True, True), self.c)
        return self.copy(2, self.src if k == 0 else slot, slot, peer)

    def to_core(self, j):
        part = self.halves(self.c)[j]
        return self.copy(3, part, part, device(self.z, self.y, self.x, 1 - self.c))

    def keep(self):
        return pltpu.make_async_copy(self.src, self.slot(self.z, self.y, self.x), self.own)

    def all_of(self, at, count):
        span = self.span(count)
        return self.copy(at, span, span, device(self.z, self.y, self.x, 1 - self.c))

    def start(self):
        self.keep().start()
        for k in range(1, LINE):
            self.to_z(k).start()
        self.to_first(0).start()
        self.to_second(0).start()
        if self.direct:
            self.to_both(0).start()

    def first(self):
        self.all_of(0, LINE - 1).wait_recv()
        for k in range(1, LINE):
            self.to_first(k).start()
            self.to_second(k).start()
            if self.direct:
                self.to_both(k).start()

    def second(self):
        self.all_of(1, LINE).wait_recv()
        for k in range(LINE):
            if not self.direct:
                self.on_to_second(k).start()

    def core(self):
        self.all_of(2, 2 * LINE).wait_recv()
        self.keep().wait()
        for j in range(len(self.halves(self.c))):
            self.to_core(j).start()

    def finish(self):
        held = len(self.halves(self.c)) > 0
        if held:
            self.all_of(3, 4 * LINE).wait_recv()
        self.all_of(0, LINE - 1).wait_send()
        self.all_of(1, LINE).wait_send()
        self.all_of(2, 2 * LINE).wait_send()
        if held:
            self.all_of(3, 4 * LINE).wait_send()


class Sum:
    COPIES = 4

    def __init__(self, take, own, theirs, ways, line, boxes, send, recv, near):
        self.take, self.own, self.theirs, self.ways, self.line, self.boxes = take, own, theirs, ways, line, boxes
        self.send, self.recv, self.near = send, recv, near
        self.z, self.y, self.x, self.c = place()

    def copy(self, at, src, dst, peer):
        return remote(src, dst, self.send.at[at], self.recv.at[at], device(*peer))

    def loads(self):
        return [pltpu.make_async_copy(src, dst, self.near.at[0]) for src, dst in self.take(self.c, self.own)]

    def to_core(self):
        peer = (self.z, self.y, self.x, 1 - self.c)
        return [self.copy(3, src, dst, peer) for src, dst in self.take(1 - self.c, self.theirs)]

    def out(self, turn):
        goes, _, x_way = self.ways[turn]
        peer = (self.z, self.y, 1 - self.x, self.c) if x_way else (self.z, 1 - self.y, self.x, self.c)
        return self.copy(turn, goes, self.boxes[turn], peer)

    def to_z(self, k):
        to = (self.z + k) & (LINE - 1)
        return self.copy(2, self.line(to), self.boxes[2].at[k - 1], (to, self.y, self.x, self.c))

    def all_loads(self):
        return pltpu.make_async_copy(self.own, self.own, self.near.at[0])

    def all_core(self):
        return self.copy(3, self.theirs, self.theirs, (self.z, self.y, self.x, 1 - self.c))

    def all_z(self):
        return self.copy(2, self.boxes[2], self.boxes[2], (self.z, self.y, self.x, 1 - self.c))

    def load(self):
        for one in self.loads() + self.to_core():
            one.start()

    def first(self):
        self.all_loads().wait()
        self.all_core().wait_recv()
        self.own[...] = self.own[...] + self.theirs[...]
        self.out(0).start()

    def second(self):
        self.out(0).wait_recv()
        stays = self.ways[0][1]
        stays[...] = stays[...] + self.boxes[0][...]
        self.out(1).start()

    def settle(self):
        self.out(1).wait_recv()
        stays = self.ways[1][1]
        stays[...] = stays[...] + self.boxes[1][...]

    def third(self):
        self.settle()
        for k in range(1, LINE):
            self.to_z(k).start()

    def total(self):
        self.all_z().wait_recv()
        out = self.line(self.z)[...].astype(F32)
        for k in range(LINE - 1):
            out = out + self.boxes[2][k].astype(F32)
        self.all_z().wait_send()
        self.left()
        return out

    def left(self):
        for one in (self.all_core(), self.out(0), self.out(1)):
            one.wait_send()


class LineSum(Sum):
    def load(self):
        self.loads()[0].start()

    def third(self):
        self.loads()[0].wait()
        for k in range(1, LINE):
            self.to_z(k).start()

    def left(self):
        pass


def rows_of(start, size, extent=None):
    return pl.ds(pl.multiple_of(start, size), size if extent is None else extent)


PICK_PARTS = 2
PICK_ROWS = PATCHES // PICK_PARTS


def pick_step(part, order_ref, patches_ref, out_ref, at, wide_ref):
    values = patches_ref[...].astype(F32).reshape(PICK_ROWS * TOGETHER, D)
    store_wide(wide_ref, slice(0, PICK_ROWS * TOGETHER), values)
    for j in range(TOGETHER):
        hot = picked(order_ref[j : j + 1, :PAD], part * PICK_ROWS, PICK_ROWS)
        own = load_wide(wide_ref, pl.ds(j, PICK_ROWS, stride=TOGETHER)).astype(BF16)
        rows = pl.ds(pl.multiple_of(at + j * PAD, PAD), PAD)
        value = t_mm(hot, own)
        out_ref[rows, :] = jnp.where(part == 0, value, value + out_ref[rows, :].astype(F32)).astype(BF16)


def pick_in(images):
    blocks = images // TOGETHER
    last = PICK_PARTS * blocks - 1
    index = lambda i: (lax.shift_right_logical(jnp.minimum(i, last), 1), 0)
    place_of = lambda i: (jnp.minimum(i, last) & 1, index(i)[0], 0)
    return [pl.BlockSpec((TOGETHER, PATCHES), index), pl.BlockSpec((PICK_ROWS, TOGETHER, D), place_of)]


def pick_kernel(order_ref, patches_ref, out_ref, wide_ref):
    pick_step(pl.program_id(0) % PICK_PARTS, order_ref, patches_ref, out_ref, 0, wide_ref)


def pick(order, patches):
    images = order.shape[0]
    return pl.pallas_call(
        pick_kernel,
        grid=(images // TOGETHER * PICK_PARTS,),
        in_specs=pick_in(images),
        out_specs=pl.BlockSpec((TOGETHER * PAD, D), lambda i: (i // PICK_PARTS, 0)),
        out_shape=jax.ShapeDtypeStruct((images * PAD, D), BF16),
        scratch_shapes=[pltpu.VMEM((D // 128, PICK_ROWS * TOGETHER, 128), F32)],
        compiler_params=params(),
        name="pick",
    )(order, patches)


HALF = 384
OWN = 24
PIECES = 3
SHARE = 4 * HALF + BLOCK


def parts_of_groups(block, g):
    return [block[:, k * D + g * WIDTH : k * D + (g + 1) * WIDTH] for k in range(3)]


def chip_row(z, y, x):
    return rows_of(((2 * z + y) * 2 + x) * 2 * OWN, 2 * OWN)


def share_out(in_ref, out_ref, vectors_ref, share_ref):
    vectors = vectors_ref[...]
    row = lax.broadcasted_iota(jnp.int32, (vectors.shape[0], BLOCK), 0)
    lane = lax.broadcasted_iota(jnp.int32, (vectors.shape[0], BLOCK), 1)
    columns = t_mm(vectors, jnp.where(row == lane, 1.0, 0.0).astype(BF16)).astype(BF16)
    share_ref[...] = jnp.zeros_like(share_ref)
    for g in range(GROUPS):
        both = jnp.concatenate(parts_of_groups(in_ref, g), axis=1)
        for h in range(2):
            share_ref[h, :OWN, g * HALF : (g + 1) * HALF] = both[:, h * HALF : (h + 1) * HALF]
    for h in range(2):
        share_ref[h, :OWN, 3 * HALF : 4 * HALF] = out_ref[:, h * HALF : (h + 1) * HALF]
        share_ref[h, :OWN, 4 * HALF :] = columns


def both_rows(mine, theirs):
    c = place()[3]
    mine, theirs = mine.astype(F32)[:OWN], theirs.astype(F32)[:OWN]
    top, low = jnp.where(c == 0, mine, theirs), jnp.where(c == 0, theirs, mine)
    return jnp.concatenate([top, low], axis=0).astype(BF16)


def hidden_bias(columns, out_ref):
    rows = 4 * OWN
    row = lax.broadcasted_iota(jnp.int32, (rows, 4 * rows * 4), 0)
    lane = lax.broadcasted_iota(jnp.int32, (rows, 4 * rows * 4), 1)
    which, hidden = lane // (4 * rows), lane % (4 * rows)
    hot = jnp.where(hidden == (row // OWN) * (4 * OWN) + which * OWN + row % OWN, 1.0, 0.0).astype(BF16)
    take = lax.broadcasted_iota(jnp.int32, (16, 4 * rows * 4), 0) == 8 + lane[:1] // (4 * rows)
    for w in range(2 * LINE):
        spread = t_mm(columns[w * rows : (w + 1) * rows, :16], hot)
        line = sum_rows(jnp.where(take, spread, 0.0))
        own = sum(line[:, k * 4 * rows : (k + 1) * 4 * rows] for k in range(4))
        for s in range(CHUNKS):
            at = s * CHUNK + (w % 2) * HIDDEN + (w // 2) * BLOCK
            out_ref[:, at : at + BLOCK] = own[:, s * BLOCK : (s + 1) * BLOCK]


def scores_of(k4, q_apart):
    return mm_t(k4, q_apart) * SCALE


BLOCKS = 3


def low_one(x, vec_ref):
    normed, _ = norm_parts(x.astype(F32))
    return (normed * vec_ref[G1 : G1 + 1, :] + vec_ref[B1 : B1 + 1, :]).astype(BF16)


def attend_step(g, low, wi, vec_ref, mixed_ref, total_ref, att, at):
    cols = rows_of(g * WIDTH, WIDTH)
    product = mm(low, wi[...])
    mixed_ref[:, :WIDTH] = (product[:, :WIDTH] + vec_ref[QB : QB + 1, cols]).astype(BF16)
    mixed_ref[:, WIDTH : 2 * WIDTH] = product[:, WIDTH : 2 * WIDTH].astype(BF16)
    mixed_ref[:, 2 * WIDTH :] = (product[:, 2 * WIDTH :] + vec_ref[VB : VB + 1, cols]).astype(BF16)
    key_row = lax.broadcasted_iota(jnp.int32, (PAD, WIDTH), 0)
    for img in range(TOGETHER):
        rows = slice(img * PAD, (img + 1) * PAD)
        q4, k4, v4 = [mixed_ref[rows, k * WIDTH : (k + 1) * WIDTH] for k in range(3)]
        scores = jnp.where(key_row < VIS, scores_of(k4, heads_apart(q4)), -1e30)
        top = jnp.max(scores, axis=0, keepdims=True)
        raised = jnp.exp(scores - top)
        total = sum_rows(raised)
        weights = (raised * (1.0 / total)).astype(BF16)
        total_ref[0, img // SIDE, img % SIDE : img % SIDE + 1, :] = top + jnp.log(total)
        att[pl.ds(pl.multiple_of(at + img * PAD, PAD), PAD), cols] = heads_together(t_mm(weights, v4)).astype(BF16)


def attend_kernel(x_ref, wi_ref, vec_ref, mixed_ref, att_ref, total_ref, low):
    step = pl.program_id(0)
    g, b = step // BLOCKS, step % BLOCKS
    at = b * (TOGETHER * PAD)
    rows = rows_of(at, TOGETHER * PAD)

    @pl.when(g == 0)
    def _():
        low[rows, :] = low_one(x_ref[rows, :], vec_ref)

    attend_step(g, low[rows, :], wi_ref.at[0], vec_ref, mixed_ref, total_ref, att_ref, at)


def full(*shape):
    return pl.BlockSpec(shape, lambda i: (0,) * len(shape))


def whole(a):
    return full(*a.shape)


def by_group(*block, lead=0, blocks=BLOCKS):
    def index(i):
        g, b = of_three(jnp.minimum(jnp.maximum(i - lead, 0), GROUPS * blocks - 1), blocks)
        return (g, b, 0, 0) if len(block) == 4 else (b, g)

    return pl.BlockSpec(block, index)


def TOTALS(lead):
    return by_group(1, TOGETHER // SIDE, 8, WIDTH, lead=lead)


def totals_shape(rows):
    return jax.ShapeDtypeStruct((GROUPS, rows // (SIDE * PAD), 8, WIDTH), F32)


def attend(x, wi, vec):
    rows = x.shape[0]
    block = TOGETHER * PAD
    shape = jax.ShapeDtypeStruct
    return pl.pallas_call(
        attend_kernel,
        grid=(GROUPS * BLOCKS,),
        in_specs=[whole(x), pl.BlockSpec((1, D, D), lambda i: (i // BLOCKS, 0, 0)), whole(vec)],
        out_specs=[by_group(block, D), full(rows, D), TOTALS(0)],
        out_shape=[
            shape((rows, 3 * D), BF16), shape((rows, D), BF16), totals_shape(rows),
        ],
        scratch_shapes=[pltpu.VMEM((rows, D), BF16)],
        compiler_params=params(),
        name="attend",
    )(x, wi, vec)


def gelu_both(x):
    bell = jnp.exp(-0.5 * x * x) * 0.3989422804014327
    below = 0.5 * (1.0 + lax.erf(x * 0.7071067811865476))
    return x * below, below + x * bell


def feed_early(cot_ref, sums_ref, middle, low, grad, low_t, grad_t, feed, back, act, inner):
    rows, held = cot_ref.shape[0], grad.shape[0]
    grad[:rows, :] = cot_ref[...]
    grad[rows:, :] = jnp.zeros((held - rows, D), BF16)
    sums_ref[DB : DB + 1, :] = sum_rows(cot_ref[...].astype(F32))
    grad_t[:, held:] = jnp.zeros((D, grad_t.shape[1] - held), BF16)
    grad_t[:, :held] = grad[...].T


def feed_start(x_ref, att_ref, cot_ref, wo_ref, vec_ref, sums_ref, middle, low, grad, low_t, grad_t, feed, back, act, inner):
    rows = cot_ref.shape[0]
    images = rows // VIS
    held = middle.shape[1]
    feed[...] = jnp.zeros_like(feed)
    back[...] = jnp.zeros_like(back)
    act[held:, :] = jnp.zeros((act.shape[0] - held, HIDDEN), BF16)
    inner[held:, :] = jnp.zeros((act.shape[0] - held, HIDDEN), BF16)
    middle[:, rows:, :] = jnp.zeros((D // 128, held - rows, 128), F32)
    for g in range(images // TOGETHER):
        at = slice(g * TOGETHER * PAD, (g + 1) * TOGETHER * PAD)
        branch = mm(att_ref[at, :], wo_ref[...]) + vec_ref[OB : OB + 1, :]
        mid = x_ref[at, :].astype(F32) + branch
        for j in range(TOGETHER):
            token = pl.ds(g * TOGETHER + j, VIS, stride=images)
            store_wide(middle, token, mid[j * PAD : j * PAD + VIS])
    normed, _ = norm_parts(load_wide(middle))
    low[...] = (normed * vec_ref[G2 : G2 + 1, :] + vec_ref[B2 : B2 + 1, :]).astype(BF16)
    low_t[:, held:] = jnp.zeros((D, low_t.shape[1] - held), BF16)
    low_t[:, :held] = low[...].T


def feed_step(up, upb, down, upbg_ref, middle, low, grad, low_t, grad_t, feed, back, act, inner):
    half = low.shape[0] // 2
    upbg = jnp.zeros((1, HIDDEN), F32)
    for part in range(2):
        at = slice(part * half, (part + 1) * half)
        before = mm(low[at, :], up[...]) + upb
        hidden_grad = mm(grad[at, :], down[...])
        value, slope = gelu_both(before)
        act[at, :] = value.astype(BF16)
        before_grad = (hidden_grad * slope).astype(BF16)
        inner[at, :] = before_grad
        upbg = upbg + sum_rows(before_grad.astype(F32))
        feed[at, :] += mm_t(act[at, :], down[...])
        back[at, :] += mm_t(before_grad, up[...])
    upbg_ref[...] = upbg


def feed_grads(upg_ref, downg_ref, middle, low, grad, low_t, grad_t, feed, back, act, inner):
    downg_ref[...] = mm(grad_t[...], act[...]).astype(BF16)
    upg_ref[...] = mm(low_t[...], inner[...]).astype(BF16)


def feed_end(vec_ref, result_ref, mg_ref, sums_ref, middle, low, grad, low_t, grad_t, feed, back, act, inner):
    rows = result_ref.shape[0]
    images = rows // VIS
    held = low.shape[0]
    mid = load_wide(middle)
    result = feed[...] + mid + vec_ref[DB : DB + 1, :]
    result_ref[...] = result[:rows].astype(BF16)
    normed, scale = norm_parts(mid)
    pull = back[...]
    sums_ref[G2 : G2 + 1, :] = sum_rows(pull * normed)
    sums_ref[B2 : B2 + 1, :] = sum_rows(pull)
    mid_grad = grad[...].astype(F32) + norm_back(pull, vec_ref[G2 : G2 + 1, :], normed, scale)
    real = lax.broadcasted_iota(jnp.int32, (held, 1), 0) < rows
    mid_grad = jnp.where(real, mid_grad, 0.0)
    sums_ref[OB : OB + 1, :] = sum_rows(mid_grad.astype(BF16).astype(F32))
    store_wide(middle, slice(None), mid_grad)
    for j in range(images):
        out = j * PAD
        token = pl.ds(j, VIS, stride=images)
        own = jnp.concatenate([load_wide(middle, token), jnp.zeros((PAD - VIS, D), F32)], axis=0)
        mg_ref[out : out + PAD, :] = own.astype(BF16)


def feed_scratch(rows):
    held = -(-rows // 32) * 32
    deep = -(-rows // 256) * 256
    return [
        pltpu.VMEM((D // 128, held, 128), F32),
        pltpu.VMEM((held, D), BF16),
        pltpu.VMEM((held, D), BF16),
        pltpu.VMEM((D, deep), BF16),
        pltpu.VMEM((D, deep), BF16),
        pltpu.VMEM((held, D), F32),
        pltpu.VMEM((held, D), F32),
        pltpu.VMEM((deep, HIDDEN), BF16),
        pltpu.VMEM((deep, HIDDEN), BF16),
    ]


def feed_kernel(
    x_ref, att_ref, cot_ref, wo_ref, vec_ref, up_ref, upb_ref, down_ref,
    result_ref, mg_ref, upg_ref, downg_ref, upbg_ref, sums_ref, *scratch,
):
    step = pl.program_id(0)

    @pl.when(step == 0)
    def _():
        feed_early(cot_ref, sums_ref, *scratch)
        feed_start(x_ref, att_ref, cot_ref, wo_ref, vec_ref, sums_ref, *scratch)

    feed_step(up_ref, upb_ref[...], down_ref, upbg_ref, *scratch)
    feed_grads(upg_ref, downg_ref, *scratch)

    @pl.when(step == pl.num_programs(0) - 1)
    def _():
        feed_end(vec_ref, result_ref, mg_ref, sums_ref, *scratch)


def feed_forward(x, att, cot, wo, vec, up, upb, down):
    rows = cot.shape[0]
    ff = up.shape[1]
    hid = lambda r: pl.BlockSpec((r, HIDDEN), lambda i: (0, i))
    return pl.pallas_call(
        feed_kernel,
        grid=(ff // HIDDEN,),
        in_specs=[whole(x), whole(att), whole(cot), whole(wo), whole(vec), hid(D), hid(1), hid(D)],
        out_specs=[whole(cot), full(x.shape[0], D), hid(D), hid(D), hid(1), full(8, D)],
        out_shape=[
            jax.ShapeDtypeStruct(cot.shape, BF16),
            jax.ShapeDtypeStruct((x.shape[0], D), BF16),
            jax.ShapeDtypeStruct((D, ff), BF16),
            jax.ShapeDtypeStruct((D, ff), BF16),
            jax.ShapeDtypeStruct((1, ff), F32),
            jax.ShapeDtypeStruct((8, D), F32),
        ],
        scratch_shapes=feed_scratch(rows),
        compiler_params=params(),
        name="feed_forward",
    )(x, att, cot, wo, vec, up, upb, down)


FORWARD = {
    0: [("start", "v"), ("start", "g0"), ("start", "g1"), ("start", "g2"), ("start", "d0")],
    3: [("first", "v")],
    4: [("first", "g0"), ("start", "u0")],
    5: [("second", "v"), ("start", "out")],
    6: [("core", "v"), ("finish", "v")],
    7: [("first", "g2")],
    8: [("second", "g1"), ("core", "g1"), ("first", "d0")],
    9: [("finish", "g1"), ("second", "g2"), ("first", "u0"), ("start", "u1")],
    10: [("first", "out")],
    11: [("core", "g2"), ("second", "d0"), ("start", "d1")],
    12: [("finish", "g2"), ("second", "u0")],
    13: [("second", "out"), ("first", "u1"), ("start", "u2")],
    14: [("core", "d0"), ("core", "u0"), ("first", "d1")],
    15: [("finish", "u0"), ("finish", "d0"), ("core", "out"), ("finish", "out"), ("start", "d2")],
    16: [("second", "u1"), ("second", "d1"), ("first", "u2")],
    17: [("first", "d2")],
    18: [("core", "u1"), ("core", "d1")],
    19: [("load", "su"), ("load", "sd"), ("finish", "u1"), ("finish", "d1"), ("second", "u2")],
    20: [("second", "d2"), ("first", "su"), ("first", "sd")],
    22: [("core", "u2"), ("core", "d2")],
    23: [("finish", "u2"), ("finish", "d2"), ("second", "su")],
    24: [("second", "sd")],
    26: [("settle", "su"), ("settle", "sd")],
}
BEFORE_ATTENTION = [("first", "g1"), ("second", "g0"), ("core", "g0"), ("finish", "g0")]


def forward_kernel(
    order_ref, patches_ref, in_ref, out_ref, vectors_ref, cot_ref, up_own, down_own,
    x_out, mixed_ref, total_ref, att_out, result_ref, mg_ref, upg_ref, downg_ref, upbg_ref, sums_ref, vec_ref, wi_ref, wo_ref,
    upf_ref, downf_ref, x_ref, att_ref, share_ref, other, piece, columns, upb, wi_all, wo_all, up_all, down_all, send, recv, own, near, *scratch,
):
    step = pl.program_id(0)
    picks = x_ref.shape[0] // (TOGETHER * PAD) * PICK_PARTS
    early = picks + GROUPS * BLOCKS
    last = pl.num_programs(0) - 1
    z, y, x, c = place()
    features = D // 4
    feed_parts, sum_parts = scratch[:9], scratch[9:]
    middle = feed_parts[0]
    low_all = mg_ref
    swap = remote(share_ref.at[1 - c], other, near.at[0], near.at[1], device(z, y, x, 1 - c))

    def weight(j, src, dst, s, x_first):
        def slot(z, y, x):
            rows = rows_of((2 * x + c) * features, features)
            return dst.at[rows, rows_of(s * CHUNK + y * HIDDEN + z * BLOCK, BLOCK)]

        def halves(c):
            return [dst.at[rows_of((2 * k + c) * features, features), pl.ds(s * CHUNK, CHUNK)] for k in range(2)]

        block = src.at[:, pl.ds(s * BLOCK, BLOCK)]
        def span(count):
            rows, count = (features, count) if count <= 8 else (2 * features, count // 2)
            return dst.at[pl.ds(0, rows), pl.ds(0, count * BLOCK)]

        return Gather(block, slot, x_first, halves, span, send.at[j], recv.at[j], own.at[j])

    def square(j, k, dst, x_first, start=0, width=HALF, direct=False):
        lanes = lambda c: rows_of(c * HALF + start, BLOCK, width)
        slot = lambda z, y, x: dst.at[chip_row(z, y, x), lanes(c)]
        halves = lambda c: [dst.at[:, lanes(c)]]
        block = piece.at[:, pl.ds(k * HALF + start, width)]
        span = lambda count: dst.at[pl.ds(0, count * 2 * OWN), pl.ds(0, width)]
        return Gather(block, slot, x_first, halves, span, send.at[j], recv.at[j], own.at[j], direct)

    items = {}
    for s in range(CHUNKS):
        items[f"u{s}"] = [weight(2 * s, up_own, up_all, s, True)]
        items[f"d{s}"] = [weight(2 * s + 1, down_own, down_all, s, False)]
    j = 2 * CHUNKS
    slot = lambda z, y, x: columns.at[chip_row(z, y, x)]
    span = lambda count: columns.at[pl.ds(0, count * 2 * OWN)]
    items["v"] = [Gather(piece.at[:, pl.ds(4 * HALF, BLOCK)], slot, True, lambda c: [], span, send.at[j], recv.at[j], own.at[j], True)]
    items["g0"] = [square(j + 1, 0, wi_all.at[0], True, direct=True)]
    items["g1"] = [square(j + 3, 1, wi_all.at[1], True, direct=True)]
    items["g2"] = [square(j + 4, 2, wi_all.at[2], False)]
    items["out"] = [square(j + 5, 3, wo_all, True)]
    for name, one in zip(("su", "sd"), feed_sums((up_all, down_all), [0], *sum_parts)[0]):
        items[name] = [one]
    copies = [
        pltpu.make_async_copy(wi_all, wi_ref, near.at[2]),
        pltpu.make_async_copy(wo_all, wo_ref, near.at[3]),
        pltpu.make_async_copy(x_ref, x_out, near.at[2 + 2 * CHUNKS]),
        pltpu.make_async_copy(att_ref, att_out, near.at[3 + 2 * CHUNKS]),
    ]
    moves = []
    kept = CHUNK // HIDDEN
    for k in range(kept, CHUNKS * kept):
        lanes, dst = pl.ds(k * HIDDEN, HIDDEN), pl.ds((k - kept) * HIDDEN, HIDDEN)
        moves.append(pltpu.make_async_copy(up_all.at[:, lanes], upg_ref.at[:, dst], near.at[10 + 2 * (k - kept)]))
        moves.append(pltpu.make_async_copy(down_all.at[:, lanes], downg_ref.at[:, dst], near.at[11 + 2 * (k - kept)]))

    @pl.when(step == 0)
    def _():
        share_out(in_ref, out_ref, vectors_ref, share_ref)
        greet()
        swap.start()
        swap.wait()
        piece[...] = both_rows(share_ref[c], other[...])

    def run(acts):
        for act, which in acts:
            for one in items[which]:
                getattr(one, act)()

    at_step(step, FORWARD, run)

    lines = rows_of(y * HIDDEN, HIDDEN)
    for j, ref in enumerate((upf_ref, downf_ref)):
        copies.append(pltpu.make_async_copy(sum_parts[0].at[j, x, :, lines], ref, near.at[18 + j]))

    @pl.when(step == 26)
    def _():
        for one in copies[4:]:
            one.start()

    @pl.when(step < picks)
    def _():
        block = lax.shift_right_logical(step, 1)
        pick_step(step & 1, order_ref, patches_ref, x_ref, block * (TOGETHER * PAD), middle)

    @pl.when(step == picks - 1)
    def _():
        feed_early(cot_ref, sums_ref, *feed_parts)

    @pl.when(step == picks)
    def _():
        copies[2].start()
        vec_ref[...] = columns[...].astype(F32).T[:16]
        hidden_bias(columns[...], upb)
        for k in range(BLOCKS):
            block = slice(k * TOGETHER * PAD, (k + 1) * TOGETHER * PAD)
            low_all[block, :] = low_one(x_ref[block, :], vec_ref)
        run(BEFORE_ATTENTION)

    g, b = of_three(jnp.minimum(jnp.maximum(step - picks, 0), GROUPS * BLOCKS - 1), BLOCKS)
    at = b * (TOGETHER * PAD)
    rows = rows_of(at, TOGETHER * PAD)

    @pl.when((step >= picks) & (step < early))
    def _():
        attend_step(g, low_all[rows, :], wi_all.at[g], vec_ref, mixed_ref, total_ref, att_ref, at)

    @pl.when(step == early)
    def _():
        for k in (0, 1, 3):
            copies[k].start()
        feed_start(x_ref, att_ref, cot_ref, wo_all, vec_ref, sums_ref, *feed_parts)

    late = jnp.maximum(step - early, 0)
    lanes = rows_of(lax.shift_right_logical(late, 1) * HIDDEN, HIDDEN)

    @pl.when((step >= early) & (late & 1 == 0))
    def _():
        feed_step(up_all.at[:, lanes], upb[:, lanes], down_all.at[:, lanes], upbg_ref, *feed_parts)

    @pl.when((step >= early) & (late & 1 == 1))
    def _():
        feed_grads(up_all.at[:, lanes], down_all.at[:, lanes], *feed_parts)

    def move(pair):
        for one in pair:
            one.start()

    at_step(step, {early + 2 * (kept + k) + 1: moves[2 * k : 2 * k + 2] for k in range(len(moves) // 2)}, move)

    @pl.when(step == last)
    def _():
        feed_end(vec_ref, result_ref, mg_ref, sums_ref, *feed_parts)
        for name in ("su", "sd"):
            items[name][0].left()
        for one in copies + moves:
            one.wait()


def forward(order, patches, project_in, project_out, vectors, cot, up, down):
    images = order.shape[0]
    rows = images * PAD
    block = TOGETHER * PAD
    picks = images // TOGETHER * PICK_PARTS
    early = picks + GROUPS * BLOCKS
    ff = CHUNKS * CHUNK
    late = 2 * ff // HIDDEN
    here = pl.BlockSpec(memory_space=pl.ANY)
    shape = jax.ShapeDtypeStruct
    count = 2 * CHUNKS + 6
    done = (D // 4, HIDDEN)
    return pl.pallas_call(
        forward_kernel,
        grid=(early + late,),
        in_specs=pick_in(images) + [whole(project_in), whole(project_out), whole(vectors), whole(cot), here, here],
        out_specs=[
            here, by_group(block, D, lead=picks), TOTALS(picks), here,
            whole(cot), full(rows, D), here, here,
            pl.BlockSpec((1, HIDDEN), lambda i: (0, lax.shift_right_logical(jnp.maximum(i - early, 0), 1))),
            full(8, D), full(16, D), here, here, here, here,
        ],
        out_shape=[
            shape((rows, D), BF16), shape((rows, 3 * D), BF16), totals_shape(rows), shape((rows, D), BF16),
            shape(cot.shape, BF16), shape((rows, D), BF16), shape((D, ff - CHUNK), BF16), shape((D, ff - CHUNK), BF16),
            shape((1, ff), F32), shape((8, D), F32), shape((16, D), F32),
            shape((GROUPS, D, D), BF16), shape((D, D), BF16), shape(done, BF16), shape(done, BF16),
        ],
        scratch_shapes=[
            pltpu.VMEM((rows, D), BF16),
            pltpu.VMEM((rows, D), BF16),
            pltpu.VMEM((2, 32, SHARE), BF16),
            pltpu.VMEM((32, SHARE), BF16),
            pltpu.VMEM((2 * OWN, SHARE), BF16),
            pltpu.VMEM((D, BLOCK), BF16),
            pltpu.VMEM((1, ff), F32),
            pltpu.VMEM((GROUPS, D, D), BF16),
            pltpu.VMEM((D, D), BF16),
            pltpu.VMEM((D, ff), BF16),
            pltpu.VMEM((D, ff), BF16),
            pltpu.SemaphoreType.DMA((count, Gather.COPIES)),
            pltpu.SemaphoreType.DMA((count, Gather.COPIES)),
            pltpu.SemaphoreType.DMA((count,)),
            pltpu.SemaphoreType.DMA((12 + 2 * (CHUNKS - 1) * (CHUNK // HIDDEN),)),
        ] + feed_scratch(cot.shape[0]) + feed_sum_scratch(1),
        compiler_params=params(collective_id=2, has_side_effects=True),
        name="forward",
    )(order, patches, project_in, project_out, vectors, cot, up, down)


BACKWARD = {
    0: [("load", 1), ("load", 2), ("load", 0)],
    1: [("first", 1), ("first", 2), ("third", 0)],
    3: [("second", 1), ("load", "out"), ("load", "g0")],
    4: [("first", "out"), ("first", "g0")],
    5: [("second", 2)],
    6: [("third", 1), ("load", "g1"), ("total", 0)],
    8: [("second", "out"), ("second", "g0"), ("first", "g1")],
    9: [("third", 2), ("total", 1), ("load", "g2"), ("load", "v")],
    10: [("third", "out"), ("third", "g0"), ("first", "g2"), ("first", "v")],
    11: [("second", "g1")],
    12: [("load", "late"), ("second", "g2"), ("second", "v"), ("first", "late")],
    13: [("third", "g1"), ("second", "late")],
    14: [("third", "g2"), ("third", "late"), ("third", "v"), ("total", 2), ("total", "out")],
}
LAST = [("total", "g0"), ("total", "g1"), ("total", "v"), ("total", "g2")]
BACK = 3


def unattend_step(mixed_ref, att_grad, totals, grads, g, at):
    key_row = lax.broadcasted_iota(jnp.int32, (PAD, WIDTH), 0)
    for img in range(TOGETHER):
        rows = slice(img * PAD, (img + 1) * PAD)
        q4, k4, v4 = [mixed_ref[rows, k * WIDTH : (k + 1) * WIDTH] for k in range(3)]
        q_apart = heads_apart(q4)
        a_apart = heads_apart(att_grad[rows, :])
        exact = jnp.exp(scores_of(k4, q_apart) - totals[0, img // SIDE, img % SIDE : img % SIDE + 1, :])
        exact = jnp.where(key_row < VIS, exact, 0.0)
        pulled = mm_t(v4, a_apart)
        centre = sum_rows(exact * pulled)
        score_grad = (exact * (pulled - centre)).astype(BF16)
        q_grad = heads_together(t_mm(score_grad, k4)) * SCALE
        k_grad = mm(score_grad, q_apart) * SCALE
        v_grad = mm(exact.astype(BF16), a_apart)
        out = pl.ds(pl.multiple_of(at + img * PAD, PAD), PAD)
        grads[g, out, :WIDTH] = q_grad.astype(BF16)
        grads[g, out, WIDTH : 2 * WIDTH] = k_grad.astype(BF16)
        grads[g, out, 2 * WIDTH :] = v_grad.astype(BF16)


def pull_step(x, grads, rows, wi_ref, pull_ref, sums_ref):
    normed, _ = norm_parts(x.astype(F32))
    pull = sum(mm_t(grads[g, rows, :], wi_ref[g]) for g in range(GROUPS))
    sums_ref[G1 : G1 + 1, :] += sum_rows(pull * normed)
    sums_ref[B1 : B1 + 1, :] += sum_rows(pull)
    pull_ref[rows, :] = pull


def unnorm_step(x, mg, pull, vec_ref, ig_ref):
    normed, scale = norm_parts(x.astype(F32))
    ig_ref[...] = (mg.astype(F32) + norm_back(pull, vec_ref[G1 : G1 + 1, :], normed, scale)).astype(BF16)


def backward_kernel(x_in, mg_in, mixed_ref, att_ref, total_ref, wi_in, wo_ref, vec_ref, *refs):
    step = pl.program_id(0)
    walk = GROUPS * BACK
    last = pl.num_programs(0) - 1
    g, b = of_three(jnp.minimum(step, walk - 1), BACK)
    b = jnp.where(step >= walk, jnp.where(step >= walk + BACK, step - walk - BACK, step - walk), b)
    at = b * (TOGETHER * PAD)
    rows = rows_of(at, TOGETHER * PAD)
    x_ref, mg_ref, wi_ref, brought = refs[-4:]
    refs = refs[:-4]
    remote_sums = len(refs) > 12
    brings = [pltpu.make_async_copy(wi_in, wi_ref, brought.at[2 * BACK])]
    for k in range(BACK):
        block = pl.ds(k * TOGETHER * PAD, TOGETHER * PAD)
        brings.insert(2 * k, pltpu.make_async_copy(x_in.at[block], x_ref.at[block], brought.at[2 * k]))
        brings.insert(2 * k + 1, pltpu.make_async_copy(mg_in.at[block], mg_ref.at[block], brought.at[2 * k + 1]))

    @pl.when(step == 0)
    def _():
        for one in brings:
            one.start()
    if remote_sums:
        upg_ref, downg_ref, sums_two_ref, upbg_ref, up_first, down_first = refs[:6]
        refs = refs[2:]
        ig_ref, wi_out, wo_out, vec_out, upf_ref, downf_ref = refs[4:10]
        low_t, att_t, grads, pull, sums_ref, wig_ref, wog_ref, end, other_end, end_send, end_recv = refs[10:21]
        feed_parts, square_parts, early_parts, late_parts, line_parts = refs[21:30], refs[30:38], refs[38:46], refs[46:54], refs[54:]
        z, y, x, c = place()
        items = dict(enumerate(feed_sums((upg_ref, downg_ref), range(1, CHUNKS), *feed_parts), 1))
        for j, name in enumerate(("g0", "g1", "out")):
            src = wog_ref if name == "out" else wig_ref.at[j]
            items[name] = [square_sum(j, j, src, slice(0, HALF), j == 0, *square_parts)]
        cuts = [slice(0, 2 * BLOCK), slice(2 * BLOCK, HALF)]
        items["g2"] = [square_sum(3, 3 + j, wig_ref.at[2], cut, j == 0, *square_parts) for j, cut in enumerate(cuts)]
        items[0] = [line_sum(j, src, *line_parts) for j, src in enumerate((up_first, down_first))]
        items["v"] = [vector_sum(*early_parts)]
        items["late"] = [vector_sum(*late_parts)]
        places = {"g0": 0, "g1": 1, "g2": 2, "out": 3}

        def swap(j):
            give = end.at[j, pl.ds(pl.multiple_of((1 - c) * OWN, 8), OWN)]
            return remote(give, other_end.at[j], end_send.at[j], end_recv.at[j], device(z, y, x, 1 - c))

        def act(name, which):
            values = [getattr(one, name)() for one in items[which]]
            if name != "total":
                return
            if which in (0, 1, 2):
                lanes = slice(which * BLOCK, (which + 1) * BLOCK)
                upf_ref[:, lanes], downf_ref[:, lanes] = values
            elif which in places:
                end[places[which]] = jnp.concatenate(values, axis=1)
                swap(places[which]).start()
            else:
                early = which == "v"
                value = jnp.where(c == 0, values[0][:, :OWN], values[0][:, OWN : 2 * OWN])
                if early:
                    vec_out[:6, :OWN] = value[:6]
                    vec_out[6:7, :] = jnp.where(c == 0, values[0][6:7], values[0][7:8])
                else:
                    vec_out[8:, :OWN] = value

        def run(acts):
            for name, which in acts:
                if (name, which) == ("load", "v"):
                    own = [sums_ref[k : k + 1, :] for k in (QB, VB)]
                    own += [sums_two_ref[k : k + 1, :] for k in (OB, G2, B2, DB)]
                    items["v"][0].fill(jnp.concatenate(own, axis=0), upbg_ref)
                if (name, which) == ("load", "late"):
                    items["late"][0].fill(sums_ref[G1 : B1 + 1, :])
                act(name, which)

        @pl.when(step == 0)
        def _():
            greet()

        at_step(step, BACKWARD, run)
    else:
        ig_ref, wi_out, wo_out, sums_ref, low_t, att_t, grads, pull, wig_ref, wog_ref = refs

    @pl.when(step == 0)
    def _():
        sums_ref[...] = jnp.zeros_like(sums_ref)
        if remote_sums:
            vec_out[...] = jnp.zeros_like(vec_out)

    for k in range(BACK):

        @pl.when(step == k)
        def _(k=k):
            brings[2 * k].wait()
            brings[2 * k + 1].wait()

    @pl.when(step == walk)
    def _():
        brings[-1].wait()

    @pl.when(step < BACK)
    def _():
        low_t[:, rows] = low_one(x_ref[rows, :], vec_ref).T
        att_t[:, rows] = att_ref[...].T

    @pl.when(step < walk)
    def _():
        cols = rows_of(g * WIDTH, WIDTH)
        att_grad = mm_t(mg_ref[rows, :], wo_ref[cols, :]).astype(BF16)
        unattend_step(mixed_ref, att_grad, total_ref, grads, g, at)
        own = grads[g, rows, :]
        sums_ref[QB : QB + 1, cols] += sum_rows(own[:, :WIDTH].astype(F32))
        sums_ref[VB : VB + 1, cols] += sum_rows(own[:, 2 * WIDTH :].astype(F32))

    @pl.when(step == BACK - 1)
    def _():
        wog_ref[...] = mm(att_t[...], mg_ref[...]).astype(BF16).reshape(wog_ref.shape)

    @pl.when((b == BACK - 1) & (step < walk))
    def _():
        wig_ref[g] = mm(low_t[...], grads[g]).astype(BF16).reshape(wig_ref.shape[1:])

    @pl.when((step >= walk) & (step < walk + BACK))
    def _():
        pull_step(x_ref[rows, :], grads, rows, wi_ref, pull, sums_ref)

    @pl.when(step >= walk + BACK)
    def _():
        unnorm_step(x_ref[rows, :], mg_ref[rows, :], pull[rows, :], vec_ref, ig_ref)

    @pl.when(step == last)
    def _():
        if not remote_sums:
            wi_out[...] = wig_ref[...].reshape(wi_out.shape)
            wo_out[...] = wog_ref[...].reshape(wo_out.shape)
            return
        for name, which in LAST:
            act(name, which)
        for j in range(PIECES + 1):
            swap(j).wait()
            mine, theirs = end[j, pl.ds(pl.multiple_of(c * OWN, 8), OWN), :], other_end[j]
            both = jnp.concatenate([jnp.where(c == 0, mine, theirs), jnp.where(c == 0, theirs, mine)], axis=1)
            if j < GROUPS:
                for k in range(3):
                    wi_out[:, k * D + j * WIDTH : k * D + (j + 1) * WIDTH] = both[:, k * WIDTH : (k + 1) * WIDTH]
            else:
                wo_out[...] = both
        act("total", "late")


CHIPS = (LINE, 2, 2, 2 * OWN)


def ways_of(mine, x_first):
    z, y, x, c = place()
    if x_first:
        return [(mine.at[:, :, 1 - x], mine.at[:, :, x], True), (mine.at[:, 1 - y, x], mine.at[:, y, x], False)]
    return [(mine.at[:, 1 - y], mine.at[:, y], False), (mine.at[:, y, 1 - x], mine.at[:, y, x], True)]


def square_sum(j, at, src, lanes, x_first, own, theirs, box_one, box_two, box_z, send, recv, near):
    z, y, x, c = place()
    width = lanes.stop - lanes.start

    def take(c, into):
        return [(src.at[:, :, :, :, rows_of(c * HALF + lanes.start, BLOCK, width)], into)]

    lanes = pl.ds(lanes.start, width)
    mine = own.at[j, :, :, :, :, lanes]
    line = lambda to: mine.at[to, y, x]
    boxes = (box_one.at[j, :, :, :, lanes], box_two.at[j, :, :, lanes], box_z.at[j, :, :, lanes])
    return Sum(
        take, mine, theirs.at[j, :, :, :, :, lanes], ways_of(mine, x_first), line, boxes, send.at[at], recv.at[at], near.at[at]
    )


class VectorSum(Sum):
    def fill(self, vectors, hidden=None):
        self.own[...] = jnp.zeros(self.own.shape, F32)
        count, width = vectors.shape[0], 4 * OWN
        for k in range(2 * LINE * 2):
            z, y, x = k // 4, k // 2 % 2, k % 2
            self.own[z, y, x, :count, : 2 * OWN] = vectors[:, k * 2 * OWN : (k + 1) * 2 * OWN]
            if hidden is not None:
                at = [s * CHUNK + y * HIDDEN + z * BLOCK for s in range(CHUNKS)]
                line = jnp.concatenate([hidden[:, a : a + BLOCK] for a in at], axis=1)
                for c in range(2):
                    start = (2 * x + c) * width
                    self.own[z, y, x, 6 + c : 7 + c, :width] = line[:, start : start + width]

    def loads(self):
        return []

    def first(self):
        self.all_core().wait_recv()
        self.all_core().wait_send()
        self.own[...] = self.own[...] + self.theirs[...]
        self.out(0).start()

    def total(self):
        self.all_z().wait_recv()
        out = self.line(self.z)[...]
        for k in range(LINE - 1):
            out = out + self.boxes[2][k]
        for one in (self.out(0), self.out(1), self.all_z()):
            one.wait_send()
        return out


def line_sum(j, src, own, box_z, send, recv, near):
    mine = own.at[j]
    line = lambda to: mine.at[:, rows_of(to * BLOCK, BLOCK)]
    take = lambda c, into: [(src, into)]
    return LineSum(take, mine, mine, None, line, (None, None, box_z.at[j]), send.at[j], recv.at[j], near.at[j])


def line_sum_scratch():
    return [
        pltpu.VMEM((2, D // 4, HIDDEN), BF16),
        pltpu.VMEM((2, LINE - 1, D // 4, BLOCK), BF16),
        pltpu.SemaphoreType.DMA((2, Sum.COPIES)),
        pltpu.SemaphoreType.DMA((2, Sum.COPIES)),
        pltpu.SemaphoreType.DMA((2, 1)),
    ]


def vector_sum(own, theirs, box_one, box_two, box_z, send, recv, near):
    z, y, x, c = place()
    mine = own.at[0]
    line = lambda to: mine.at[to, y, x]
    boxes = (box_one.at[0], box_two.at[0], box_z.at[0])
    return VectorSum(
        lambda c, into: [(mine, into)], mine, theirs.at[0], ways_of(mine, False), line, boxes, send.at[0], recv.at[0], near.at[0]
    )


def square_sum_scratch(count, lanes=HALF, dtype=BF16, rows=2 * OWN, copies=None):
    chips = CHIPS[:3] + (rows,)
    copies = count if copies is None else copies
    return [
        pltpu.VMEM((count,) + chips + (lanes,), dtype),
        pltpu.VMEM((count,) + chips + (lanes,), dtype),
        pltpu.VMEM((count, LINE, 2, rows, lanes), dtype),
        pltpu.VMEM((count, LINE, rows, lanes), dtype),
        pltpu.VMEM((count, LINE - 1, rows, lanes), dtype),
        pltpu.SemaphoreType.DMA((copies, Sum.COPIES)),
        pltpu.SemaphoreType.DMA((copies, Sum.COPIES)),
        pltpu.SemaphoreType.DMA((copies, 1)),
    ]


def feed_sums(grads_refs, which_chunks, own, theirs, box_y, box_x, box_two, box_z, send, recv, near):
    z, y, x, c = place()
    features = D // 4

    def one(s, which):
        grads = grads_refs[which]
        j = 2 * s + which

        def take(c, into):
            return [
                (grads.at[rows_of((2 * k + c) * features, features), pl.ds(s * CHUNK, CHUNK)], into.at[k])
                for k in range(2)
            ]

        mine = own.at[j]
        keep, give = rows_of(y * HIDDEN, HIDDEN), rows_of((1 - y) * HIDDEN, HIDDEN)
        if which == 0:
            ways = [
                (mine.at[:, :, give], mine.at[:, :, keep], False),
                (mine.at[1 - x, :, keep], mine.at[x, :, keep], True),
            ]
            box_one = box_y.at[s]
        else:
            ways = [(mine.at[1 - x], mine.at[x], True), (mine.at[x, :, give], mine.at[x, :, keep], False)]
            box_one = box_x.at[s]
        line = lambda to: mine.at[x, :, rows_of(y * HIDDEN + to * BLOCK, BLOCK)]
        boxes = (box_one, box_two.at[j], box_z.at[j])
        return Sum(lambda c, into: take(c, into), mine, theirs.at[j], ways, line, boxes, send.at[j], recv.at[j], near.at[j])

    return [[one(s, 0), one(s, 1)] for s in range(len(which_chunks))]


def feed_sum_scratch(chunks):
    features = D // 4
    count = 2 * chunks
    return [
        pltpu.VMEM((count, 2, features, CHUNK), BF16),
        pltpu.VMEM((count, 2, features, CHUNK), BF16),
        pltpu.VMEM((chunks, 2, features, HIDDEN), BF16),
        pltpu.VMEM((chunks, features, CHUNK), BF16),
        pltpu.VMEM((count, features, HIDDEN), BF16),
        pltpu.VMEM((count, LINE - 1, features, BLOCK), BF16),
        pltpu.SemaphoreType.DMA((count, Sum.COPIES)),
        pltpu.SemaphoreType.DMA((count, Sum.COPIES)),
        pltpu.SemaphoreType.DMA((count, 1)),
    ]


def backward(x, mg, mixed, att, totals, wi, wo, vec, *more):
    rows = x.shape[0]
    block = TOGETHER * PAD
    walk = GROUPS * BACK
    here = pl.BlockSpec(memory_space=pl.ANY)
    shape = jax.ShapeDtypeStruct
    scratch = [pltpu.VMEM((D, rows), BF16), pltpu.VMEM((D, rows), BF16), pltpu.VMEM((GROUPS, rows, D), BF16)]
    scratch += [pltpu.VMEM((rows, D), F32)]
    sums = [pltpu.VMEM((8, D), F32)]
    weights = [pltpu.VMEM((GROUPS,) + CHIPS + (D,), BF16), pltpu.VMEM(CHIPS + (D,), BF16)]
    specs = []
    if more:
        specs = [here, here] + [whole(a) for a in more[2:4]] + [here, here]
        own = (D // 4, CHUNKS * BLOCK)
        out = [(OWN, 3 * D), (OWN, D), (16, BLOCK), own, own]
        scratch += sums + weights + [
            pltpu.VMEM((PIECES + 1, 2 * OWN, HALF), F32),
            pltpu.VMEM((PIECES + 1, OWN, HALF), F32),
            pltpu.SemaphoreType.DMA((PIECES + 1,)),
            pltpu.SemaphoreType.DMA((PIECES + 1,)),
        ] + feed_sum_scratch(CHUNKS - 1) + square_sum_scratch(PIECES + 1, copies=PIECES + 2)
        scratch += square_sum_scratch(1, BLOCK, F32, 8) + square_sum_scratch(1, BLOCK, F32, 8) + line_sum_scratch()
        out_shape = [shape(s, F32) for s in out]
    else:
        out = [(GROUPS, D, D), (D, D), (8, D)]
        out_shape = [shape(s, F32 if s[0] == 8 else BF16) for s in out]
        scratch += weights
    return pl.pallas_call(
        backward_kernel,
        grid=(walk + BACK + BLOCKS,),
        in_specs=[
            here, here, by_group(block, D, blocks=BACK),
            pl.BlockSpec((block, D), lambda i: (jnp.minimum(i, BACK - 1), 0)),
            TOTALS(0), here, whole(wo), whole(vec),
        ] + specs,
        out_specs=[pl.BlockSpec((block, D), lambda i: (jnp.maximum(i - walk - BACK, 0), 0))] + [full(*s) for s in out],
        out_shape=[shape((rows, D), BF16)] + out_shape,
        scratch_shapes=scratch + [
            pltpu.VMEM((rows, D), BF16),
            pltpu.VMEM((rows, D), BF16),
            pltpu.VMEM((GROUPS, D, D), BF16),
            pltpu.SemaphoreType.DMA((2 * BACK + 1,)),
        ],
        compiler_params=params(collective_id=3, has_side_effects=True) if more else params(),
        name="backward",
    )(x, mg, mixed, att, totals, wi, wo, vec, *more)


def spread_kernel(order_ref, ig_ref, *refs):
    count = (len(refs) - 2) // 3
    out_ref, near = refs[count], refs[-1]
    given, outs, held = refs[:count], refs[count + 1 : 2 * count + 1], refs[2 * count + 1 : -1]
    step = pl.program_id(0)
    ins = [pltpu.make_async_copy(src, dst, near.at[j]) for j, (src, dst) in enumerate(zip(given, held))]
    outs = [pltpu.make_async_copy(src, dst, near.at[j]) for j, (src, dst) in enumerate(zip(held, outs))]

    @pl.when(step == 0)
    def _():
        for one in ins:
            one.start()

    @pl.when(step == 1)
    def _():
        for one in ins:
            one.wait()
        for one in outs:
            one.start()

    @pl.when(step == pl.num_programs(0) - 1)
    def _():
        for one in outs:
            one.wait()

    blocks = D // 128
    rows = out_ref.reshape(PATCHES * blocks * TOGETHER, 128)
    for j in range(TOGETHER):
        hot = picked(order_ref[j : j + 1, :PAD])
        own = mm(hot, ig_ref[j * PAD : (j + 1) * PAD, :])
        for k in range(blocks):
            at = pl.ds(k * TOGETHER + j, PATCHES, stride=blocks * TOGETHER)
            rows[at, :] = own[:, k * 128 : (k + 1) * 128]


def spread(order, ig, result, *more):
    images = order.shape[0]
    steps = images // TOGETHER
    passed = [pl.BlockSpec(memory_space=pl.ANY)] * (1 + len(more))
    shape = jax.ShapeDtypeStruct
    return pl.pallas_call(
        spread_kernel,
        grid=(steps,),
        in_specs=[
            pl.BlockSpec((TOGETHER, PATCHES), lambda i: (i, 0)),
            pl.BlockSpec((TOGETHER * PAD, D), lambda i: (i, 0)),
        ] + passed,
        out_specs=[pl.BlockSpec((PATCHES, 1, D // 128, TOGETHER, 128), lambda i: (0, i, 0, 0, 0))] + passed,
        out_shape=[shape((PATCHES, steps, D // 128, TOGETHER, 128), F32)] + [shape(a.shape, a.dtype) for a in (result,) + more],
        scratch_shapes=[pltpu.VMEM(a.shape, a.dtype) for a in (result,) + more] + [pltpu.SemaphoreType.DMA((1 + len(more),))],
        compiler_params=params(),
        name="spread",
    )(order, ig, result, *more)


def local(
    patches, keep_order, cotangent, first_gain, first_shift, project_in, query_bias, value_bias,
    project_out, output_bias, second_gain, second_shift, up_weight, up_bias, down_weight, down_bias,
):
    rows_own = project_in.shape[0]
    hidden_own = up_bias.shape[0]
    images = patches.shape[0]
    wide, narrow = lax.axis_size("wide"), lax.axis_size("narrow")
    vectors = [first_gain, first_shift, query_bias, value_bias, output_bias, second_gain, second_shift, down_bias]
    order = keep_order
    patches = patches.transpose(1, 0, 2)
    cot = cotangent.transpose(1, 0, 2).reshape(VIS * images, D)
    if (wide, narrow) == (8, 4):
        flat = jnp.concatenate([jnp.stack(vectors), up_bias.reshape(4, rows_own)], axis=0)
        x, mixed, totals, att, result, mg, upg, downg, upbg, sums_two, vec, wi, wo, up_zero, down_zero = forward(
            order, patches, project_in, project_out, flat, cot, up_weight.T, down_weight.T
        )
        ig, wig, wog, s, upf, downf = backward(
            x, mg, mixed, att, totals, wi, wo, vec, upg, downg, sums_two, upbg, up_zero, down_zero
        )
        patch_grad, result, wig, wog, s, upf, downf = spread(order, ig, result, wig, wog, s, upf, downf)
        upf, downf, upbf = upf.T, downf.T, s[6, : 4 * rows_own]
        s = [s[k, :rows_own] for k in (8, 9, 0, 1, 2, 3, 4, 5)]
    else:
        share = jnp.concatenate([jnp.stack(vectors).reshape(1, -1), up_bias.reshape(1, -1)], axis=1)
        shares = lax.all_gather(share, AXES, axis=0, tiled=True)
        vec = shares[:, : 8 * rows_own].reshape(-1, 8, rows_own).transpose(1, 0, 2).reshape(8, D)
        vec = jnp.pad(vec.astype(F32), ((0, 8), (0, 0)))
        upb = shares[:, 8 * rows_own :].reshape(1, -1).astype(F32)
        wi = lax.all_gather(project_in, AXES, axis=0, tiled=True)
        wo = lax.all_gather(project_out, AXES, axis=0, tiled=True)
        ffw = jnp.stack([up_weight.T, down_weight.T])
        ffw = lax.all_gather(ffw, "narrow", axis=1, tiled=True)
        ffw = lax.all_gather(ffw, "wide", axis=2, tiled=True)
        wi = wi.reshape(D, 3, GROUPS, WIDTH).transpose(2, 0, 1, 3).reshape(GROUPS, D, D)
        x = pick(order, patches)
        mixed, att, totals = attend(x, wi, vec)
        result, mg, upg, downg, upbg, sums_two = feed_forward(x, att, cot, wo, vec, ffw[0], upb, ffw[1])
        ig, wig, wog, sums_one = backward(x, mg, mixed, att, totals, wi, wo, vec)
        wig = wig.reshape(GROUPS, D, 3, WIDTH).transpose(1, 2, 0, 3).reshape(D, 3 * D)
        ffg = jnp.stack([upg, downg])
        ffg = lax.psum_scatter(ffg, "wide", scatter_dimension=2, tiled=True)
        ffg = lax.psum_scatter(ffg, "narrow", scatter_dimension=1, tiled=True).astype(F32)
        wig = lax.psum_scatter(wig, AXES, scatter_dimension=0, tiled=True).astype(F32)
        wog = lax.psum_scatter(wog, AXES, scatter_dimension=0, tiled=True).astype(F32)
        picks = [sums_one[G1], sums_one[B1], sums_one[QB], sums_one[VB]]
        picks += [sums_two[OB], sums_two[G2], sums_two[B2], sums_two[DB]]
        parts = jnp.stack(picks).reshape(8, -1, rows_own).transpose(1, 0, 2).reshape(-1, 8 * rows_own)
        parts = jnp.concatenate([parts, upbg.reshape(-1, hidden_own)], axis=1)
        own = lax.psum_scatter(parts, AXES, scatter_dimension=0, tiled=True)[0]
        s = [own[k * rows_own : (k + 1) * rows_own] for k in range(8)]
        upf, downf, upbf = ffg[0].T, ffg[1].T, own[8 * rows_own :]
        patch_grad, result = spread(order, ig, result)
    patch_grad = patch_grad.transpose(1, 3, 0, 2, 4).reshape(images, PATCHES, D)
    result = result.reshape(VIS, images, D).transpose(1, 0, 2)
    return (
        result, patch_grad, s[0], s[1], wig, s[2], s[3], wog, s[4], s[5], s[6], upf, upbf, downf, s[7],
    )


def solution(mesh):
    both = P(AXES)
    rows = P(AXES, None)
    cube = P(AXES, None, None)
    tile = P("wide", "narrow")
    return jax.shard_map(
        local,
        mesh=mesh,
        in_specs=(
            cube, rows, cube, both, both, rows, both, both, rows, both, both, both, tile, both, tile, both,
        ),
        out_specs=(
            cube, cube, both, both, rows, both, both, rows, both, both, both, tile, both, tile, both,
        ),
        check_vma=False,
    )
```

```python
import functools

import jax
import jax.numpy as jnp
from jax import lax
from jax.experimental import pallas as pl
from jax.experimental.pallas import tpu as pltpu
from jax.sharding import PartitionSpec as P

D = 768
HEADS = 12
HEAD_DIM = 64
PATCHES = 196
VIS = 49
PAD = 64
SIDE = 4
WIDTH = SIDE * HEAD_DIM
GROUPS = HEADS // SIDE
TOGETHER = 8
HIDDEN = 512
EPSILON = 1e-06
SCALE = HEAD_DIM ** (-0.5)
F32 = jnp.float32
BF16 = jnp.bfloat16
AXES = ("wide", "narrow")
G1, B1, QB, VB, OB, G2, B2, DB = range(8)


def params(**more):
    return pltpu.CompilerParams(vmem_limit_bytes=60 * 1024 * 1024, **more)


def mm(left, right):
    return jnp.dot(left, right, preferred_element_type=F32)


def mm_t(left, right):
    return lax.dot_general(left, right, (((1,), (1,)), ((), ())), preferred_element_type=F32)


def t_mm(left, right):
    return lax.dot_general(left, right, (((0,), (0,)), ((), ())), preferred_element_type=F32)


def norm_parts(values):
    mean = jnp.mean(values, axis=-1, keepdims=True)
    centred = values - mean
    spread = jnp.mean(centred * centred, axis=-1, keepdims=True)
    scale = lax.rsqrt(spread + EPSILON)
    return centred * scale, scale


def norm_back(grad, gain, normed, scale):
    pulled = grad * gain
    inner = jnp.mean(pulled * normed, axis=-1, keepdims=True)
    return scale * (pulled - jnp.mean(pulled, axis=-1, keepdims=True) - normed * inner)


def sum_rows(values):
    return jnp.sum(values, axis=0, keepdims=True)


def load_wide(ref, rows=slice(None)):
    return jnp.concatenate([ref[k, rows, :] for k in range(D // 128)], axis=1)


def store_wide(ref, rows, values):
    for k in range(D // 128):
        ref[k, rows, :] = values[:, k * 128 : (k + 1) * 128]


def heads_apart(block):
    lane = lax.broadcasted_iota(jnp.int32, block.shape, 1) // HEAD_DIM
    zero = jnp.zeros_like(block)
    return jnp.concatenate([jnp.where(lane == h, block, zero) for h in range(SIDE)], axis=0)


def heads_together(product):
    lane = lax.broadcasted_iota(jnp.int32, (HEAD_DIM, WIDTH), 1) // HEAD_DIM
    out = jnp.zeros((HEAD_DIM, WIDTH), F32)
    for h in range(SIDE):
        out = jnp.where(lane == h, product[h * HEAD_DIM : (h + 1) * HEAD_DIM], out)
    return out


def picked(order, first=0, count=PATCHES):
    lane = lax.broadcasted_iota(jnp.int32, (1, PAD), 1)
    order = jnp.where(lane < VIS, order, -1)
    row = lax.broadcasted_iota(jnp.int32, (count, PAD), 0) + first
    return jnp.where(row == order, 1.0, 0.0).astype(BF16)


LINE = 4
BLOCK = 128
CHUNK = 1024
CHUNKS = 3
MESH = pl.DeviceIdType.MESH


def place():
    wide, narrow = lax.axis_index("wide"), lax.axis_index("narrow")
    return lax.shift_right_logical(wide, 1), wide & 1, lax.shift_right_logical(narrow, 1), narrow & 1


def device(z, y, x, c):
    return (2 * z + y, 2 * x + c)


def at_step(step, plan, run):
    keys = sorted(plan)
    if len(keys) <= 2:
        for key in keys:
            pl.when(step == key)(functools.partial(run, plan[key]))
        return
    middle = keys[len(keys) // 2]
    low = {key: plan[key] for key in keys if key < middle}
    high = {key: plan[key] for key in keys if key >= middle}
    pl.when(step < middle)(lambda: at_step(step, low, run))
    pl.when(step >= middle)(lambda: at_step(step, high, run))


def of_three(i, size):
    group = (i >= size).astype(jnp.int32) + (i >= 2 * size).astype(jnp.int32)
    return group, i - group * size


def greet():
    z, y, x, c = place()
    barrier = pltpu.get_barrier_semaphore()
    peers = [device((z + k) & (LINE - 1), y, x, c) for k in range(1, LINE)]
    peers += [device(z, 1 - y, x, c), device(z, y, 1 - x, c), device(z, y, x, 1 - c), device(z, 1 - y, 1 - x, c)]
    for peer in peers:
        pl.semaphore_signal(barrier, inc=1, device_id=peer, device_id_type=MESH)
    pl.semaphore_wait(barrier, len(peers))


def remote(src, dst, send, recv, peer):
    return pltpu.make_async_remote_copy(
        src_ref=src, dst_ref=dst, send_sem=send, recv_sem=recv, device_id=peer, device_id_type=MESH
    )


class Gather:
    COPIES = 4

    def __init__(self, src, slot, x_first, halves, span, send, recv, own, direct=False):
        self.direct, self.span = direct, span
        self.src, self.slot, self.x_first, self.halves = src, slot, x_first, halves
        self.send, self.recv, self.own = send, recv, own
        self.z, self.y, self.x, self.c = place()

    def flip(self, z, first, second):
        y, x = self.y, self.x
        if first if self.x_first else second:
            x = 1 - x
        if second if self.x_first else first:
            y = 1 - y
        return z, y, x

    def line(self, k):
        return (self.z - k) & (LINE - 1)

    def copy(self, at, src, dst, peer):
        return remote(src, dst, self.send.at[at], self.recv.at[at], peer)

    def to_z(self, k):
        peer = device((self.z + k) & (LINE - 1), self.y, self.x, self.c)
        return self.copy(0, self.src, self.slot(self.z, self.y, self.x), peer)

    def to_first(self, k):
        slot = self.slot(self.line(k), self.y, self.x)
        peer = device(*self.flip(self.z, True, False), self.c)
        return self.copy(1, self.src if k == 0 else slot, slot, peer)

    def to_second(self, k):
        slot = self.slot(self.line(k), self.y, self.x)
        peer = device(*self.flip(self.z, False, True), self.c)
        return self.copy(2, self.src if k == 0 else slot, slot, peer)

    def on_to_second(self, k):
        slot = self.slot(*self.flip(self.line(k), True, False))
        peer = device(*self.flip(self.z, False, True), self.c)
        return self.copy(2, slot, slot, peer)

    def to_both(self, k):
        slot = self.slot(self.line(k), self.y, self.x)
        peer = device(*self.flip(self.z, True, True), self.c)
        return self.copy(2, self.src if k == 0 else slot, slot, peer)

    def to_core(self, j):
        part = self.halves(self.c)[j]
        return self.copy(3, part, part, device(self.z, self.y, self.x, 1 - self.c))

    def keep(self):
        return pltpu.make_async_copy(self.src, self.slot(self.z, self.y, self.x), self.own)

    def all_of(self, at, count):
        span = self.span(count)
        return self.copy(at, span, span, device(self.z, self.y, self.x, 1 - self.c))

    def start(self):
        self.keep().start()
        for k in range(1, LINE):
            self.to_z(k).start()
        self.to_first(0).start()
        self.to_second(0).start()
        if self.direct:
            self.to_both(0).start()

    def first(self):
        self.all_of(0, LINE - 1).wait_recv()
        for k in range(1, LINE):
            self.to_first(k).start()
            self.to_second(k).start()
            if self.direct:
                self.to_both(k).start()

    def second(self):
        self.all_of(1, LINE).wait_recv()
        for k in range(LINE):
            if not self.direct:
                self.on_to_second(k).start()

    def core(self):
        self.all_of(2, 2 * LINE).wait_recv()
        self.keep().wait()
        for j in range(len(self.halves(self.c))):
            self.to_core(j).start()

    def finish(self):
        held = len(self.halves(self.c)) > 0
        if held:
            self.all_of(3, 4 * LINE).wait_recv()
        self.all_of(0, LINE - 1).wait_send()
        self.all_of(1, LINE).wait_send()
        self.all_of(2, 2 * LINE).wait_send()
        if held:
            self.all_of(3, 4 * LINE).wait_send()


class Sum:
    COPIES = 4

    def __init__(self, take, own, theirs, ways, line, boxes, send, recv, near):
        self.take, self.own, self.theirs, self.ways, self.line, self.boxes = take, own, theirs, ways, line, boxes
        self.send, self.recv, self.near = send, recv, near
        self.z, self.y, self.x, self.c = place()

    def copy(self, at, src, dst, peer):
        return remote(src, dst, self.send.at[at], self.recv.at[at], device(*peer))

    def loads(self):
        return [pltpu.make_async_copy(src, dst, self.near.at[0]) for src, dst in self.take(self.c, self.own)]

    def to_core(self):
        peer = (self.z, self.y, self.x, 1 - self.c)
        return [self.copy(3, src, dst, peer) for src, dst in self.take(1 - self.c, self.theirs)]

    def out(self, turn):
        goes, _, x_way = self.ways[turn]
        peer = (self.z, self.y, 1 - self.x, self.c) if x_way else (self.z, 1 - self.y, self.x, self.c)
        return self.copy(turn, goes, self.boxes[turn], peer)

    def to_z(self, k):
        to = (self.z + k) & (LINE - 1)
        return self.copy(2, self.line(to), self.boxes[2].at[k - 1], (to, self.y, self.x, self.c))

    def all_loads(self):
        return pltpu.make_async_copy(self.own, self.own, self.near.at[0])

    def all_core(self):
        return self.copy(3, self.theirs, self.theirs, (self.z, self.y, self.x, 1 - self.c))

    def all_z(self):
        return self.copy(2, self.boxes[2], self.boxes[2], (self.z, self.y, self.x, 1 - self.c))

    def load(self):
        for one in self.loads() + self.to_core():
            one.start()

    def first(self):
        self.all_loads().wait()
        self.all_core().wait_recv()
        self.own[...] = self.own[...] + self.theirs[...]
        self.out(0).start()

    def second(self):
        self.out(0).wait_recv()
        stays = self.ways[0][1]
        stays[...] = stays[...] + self.boxes[0][...]
        self.out(1).start()

    def settle(self):
        self.out(1).wait_recv()
        stays = self.ways[1][1]
        stays[...] = stays[...] + self.boxes[1][...]

    def third(self):
        self.settle()
        for k in range(1, LINE):
            self.to_z(k).start()

    def total(self):
        self.all_z().wait_recv()
        out = self.line(self.z)[...].astype(F32)
        for k in range(LINE - 1):
            out = out + self.boxes[2][k].astype(F32)
        self.all_z().wait_send()
        self.left()
        return out

    def left(self):
        for one in (self.all_core(), self.out(0), self.out(1)):
            one.wait_send()


class LineSum(Sum):
    def load(self):
        self.loads()[0].start()

    def third(self):
        self.loads()[0].wait()
        for k in range(1, LINE):
            self.to_z(k).start()

    def left(self):
        pass


def rows_of(start, size, extent=None):
    return pl.ds(pl.multiple_of(start, size), size if extent is None else extent)


PICK_PARTS = 2
PICK_ROWS = PATCHES // PICK_PARTS


def pick_step(part, order_ref, patches_ref, out_ref, at, wide_ref):
    values = patches_ref[...].astype(F32).reshape(PICK_ROWS * TOGETHER, D)
    store_wide(wide_ref, slice(0, PICK_ROWS * TOGETHER), values)
    for j in range(TOGETHER):
        hot = picked(order_ref[j : j + 1, :PAD], part * PICK_ROWS, PICK_ROWS)
        own = load_wide(wide_ref, pl.ds(j, PICK_ROWS, stride=TOGETHER)).astype(BF16)
        rows = pl.ds(pl.multiple_of(at + j * PAD, PAD), PAD)
        value = t_mm(hot, own)
        out_ref[rows, :] = jnp.where(part == 0, value, value + out_ref[rows, :].astype(F32)).astype(BF16)


def pick_in(images):
    blocks = images // TOGETHER
    last = PICK_PARTS * blocks - 1
    index = lambda i: (lax.shift_right_logical(jnp.minimum(i, last), 1), 0)
    place_of = lambda i: (jnp.minimum(i, last) & 1, index(i)[0], 0)
    return [pl.BlockSpec((TOGETHER, PATCHES), index), pl.BlockSpec((PICK_ROWS, TOGETHER, D), place_of)]


def pick_kernel(order_ref, patches_ref, out_ref, wide_ref):
    pick_step(pl.program_id(0) % PICK_PARTS, order_ref, patches_ref, out_ref, 0, wide_ref)


def pick(order, patches):
    images = order.shape[0]
    return pl.pallas_call(
        pick_kernel,
        grid=(images // TOGETHER * PICK_PARTS,),
        in_specs=pick_in(images),
        out_specs=pl.BlockSpec((TOGETHER * PAD, D), lambda i: (i // PICK_PARTS, 0)),
        out_shape=jax.ShapeDtypeStruct((images * PAD, D), BF16),
        scratch_shapes=[pltpu.VMEM((D // 128, PICK_ROWS * TOGETHER, 128), F32)],
        compiler_params=params(),
        name="pick",
    )(order, patches)


HALF = 384
OWN = 24
PIECES = 3
SHARE = 4 * HALF + BLOCK


def parts_of_groups(block, g):
    return [block[:, k * D + g * WIDTH : k * D + (g + 1) * WIDTH] for k in range(3)]


def chip_row(z, y, x):
    return rows_of(((2 * z + y) * 2 + x) * 2 * OWN, 2 * OWN)


def share_out(in_ref, out_ref, vector_refs, share_ref):
    lines = [ref[...].astype(F32) for ref in vector_refs]
    lines = lines[:8] + [lines[8][:, k * OWN : (k + 1) * OWN] for k in range(4)]
    vectors = jnp.concatenate(lines, axis=0).astype(BF16)
    row = lax.broadcasted_iota(jnp.int32, (vectors.shape[0], BLOCK), 0)
    lane = lax.broadcasted_iota(jnp.int32, (vectors.shape[0], BLOCK), 1)
    columns = t_mm(vectors, jnp.where(row == lane, 1.0, 0.0).astype(BF16)).astype(BF16)
    share_ref[...] = jnp.zeros_like(share_ref)
    for g in range(GROUPS):
        both = jnp.concatenate(parts_of_groups(in_ref, g), axis=1)
        for h in range(2):
            share_ref[h, :OWN, g * HALF : (g + 1) * HALF] = both[:, h * HALF : (h + 1) * HALF]
    for h in range(2):
        share_ref[h, :OWN, 3 * HALF : 4 * HALF] = out_ref[:, h * HALF : (h + 1) * HALF]
        share_ref[h, :OWN, 4 * HALF :] = columns


def both_rows(mine, theirs):
    c = place()[3]
    mine, theirs = mine.astype(F32)[:OWN], theirs.astype(F32)[:OWN]
    top, low = jnp.where(c == 0, mine, theirs), jnp.where(c == 0, theirs, mine)
    return jnp.concatenate([top, low], axis=0).astype(BF16)


def hidden_bias(columns, out_ref):
    rows = 4 * OWN
    row = lax.broadcasted_iota(jnp.int32, (rows, 4 * rows * 4), 0)
    lane = lax.broadcasted_iota(jnp.int32, (rows, 4 * rows * 4), 1)
    which, hidden = lane // (4 * rows), lane % (4 * rows)
    hot = jnp.where(hidden == (row // OWN) * (4 * OWN) + which * OWN + row % OWN, 1.0, 0.0).astype(BF16)
    take = lax.broadcasted_iota(jnp.int32, (16, 4 * rows * 4), 0) == 8 + lane[:1] // (4 * rows)
    for w in range(2 * LINE):
        spread = t_mm(columns[w * rows : (w + 1) * rows, :16], hot)
        line = sum_rows(jnp.where(take, spread, 0.0))
        own = sum(line[:, k * 4 * rows : (k + 1) * 4 * rows] for k in range(4))
        for s in range(CHUNKS):
            at = s * CHUNK + (w % 2) * HIDDEN + (w // 2) * BLOCK
            out_ref[:, at : at + BLOCK] = own[:, s * BLOCK : (s + 1) * BLOCK]


def scores_of(k4, q_apart):
    return mm_t(k4, q_apart) * SCALE


BLOCKS = 3


def low_one(x, vec_ref):
    normed, _ = norm_parts(x.astype(F32))
    return (normed * vec_ref[G1 : G1 + 1, :] + vec_ref[B1 : B1 + 1, :]).astype(BF16)


def attend_step(g, low, wi, vec_ref, mixed_ref, total_ref, att, at):
    cols = rows_of(g * WIDTH, WIDTH)
    product = mm(low, wi[...])
    mixed_ref[:, :WIDTH] = (product[:, :WIDTH] + vec_ref[QB : QB + 1, cols]).astype(BF16)
    mixed_ref[:, WIDTH : 2 * WIDTH] = product[:, WIDTH : 2 * WIDTH].astype(BF16)
    mixed_ref[:, 2 * WIDTH :] = (product[:, 2 * WIDTH :] + vec_ref[VB : VB + 1, cols]).astype(BF16)
    images = range(TOGETHER)
    rows = [slice(img * PAD, (img + 1) * PAD) for img in images]
    real = lax.broadcasted_iota(jnp.int32, (PAD, WIDTH), 0) < VIS
    scores = [
        scores_of(mixed_ref[r, WIDTH : 2 * WIDTH], heads_apart(mixed_ref[r, :WIDTH])) for r in rows
    ]
    weights = []
    for img in images:
        own = jnp.where(real, scores[img], -1e30)
        top = jnp.max(own, axis=0, keepdims=True)
        raised = jnp.exp(own - top)
        total = sum_rows(raised)
        weights.append((raised * (1.0 / total)).astype(BF16))
        total_ref[0, img // SIDE, img % SIDE : img % SIDE + 1, :] = top + jnp.log(total)
    for img in images:
        value = heads_together(t_mm(weights[img], mixed_ref[rows[img], 2 * WIDTH :]))
        att[pl.ds(pl.multiple_of(at + img * PAD, PAD), PAD), cols] = value.astype(BF16)


def attend_kernel(x_ref, wi_ref, vec_ref, mixed_ref, att_ref, total_ref, low):
    step = pl.program_id(0)
    g, b = step // BLOCKS, step % BLOCKS
    at = b * (TOGETHER * PAD)
    rows = rows_of(at, TOGETHER * PAD)

    @pl.when(g == 0)
    def _():
        low[rows, :] = low_one(x_ref[rows, :], vec_ref)

    attend_step(g, low[rows, :], wi_ref.at[0], vec_ref, mixed_ref, total_ref, att_ref, at)


def full(*shape):
    return pl.BlockSpec(shape, lambda i: (0,) * len(shape))


def whole(a):
    return full(*a.shape)


def by_group(*block, lead=0, blocks=BLOCKS):
    def index(i):
        g, b = of_three(jnp.minimum(jnp.maximum(i - lead, 0), GROUPS * blocks - 1), blocks)
        return (g, b, 0, 0) if len(block) == 4 else (b, g)

    return pl.BlockSpec(block, index)


def TOTALS(lead):
    return by_group(1, TOGETHER // SIDE, 8, WIDTH, lead=lead)


def totals_shape(rows):
    return jax.ShapeDtypeStruct((GROUPS, rows // (SIDE * PAD), 8, WIDTH), F32)


def attend(x, wi, vec):
    rows = x.shape[0]
    block = TOGETHER * PAD
    shape = jax.ShapeDtypeStruct
    return pl.pallas_call(
        attend_kernel,
        grid=(GROUPS * BLOCKS,),
        in_specs=[whole(x), pl.BlockSpec((1, D, D), lambda i: (i // BLOCKS, 0, 0)), whole(vec)],
        out_specs=[by_group(block, D), full(rows, D), TOTALS(0)],
        out_shape=[
            shape((rows, 3 * D), BF16), shape((rows, D), BF16), totals_shape(rows),
        ],
        scratch_shapes=[pltpu.VMEM((rows, D), BF16)],
        compiler_params=params(),
        name="attend",
    )(x, wi, vec)


def gelu_both(x):
    bell = jnp.exp(-0.5 * x * x) * 0.3989422804014327
    below = 0.5 * (1.0 + lax.erf(x * 0.7071067811865476))
    return x * below, below + x * bell


def feed_early(cot_ref, sums_ref, middle, low, grad, low_t, grad_t, feed, back, act, inner):
    rows, held = cot_ref.shape[0], grad.shape[0]
    grad[:rows, :] = cot_ref[...]
    grad[rows:, :] = jnp.zeros((held - rows, D), BF16)
    sums_ref[DB : DB + 1, :] = sum_rows(cot_ref[...].astype(F32))
    grad_t[:, held:] = jnp.zeros((D, grad_t.shape[1] - held), BF16)
    grad_t[:, :held] = grad[...].T


def feed_start(x_ref, att_ref, cot_ref, wo_ref, vec_ref, sums_ref, middle, low, grad, low_t, grad_t, feed, back, act, inner):
    rows = cot_ref.shape[0]
    images = rows // VIS
    held = middle.shape[1]
    feed[...] = jnp.zeros_like(feed)
    back[...] = jnp.zeros_like(back)
    act[held:, :] = jnp.zeros((act.shape[0] - held, HIDDEN), BF16)
    inner[held:, :] = jnp.zeros((act.shape[0] - held, HIDDEN), BF16)
    middle[:, rows:, :] = jnp.zeros((D // 128, held - rows, 128), F32)
    for g in range(images // TOGETHER):
        at = slice(g * TOGETHER * PAD, (g + 1) * TOGETHER * PAD)
        branch = mm(att_ref[at, :], wo_ref[...]) + vec_ref[OB : OB + 1, :]
        mid = x_ref[at, :].astype(F32) + branch
        for j in range(TOGETHER):
            token = pl.ds(g * TOGETHER + j, VIS, stride=images)
            store_wide(middle, token, mid[j * PAD : j * PAD + VIS])
    normed, _ = norm_parts(load_wide(middle))
    low[...] = (normed * vec_ref[G2 : G2 + 1, :] + vec_ref[B2 : B2 + 1, :]).astype(BF16)
    low_t[:, held:] = jnp.zeros((D, low_t.shape[1] - held), BF16)
    low_t[:, :held] = low[...].T


def feed_step(up, upb, down, upbg_ref, middle, low, grad, low_t, grad_t, feed, back, act, inner):
    held = low.shape[0]
    before = mm(low[...], up[...]) + upb
    hidden_grad = mm(grad[...], down[...])
    value, slope = gelu_both(before)
    act[:held, :] = value.astype(BF16)
    before_grad = (hidden_grad * slope).astype(BF16)
    inner[:held, :] = before_grad
    upbg_ref[...] = sum_rows(before_grad.astype(F32))
    feed[...] += mm_t(act[:held, :], down[...])
    back[...] += mm_t(inner[:held, :], up[...])


def feed_grads(upg_ref, downg_ref, middle, low, grad, low_t, grad_t, feed, back, act, inner):
    downg_ref[...] = mm(grad_t[...], act[...]).astype(BF16)
    upg_ref[...] = mm(low_t[...], inner[...]).astype(BF16)


def feed_end(vec_ref, result_ref, mg_ref, sums_ref, middle, low, grad, low_t, grad_t, feed, back, act, inner):
    rows = result_ref.shape[0]
    images = rows // VIS
    held = low.shape[0]
    mid = load_wide(middle)
    result = feed[...] + mid + vec_ref[DB : DB + 1, :]
    result_ref[...] = result[:rows].astype(BF16)
    normed, scale = norm_parts(mid)
    pull = back[...]
    sums_ref[G2 : G2 + 1, :] = sum_rows(pull * normed)
    sums_ref[B2 : B2 + 1, :] = sum_rows(pull)
    mid_grad = grad[...].astype(F32) + norm_back(pull, vec_ref[G2 : G2 + 1, :], normed, scale)
    real = lax.broadcasted_iota(jnp.int32, (held, 1), 0) < rows
    mid_grad = jnp.where(real, mid_grad, 0.0)
    sums_ref[OB : OB + 1, :] = sum_rows(mid_grad.astype(BF16).astype(F32))
    store_wide(middle, slice(None), mid_grad)
    for j in range(images):
        out = j * PAD
        token = pl.ds(j, VIS, stride=images)
        own = jnp.concatenate([load_wide(middle, token), jnp.zeros((PAD - VIS, D), F32)], axis=0)
        mg_ref[out : out + PAD, :] = own.astype(BF16)


def feed_scratch(rows):
    held = -(-rows // 32) * 32
    deep = -(-rows // 256) * 256
    return [
        pltpu.VMEM((D // 128, held, 128), F32),
        pltpu.VMEM((held, D), BF16),
        pltpu.VMEM((held, D), BF16),
        pltpu.VMEM((D, deep), BF16),
        pltpu.VMEM((D, deep), BF16),
        pltpu.VMEM((held, D), F32),
        pltpu.VMEM((held, D), F32),
        pltpu.VMEM((deep, HIDDEN), BF16),
        pltpu.VMEM((deep, HIDDEN), BF16),
    ]


def feed_kernel(
    x_ref, att_ref, cot_ref, wo_ref, vec_ref, up_ref, upb_ref, down_ref,
    result_ref, mg_ref, upg_ref, downg_ref, upbg_ref, sums_ref, *scratch,
):
    step = pl.program_id(0)

    @pl.when(step == 0)
    def _():
        feed_early(cot_ref, sums_ref, *scratch)
        feed_start(x_ref, att_ref, cot_ref, wo_ref, vec_ref, sums_ref, *scratch)

    feed_step(up_ref, upb_ref[...], down_ref, upbg_ref, *scratch)
    feed_grads(upg_ref, downg_ref, *scratch)

    @pl.when(step == pl.num_programs(0) - 1)
    def _():
        feed_end(vec_ref, result_ref, mg_ref, sums_ref, *scratch)


def feed_forward(x, att, cot, wo, vec, up, upb, down):
    rows = cot.shape[0]
    ff = up.shape[1]
    hid = lambda r: pl.BlockSpec((r, HIDDEN), lambda i: (0, i))
    return pl.pallas_call(
        feed_kernel,
        grid=(ff // HIDDEN,),
        in_specs=[whole(x), whole(att), whole(cot), whole(wo), whole(vec), hid(D), hid(1), hid(D)],
        out_specs=[whole(cot), full(x.shape[0], D), hid(D), hid(D), hid(1), full(8, D)],
        out_shape=[
            jax.ShapeDtypeStruct(cot.shape, BF16),
            jax.ShapeDtypeStruct((x.shape[0], D), BF16),
            jax.ShapeDtypeStruct((D, ff), BF16),
            jax.ShapeDtypeStruct((D, ff), BF16),
            jax.ShapeDtypeStruct((1, ff), F32),
            jax.ShapeDtypeStruct((8, D), F32),
        ],
        scratch_shapes=feed_scratch(rows),
        compiler_params=params(),
        name="feed_forward",
    )(x, att, cot, wo, vec, up, upb, down)


FORWARD = {
    0: [("start", "v"), ("start", "g0"), ("start", "g1"), ("start", "g2"), ("start", "out")],
    3: [("first", "v")],
    4: [("first", "g0"), ("start", "d0"), ("start", "u0")],
    5: [("second", "v")],
    6: [("core", "v"), ("finish", "v")],
    7: [("first", "g2")],
    8: [("first", "out")],
    9: [("second", "g1"), ("core", "g1"), ("finish", "g1"), ("second", "g2"), ("first", "d0"), ("first", "u0")],
    10: [("start", "u1"), ("start", "d1")],
    11: [("second", "out"), ("core", "g2")],
    12: [("finish", "g2"), ("start", "u2")],
    14: [("second", "d0"), ("second", "u0"), ("start", "d2")],
    15: [("core", "out"), ("first", "u1"), ("first", "d1"), ("finish", "out")],
    16: [("second", "u1"), ("second", "d1"), ("first", "u2")],
    17: [("first", "d2")],
    18: [("core", "u1"), ("core", "d1")],
    19: [("load", "su"), ("load", "sd"), ("finish", "u1"), ("finish", "d1"), ("second", "u2")],
    20: [("second", "d2"), ("first", "su"), ("first", "sd")],
    22: [("core", "u2"), ("core", "d2")],
    23: [("finish", "u2"), ("finish", "d2")],
    24: [("second", "su"), ("second", "sd")],
    26: [("settle", "su"), ("settle", "sd")],
}
BEFORE_ATTENTION = [("first", "g1"), ("second", "g0"), ("core", "g0"), ("finish", "g0")]
BEFORE_FEED = [("core", "d0"), ("core", "u0"), ("finish", "d0"), ("finish", "u0")]


def forward_kernel(
    order_ref, patches_ref, in_ref, out_ref, cot_ref, up_own, down_own, *refs,
):
    vector_refs, refs = refs[:9], refs[9:]
    (
    x_out, mixed_ref, total_ref, att_out, result_ref, mg_ref, upg_ref, downg_ref, upbg_ref, sums_ref, vec_ref, wi_ref, wo_ref,
    upf_ref, downf_ref, x_ref, att_ref, share_ref, other, piece, columns, upb, wi_all, wo_all, up_all, down_all, send, recv, own, near, *scratch,
    ) = refs
    step = pl.program_id(0)
    picks = x_ref.shape[0] // (TOGETHER * PAD) * PICK_PARTS
    early = picks + GROUPS * BLOCKS
    last = pl.num_programs(0) - 1
    z, y, x, c = place()
    features = D // 4
    feed_parts, sum_parts = scratch[:9], scratch[9:]
    middle = feed_parts[0]
    low_all = mg_ref
    swap = remote(share_ref.at[1 - c], other, near.at[0], near.at[1], device(z, y, x, 1 - c))

    def weight(j, src, dst, s, x_first):
        def slot(z, y, x):
            rows = rows_of((2 * x + c) * features, features)
            return dst.at[rows, rows_of(s * CHUNK + y * HIDDEN + z * BLOCK, BLOCK)]

        def halves(c):
            return [dst.at[rows_of((2 * k + c) * features, features), pl.ds(s * CHUNK, CHUNK)] for k in range(2)]

        block = src.at[:, pl.ds(s * BLOCK, BLOCK)]
        def span(count):
            rows, count = (features, count) if count <= 8 else (2 * features, count // 2)
            return dst.at[pl.ds(0, rows), pl.ds(0, count * BLOCK)]

        return Gather(block, slot, x_first, halves, span, send.at[j], recv.at[j], own.at[j])

    def square(j, k, dst, x_first, start=0, width=HALF, direct=False):
        lanes = lambda c: rows_of(c * HALF + start, BLOCK, width)
        slot = lambda z, y, x: dst.at[chip_row(z, y, x), lanes(c)]
        halves = lambda c: [dst.at[:, lanes(c)]]
        block = piece.at[:, pl.ds(k * HALF + start, width)]
        span = lambda count: dst.at[pl.ds(0, count * 2 * OWN), pl.ds(0, width)]
        return Gather(block, slot, x_first, halves, span, send.at[j], recv.at[j], own.at[j], direct)

    items = {}
    for s in range(CHUNKS):
        items[f"u{s}"] = [weight(2 * s, up_own, up_all, s, True)]
        items[f"d{s}"] = [weight(2 * s + 1, down_own, down_all, s, False)]
    j = 2 * CHUNKS
    slot = lambda z, y, x: columns.at[chip_row(z, y, x)]
    span = lambda count: columns.at[pl.ds(0, count * 2 * OWN)]
    items["v"] = [Gather(piece.at[:, pl.ds(4 * HALF, BLOCK)], slot, True, lambda c: [], span, send.at[j], recv.at[j], own.at[j], True)]
    items["g0"] = [square(j + 1, 0, wi_all.at[0], True, direct=True)]
    items["g1"] = [square(j + 3, 1, wi_all.at[1], True, direct=True)]
    items["g2"] = [square(j + 4, 2, wi_all.at[2], False)]
    items["out"] = [square(j + 5, 3, wo_all, True)]
    for name, one in zip(("su", "sd"), feed_sums((up_all, down_all), [0], *sum_parts)[0]):
        items[name] = [one]
    copies = [
        pltpu.make_async_copy(wi_all, wi_ref, near.at[2]),
        pltpu.make_async_copy(wo_all, wo_ref, near.at[3]),
        pltpu.make_async_copy(x_ref, x_out, near.at[2 + 2 * CHUNKS]),
        pltpu.make_async_copy(att_ref, att_out, near.at[3 + 2 * CHUNKS]),
    ]
    moves = []
    kept = CHUNK // HIDDEN
    for k in range(kept, CHUNKS * kept):
        lanes, dst = pl.ds(k * HIDDEN, HIDDEN), pl.ds((k - kept) * HIDDEN, HIDDEN)
        moves.append(pltpu.make_async_copy(up_all.at[:, lanes], upg_ref.at[:, dst], near.at[10 + 2 * (k - kept)]))
        moves.append(pltpu.make_async_copy(down_all.at[:, lanes], downg_ref.at[:, dst], near.at[11 + 2 * (k - kept)]))

    @pl.when(step == 0)
    def _():
        share_out(in_ref, out_ref, vector_refs, share_ref)
        greet()
        swap.start()
        swap.wait()
        piece[...] = both_rows(share_ref[c], other[...])

    def run(acts):
        for act, which in acts:
            for one in items[which]:
                getattr(one, act)()

    at_step(step, FORWARD, run)

    lines = rows_of(y * HIDDEN, HIDDEN)
    for j, ref in enumerate((upf_ref, downf_ref)):
        copies.append(pltpu.make_async_copy(sum_parts[0].at[j, x, :, lines], ref, near.at[18 + j]))

    @pl.when(step == 26)
    def _():
        for one in copies[4:]:
            one.start()

    @pl.when(step < picks)
    def _():
        block = lax.shift_right_logical(step, 1)
        pick_step(step & 1, order_ref, patches_ref, x_ref, block * (TOGETHER * PAD), middle)

    @pl.when(step == picks - 1)
    def _():
        feed_early(cot_ref, sums_ref, *feed_parts)

    @pl.when(step == picks)
    def _():
        copies[2].start()
        vec_ref[...] = columns[...].astype(F32).T[:16]
        hidden_bias(columns[...], upb)
        for k in range(BLOCKS):
            block = slice(k * TOGETHER * PAD, (k + 1) * TOGETHER * PAD)
            low_all[block, :] = low_one(x_ref[block, :], vec_ref)
        run(BEFORE_ATTENTION)

    g, b = of_three(jnp.minimum(jnp.maximum(step - picks, 0), GROUPS * BLOCKS - 1), BLOCKS)
    at = b * (TOGETHER * PAD)
    rows = rows_of(at, TOGETHER * PAD)

    @pl.when((step >= picks) & (step < early))
    def _():
        attend_step(g, low_all[rows, :], wi_all.at[g], vec_ref, mixed_ref, total_ref, att_ref, at)

    @pl.when(step == early)
    def _():
        for k in (0, 1, 3):
            copies[k].start()
        feed_start(x_ref, att_ref, cot_ref, wo_all, vec_ref, sums_ref, *feed_parts)

    late = jnp.maximum(step - early, 0)
    lanes = rows_of(lax.shift_right_logical(late, 1) * HIDDEN, HIDDEN)

    @pl.when(step == early)
    def _():
        run(BEFORE_FEED)

    @pl.when((step >= early) & (late & 1 == 0))
    def _():
        feed_step(up_all.at[:, lanes], upb[:, lanes], down_all.at[:, lanes], upbg_ref, *feed_parts)

    @pl.when((step >= early) & (late & 1 == 1))
    def _():
        feed_grads(up_all.at[:, lanes], down_all.at[:, lanes], *feed_parts)

    def move(pair):
        for one in pair:
            one.start()

    at_step(step, {early + 2 * (kept + k) + 1: moves[2 * k : 2 * k + 2] for k in range(len(moves) // 2)}, move)

    @pl.when(step == last)
    def _():
        feed_end(vec_ref, result_ref, mg_ref, sums_ref, *feed_parts)
        for name in ("su", "sd"):
            items[name][0].left()
        for one in copies + moves:
            one.wait()


def forward(order, patches, project_in, project_out, cot, up, down, *vectors):
    images = order.shape[0]
    rows = images * PAD
    block = TOGETHER * PAD
    picks = images // TOGETHER * PICK_PARTS
    early = picks + GROUPS * BLOCKS
    ff = CHUNKS * CHUNK
    late = 2 * ff // HIDDEN
    here = pl.BlockSpec(memory_space=pl.ANY)
    shape = jax.ShapeDtypeStruct
    count = 2 * CHUNKS + 6
    done = (D // 4, HIDDEN)
    return pl.pallas_call(
        forward_kernel,
        grid=(early + late,),
        in_specs=pick_in(images) + [whole(project_in), whole(project_out), whole(cot), here, here] + [whole(v) for v in vectors],
        out_specs=[
            here, by_group(block, D, lead=picks), TOTALS(picks), here,
            whole(cot), full(rows, D), here, here,
            pl.BlockSpec((1, HIDDEN), lambda i: (0, lax.shift_right_logical(jnp.maximum(i - early, 0), 1))),
            full(8, D), full(16, D), here, here, here, here,
        ],
        out_shape=[
            shape((rows, D), BF16), shape((rows, 3 * D), BF16), totals_shape(rows), shape((rows, D), BF16),
            shape(cot.shape, BF16), shape((rows, D), BF16), shape((D, ff - CHUNK), BF16), shape((D, ff - CHUNK), BF16),
            shape((1, ff), F32), shape((8, D), F32), shape((16, D), F32),
            shape((GROUPS, D, D), BF16), shape((D, D), BF16), shape(done, BF16), shape(done, BF16),
        ],
        scratch_shapes=[
            pltpu.VMEM((rows, D), BF16),
            pltpu.VMEM((rows, D), BF16),
            pltpu.VMEM((2, 32, SHARE), BF16),
            pltpu.VMEM((32, SHARE), BF16),
            pltpu.VMEM((2 * OWN, SHARE), BF16),
            pltpu.VMEM((D, BLOCK), BF16),
            pltpu.VMEM((1, ff), F32),
            pltpu.VMEM((GROUPS, D, D), BF16),
            pltpu.VMEM((D, D), BF16),
            pltpu.VMEM((D, ff), BF16),
            pltpu.VMEM((D, ff), BF16),
            pltpu.SemaphoreType.DMA((count, Gather.COPIES)),
            pltpu.SemaphoreType.DMA((count, Gather.COPIES)),
            pltpu.SemaphoreType.DMA((count,)),
            pltpu.SemaphoreType.DMA((12 + 2 * (CHUNKS - 1) * (CHUNK // HIDDEN),)),
        ] + feed_scratch(cot.shape[0]) + feed_sum_scratch(1),
        compiler_params=params(collective_id=2, has_side_effects=True),
        name="forward",
    )(order, patches, project_in, project_out, cot, up, down, *vectors)


BACKWARD = {
    0: [("load", 1), ("load", 2), ("load", 0)],
    1: [("first", 1), ("third", 0)],
    2: [("first", 2)],
    3: [("load", "out"), ("load", "g0")],
    4: [("second", 1), ("first", "out"), ("first", "g0")],
    6: [("second", 2), ("load", "g1")],
    7: [("third", 1), ("total", 0)],
    8: [("first", "g1")],
    9: [("second", "out"), ("second", "g0"), ("load", "g2"), ("load", "v")],
    10: [("first", "g2"), ("first", "v"), ("third", 2), ("total", 1)],
    12: [("third", "out"), ("third", "g0"), ("load", "late"), ("second", "g1")],
    13: [("first", "late"), ("second", "g2"), ("second", "v")],
    14: [("third", "g1"), ("second", "late"), ("third", "g2"), ("third", "v")],
}
LAST = [("total", 2), ("third", "late"), ("total", "out"), ("total", "g0"), ("total", "g1"), ("total", "g2"), ("total", "v")]
BACK = 3


def unattend_step(mixed_ref, att_grad, totals, grads, g, at):
    real = lax.broadcasted_iota(jnp.int32, (PAD, WIDTH), 0) < VIS
    for first in range(0, TOGETHER, SIDE):
        images = range(first, first + SIDE)
        held = []
        for img in images:
            rows = slice(img * PAD, (img + 1) * PAD)
            q4, k4, v4 = [mixed_ref[rows, k * WIDTH : (k + 1) * WIDTH] for k in range(3)]
            q_apart, a_apart = heads_apart(q4), heads_apart(att_grad[rows, :])
            held.append((k4, q_apart, a_apart, scores_of(k4, q_apart), mm_t(v4, a_apart)))
        ready = []
        for img, (k4, q_apart, a_apart, scores, pulled) in zip(images, held):
            exact = jnp.exp(scores - totals[0, img // SIDE, img % SIDE : img % SIDE + 1, :])
            exact = jnp.where(real, exact, 0.0)
            centre = sum_rows(exact * pulled)
            score_grad = (exact * (pulled - centre)).astype(BF16)
            ready.append((k4, q_apart, a_apart, score_grad, exact.astype(BF16)))
        for img, (k4, q_apart, a_apart, score_grad, weights) in zip(images, ready):
            q_grad = heads_together(t_mm(score_grad, k4)) * SCALE
            k_grad = mm(score_grad, q_apart) * SCALE
            v_grad = mm(weights, a_apart)
            out = pl.ds(pl.multiple_of(at + img * PAD, PAD), PAD)
            grads[g, out, :WIDTH] = q_grad.astype(BF16)
            grads[g, out, WIDTH : 2 * WIDTH] = k_grad.astype(BF16)
            grads[g, out, 2 * WIDTH :] = v_grad.astype(BF16)


def pull_step(x, grads, rows, wi_ref, pull_ref, sums_ref):
    normed, _ = norm_parts(x.astype(F32))
    pull = sum(mm_t(grads[g, rows, :], wi_ref[g]) for g in range(GROUPS))
    sums_ref[G1 : G1 + 1, :] += sum_rows(pull * normed)
    sums_ref[B1 : B1 + 1, :] += sum_rows(pull)
    pull_ref[rows, :] = pull


def unnorm_step(x, mg, pull, vec_ref, ig_ref):
    normed, scale = norm_parts(x.astype(F32))
    ig_ref[...] = (mg.astype(F32) + norm_back(pull, vec_ref[G1 : G1 + 1, :], normed, scale)).astype(BF16)


def backward_kernel(x_in, mg_in, mixed_ref, att_ref, total_ref, wi_in, wo_ref, vec_ref, *refs):
    step = pl.program_id(0)
    walk = GROUPS * BACK
    last = pl.num_programs(0) - 1
    g, b = of_three(jnp.minimum(step, walk - 1), BACK)
    b = jnp.where(step >= walk, jnp.where(step >= walk + BACK, step - walk - BACK, step - walk), b)
    at = b * (TOGETHER * PAD)
    rows = rows_of(at, TOGETHER * PAD)
    x_ref, mg_ref, wi_ref, brought = refs[-4:]
    refs = refs[:-4]
    remote_sums = len(refs) > 12
    brings = [pltpu.make_async_copy(wi_in, wi_ref, brought.at[2 * BACK])]
    for k in range(BACK):
        block = pl.ds(k * TOGETHER * PAD, TOGETHER * PAD)
        brings.insert(2 * k, pltpu.make_async_copy(x_in.at[block], x_ref.at[block], brought.at[2 * k]))
        brings.insert(2 * k + 1, pltpu.make_async_copy(mg_in.at[block], mg_ref.at[block], brought.at[2 * k + 1]))

    @pl.when(step == 0)
    def _():
        for one in brings:
            one.start()
    if remote_sums:
        upg_ref, downg_ref, sums_two_ref, upbg_ref, up_first, down_first = refs[:6]
        refs = refs[2:]
        ig_ref, wi_out, wo_out, vec_out, upf_ref, downf_ref = refs[4:10]
        low_t, att_t, grads, pull, sums_ref, wig_ref, wog_ref, end, other_end, end_send, end_recv = refs[10:21]
        feed_parts, square_parts, early_parts, late_parts, line_parts = refs[21:30], refs[30:38], refs[38:46], refs[46:54], refs[54:]
        z, y, x, c = place()
        items = dict(enumerate(feed_sums((upg_ref, downg_ref), range(1, CHUNKS), *feed_parts), 1))
        for j, name in enumerate(("g0", "g1", "out")):
            src = wog_ref if name == "out" else wig_ref.at[j]
            items[name] = [square_sum(j, j, src, slice(0, HALF), j == 0, *square_parts)]
        cuts = [slice(0, 2 * BLOCK), slice(2 * BLOCK, HALF)]
        items["g2"] = [square_sum(3, 3 + j, wig_ref.at[2], cut, j == 0, *square_parts) for j, cut in enumerate(cuts)]
        items[0] = [line_sum(j, src, *line_parts) for j, src in enumerate((up_first, down_first))]
        items["v"] = [vector_sum(*early_parts)]
        items["late"] = [vector_sum(*late_parts)]
        places = {"g0": 0, "g1": 1, "g2": 2, "out": 3}

        def swap(j):
            give = end.at[j, pl.ds(pl.multiple_of((1 - c) * OWN, 8), OWN)]
            return remote(give, other_end.at[j], end_send.at[j], end_recv.at[j], device(z, y, x, 1 - c))

        def act(name, which):
            values = [getattr(one, name)() for one in items[which]]
            if name != "total":
                return
            if which in (0, 1, 2):
                lanes = slice(which * BLOCK, (which + 1) * BLOCK)
                upf_ref[:, lanes], downf_ref[:, lanes] = values
            elif which in places:
                end[places[which]] = jnp.concatenate(values, axis=1)
                swap(places[which]).start()
            else:
                early = which == "v"
                value = jnp.where(c == 0, values[0][:, :OWN], values[0][:, OWN : 2 * OWN])
                if early:
                    vec_out[:6, :OWN] = value[:6]
                    vec_out[6:7, :] = jnp.where(c == 0, values[0][6:7], values[0][7:8])
                else:
                    vec_out[8:, :OWN] = value

        def run(acts):
            for name, which in acts:
                if (name, which) == ("load", "v"):
                    own = [sums_ref[k : k + 1, :] for k in (QB, VB)]
                    own += [sums_two_ref[k : k + 1, :] for k in (OB, G2, B2, DB)]
                    items["v"][0].fill(jnp.concatenate(own, axis=0), upbg_ref)
                if (name, which) == ("load", "late"):
                    items["late"][0].fill(sums_ref[G1 : B1 + 1, :])
                act(name, which)

        @pl.when(step == 0)
        def _():
            greet()

        at_step(step, BACKWARD, run)
    else:
        ig_ref, wi_out, wo_out, sums_ref, low_t, att_t, grads, pull, wig_ref, wog_ref = refs

    @pl.when(step == 0)
    def _():
        sums_ref[...] = jnp.zeros_like(sums_ref)
        if remote_sums:
            vec_out[...] = jnp.zeros_like(vec_out)

    for k in range(BACK):

        @pl.when(step == k)
        def _(k=k):
            brings[2 * k].wait()
            brings[2 * k + 1].wait()

    @pl.when(step == walk)
    def _():
        brings[-1].wait()

    @pl.when(step < BACK)
    def _():
        low_t[:, rows] = low_one(x_ref[rows, :], vec_ref).T
        att_t[:, rows] = att_ref[...].T

    @pl.when(step < walk)
    def _():
        cols = rows_of(g * WIDTH, WIDTH)
        att_grad = mm_t(mg_ref[rows, :], wo_ref[cols, :]).astype(BF16)
        unattend_step(mixed_ref, att_grad, total_ref, grads, g, at)
        own = grads[g, rows, :]
        sums_ref[QB : QB + 1, cols] += sum_rows(own[:, :WIDTH].astype(F32))
        sums_ref[VB : VB + 1, cols] += sum_rows(own[:, 2 * WIDTH :].astype(F32))

    @pl.when(step == BACK - 1)
    def _():
        wog_ref[...] = mm(att_t[...], mg_ref[...]).astype(BF16).reshape(wog_ref.shape)

    @pl.when((b == BACK - 1) & (step < walk))
    def _():
        wig_ref[g] = mm(low_t[...], grads[g]).astype(BF16).reshape(wig_ref.shape[1:])

    @pl.when((step >= walk) & (step < walk + BACK))
    def _():
        pull_step(x_ref[rows, :], grads, rows, wi_ref, pull, sums_ref)

    @pl.when(step >= walk + BACK)
    def _():
        unnorm_step(x_ref[rows, :], mg_ref[rows, :], pull[rows, :], vec_ref, ig_ref)

    @pl.when(step == last)
    def _():
        if not remote_sums:
            wi_out[...] = wig_ref[...].reshape(wi_out.shape)
            wo_out[...] = wog_ref[...].reshape(wo_out.shape)
            return
        for name, which in LAST:
            act(name, which)
        for j in range(PIECES + 1):
            swap(j).wait()
            mine, theirs = end[j, pl.ds(pl.multiple_of(c * OWN, 8), OWN), :], other_end[j]
            both = jnp.concatenate([jnp.where(c == 0, mine, theirs), jnp.where(c == 0, theirs, mine)], axis=1)
            if j < GROUPS:
                for k in range(3):
                    wi_out[:, k * D + j * WIDTH : k * D + (j + 1) * WIDTH] = both[:, k * WIDTH : (k + 1) * WIDTH]
            else:
                wo_out[...] = both
        act("total", "late")


CHIPS = (LINE, 2, 2, 2 * OWN)


def ways_of(mine, x_first):
    z, y, x, c = place()
    if x_first:
        return [(mine.at[:, :, 1 - x], mine.at[:, :, x], True), (mine.at[:, 1 - y, x], mine.at[:, y, x], False)]
    return [(mine.at[:, 1 - y], mine.at[:, y], False), (mine.at[:, y, 1 - x], mine.at[:, y, x], True)]


def square_sum(j, at, src, lanes, x_first, own, theirs, box_one, box_two, box_z, send, recv, near):
    z, y, x, c = place()
    width = lanes.stop - lanes.start

    def take(c, into):
        return [(src.at[:, :, :, :, rows_of(c * HALF + lanes.start, BLOCK, width)], into)]

    lanes = pl.ds(lanes.start, width)
    mine = own.at[j, :, :, :, :, lanes]
    line = lambda to: mine.at[to, y, x]
    boxes = (box_one.at[j, :, :, :, lanes], box_two.at[j, :, :, lanes], box_z.at[j, :, :, lanes])
    return Sum(
        take, mine, theirs.at[j, :, :, :, :, lanes], ways_of(mine, x_first), line, boxes, send.at[at], recv.at[at], near.at[at]
    )


class VectorSum(Sum):
    def fill(self, vectors, hidden=None):
        self.own[...] = jnp.zeros(self.own.shape, F32)
        count, width = vectors.shape[0], 4 * OWN
        for k in range(2 * LINE * 2):
            z, y, x = k // 4, k // 2 % 2, k % 2
            self.own[z, y, x, :count, : 2 * OWN] = vectors[:, k * 2 * OWN : (k + 1) * 2 * OWN]
            if hidden is not None:
                at = [s * CHUNK + y * HIDDEN + z * BLOCK for s in range(CHUNKS)]
                line = jnp.concatenate([hidden[:, a : a + BLOCK] for a in at], axis=1)
                for c in range(2):
                    start = (2 * x + c) * width
                    self.own[z, y, x, 6 + c : 7 + c, :width] = line[:, start : start + width]

    def loads(self):
        return []

    def first(self):
        self.all_core().wait_recv()
        self.all_core().wait_send()
        self.own[...] = self.own[...] + self.theirs[...]
        self.out(0).start()

    def total(self):
        self.all_z().wait_recv()
        out = self.line(self.z)[...]
        for k in range(LINE - 1):
            out = out + self.boxes[2][k]
        for one in (self.out(0), self.out(1), self.all_z()):
            one.wait_send()
        return out


def line_sum(j, src, own, box_z, send, recv, near):
    mine = own.at[j]
    line = lambda to: mine.at[:, rows_of(to * BLOCK, BLOCK)]
    take = lambda c, into: [(src, into)]
    return LineSum(take, mine, mine, None, line, (None, None, box_z.at[j]), send.at[j], recv.at[j], near.at[j])


def line_sum_scratch():
    return [
        pltpu.VMEM((2, D // 4, HIDDEN), BF16),
        pltpu.VMEM((2, LINE - 1, D // 4, BLOCK), BF16),
        pltpu.SemaphoreType.DMA((2, Sum.COPIES)),
        pltpu.SemaphoreType.DMA((2, Sum.COPIES)),
        pltpu.SemaphoreType.DMA((2, 1)),
    ]


def vector_sum(own, theirs, box_one, box_two, box_z, send, recv, near):
    z, y, x, c = place()
    mine = own.at[0]
    line = lambda to: mine.at[to, y, x]
    boxes = (box_one.at[0], box_two.at[0], box_z.at[0])
    return VectorSum(
        lambda c, into: [(mine, into)], mine, theirs.at[0], ways_of(mine, False), line, boxes, send.at[0], recv.at[0], near.at[0]
    )


def square_sum_scratch(count, lanes=HALF, dtype=BF16, rows=2 * OWN, copies=None):
    chips = CHIPS[:3] + (rows,)
    copies = count if copies is None else copies
    return [
        pltpu.VMEM((count,) + chips + (lanes,), dtype),
        pltpu.VMEM((count,) + chips + (lanes,), dtype),
        pltpu.VMEM((count, LINE, 2, rows, lanes), dtype),
        pltpu.VMEM((count, LINE, rows, lanes), dtype),
        pltpu.VMEM((count, LINE - 1, rows, lanes), dtype),
        pltpu.SemaphoreType.DMA((copies, Sum.COPIES)),
        pltpu.SemaphoreType.DMA((copies, Sum.COPIES)),
        pltpu.SemaphoreType.DMA((copies, 1)),
    ]


def feed_sums(grads_refs, which_chunks, own, theirs, box_y, box_x, box_two, box_z, send, recv, near):
    z, y, x, c = place()
    features = D // 4

    def one(s, which):
        grads = grads_refs[which]
        j = 2 * s + which

        def take(c, into):
            return [
                (grads.at[rows_of((2 * k + c) * features, features), pl.ds(s * CHUNK, CHUNK)], into.at[k])
                for k in range(2)
            ]

        mine = own.at[j]
        keep, give = rows_of(y * HIDDEN, HIDDEN), rows_of((1 - y) * HIDDEN, HIDDEN)
        if which == 0:
            ways = [
                (mine.at[:, :, give], mine.at[:, :, keep], False),
                (mine.at[1 - x, :, keep], mine.at[x, :, keep], True),
            ]
            box_one = box_y.at[s]
        else:
            ways = [(mine.at[1 - x], mine.at[x], True), (mine.at[x, :, give], mine.at[x, :, keep], False)]
            box_one = box_x.at[s]
        line = lambda to: mine.at[x, :, rows_of(y * HIDDEN + to * BLOCK, BLOCK)]
        boxes = (box_one, box_two.at[j], box_z.at[j])
        return Sum(lambda c, into: take(c, into), mine, theirs.at[j], ways, line, boxes, send.at[j], recv.at[j], near.at[j])

    return [[one(s, 0), one(s, 1)] for s in range(len(which_chunks))]


def feed_sum_scratch(chunks):
    features = D // 4
    count = 2 * chunks
    return [
        pltpu.VMEM((count, 2, features, CHUNK), BF16),
        pltpu.VMEM((count, 2, features, CHUNK), BF16),
        pltpu.VMEM((chunks, 2, features, HIDDEN), BF16),
        pltpu.VMEM((chunks, features, CHUNK), BF16),
        pltpu.VMEM((count, features, HIDDEN), BF16),
        pltpu.VMEM((count, LINE - 1, features, BLOCK), BF16),
        pltpu.SemaphoreType.DMA((count, Sum.COPIES)),
        pltpu.SemaphoreType.DMA((count, Sum.COPIES)),
        pltpu.SemaphoreType.DMA((count, 1)),
    ]


def backward(x, mg, mixed, att, totals, wi, wo, vec, *more):
    rows = x.shape[0]
    block = TOGETHER * PAD
    walk = GROUPS * BACK
    here = pl.BlockSpec(memory_space=pl.ANY)
    shape = jax.ShapeDtypeStruct
    scratch = [pltpu.VMEM((D, rows), BF16), pltpu.VMEM((D, rows), BF16), pltpu.VMEM((GROUPS, rows, D), BF16)]
    scratch += [pltpu.VMEM((rows, D), F32)]
    sums = [pltpu.VMEM((8, D), F32)]
    weights = [pltpu.VMEM((GROUPS,) + CHIPS + (D,), BF16), pltpu.VMEM(CHIPS + (D,), BF16)]
    specs = []
    if more:
        specs = [here, here] + [whole(a) for a in more[2:4]] + [here, here]
        own = (D // 4, CHUNKS * BLOCK)
        out = [(OWN, 3 * D), (OWN, D), (16, BLOCK), own, own]
        scratch += sums + weights + [
            pltpu.VMEM((PIECES + 1, 2 * OWN, HALF), F32),
            pltpu.VMEM((PIECES + 1, OWN, HALF), F32),
            pltpu.SemaphoreType.DMA((PIECES + 1,)),
            pltpu.SemaphoreType.DMA((PIECES + 1,)),
        ] + feed_sum_scratch(CHUNKS - 1) + square_sum_scratch(PIECES + 1, copies=PIECES + 2)
        scratch += square_sum_scratch(1, BLOCK, F32, 8) + square_sum_scratch(1, BLOCK, F32, 8) + line_sum_scratch()
        out_shape = [shape(s, F32) for s in out]
    else:
        out = [(GROUPS, D, D), (D, D), (8, D)]
        out_shape = [shape(s, F32 if s[0] == 8 else BF16) for s in out]
        scratch += weights
    return pl.pallas_call(
        backward_kernel,
        grid=(walk + BACK + BLOCKS,),
        in_specs=[
            here, here, by_group(block, D, blocks=BACK),
            pl.BlockSpec((block, D), lambda i: (jnp.minimum(i, BACK - 1), 0)),
            TOTALS(0), here, whole(wo), whole(vec),
        ] + specs,
        out_specs=[pl.BlockSpec((block, D), lambda i: (jnp.maximum(i - walk - BACK, 0), 0))] + [full(*s) for s in out],
        out_shape=[shape((rows, D), BF16)] + out_shape,
        scratch_shapes=scratch + [
            pltpu.VMEM((rows, D), BF16),
            pltpu.VMEM((rows, D), BF16),
            pltpu.VMEM((GROUPS, D, D), BF16),
            pltpu.SemaphoreType.DMA((2 * BACK + 1,)),
        ],
        compiler_params=params(collective_id=3, has_side_effects=True) if more else params(),
        name="backward",
    )(x, mg, mixed, att, totals, wi, wo, vec, *more)


def spread_kernel(order_ref, ig_ref, *refs):
    count = (len(refs) - 2) // 3
    out_ref, near = refs[count], refs[-1]
    given, outs, held = refs[:count], refs[count + 1 : 2 * count + 1], refs[2 * count + 1 : -1]
    step = pl.program_id(0)
    ins = [pltpu.make_async_copy(src, dst, near.at[j]) for j, (src, dst) in enumerate(zip(given, held))]
    outs = [pltpu.make_async_copy(src, dst, near.at[j]) for j, (src, dst) in enumerate(zip(held, outs))]

    @pl.when(step == 0)
    def _():
        for one in ins:
            one.start()

    @pl.when(step == 1)
    def _():
        for one in ins:
            one.wait()
        for one in outs:
            one.start()

    @pl.when(step == pl.num_programs(0) - 1)
    def _():
        for one in outs:
            one.wait()

    blocks = D // 128
    rows = out_ref.reshape(PATCHES * blocks * TOGETHER, 128)
    for j in range(TOGETHER):
        hot = picked(order_ref[j : j + 1, :PAD])
        own = mm(hot, ig_ref[j * PAD : (j + 1) * PAD, :])
        for k in range(blocks):
            at = pl.ds(k * TOGETHER + j, PATCHES, stride=blocks * TOGETHER)
            rows[at, :] = own[:, k * 128 : (k + 1) * 128]


def spread(order, ig, result, *more):
    images = order.shape[0]
    steps = images // TOGETHER
    passed = [pl.BlockSpec(memory_space=pl.ANY)] * (1 + len(more))
    shape = jax.ShapeDtypeStruct
    return pl.pallas_call(
        spread_kernel,
        grid=(steps,),
        in_specs=[
            pl.BlockSpec((TOGETHER, PATCHES), lambda i: (i, 0)),
            pl.BlockSpec((TOGETHER * PAD, D), lambda i: (i, 0)),
        ] + passed,
        out_specs=[pl.BlockSpec((PATCHES, 1, D // 128, TOGETHER, 128), lambda i: (0, i, 0, 0, 0))] + passed,
        out_shape=[shape((PATCHES, steps, D // 128, TOGETHER, 128), F32)] + [shape(a.shape, a.dtype) for a in (result,) + more],
        scratch_shapes=[pltpu.VMEM(a.shape, a.dtype) for a in (result,) + more] + [pltpu.SemaphoreType.DMA((1 + len(more),))],
        compiler_params=params(),
        name="spread",
    )(order, ig, result, *more)


def local(
    patches, keep_order, cotangent, first_gain, first_shift, project_in, query_bias, value_bias,
    project_out, output_bias, second_gain, second_shift, up_weight, up_bias, down_weight, down_bias,
):
    rows_own = project_in.shape[0]
    hidden_own = up_bias.shape[0]
    images = patches.shape[0]
    wide, narrow = lax.axis_size("wide"), lax.axis_size("narrow")
    vectors = [first_gain, first_shift, query_bias, value_bias, output_bias, second_gain, second_shift, down_bias]
    order = keep_order
    patches = patches.transpose(1, 0, 2)
    cot = cotangent.transpose(1, 0, 2).reshape(VIS * images, D)
    if (wide, narrow) == (8, 4):
        x, mixed, totals, att, result, mg, upg, downg, upbg, sums_two, vec, wi, wo, up_zero, down_zero = forward(
            order, patches, project_in, project_out, cot, up_weight.T, down_weight.T,
            *[v.reshape(1, -1) for v in vectors + [up_bias]],
        )
        ig, wig, wog, s, upf, downf = backward(
            x, mg, mixed, att, totals, wi, wo, vec, upg, downg, sums_two, upbg, up_zero, down_zero
        )
        patch_grad, result, wig, wog, s, upf, downf = spread(order, ig, result, wig, wog, s, upf, downf)
        upf, downf, upbf = upf.T, downf.T, s[6, : 4 * rows_own]
        s = [s[k, :rows_own] for k in (8, 9, 0, 1, 2, 3, 4, 5)]
    else:
        share = jnp.concatenate([jnp.stack(vectors).reshape(1, -1), up_bias.reshape(1, -1)], axis=1)
        shares = lax.all_gather(share, AXES, axis=0, tiled=True)
        vec = shares[:, : 8 * rows_own].reshape(-1, 8, rows_own).transpose(1, 0, 2).reshape(8, D)
        vec = jnp.pad(vec.astype(F32), ((0, 8), (0, 0)))
        upb = shares[:, 8 * rows_own :].reshape(1, -1).astype(F32)
        wi = lax.all_gather(project_in, AXES, axis=0, tiled=True)
        wo = lax.all_gather(project_out, AXES, axis=0, tiled=True)
        ffw = jnp.stack([up_weight.T, down_weight.T])
        ffw = lax.all_gather(ffw, "narrow", axis=1, tiled=True)
        ffw = lax.all_gather(ffw, "wide", axis=2, tiled=True)
        wi = wi.reshape(D, 3, GROUPS, WIDTH).transpose(2, 0, 1, 3).reshape(GROUPS, D, D)
        x = pick(order, patches)
        mixed, att, totals = attend(x, wi, vec)
        result, mg, upg, downg, upbg, sums_two = feed_forward(x, att, cot, wo, vec, ffw[0], upb, ffw[1])
        ig, wig, wog, sums_one = backward(x, mg, mixed, att, totals, wi, wo, vec)
        wig = wig.reshape(GROUPS, D, 3, WIDTH).transpose(1, 2, 0, 3).reshape(D, 3 * D)
        ffg = jnp.stack([upg, downg])
        ffg = lax.psum_scatter(ffg, "wide", scatter_dimension=2, tiled=True)
        ffg = lax.psum_scatter(ffg, "narrow", scatter_dimension=1, tiled=True).astype(F32)
        wig = lax.psum_scatter(wig, AXES, scatter_dimension=0, tiled=True).astype(F32)
        wog = lax.psum_scatter(wog, AXES, scatter_dimension=0, tiled=True).astype(F32)
        picks = [sums_one[G1], sums_one[B1], sums_one[QB], sums_one[VB]]
        picks += [sums_two[OB], sums_two[G2], sums_two[B2], sums_two[DB]]
        parts = jnp.stack(picks).reshape(8, -1, rows_own).transpose(1, 0, 2).reshape(-1, 8 * rows_own)
        parts = jnp.concatenate([parts, upbg.reshape(-1, hidden_own)], axis=1)
        own = lax.psum_scatter(parts, AXES, scatter_dimension=0, tiled=True)[0]
        s = [own[k * rows_own : (k + 1) * rows_own] for k in range(8)]
        upf, downf, upbf = ffg[0].T, ffg[1].T, own[8 * rows_own :]
        patch_grad, result = spread(order, ig, result)
    patch_grad = patch_grad.transpose(1, 3, 0, 2, 4).reshape(images, PATCHES, D)
    result = result.reshape(VIS, images, D).transpose(1, 0, 2)
    return (
        result, patch_grad, s[0], s[1], wig, s[2], s[3], wog, s[4], s[5], s[6], upf, upbf, downf, s[7],
    )


def solution(mesh):
    both = P(AXES)
    rows = P(AXES, None)
    cube = P(AXES, None, None)
    tile = P("wide", "narrow")
    return jax.shard_map(
        local,
        mesh=mesh,
        in_specs=(
            cube, rows, cube, both, both, rows, both, both, rows, both, both, both, tile, both, tile, both,
        ),
        out_specs=(
            cube, cube, both, both, rows, both, both, rows, both, both, both, tile, both, tile, both,
        ),
        check_vma=False,
    )
```

```python
import functools

import jax
import jax.numpy as jnp
from jax import lax
from jax.experimental import pallas as pl
from jax.experimental.pallas import tpu as pltpu
from jax.sharding import PartitionSpec as P

D = 768
HEADS = 12
HEAD_DIM = 64
PATCHES = 196
VIS = 49
PAD = 64
SIDE = 4
WIDTH = SIDE * HEAD_DIM
GROUPS = HEADS // SIDE
TOGETHER = 8
HIDDEN = 512
EPSILON = 1e-06
SCALE = HEAD_DIM ** (-0.5)
F32 = jnp.float32
BF16 = jnp.bfloat16
AXES = ("wide", "narrow")
G1, B1, QB, VB, OB, G2, B2, DB = range(8)


def params(**more):
    return pltpu.CompilerParams(vmem_limit_bytes=60 * 1024 * 1024, **more)


def mm(left, right):
    return jnp.dot(left, right, preferred_element_type=F32)


def mm_t(left, right):
    return lax.dot_general(left, right, (((1,), (1,)), ((), ())), preferred_element_type=F32)


def t_mm(left, right):
    return lax.dot_general(left, right, (((0,), (0,)), ((), ())), preferred_element_type=F32)


def norm_parts(values):
    mean = jnp.mean(values, axis=-1, keepdims=True)
    centred = values - mean
    spread = jnp.mean(centred * centred, axis=-1, keepdims=True)
    scale = lax.rsqrt(spread + EPSILON)
    return centred * scale, scale


def norm_back(grad, gain, normed, scale):
    pulled = grad * gain
    inner = jnp.mean(pulled * normed, axis=-1, keepdims=True)
    return scale * (pulled - jnp.mean(pulled, axis=-1, keepdims=True) - normed * inner)


def sum_rows(values):
    return jnp.sum(values, axis=0, keepdims=True)


def load_wide(ref, rows=slice(None)):
    return jnp.concatenate([ref[k, rows, :] for k in range(D // 128)], axis=1)


def store_wide(ref, rows, values):
    for k in range(D // 128):
        ref[k, rows, :] = values[:, k * 128 : (k + 1) * 128]


def heads_apart(block):
    lane = lax.broadcasted_iota(jnp.int32, block.shape, 1) // HEAD_DIM
    zero = jnp.zeros_like(block)
    return jnp.concatenate([jnp.where(lane == h, block, zero) for h in range(SIDE)], axis=0)


def heads_together(product):
    lane = lax.broadcasted_iota(jnp.int32, (HEAD_DIM, WIDTH), 1) // HEAD_DIM
    out = jnp.zeros((HEAD_DIM, WIDTH), F32)
    for h in range(SIDE):
        out = jnp.where(lane == h, product[h * HEAD_DIM : (h + 1) * HEAD_DIM], out)
    return out


def picked(order, first=0, count=PATCHES):
    lane = lax.broadcasted_iota(jnp.int32, (1, PAD), 1)
    order = jnp.where(lane < VIS, order, -1)
    row = lax.broadcasted_iota(jnp.int32, (count, PAD), 0) + first
    return jnp.where(row == order, 1.0, 0.0).astype(BF16)


LINE = 4
BLOCK = 128
CHUNK = 1024
CHUNKS = 3
MESH = pl.DeviceIdType.MESH


def place():
    wide, narrow = lax.axis_index("wide"), lax.axis_index("narrow")
    return lax.shift_right_logical(wide, 1), wide & 1, lax.shift_right_logical(narrow, 1), narrow & 1


def device(z, y, x, c):
    return (2 * z + y, 2 * x + c)


def at_step(step, plan, run):
    keys = sorted(plan)
    if len(keys) <= 2:
        for key in keys:
            pl.when(step == key)(functools.partial(run, plan[key]))
        return
    middle = keys[len(keys) // 2]
    low = {key: plan[key] for key in keys if key < middle}
    high = {key: plan[key] for key in keys if key >= middle}
    pl.when(step < middle)(lambda: at_step(step, low, run))
    pl.when(step >= middle)(lambda: at_step(step, high, run))


def of_three(i, size):
    group = (i >= size).astype(jnp.int32) + (i >= 2 * size).astype(jnp.int32)
    return group, i - group * size


def greet():
    z, y, x, c = place()
    barrier = pltpu.get_barrier_semaphore()
    peers = [device((z + k) & (LINE - 1), y, x, c) for k in range(1, LINE)]
    peers += [device(z, 1 - y, x, c), device(z, y, 1 - x, c), device(z, y, x, 1 - c), device(z, 1 - y, 1 - x, c)]
    for peer in peers:
        pl.semaphore_signal(barrier, inc=1, device_id=peer, device_id_type=MESH)
    pl.semaphore_wait(barrier, len(peers))


def remote(src, dst, send, recv, peer):
    return pltpu.make_async_remote_copy(
        src_ref=src, dst_ref=dst, send_sem=send, recv_sem=recv, device_id=peer, device_id_type=MESH
    )


class Gather:
    COPIES = 4

    def __init__(self, src, slot, x_first, halves, span, send, recv, own, direct=False):
        self.direct, self.span = direct, span
        self.src, self.slot, self.x_first, self.halves = src, slot, x_first, halves
        self.send, self.recv, self.own = send, recv, own
        self.z, self.y, self.x, self.c = place()

    def flip(self, z, first, second):
        y, x = self.y, self.x
        if first if self.x_first else second:
            x = 1 - x
        if second if self.x_first else first:
            y = 1 - y
        return z, y, x

    def line(self, k):
        return (self.z - k) & (LINE - 1)

    def copy(self, at, src, dst, peer):
        return remote(src, dst, self.send.at[at], self.recv.at[at], peer)

    def to_z(self, k):
        peer = device((self.z + k) & (LINE - 1), self.y, self.x, self.c)
        return self.copy(0, self.src, self.slot(self.z, self.y, self.x), peer)

    def to_first(self, k):
        slot = self.slot(self.line(k), self.y, self.x)
        peer = device(*self.flip(self.z, True, False), self.c)
        return self.copy(1, self.src if k == 0 else slot, slot, peer)

    def to_second(self, k):
        slot = self.slot(self.line(k), self.y, self.x)
        peer = device(*self.flip(self.z, False, True), self.c)
        return self.copy(2, self.src if k == 0 else slot, slot, peer)

    def on_to_second(self, k):
        slot = self.slot(*self.flip(self.line(k), True, False))
        peer = device(*self.flip(self.z, False, True), self.c)
        return self.copy(2, slot, slot, peer)

    def to_both(self, k):
        slot = self.slot(self.line(k), self.y, self.x)
        peer = device(*self.flip(self.z, True, True), self.c)
        return self.copy(2, self.src if k == 0 else slot, slot, peer)

    def to_core(self, j):
        part = self.halves(self.c)[j]
        return self.copy(3, part, part, device(self.z, self.y, self.x, 1 - self.c))

    def keep(self):
        return pltpu.make_async_copy(self.src, self.slot(self.z, self.y, self.x), self.own)

    def all_of(self, at, count):
        span = self.span(count)
        return self.copy(at, span, span, device(self.z, self.y, self.x, 1 - self.c))

    def start(self):
        self.keep().start()
        for k in range(1, LINE):
            self.to_z(k).start()
        self.to_first(0).start()
        self.to_second(0).start()
        if self.direct:
            self.to_both(0).start()

    def first(self):
        self.all_of(0, LINE - 1).wait_recv()
        for k in range(1, LINE):
            self.to_first(k).start()
            self.to_second(k).start()
            if self.direct:
                self.to_both(k).start()

    def second(self):
        self.all_of(1, LINE).wait_recv()
        for k in range(LINE):
            if not self.direct:
                self.on_to_second(k).start()

    def core(self):
        self.all_of(2, 2 * LINE).wait_recv()
        self.keep().wait()
        for j in range(len(self.halves(self.c))):
            self.to_core(j).start()

    def finish(self):
        held = len(self.halves(self.c)) > 0
        if held:
            self.all_of(3, 4 * LINE).wait_recv()
        self.all_of(0, LINE - 1).wait_send()
        self.all_of(1, LINE).wait_send()
        self.all_of(2, 2 * LINE).wait_send()
        if held:
            self.all_of(3, 4 * LINE).wait_send()


class Sum:
    COPIES = 4

    def __init__(self, take, own, theirs, ways, line, boxes, send, recv, near):
        self.take, self.own, self.theirs, self.ways, self.line, self.boxes = take, own, theirs, ways, line, boxes
        self.send, self.recv, self.near = send, recv, near
        self.z, self.y, self.x, self.c = place()

    def copy(self, at, src, dst, peer):
        return remote(src, dst, self.send.at[at], self.recv.at[at], device(*peer))

    def loads(self):
        return [pltpu.make_async_copy(src, dst, self.near.at[0]) for src, dst in self.take(self.c, self.own)]

    def to_core(self):
        peer = (self.z, self.y, self.x, 1 - self.c)
        return [self.copy(3, src, dst, peer) for src, dst in self.take(1 - self.c, self.theirs)]

    def out(self, turn):
        goes, _, x_way = self.ways[turn]
        peer = (self.z, self.y, 1 - self.x, self.c) if x_way else (self.z, 1 - self.y, self.x, self.c)
        return self.copy(turn, goes, self.boxes[turn], peer)

    def to_z(self, k):
        to = (self.z + k) & (LINE - 1)
        return self.copy(2, self.line(to), self.boxes[2].at[k - 1], (to, self.y, self.x, self.c))

    def all_loads(self):
        return pltpu.make_async_copy(self.own, self.own, self.near.at[0])

    def all_core(self):
        return self.copy(3, self.theirs, self.theirs, (self.z, self.y, self.x, 1 - self.c))

    def all_z(self):
        return self.copy(2, self.boxes[2], self.boxes[2], (self.z, self.y, self.x, 1 - self.c))

    def load(self):
        for one in self.loads() + self.to_core():
            one.start()

    def first(self):
        self.all_loads().wait()
        self.all_core().wait_recv()
        self.own[...] = self.own[...] + self.theirs[...]
        self.out(0).start()

    def second(self):
        self.out(0).wait_recv()
        stays = self.ways[0][1]
        stays[...] = stays[...] + self.boxes[0][...]
        self.out(1).start()

    def settle(self):
        self.out(1).wait_recv()
        stays = self.ways[1][1]
        stays[...] = stays[...] + self.boxes[1][...]

    def third(self):
        self.settle()
        for k in range(1, LINE):
            self.to_z(k).start()

    def total(self):
        self.all_z().wait_recv()
        out = self.line(self.z)[...].astype(F32)
        for k in range(LINE - 1):
            out = out + self.boxes[2][k].astype(F32)
        self.all_z().wait_send()
        self.left()
        return out

    def left(self):
        for one in (self.all_core(), self.out(0), self.out(1)):
            one.wait_send()


class LineSum(Sum):
    def load(self):
        self.loads()[0].start()

    def third(self):
        self.loads()[0].wait()
        for k in range(1, LINE):
            self.to_z(k).start()

    def left(self):
        pass


def rows_of(start, size, extent=None):
    return pl.ds(pl.multiple_of(start, size), size if extent is None else extent)


PICK_PARTS = 2
PICK_ROWS = PATCHES // PICK_PARTS


def pick_step(part, order_ref, patches_ref, out_ref, at, wide_ref):
    values = patches_ref[...].astype(F32).reshape(PICK_ROWS * TOGETHER, D)
    store_wide(wide_ref, slice(0, PICK_ROWS * TOGETHER), values)
    for j in range(TOGETHER):
        hot = picked(order_ref[j : j + 1, :PAD], part * PICK_ROWS, PICK_ROWS)
        own = load_wide(wide_ref, pl.ds(j, PICK_ROWS, stride=TOGETHER)).astype(BF16)
        rows = pl.ds(pl.multiple_of(at + j * PAD, PAD), PAD)
        value = t_mm(hot, own)
        out_ref[rows, :] = jnp.where(part == 0, value, value + out_ref[rows, :].astype(F32)).astype(BF16)


def pick_in(images):
    blocks = images // TOGETHER
    last = PICK_PARTS * blocks - 1
    index = lambda i: (lax.shift_right_logical(jnp.minimum(i, last), 1), 0)
    place_of = lambda i: (jnp.minimum(i, last) & 1, index(i)[0], 0)
    return [pl.BlockSpec((TOGETHER, PATCHES), index), pl.BlockSpec((PICK_ROWS, TOGETHER, D), place_of)]


def pick_kernel(order_ref, patches_ref, out_ref, wide_ref):
    pick_step(pl.program_id(0) % PICK_PARTS, order_ref, patches_ref, out_ref, 0, wide_ref)


def pick(order, patches):
    images = order.shape[0]
    return pl.pallas_call(
        pick_kernel,
        grid=(images // TOGETHER * PICK_PARTS,),
        in_specs=pick_in(images),
        out_specs=pl.BlockSpec((TOGETHER * PAD, D), lambda i: (i // PICK_PARTS, 0)),
        out_shape=jax.ShapeDtypeStruct((images * PAD, D), BF16),
        scratch_shapes=[pltpu.VMEM((D // 128, PICK_ROWS * TOGETHER, 128), F32)],
        compiler_params=params(),
        name="pick",
    )(order, patches)


HALF = 384
OWN = 24
PIECES = 3
SHARE = 4 * HALF + BLOCK


def parts_of_groups(block, g):
    return [block[:, k * D + g * WIDTH : k * D + (g + 1) * WIDTH] for k in range(3)]


def chip_row(z, y, x):
    return rows_of(((2 * z + y) * 2 + x) * 2 * OWN, 2 * OWN)


def share_out(in_ref, out_ref, vector_refs, share_ref):
    lines = [ref[...].astype(F32) for ref in vector_refs]
    lines = lines[:8] + [lines[8][:, k * OWN : (k + 1) * OWN] for k in range(4)]
    vectors = jnp.concatenate(lines, axis=0).astype(BF16)
    row = lax.broadcasted_iota(jnp.int32, (vectors.shape[0], BLOCK), 0)
    lane = lax.broadcasted_iota(jnp.int32, (vectors.shape[0], BLOCK), 1)
    columns = t_mm(vectors, jnp.where(row == lane, 1.0, 0.0).astype(BF16)).astype(BF16)
    share_ref[...] = jnp.zeros_like(share_ref)
    for g in range(GROUPS):
        both = jnp.concatenate(parts_of_groups(in_ref, g), axis=1)
        for h in range(2):
            share_ref[h, :OWN, g * HALF : (g + 1) * HALF] = both[:, h * HALF : (h + 1) * HALF]
    for h in range(2):
        share_ref[h, :OWN, 3 * HALF : 4 * HALF] = out_ref[:, h * HALF : (h + 1) * HALF]
        share_ref[h, :OWN, 4 * HALF :] = columns


def both_rows(mine, theirs):
    c = place()[3]
    mine, theirs = mine.astype(F32)[:OWN], theirs.astype(F32)[:OWN]
    top, low = jnp.where(c == 0, mine, theirs), jnp.where(c == 0, theirs, mine)
    return jnp.concatenate([top, low], axis=0).astype(BF16)


def hidden_bias(columns, out_ref):
    rows = 4 * OWN
    row = lax.broadcasted_iota(jnp.int32, (rows, 4 * rows * 4), 0)
    lane = lax.broadcasted_iota(jnp.int32, (rows, 4 * rows * 4), 1)
    which, hidden = lane // (4 * rows), lane % (4 * rows)
    hot = jnp.where(hidden == (row // OWN) * (4 * OWN) + which * OWN + row % OWN, 1.0, 0.0).astype(BF16)
    take = lax.broadcasted_iota(jnp.int32, (16, 4 * rows * 4), 0) == 8 + lane[:1] // (4 * rows)
    for w in range(2 * LINE):
        spread = t_mm(columns[w * rows : (w + 1) * rows, :16], hot)
        line = sum_rows(jnp.where(take, spread, 0.0))
        own = sum(line[:, k * 4 * rows : (k + 1) * 4 * rows] for k in range(4))
        for s in range(CHUNKS):
            at = s * CHUNK + (w % 2) * HIDDEN + (w // 2) * BLOCK
            out_ref[:, at : at + BLOCK] = own[:, s * BLOCK : (s + 1) * BLOCK]


def scores_of(k4, q_apart):
    return mm_t(k4, q_apart) * SCALE


BLOCKS = 3


def low_one(x, vec_ref):
    normed, _ = norm_parts(x.astype(F32))
    return (normed * vec_ref[G1 : G1 + 1, :] + vec_ref[B1 : B1 + 1, :]).astype(BF16)


def attend_step(g, low, wi, vec_ref, mixed_ref, total_ref, att, at):
    cols = rows_of(g * WIDTH, WIDTH)
    product = mm(low, wi[...])
    mixed_ref[:, :WIDTH] = (product[:, :WIDTH] + vec_ref[QB : QB + 1, cols]).astype(BF16)
    mixed_ref[:, WIDTH : 2 * WIDTH] = product[:, WIDTH : 2 * WIDTH].astype(BF16)
    mixed_ref[:, 2 * WIDTH :] = (product[:, 2 * WIDTH :] + vec_ref[VB : VB + 1, cols]).astype(BF16)
    images = range(TOGETHER)
    rows = [slice(img * PAD, (img + 1) * PAD) for img in images]
    real = lax.broadcasted_iota(jnp.int32, (PAD, WIDTH), 0) < VIS
    scores = [
        scores_of(mixed_ref[r, WIDTH : 2 * WIDTH], heads_apart(mixed_ref[r, :WIDTH])) for r in rows
    ]
    weights = []
    for img in images:
        own = jnp.where(real, scores[img], -1e30)
        top = jnp.max(own, axis=0, keepdims=True)
        raised = jnp.exp(own - top)
        total = sum_rows(raised)
        weights.append((raised * (1.0 / total)).astype(BF16))
        total_ref[0, img // SIDE, img % SIDE : img % SIDE + 1, :] = top + jnp.log(total)
    for img in images:
        value = heads_together(t_mm(weights[img], mixed_ref[rows[img], 2 * WIDTH :]))
        att[pl.ds(pl.multiple_of(at + img * PAD, PAD), PAD), cols] = value.astype(BF16)


def attend_kernel(x_ref, wi_ref, vec_ref, mixed_ref, att_ref, total_ref, low):
    step = pl.program_id(0)
    g, b = step // BLOCKS, step % BLOCKS
    at = b * (TOGETHER * PAD)
    rows = rows_of(at, TOGETHER * PAD)

    @pl.when(g == 0)
    def _():
        low[rows, :] = low_one(x_ref[rows, :], vec_ref)

    attend_step(g, low[rows, :], wi_ref.at[0], vec_ref, mixed_ref, total_ref, att_ref, at)


def full(*shape):
    return pl.BlockSpec(shape, lambda i: (0,) * len(shape))


def whole(a):
    return full(*a.shape)


def by_group(*block, lead=0, blocks=BLOCKS):
    def index(i):
        g, b = of_three(jnp.minimum(jnp.maximum(i - lead, 0), GROUPS * blocks - 1), blocks)
        return (g, b, 0, 0) if len(block) == 4 else (b, g)

    return pl.BlockSpec(block, index)


def TOTALS(lead):
    return by_group(1, TOGETHER // SIDE, 8, WIDTH, lead=lead)


def totals_shape(rows):
    return jax.ShapeDtypeStruct((GROUPS, rows // (SIDE * PAD), 8, WIDTH), F32)


def attend(x, wi, vec):
    rows = x.shape[0]
    block = TOGETHER * PAD
    shape = jax.ShapeDtypeStruct
    return pl.pallas_call(
        attend_kernel,
        grid=(GROUPS * BLOCKS,),
        in_specs=[whole(x), pl.BlockSpec((1, D, D), lambda i: (i // BLOCKS, 0, 0)), whole(vec)],
        out_specs=[by_group(block, D), full(rows, D), TOTALS(0)],
        out_shape=[
            shape((rows, 3 * D), BF16), shape((rows, D), BF16), totals_shape(rows),
        ],
        scratch_shapes=[pltpu.VMEM((rows, D), BF16)],
        compiler_params=params(),
        name="attend",
    )(x, wi, vec)


def gelu_both(x):
    bell = jnp.exp(-0.5 * x * x) * 0.3989422804014327
    below = 0.5 * (1.0 + lax.erf(x * 0.7071067811865476))
    return x * below, below + x * bell


def feed_early(cot_ref, sums_ref, middle, low, grad, low_t, grad_t, feed, back, act, inner):
    rows, held = cot_ref.shape[0], grad.shape[0]
    grad[:rows, :] = cot_ref[...]
    grad[rows:, :] = jnp.zeros((held - rows, D), BF16)
    sums_ref[DB : DB + 1, :] = sum_rows(cot_ref[...].astype(F32))
    grad_t[:, held:] = jnp.zeros((D, grad_t.shape[1] - held), BF16)
    grad_t[:, :held] = grad[...].T


def feed_start(x_ref, att_ref, cot_ref, wo_ref, vec_ref, sums_ref, middle, low, grad, low_t, grad_t, feed, back, act, inner):
    rows = cot_ref.shape[0]
    images = rows // VIS
    held = middle.shape[1]
    feed[...] = jnp.zeros_like(feed)
    back[...] = jnp.zeros_like(back)
    act[held:, :] = jnp.zeros((act.shape[0] - held, HIDDEN), BF16)
    inner[held:, :] = jnp.zeros((act.shape[0] - held, HIDDEN), BF16)
    middle[:, rows:, :] = jnp.zeros((D // 128, held - rows, 128), F32)
    for g in range(images // TOGETHER):
        at = slice(g * TOGETHER * PAD, (g + 1) * TOGETHER * PAD)
        branch = mm(att_ref[at, :], wo_ref[...]) + vec_ref[OB : OB + 1, :]
        mid = x_ref[at, :].astype(F32) + branch
        for j in range(TOGETHER):
            token = pl.ds(g * TOGETHER + j, VIS, stride=images)
            store_wide(middle, token, mid[j * PAD : j * PAD + VIS])
    normed, _ = norm_parts(load_wide(middle))
    low[...] = (normed * vec_ref[G2 : G2 + 1, :] + vec_ref[B2 : B2 + 1, :]).astype(BF16)
    low_t[:, held:] = jnp.zeros((D, low_t.shape[1] - held), BF16)
    low_t[:, :held] = low[...].T


def feed_step(up, upb, down, upbg_ref, middle, low, grad, low_t, grad_t, feed, back, act, inner):
    held = low.shape[0]
    before = mm(low[...], up[...]) + upb
    hidden_grad = mm(grad[...], down[...])
    value, slope = gelu_both(before)
    act[:held, :] = value.astype(BF16)
    before_grad = (hidden_grad * slope).astype(BF16)
    inner[:held, :] = before_grad
    upbg_ref[...] = sum_rows(before_grad.astype(F32))
    feed[...] += mm_t(act[:held, :], down[...])
    back[...] += mm_t(inner[:held, :], up[...])


def feed_grads(upg_ref, downg_ref, middle, low, grad, low_t, grad_t, feed, back, act, inner):
    downg_ref[...] = mm(grad_t[...], act[...]).astype(BF16)
    upg_ref[...] = mm(low_t[...], inner[...]).astype(BF16)


def feed_end(vec_ref, result_ref, mg_ref, sums_ref, middle, low, grad, low_t, grad_t, feed, back, act, inner):
    rows = result_ref.shape[0]
    images = rows // VIS
    held = low.shape[0]
    mid = load_wide(middle)
    result = feed[...] + mid + vec_ref[DB : DB + 1, :]
    result_ref[...] = result[:rows].astype(BF16)
    normed, scale = norm_parts(mid)
    pull = back[...]
    sums_ref[G2 : G2 + 1, :] = sum_rows(pull * normed)
    sums_ref[B2 : B2 + 1, :] = sum_rows(pull)
    mid_grad = grad[...].astype(F32) + norm_back(pull, vec_ref[G2 : G2 + 1, :], normed, scale)
    real = lax.broadcasted_iota(jnp.int32, (held, 1), 0) < rows
    mid_grad = jnp.where(real, mid_grad, 0.0)
    sums_ref[OB : OB + 1, :] = sum_rows(mid_grad.astype(BF16).astype(F32))
    store_wide(middle, slice(None), mid_grad)
    for j in range(images):
        out = j * PAD
        token = pl.ds(j, VIS, stride=images)
        own = jnp.concatenate([load_wide(middle, token), jnp.zeros((PAD - VIS, D), F32)], axis=0)
        mg_ref[out : out + PAD, :] = own.astype(BF16)


def feed_scratch(rows):
    held = -(-rows // 32) * 32
    deep = -(-rows // 256) * 256
    return [
        pltpu.VMEM((D // 128, held, 128), F32),
        pltpu.VMEM((held, D), BF16),
        pltpu.VMEM((held, D), BF16),
        pltpu.VMEM((D, deep), BF16),
        pltpu.VMEM((D, deep), BF16),
        pltpu.VMEM((held, D), F32),
        pltpu.VMEM((held, D), F32),
        pltpu.VMEM((deep, HIDDEN), BF16),
        pltpu.VMEM((deep, HIDDEN), BF16),
    ]


def feed_kernel(
    x_ref, att_ref, cot_ref, wo_ref, vec_ref, up_ref, upb_ref, down_ref,
    result_ref, mg_ref, upg_ref, downg_ref, upbg_ref, sums_ref, *scratch,
):
    step = pl.program_id(0)

    @pl.when(step == 0)
    def _():
        feed_early(cot_ref, sums_ref, *scratch)
        feed_start(x_ref, att_ref, cot_ref, wo_ref, vec_ref, sums_ref, *scratch)

    feed_step(up_ref, upb_ref[...], down_ref, upbg_ref, *scratch)
    feed_grads(upg_ref, downg_ref, *scratch)

    @pl.when(step == pl.num_programs(0) - 1)
    def _():
        feed_end(vec_ref, result_ref, mg_ref, sums_ref, *scratch)


def feed_forward(x, att, cot, wo, vec, up, upb, down):
    rows = cot.shape[0]
    ff = up.shape[1]
    hid = lambda r: pl.BlockSpec((r, HIDDEN), lambda i: (0, i))
    return pl.pallas_call(
        feed_kernel,
        grid=(ff // HIDDEN,),
        in_specs=[whole(x), whole(att), whole(cot), whole(wo), whole(vec), hid(D), hid(1), hid(D)],
        out_specs=[whole(cot), full(x.shape[0], D), hid(D), hid(D), hid(1), full(8, D)],
        out_shape=[
            jax.ShapeDtypeStruct(cot.shape, BF16),
            jax.ShapeDtypeStruct((x.shape[0], D), BF16),
            jax.ShapeDtypeStruct((D, ff), BF16),
            jax.ShapeDtypeStruct((D, ff), BF16),
            jax.ShapeDtypeStruct((1, ff), F32),
            jax.ShapeDtypeStruct((8, D), F32),
        ],
        scratch_shapes=feed_scratch(rows),
        compiler_params=params(),
        name="feed_forward",
    )(x, att, cot, wo, vec, up, upb, down)


FORWARD = {
    0: [("start", "v"), ("start", "g0"), ("start", "g1"), ("start", "g2"), ("start", "out")],
    3: [("first", "v")],
    4: [("first", "g0"), ("start", "d0"), ("start", "u0")],
    5: [("second", "v")],
    6: [("core", "v"), ("finish", "v")],
    7: [("first", "g2")],
    8: [("first", "out")],
    9: [("second", "g1"), ("core", "g1"), ("finish", "g1"), ("second", "g2"), ("first", "d0"), ("first", "u0")],
    10: [("start", "u1"), ("start", "d1")],
    11: [("second", "out"), ("core", "g2")],
    12: [("finish", "g2"), ("start", "u2")],
    14: [("second", "d0"), ("second", "u0"), ("start", "d2")],
    15: [("core", "out"), ("first", "u1"), ("first", "d1"), ("finish", "out")],
    16: [("first", "d2")],
    17: [("load", "su"), ("load", "sd"), ("finish", "u1"), ("finish", "d1"), ("second", "u2")],
    19: [("finish", "u2"), ("finish", "d2")],
}
MIDDLE = {
    15: [("second", "u1"), ("second", "d1"), ("first", "u2")],
    16: [("core", "u1"), ("core", "d1")],
    17: [("second", "d2"), ("first", "su"), ("first", "sd")],
    18: [("core", "u2"), ("core", "d2")],
    19: [("second", "su"), ("second", "sd")],
}
BEFORE_ATTENTION = [("first", "g1"), ("second", "g0"), ("core", "g0"), ("finish", "g0")]
BEFORE_FEED = [("core", "d0"), ("core", "u0"), ("finish", "d0"), ("finish", "u0")]
LAST_FORWARD = [("settle", "su"), ("settle", "sd")]


def forward_kernel(
    order_ref, patches_ref, in_ref, out_ref, cot_in, up_own, down_own, *refs,
):
    vector_refs, refs = refs[:9], refs[9:]
    (
    x_out, mixed_ref, total_ref, att_out, result_ref, mg_ref, upg_ref, downg_ref, upbg_ref, sums_ref, vec_ref, wi_ref, wo_ref,
    upf_ref, downf_ref, cot_ref, x_ref, att_ref, share_ref, other, piece, columns, upb, wi_all, wo_all, up_all, down_all, send, recv, own, near, *scratch,
    ) = refs
    step = pl.program_id(0)
    picks = x_ref.shape[0] // (TOGETHER * PAD) * PICK_PARTS
    early = picks + GROUPS * BLOCKS
    last = pl.num_programs(0) - 1
    z, y, x, c = place()
    features = D // 4
    feed_parts, sum_parts = scratch[:9], scratch[9:]
    middle = feed_parts[0]
    low_all = mg_ref
    swap = remote(share_ref.at[1 - c], other, near.at[0], near.at[1], device(z, y, x, 1 - c))

    def weight(j, src, dst, s, x_first):
        def slot(z, y, x):
            rows = rows_of((2 * x + c) * features, features)
            return dst.at[rows, rows_of(s * CHUNK + y * HIDDEN + z * BLOCK, BLOCK)]

        def halves(c):
            return [dst.at[rows_of((2 * k + c) * features, features), pl.ds(s * CHUNK, CHUNK)] for k in range(2)]

        block = src.at[:, pl.ds(s * BLOCK, BLOCK)]
        def span(count):
            rows, count = (features, count) if count <= 8 else (2 * features, count // 2)
            return dst.at[pl.ds(0, rows), pl.ds(0, count * BLOCK)]

        return Gather(block, slot, x_first, halves, span, send.at[j], recv.at[j], own.at[j])

    def square(j, k, dst, x_first, start=0, width=HALF, direct=False):
        lanes = lambda c: rows_of(c * HALF + start, BLOCK, width)
        slot = lambda z, y, x: dst.at[chip_row(z, y, x), lanes(c)]
        halves = lambda c: [dst.at[:, lanes(c)]]
        block = piece.at[:, pl.ds(k * HALF + start, width)]
        span = lambda count: dst.at[pl.ds(0, count * 2 * OWN), pl.ds(0, width)]
        return Gather(block, slot, x_first, halves, span, send.at[j], recv.at[j], own.at[j], direct)

    items = {}
    for s in range(CHUNKS):
        items[f"u{s}"] = [weight(2 * s, up_own, up_all, s, True)]
        items[f"d{s}"] = [weight(2 * s + 1, down_own, down_all, s, False)]
    j = 2 * CHUNKS
    slot = lambda z, y, x: columns.at[chip_row(z, y, x)]
    span = lambda count: columns.at[pl.ds(0, count * 2 * OWN)]
    items["v"] = [Gather(piece.at[:, pl.ds(4 * HALF, BLOCK)], slot, True, lambda c: [], span, send.at[j], recv.at[j], own.at[j], True)]
    items["g0"] = [square(j + 1, 0, wi_all.at[0], True, direct=True)]
    items["g1"] = [square(j + 3, 1, wi_all.at[1], True, direct=True)]
    items["g2"] = [square(j + 4, 2, wi_all.at[2], False)]
    items["out"] = [square(j + 5, 3, wo_all, True)]
    for name, one in zip(("su", "sd"), feed_sums((up_all, down_all), [0], *sum_parts)[0]):
        items[name] = [one]
    copies = [
        pltpu.make_async_copy(wi_all, wi_ref, near.at[2]),
        pltpu.make_async_copy(wo_all, wo_ref, near.at[3]),
        pltpu.make_async_copy(x_ref, x_out, near.at[2 + 2 * CHUNKS]),
        pltpu.make_async_copy(att_ref, att_out, near.at[3 + 2 * CHUNKS]),
    ]
    moves = []
    kept = CHUNK // HIDDEN
    for k in range(kept, CHUNKS * kept):
        lanes, dst = pl.ds(k * HIDDEN, HIDDEN), pl.ds((k - kept) * HIDDEN, HIDDEN)
        moves.append(pltpu.make_async_copy(up_all.at[:, lanes], upg_ref.at[:, dst], near.at[10 + 2 * (k - kept)]))
        moves.append(pltpu.make_async_copy(down_all.at[:, lanes], downg_ref.at[:, dst], near.at[11 + 2 * (k - kept)]))

    bring = pltpu.make_async_copy(cot_in, cot_ref, near.at[2])

    @pl.when(step == 0)
    def _():
        bring.start()
        share_out(in_ref, out_ref, vector_refs, share_ref)
        greet()
        swap.start()
        swap.wait()
        piece[...] = both_rows(share_ref[c], other[...])

    def run(acts):
        for act, which in acts:
            for one in items[which]:
                getattr(one, act)()

    at_step(step, FORWARD, run)

    lines = rows_of(y * HIDDEN, HIDDEN)
    for j, ref in enumerate((upf_ref, downf_ref)):
        copies.append(pltpu.make_async_copy(sum_parts[0].at[j, x, :, lines], ref, near.at[18 + j]))


    @pl.when(step < picks)
    def _():
        block = lax.shift_right_logical(step, 1)
        pick_step(step & 1, order_ref, patches_ref, x_ref, block * (TOGETHER * PAD), middle)

    @pl.when(step == picks - 1)
    def _():
        bring.wait()
        feed_early(cot_ref, sums_ref, *feed_parts)

    @pl.when(step == picks)
    def _():
        copies[2].start()
        vec_ref[...] = columns[...].astype(F32).T[:16]
        hidden_bias(columns[...], upb)
        for k in range(BLOCKS):
            block = slice(k * TOGETHER * PAD, (k + 1) * TOGETHER * PAD)
            low_all[block, :] = low_one(x_ref[block, :], vec_ref)
        run(BEFORE_ATTENTION)

    g, b = of_three(jnp.minimum(jnp.maximum(step - picks, 0), GROUPS * BLOCKS - 1), BLOCKS)
    at = b * (TOGETHER * PAD)
    rows = rows_of(at, TOGETHER * PAD)

    @pl.when((step >= picks) & (step < early))
    def _():
        attend_step(g, low_all[rows, :], wi_all.at[g], vec_ref, mixed_ref, total_ref, att_ref, at)

    @pl.when(step == early)
    def _():
        for k in (0, 1, 3):
            copies[k].start()
        feed_start(x_ref, att_ref, cot_ref, wo_all, vec_ref, sums_ref, *feed_parts)

    late = jnp.maximum(step - early, 0)
    lanes = rows_of(late * HIDDEN, HIDDEN)

    @pl.when(step == early)
    def _():
        run(BEFORE_FEED)

    @pl.when(step >= early)
    def _():
        feed_step(up_all.at[:, lanes], upb[:, lanes], down_all.at[:, lanes], upbg_ref, *feed_parts)
        at_step(step, MIDDLE, run)
        feed_grads(up_all.at[:, lanes], down_all.at[:, lanes], *feed_parts)

    def move(pair):
        for one in pair:
            one.start()

    at_step(step, {early + kept + k: moves[2 * k : 2 * k + 2] for k in range(len(moves) // 2)}, move)

    @pl.when(step == last)
    def _():
        feed_end(vec_ref, result_ref, mg_ref, sums_ref, *feed_parts)
        run(LAST_FORWARD)
        for one in copies[4:]:
            one.start()
        for name in ("su", "sd"):
            items[name][0].left()
        for one in copies + moves:
            one.wait()


def forward(order, patches, project_in, project_out, cot, up, down, *vectors):
    images = order.shape[0]
    rows = images * PAD
    block = TOGETHER * PAD
    picks = images // TOGETHER * PICK_PARTS
    early = picks + GROUPS * BLOCKS
    ff = CHUNKS * CHUNK
    late = ff // HIDDEN
    here = pl.BlockSpec(memory_space=pl.ANY)
    shape = jax.ShapeDtypeStruct
    count = 2 * CHUNKS + 6
    done = (D // 4, HIDDEN)
    return pl.pallas_call(
        forward_kernel,
        grid=(early + late,),
        in_specs=pick_in(images) + [whole(project_in), whole(project_out), here, here, here] + [whole(v) for v in vectors],
        out_specs=[
            here, by_group(block, D, lead=picks), TOTALS(picks), here,
            whole(cot), full(rows, D), here, here,
            pl.BlockSpec((1, HIDDEN), lambda i: (0, jnp.maximum(i - early, 0))),
            full(8, D), full(16, D), here, here, here, here,
        ],
        out_shape=[
            shape((rows, D), BF16), shape((rows, 3 * D), BF16), totals_shape(rows), shape((rows, D), BF16),
            shape(cot.shape, BF16), shape((rows, D), BF16), shape((D, ff - CHUNK), BF16), shape((D, ff - CHUNK), BF16),
            shape((1, ff), F32), shape((8, D), F32), shape((16, D), F32),
            shape((GROUPS, D, D), BF16), shape((D, D), BF16), shape(done, BF16), shape(done, BF16),
        ],
        scratch_shapes=[
            pltpu.VMEM(cot.shape, BF16),
            pltpu.VMEM((rows, D), BF16),
            pltpu.VMEM((rows, D), BF16),
            pltpu.VMEM((2, 32, SHARE), BF16),
            pltpu.VMEM((32, SHARE), BF16),
            pltpu.VMEM((2 * OWN, SHARE), BF16),
            pltpu.VMEM((D, BLOCK), BF16),
            pltpu.VMEM((1, ff), F32),
            pltpu.VMEM((GROUPS, D, D), BF16),
            pltpu.VMEM((D, D), BF16),
            pltpu.VMEM((D, ff), BF16),
            pltpu.VMEM((D, ff), BF16),
            pltpu.SemaphoreType.DMA((count, Gather.COPIES)),
            pltpu.SemaphoreType.DMA((count, Gather.COPIES)),
            pltpu.SemaphoreType.DMA((count,)),
            pltpu.SemaphoreType.DMA((12 + 2 * (CHUNKS - 1) * (CHUNK // HIDDEN),)),
        ] + feed_scratch(cot.shape[0]) + feed_sum_scratch(1),
        compiler_params=params(collective_id=2, has_side_effects=True),
        name="forward",
    )(order, patches, project_in, project_out, cot, up, down, *vectors)


BACKWARD = {
    0: [("load", 1), ("load", 2), ("load", 0)],
    1: [("first", 1), ("third", 0)],
    2: [("first", 2)],
    3: [("load", "out"), ("load", "g0")],
    4: [("second", 1), ("first", "out"), ("first", "g0")],
    6: [("second", 2), ("load", "g1")],
    7: [("third", 1), ("total", 0)],
    8: [("first", "g1")],
    9: [("second", "out"), ("second", "g0"), ("load", "g2"), ("load", "v")],
    10: [("first", "g2"), ("first", "v"), ("third", 2), ("total", 1)],
    12: [("third", "out"), ("third", "g0"), ("load", "late"), ("second", "g1")],
    13: [("first", "late"), ("second", "g2"), ("second", "v")],
    14: [("third", "g1"), ("second", "late"), ("third", "g2"), ("third", "v")],
}
LAST = [("total", 2), ("third", "late"), ("total", "out"), ("total", "g0"), ("total", "g1"), ("total", "g2"), ("total", "v")]
BACK = 3


def unattend_step(mixed_ref, att_grad, totals, grads, g, at):
    real = lax.broadcasted_iota(jnp.int32, (PAD, WIDTH), 0) < VIS
    for first in range(0, TOGETHER, SIDE):
        images = range(first, first + SIDE)
        held = []
        for img in images:
            rows = slice(img * PAD, (img + 1) * PAD)
            q4, k4, v4 = [mixed_ref[rows, k * WIDTH : (k + 1) * WIDTH] for k in range(3)]
            q_apart, a_apart = heads_apart(q4), heads_apart(att_grad[rows, :])
            held.append((k4, q_apart, a_apart, scores_of(k4, q_apart), mm_t(v4, a_apart)))
        ready = []
        for img, (k4, q_apart, a_apart, scores, pulled) in zip(images, held):
            exact = jnp.exp(scores - totals[0, img // SIDE, img % SIDE : img % SIDE + 1, :])
            exact = jnp.where(real, exact, 0.0)
            centre = sum_rows(exact * pulled)
            score_grad = (exact * (pulled - centre)).astype(BF16)
            ready.append((k4, q_apart, a_apart, score_grad, exact.astype(BF16)))
        for img, (k4, q_apart, a_apart, score_grad, weights) in zip(images, ready):
            q_grad = heads_together(t_mm(score_grad, k4)) * SCALE
            k_grad = mm(score_grad, q_apart) * SCALE
            v_grad = mm(weights, a_apart)
            out = pl.ds(pl.multiple_of(at + img * PAD, PAD), PAD)
            grads[g, out, :WIDTH] = q_grad.astype(BF16)
            grads[g, out, WIDTH : 2 * WIDTH] = k_grad.astype(BF16)
            grads[g, out, 2 * WIDTH :] = v_grad.astype(BF16)


def pull_step(x, grads, rows, wi_ref, pull_ref, sums_ref):
    normed, _ = norm_parts(x.astype(F32))
    pull = sum(mm_t(grads[g, rows, :], wi_ref[g]) for g in range(GROUPS))
    sums_ref[G1 : G1 + 1, :] += sum_rows(pull * normed)
    sums_ref[B1 : B1 + 1, :] += sum_rows(pull)
    pull_ref[rows, :] = pull


def unnorm_step(x, mg, pull, vec_ref, ig_ref):
    normed, scale = norm_parts(x.astype(F32))
    ig_ref[...] = (mg.astype(F32) + norm_back(pull, vec_ref[G1 : G1 + 1, :], normed, scale)).astype(BF16)


def backward_kernel(x_in, mg_in, mixed_ref, att_ref, total_ref, wi_in, wo_ref, vec_ref, *refs):
    step = pl.program_id(0)
    walk = GROUPS * BACK
    last = pl.num_programs(0) - 1
    g, b = of_three(jnp.minimum(step, walk - 1), BACK)
    b = jnp.where(step >= walk, jnp.where(step >= walk + BACK, step - walk - BACK, step - walk), b)
    at = b * (TOGETHER * PAD)
    rows = rows_of(at, TOGETHER * PAD)
    x_ref, mg_ref, wi_ref, brought = refs[-4:]
    refs = refs[:-4]
    remote_sums = len(refs) > 12
    brings = [pltpu.make_async_copy(wi_in, wi_ref, brought.at[2 * BACK])]
    for k in range(BACK):
        block = pl.ds(k * TOGETHER * PAD, TOGETHER * PAD)
        brings.insert(2 * k, pltpu.make_async_copy(x_in.at[block], x_ref.at[block], brought.at[2 * k]))
        brings.insert(2 * k + 1, pltpu.make_async_copy(mg_in.at[block], mg_ref.at[block], brought.at[2 * k + 1]))

    @pl.when(step == 0)
    def _():
        for one in brings:
            one.start()
    if remote_sums:
        upg_ref, downg_ref, sums_two_ref, upbg_ref, up_first, down_first = refs[:6]
        refs = refs[2:]
        ig_ref, wi_out, wo_out, vec_out, upf_ref, downf_ref = refs[4:10]
        low_t, att_t, grads, pull, sums_ref, wig_ref, wog_ref, end, other_end, end_send, end_recv = refs[10:21]
        feed_parts, square_parts, early_parts, late_parts, line_parts = refs[21:30], refs[30:38], refs[38:46], refs[46:54], refs[54:]
        z, y, x, c = place()
        items = dict(enumerate(feed_sums((upg_ref, downg_ref), range(1, CHUNKS), *feed_parts), 1))
        for j, name in enumerate(("g0", "g1", "out")):
            src = wog_ref if name == "out" else wig_ref.at[j]
            items[name] = [square_sum(j, j, src, slice(0, HALF), j == 0, *square_parts)]
        cuts = [slice(0, 2 * BLOCK), slice(2 * BLOCK, HALF)]
        items["g2"] = [square_sum(3, 3 + j, wig_ref.at[2], cut, j == 0, *square_parts) for j, cut in enumerate(cuts)]
        items[0] = [line_sum(j, src, *line_parts) for j, src in enumerate((up_first, down_first))]
        items["v"] = [vector_sum(*early_parts)]
        items["late"] = [vector_sum(*late_parts)]
        places = {"g0": 0, "g1": 1, "g2": 2, "out": 3}

        def swap(j):
            give = end.at[j, pl.ds(pl.multiple_of((1 - c) * OWN, 8), OWN)]
            return remote(give, other_end.at[j], end_send.at[j], end_recv.at[j], device(z, y, x, 1 - c))

        def act(name, which):
            values = [getattr(one, name)() for one in items[which]]
            if name != "total":
                return
            if which in (0, 1, 2):
                lanes = slice(which * BLOCK, (which + 1) * BLOCK)
                upf_ref[:, lanes], downf_ref[:, lanes] = values
            elif which in places:
                end[places[which]] = jnp.concatenate(values, axis=1)
                swap(places[which]).start()
            else:
                early = which == "v"
                value = jnp.where(c == 0, values[0][:, :OWN], values[0][:, OWN : 2 * OWN])
                if early:
                    vec_out[:6, :OWN] = value[:6]
                    vec_out[6:7, :] = jnp.where(c == 0, values[0][6:7], values[0][7:8])
                else:
                    vec_out[8:, :OWN] = value

        def run(acts):
            for name, which in acts:
                if (name, which) == ("load", "v"):
                    own = [sums_ref[k : k + 1, :] for k in (QB, VB)]
                    own += [sums_two_ref[k : k + 1, :] for k in (OB, G2, B2, DB)]
                    items["v"][0].fill(jnp.concatenate(own, axis=0), upbg_ref)
                if (name, which) == ("load", "late"):
                    items["late"][0].fill(sums_ref[G1 : B1 + 1, :])
                act(name, which)

        @pl.when(step == 0)
        def _():
            greet()

        at_step(step, BACKWARD, run)
    else:
        ig_ref, wi_out, wo_out, sums_ref, low_t, att_t, grads, pull, wig_ref, wog_ref = refs

    @pl.when(step == 0)
    def _():
        sums_ref[...] = jnp.zeros_like(sums_ref)
        if remote_sums:
            vec_out[...] = jnp.zeros_like(vec_out)

    for k in range(BACK):

        @pl.when(step == k)
        def _(k=k):
            brings[2 * k].wait()
            brings[2 * k + 1].wait()

    @pl.when(step == walk)
    def _():
        brings[-1].wait()

    @pl.when(step < BACK)
    def _():
        low_t[:, rows] = low_one(x_ref[rows, :], vec_ref).T
        att_t[:, rows] = att_ref[...].T

    @pl.when(step < walk)
    def _():
        cols = rows_of(g * WIDTH, WIDTH)
        att_grad = mm_t(mg_ref[rows, :], wo_ref[cols, :]).astype(BF16)
        unattend_step(mixed_ref, att_grad, total_ref, grads, g, at)
        own = grads[g, rows, :]
        sums_ref[QB : QB + 1, cols] += sum_rows(own[:, :WIDTH].astype(F32))
        sums_ref[VB : VB + 1, cols] += sum_rows(own[:, 2 * WIDTH :].astype(F32))

    @pl.when(step == BACK - 1)
    def _():
        wog_ref[...] = mm(att_t[...], mg_ref[...]).astype(BF16).reshape(wog_ref.shape)

    @pl.when((b == BACK - 1) & (step < walk))
    def _():
        wig_ref[g] = mm(low_t[...], grads[g]).astype(BF16).reshape(wig_ref.shape[1:])

    @pl.when((step >= walk) & (step < walk + BACK))
    def _():
        pull_step(x_ref[rows, :], grads, rows, wi_ref, pull, sums_ref)

    @pl.when(step >= walk + BACK)
    def _():
        unnorm_step(x_ref[rows, :], mg_ref[rows, :], pull[rows, :], vec_ref, ig_ref)

    @pl.when(step == last)
    def _():
        if not remote_sums:
            wi_out[...] = wig_ref[...].reshape(wi_out.shape)
            wo_out[...] = wog_ref[...].reshape(wo_out.shape)
            return
        for name, which in LAST:
            act(name, which)
        for j in range(PIECES + 1):
            swap(j).wait()
            mine, theirs = end[j, pl.ds(pl.multiple_of(c * OWN, 8), OWN), :], other_end[j]
            both = jnp.concatenate([jnp.where(c == 0, mine, theirs), jnp.where(c == 0, theirs, mine)], axis=1)
            if j < GROUPS:
                for k in range(3):
                    wi_out[:, k * D + j * WIDTH : k * D + (j + 1) * WIDTH] = both[:, k * WIDTH : (k + 1) * WIDTH]
            else:
                wo_out[...] = both
        act("total", "late")


CHIPS = (LINE, 2, 2, 2 * OWN)


def ways_of(mine, x_first):
    z, y, x, c = place()
    if x_first:
        return [(mine.at[:, :, 1 - x], mine.at[:, :, x], True), (mine.at[:, 1 - y, x], mine.at[:, y, x], False)]
    return [(mine.at[:, 1 - y], mine.at[:, y], False), (mine.at[:, y, 1 - x], mine.at[:, y, x], True)]


def square_sum(j, at, src, lanes, x_first, own, theirs, box_one, box_two, box_z, send, recv, near):
    z, y, x, c = place()
    width = lanes.stop - lanes.start

    def take(c, into):
        return [(src.at[:, :, :, :, rows_of(c * HALF + lanes.start, BLOCK, width)], into)]

    lanes = pl.ds(lanes.start, width)
    mine = own.at[j, :, :, :, :, lanes]
    line = lambda to: mine.at[to, y, x]
    boxes = (box_one.at[j, :, :, :, lanes], box_two.at[j, :, :, lanes], box_z.at[j, :, :, lanes])
    return Sum(
        take, mine, theirs.at[j, :, :, :, :, lanes], ways_of(mine, x_first), line, boxes, send.at[at], recv.at[at], near.at[at]
    )


class VectorSum(Sum):
    def fill(self, vectors, hidden=None):
        self.own[...] = jnp.zeros(self.own.shape, F32)
        count, width = vectors.shape[0], 4 * OWN
        for k in range(2 * LINE * 2):
            z, y, x = k // 4, k // 2 % 2, k % 2
            self.own[z, y, x, :count, : 2 * OWN] = vectors[:, k * 2 * OWN : (k + 1) * 2 * OWN]
            if hidden is not None:
                at = [s * CHUNK + y * HIDDEN + z * BLOCK for s in range(CHUNKS)]
                line = jnp.concatenate([hidden[:, a : a + BLOCK] for a in at], axis=1)
                for c in range(2):
                    start = (2 * x + c) * width
                    self.own[z, y, x, 6 + c : 7 + c, :width] = line[:, start : start + width]

    def loads(self):
        return []

    def first(self):
        self.all_core().wait_recv()
        self.all_core().wait_send()
        self.own[...] = self.own[...] + self.theirs[...]
        self.out(0).start()

    def total(self):
        self.all_z().wait_recv()
        out = self.line(self.z)[...]
        for k in range(LINE - 1):
            out = out + self.boxes[2][k]
        for one in (self.out(0), self.out(1), self.all_z()):
            one.wait_send()
        return out


def line_sum(j, src, own, box_z, send, recv, near):
    mine = own.at[j]
    line = lambda to: mine.at[:, rows_of(to * BLOCK, BLOCK)]
    take = lambda c, into: [(src, into)]
    return LineSum(take, mine, mine, None, line, (None, None, box_z.at[j]), send.at[j], recv.at[j], near.at[j])


def line_sum_scratch():
    return [
        pltpu.VMEM((2, D // 4, HIDDEN), BF16),
        pltpu.VMEM((2, LINE - 1, D // 4, BLOCK), BF16),
        pltpu.SemaphoreType.DMA((2, Sum.COPIES)),
        pltpu.SemaphoreType.DMA((2, Sum.COPIES)),
        pltpu.SemaphoreType.DMA((2, 1)),
    ]


def vector_sum(own, theirs, box_one, box_two, box_z, send, recv, near):
    z, y, x, c = place()
    mine = own.at[0]
    line = lambda to: mine.at[to, y, x]
    boxes = (box_one.at[0], box_two.at[0], box_z.at[0])
    return VectorSum(
        lambda c, into: [(mine, into)], mine, theirs.at[0], ways_of(mine, False), line, boxes, send.at[0], recv.at[0], near.at[0]
    )


def square_sum_scratch(count, lanes=HALF, dtype=BF16, rows=2 * OWN, copies=None):
    chips = CHIPS[:3] + (rows,)
    copies = count if copies is None else copies
    return [
        pltpu.VMEM((count,) + chips + (lanes,), dtype),
        pltpu.VMEM((count,) + chips + (lanes,), dtype),
        pltpu.VMEM((count, LINE, 2, rows, lanes), dtype),
        pltpu.VMEM((count, LINE, rows, lanes), dtype),
        pltpu.VMEM((count, LINE - 1, rows, lanes), dtype),
        pltpu.SemaphoreType.DMA((copies, Sum.COPIES)),
        pltpu.SemaphoreType.DMA((copies, Sum.COPIES)),
        pltpu.SemaphoreType.DMA((copies, 1)),
    ]


def feed_sums(grads_refs, which_chunks, own, theirs, box_y, box_x, box_two, box_z, send, recv, near):
    z, y, x, c = place()
    features = D // 4

    def one(s, which):
        grads = grads_refs[which]
        j = 2 * s + which

        def take(c, into):
            return [
                (grads.at[rows_of((2 * k + c) * features, features), pl.ds(s * CHUNK, CHUNK)], into.at[k])
                for k in range(2)
            ]

        mine = own.at[j]
        keep, give = rows_of(y * HIDDEN, HIDDEN), rows_of((1 - y) * HIDDEN, HIDDEN)
        if which == 0:
            ways = [
                (mine.at[:, :, give], mine.at[:, :, keep], False),
                (mine.at[1 - x, :, keep], mine.at[x, :, keep], True),
            ]
            box_one = box_y.at[s]
        else:
            ways = [(mine.at[1 - x], mine.at[x], True), (mine.at[x, :, give], mine.at[x, :, keep], False)]
            box_one = box_x.at[s]
        line = lambda to: mine.at[x, :, rows_of(y * HIDDEN + to * BLOCK, BLOCK)]
        boxes = (box_one, box_two.at[j], box_z.at[j])
        return Sum(lambda c, into: take(c, into), mine, theirs.at[j], ways, line, boxes, send.at[j], recv.at[j], near.at[j])

    return [[one(s, 0), one(s, 1)] for s in range(len(which_chunks))]


def feed_sum_scratch(chunks):
    features = D // 4
    count = 2 * chunks
    return [
        pltpu.VMEM((count, 2, features, CHUNK), BF16),
        pltpu.VMEM((count, 2, features, CHUNK), BF16),
        pltpu.VMEM((chunks, 2, features, HIDDEN), BF16),
        pltpu.VMEM((chunks, features, CHUNK), BF16),
        pltpu.VMEM((count, features, HIDDEN), BF16),
        pltpu.VMEM((count, LINE - 1, features, BLOCK), BF16),
        pltpu.SemaphoreType.DMA((count, Sum.COPIES)),
        pltpu.SemaphoreType.DMA((count, Sum.COPIES)),
        pltpu.SemaphoreType.DMA((count, 1)),
    ]


def backward(x, mg, mixed, att, totals, wi, wo, vec, *more):
    rows = x.shape[0]
    block = TOGETHER * PAD
    walk = GROUPS * BACK
    here = pl.BlockSpec(memory_space=pl.ANY)
    shape = jax.ShapeDtypeStruct
    scratch = [pltpu.VMEM((D, rows), BF16), pltpu.VMEM((D, rows), BF16), pltpu.VMEM((GROUPS, rows, D), BF16)]
    scratch += [pltpu.VMEM((rows, D), F32)]
    sums = [pltpu.VMEM((8, D), F32)]
    weights = [pltpu.VMEM((GROUPS,) + CHIPS + (D,), BF16), pltpu.VMEM(CHIPS + (D,), BF16)]
    specs = []
    if more:
        specs = [here, here] + [whole(a) for a in more[2:4]] + [here, here]
        own = (D // 4, CHUNKS * BLOCK)
        out = [(OWN, 3 * D), (OWN, D), (16, BLOCK), own, own]
        scratch += sums + weights + [
            pltpu.VMEM((PIECES + 1, 2 * OWN, HALF), F32),
            pltpu.VMEM((PIECES + 1, OWN, HALF), F32),
            pltpu.SemaphoreType.DMA((PIECES + 1,)),
            pltpu.SemaphoreType.DMA((PIECES + 1,)),
        ] + feed_sum_scratch(CHUNKS - 1) + square_sum_scratch(PIECES + 1, copies=PIECES + 2)
        scratch += square_sum_scratch(1, BLOCK, F32, 8) + square_sum_scratch(1, BLOCK, F32, 8) + line_sum_scratch()
        out_shape = [shape(s, F32) for s in out]
    else:
        out = [(GROUPS, D, D), (D, D), (8, D)]
        out_shape = [shape(s, F32 if s[0] == 8 else BF16) for s in out]
        scratch += weights
    return pl.pallas_call(
        backward_kernel,
        grid=(walk + BACK + BLOCKS,),
        in_specs=[
            here, here, by_group(block, D, blocks=BACK),
            pl.BlockSpec((block, D), lambda i: (jnp.minimum(i, BACK - 1), 0)),
            TOTALS(0), here, whole(wo), whole(vec),
        ] + specs,
        out_specs=[pl.BlockSpec((block, D), lambda i: (jnp.maximum(i - walk - BACK, 0), 0))] + [full(*s) for s in out],
        out_shape=[shape((rows, D), BF16)] + out_shape,
        scratch_shapes=scratch + [
            pltpu.VMEM((rows, D), BF16),
            pltpu.VMEM((rows, D), BF16),
            pltpu.VMEM((GROUPS, D, D), BF16),
            pltpu.SemaphoreType.DMA((2 * BACK + 1,)),
        ],
        compiler_params=params(collective_id=3, has_side_effects=True) if more else params(),
        name="backward",
    )(x, mg, mixed, att, totals, wi, wo, vec, *more)


def spread_kernel(lines, order_ref, ig_ref, *refs):
    near, refs = refs[-1], refs[:-1]
    count = (len(refs) - 1 - len(lines)) // 3
    given, out_ref, refs = refs[:count], refs[count], refs[count + 1 :]
    outs, ones, held = refs[:count], refs[count : count + len(lines)], refs[count + len(lines) :]
    step = pl.program_id(0)
    ins = [pltpu.make_async_copy(src, dst, near.at[j]) for j, (src, dst) in enumerate(zip(given, held))]
    outs = [pltpu.make_async_copy(src, dst, near.at[j]) for j, (src, dst) in enumerate(zip(held, outs))]

    @pl.when(step == 0)
    def _():
        for one in ins:
            one.start()

    @pl.when(step == 1)
    def _():
        for one in ins:
            one.wait()
        for one in outs:
            one.start()
        for (row, lanes), one in zip(lines, ones):
            one[...] = held[-1][row, :lanes]

    @pl.when(step == pl.num_programs(0) - 1)
    def _():
        for one in outs:
            one.wait()

    blocks = D // 128
    rows = out_ref.reshape(PATCHES * blocks * TOGETHER, 128)
    own = [mm(picked(order_ref[j : j + 1, :PAD]), ig_ref[j * PAD : (j + 1) * PAD, :]) for j in range(TOGETHER)]
    for j in range(TOGETHER):
        for k in range(blocks):
            at = pl.ds(k * TOGETHER + j, PATCHES, stride=blocks * TOGETHER)
            rows[at, :] = own[j][:, k * 128 : (k + 1) * 128]


def spread(order, ig, result, *more, lines=()):
    images = order.shape[0]
    steps = images // TOGETHER
    passed = [pl.BlockSpec(memory_space=pl.ANY)] * (1 + len(more))
    shape = jax.ShapeDtypeStruct
    return pl.pallas_call(
        functools.partial(spread_kernel, lines),
        grid=(steps,),
        in_specs=[
            pl.BlockSpec((TOGETHER, PATCHES), lambda i: (i, 0)),
            pl.BlockSpec((TOGETHER * PAD, D), lambda i: (i, 0)),
        ] + passed,
        out_specs=[pl.BlockSpec((PATCHES, 1, D // 128, TOGETHER, 128), lambda i: (0, i, 0, 0, 0))] + passed
        + [full(lanes) for _, lanes in lines],
        out_shape=[shape((PATCHES, steps, D // 128, TOGETHER, 128), F32)] + [shape(a.shape, a.dtype) for a in (result,) + more]
        + [shape((lanes,), F32) for _, lanes in lines],
        scratch_shapes=[pltpu.VMEM(a.shape, a.dtype) for a in (result,) + more] + [pltpu.SemaphoreType.DMA((1 + len(more),))],
        compiler_params=params(),
        name="spread",
    )(order, ig, result, *more)


def local(
    patches, keep_order, cotangent, first_gain, first_shift, project_in, query_bias, value_bias,
    project_out, output_bias, second_gain, second_shift, up_weight, up_bias, down_weight, down_bias,
):
    rows_own = project_in.shape[0]
    hidden_own = up_bias.shape[0]
    images = patches.shape[0]
    wide, narrow = lax.axis_size("wide"), lax.axis_size("narrow")
    vectors = [first_gain, first_shift, query_bias, value_bias, output_bias, second_gain, second_shift, down_bias]
    order = keep_order
    patches = patches.transpose(1, 0, 2)
    cot = cotangent.transpose(1, 0, 2).reshape(VIS * images, D)
    if (wide, narrow) == (8, 4):
        x, mixed, totals, att, result, mg, upg, downg, upbg, sums_two, vec, wi, wo, up_zero, down_zero = forward(
            order, patches, project_in, project_out, cot, up_weight.T, down_weight.T,
            *[v.reshape(1, -1) for v in vectors + [up_bias]],
        )
        ig, wig, wog, s, upf, downf = backward(
            x, mg, mixed, att, totals, wi, wo, vec, upg, downg, sums_two, upbg, up_zero, down_zero
        )
        lines = [(k, rows_own) for k in (8, 9, 0, 1, 2, 3, 4, 5)] + [(6, 4 * rows_own)]
        patch_grad, result, wig, wog, upf, downf, _, *s, upbf = spread(
            order, ig, result, wig, wog, upf, downf, s, lines=lines
        )
        upf, downf = upf.T, downf.T
    else:
        share = jnp.concatenate([jnp.stack(vectors).reshape(1, -1), up_bias.reshape(1, -1)], axis=1)
        shares = lax.all_gather(share, AXES, axis=0, tiled=True)
        vec = shares[:, : 8 * rows_own].reshape(-1, 8, rows_own).transpose(1, 0, 2).reshape(8, D)
        vec = jnp.pad(vec.astype(F32), ((0, 8), (0, 0)))
        upb = shares[:, 8 * rows_own :].reshape(1, -1).astype(F32)
        wi = lax.all_gather(project_in, AXES, axis=0, tiled=True)
        wo = lax.all_gather(project_out, AXES, axis=0, tiled=True)
        ffw = jnp.stack([up_weight.T, down_weight.T])
        ffw = lax.all_gather(ffw, "narrow", axis=1, tiled=True)
        ffw = lax.all_gather(ffw, "wide", axis=2, tiled=True)
        wi = wi.reshape(D, 3, GROUPS, WIDTH).transpose(2, 0, 1, 3).reshape(GROUPS, D, D)
        x = pick(order, patches)
        mixed, att, totals = attend(x, wi, vec)
        result, mg, upg, downg, upbg, sums_two = feed_forward(x, att, cot, wo, vec, ffw[0], upb, ffw[1])
        ig, wig, wog, sums_one = backward(x, mg, mixed, att, totals, wi, wo, vec)
        wig = wig.reshape(GROUPS, D, 3, WIDTH).transpose(1, 2, 0, 3).reshape(D, 3 * D)
        ffg = jnp.stack([upg, downg])
        ffg = lax.psum_scatter(ffg, "wide", scatter_dimension=2, tiled=True)
        ffg = lax.psum_scatter(ffg, "narrow", scatter_dimension=1, tiled=True).astype(F32)
        wig = lax.psum_scatter(wig, AXES, scatter_dimension=0, tiled=True).astype(F32)
        wog = lax.psum_scatter(wog, AXES, scatter_dimension=0, tiled=True).astype(F32)
        picks = [sums_one[G1], sums_one[B1], sums_one[QB], sums_one[VB]]
        picks += [sums_two[OB], sums_two[G2], sums_two[B2], sums_two[DB]]
        parts = jnp.stack(picks).reshape(8, -1, rows_own).transpose(1, 0, 2).reshape(-1, 8 * rows_own)
        parts = jnp.concatenate([parts, upbg.reshape(-1, hidden_own)], axis=1)
        own = lax.psum_scatter(parts, AXES, scatter_dimension=0, tiled=True)[0]
        s = [own[k * rows_own : (k + 1) * rows_own] for k in range(8)]
        upf, downf, upbf = ffg[0].T, ffg[1].T, own[8 * rows_own :]
        patch_grad, result = spread(order, ig, result)
    patch_grad = patch_grad.transpose(1, 3, 0, 2, 4).reshape(images, PATCHES, D)
    result = result.reshape(VIS, images, D).transpose(1, 0, 2)
    return (
        result, patch_grad, s[0], s[1], wig, s[2], s[3], wog, s[4], s[5], s[6], upf, upbf, downf, s[7],
    )


def solution(mesh):
    both = P(AXES)
    rows = P(AXES, None)
    cube = P(AXES, None, None)
    tile = P("wide", "narrow")
    return jax.shard_map(
        local,
        mesh=mesh,
        in_specs=(
            cube, rows, cube, both, both, rows, both, both, rows, both, both, both, tile, both, tile, both,
        ),
        out_specs=(
            cube, cube, both, both, rows, both, both, rows, both, both, both, tile, both, tile, both,
        ),
        check_vma=False,
    )
```

```python
import functools

import jax
import jax.numpy as jnp
from jax import lax
from jax.experimental import pallas as pl
from jax.experimental.pallas import tpu as pltpu
from jax.sharding import PartitionSpec as P

D = 768
HEADS = 12
HEAD_DIM = 64
PATCHES = 196
VIS = 49
PAD = 64
SIDE = 4
WIDTH = SIDE * HEAD_DIM
GROUPS = HEADS // SIDE
TOGETHER = 8
HIDDEN = 512
EPSILON = 1e-06
SCALE = HEAD_DIM ** (-0.5)
F32 = jnp.float32
BF16 = jnp.bfloat16
AXES = ("wide", "narrow")
G1, B1, QB, VB, OB, G2, B2, DB = range(8)


def params(**more):
    return pltpu.CompilerParams(vmem_limit_bytes=60 * 1024 * 1024, **more)


def mm(left, right):
    return jnp.dot(left, right, preferred_element_type=F32)


def mm_t(left, right):
    return lax.dot_general(left, right, (((1,), (1,)), ((), ())), preferred_element_type=F32)


def t_mm(left, right):
    return lax.dot_general(left, right, (((0,), (0,)), ((), ())), preferred_element_type=F32)


def norm_parts(values):
    mean = jnp.mean(values, axis=-1, keepdims=True)
    centred = values - mean
    spread = jnp.mean(centred * centred, axis=-1, keepdims=True)
    scale = lax.rsqrt(spread + EPSILON)
    return centred * scale, scale


def norm_back(grad, gain, normed, scale):
    pulled = grad * gain
    inner = jnp.mean(pulled * normed, axis=-1, keepdims=True)
    return scale * (pulled - jnp.mean(pulled, axis=-1, keepdims=True) - normed * inner)


def sum_rows(values):
    return jnp.sum(values, axis=0, keepdims=True)


def load_wide(ref, rows=slice(None)):
    return jnp.concatenate([ref[k, rows, :] for k in range(D // 128)], axis=1)


def store_wide(ref, rows, values):
    for k in range(D // 128):
        ref[k, rows, :] = values[:, k * 128 : (k + 1) * 128]


def heads_apart(block):
    lane = lax.broadcasted_iota(jnp.int32, block.shape, 1) // HEAD_DIM
    zero = jnp.zeros_like(block)
    return jnp.concatenate([jnp.where(lane == h, block, zero) for h in range(SIDE)], axis=0)


def heads_together(product):
    lane = lax.broadcasted_iota(jnp.int32, (HEAD_DIM, WIDTH), 1) // HEAD_DIM
    out = jnp.zeros((HEAD_DIM, WIDTH), F32)
    for h in range(SIDE):
        out = jnp.where(lane == h, product[h * HEAD_DIM : (h + 1) * HEAD_DIM], out)
    return out


def picked(order, first=0, count=PATCHES):
    lane = lax.broadcasted_iota(jnp.int32, (1, PAD), 1)
    order = jnp.where(lane < VIS, order, -1)
    row = lax.broadcasted_iota(jnp.int32, (count, PAD), 0) + first
    return jnp.where(row == order, 1.0, 0.0).astype(BF16)


LINE = 4
BLOCK = 128
CHUNK = 1024
CHUNKS = 3
MESH = pl.DeviceIdType.MESH


def place():
    wide, narrow = lax.axis_index("wide"), lax.axis_index("narrow")
    return lax.shift_right_logical(wide, 1), wide & 1, lax.shift_right_logical(narrow, 1), narrow & 1


def device(z, y, x, c):
    return (2 * z + y, 2 * x + c)


def at_step(step, plan, run):
    keys = sorted(plan)
    if len(keys) <= 2:
        for key in keys:
            pl.when(step == key)(functools.partial(run, plan[key]))
        return
    middle = keys[len(keys) // 2]
    low = {key: plan[key] for key in keys if key < middle}
    high = {key: plan[key] for key in keys if key >= middle}
    pl.when(step < middle)(lambda: at_step(step, low, run))
    pl.when(step >= middle)(lambda: at_step(step, high, run))


def of_three(i, size):
    group = (i >= size).astype(jnp.int32) + (i >= 2 * size).astype(jnp.int32)
    return group, i - group * size


def greet():
    z, y, x, c = place()
    barrier = pltpu.get_barrier_semaphore()
    peers = [device((z + k) & (LINE - 1), y, x, c) for k in range(1, LINE)]
    peers += [device(z, 1 - y, x, c), device(z, y, 1 - x, c), device(z, y, x, 1 - c), device(z, 1 - y, 1 - x, c)]
    for peer in peers:
        pl.semaphore_signal(barrier, inc=1, device_id=peer, device_id_type=MESH)
    pl.semaphore_wait(barrier, len(peers))


def remote(src, dst, send, recv, peer):
    return pltpu.make_async_remote_copy(
        src_ref=src, dst_ref=dst, send_sem=send, recv_sem=recv, device_id=peer, device_id_type=MESH
    )


class Gather:
    COPIES = 4

    def __init__(self, src, slot, x_first, halves, span, send, recv, own, direct=False):
        self.direct, self.span = direct, span
        self.src, self.slot, self.x_first, self.halves = src, slot, x_first, halves
        self.send, self.recv, self.own = send, recv, own
        self.z, self.y, self.x, self.c = place()

    def flip(self, z, first, second):
        y, x = self.y, self.x
        if first if self.x_first else second:
            x = 1 - x
        if second if self.x_first else first:
            y = 1 - y
        return z, y, x

    def line(self, k):
        return (self.z - k) & (LINE - 1)

    def copy(self, at, src, dst, peer):
        return remote(src, dst, self.send.at[at], self.recv.at[at], peer)

    def to_z(self, k):
        peer = device((self.z + k) & (LINE - 1), self.y, self.x, self.c)
        return self.copy(0, self.src, self.slot(self.z, self.y, self.x), peer)

    def to_first(self, k):
        slot = self.slot(self.line(k), self.y, self.x)
        peer = device(*self.flip(self.z, True, False), self.c)
        return self.copy(1, self.src if k == 0 else slot, slot, peer)

    def to_second(self, k):
        slot = self.slot(self.line(k), self.y, self.x)
        peer = device(*self.flip(self.z, False, True), self.c)
        return self.copy(2, self.src if k == 0 else slot, slot, peer)

    def on_to_second(self, k):
        slot = self.slot(*self.flip(self.line(k), True, False))
        peer = device(*self.flip(self.z, False, True), self.c)
        return self.copy(2, slot, slot, peer)

    def to_both(self, k):
        slot = self.slot(self.line(k), self.y, self.x)
        peer = device(*self.flip(self.z, True, True), self.c)
        return self.copy(2, self.src if k == 0 else slot, slot, peer)

    def to_core(self, j):
        part = self.halves(self.c)[j]
        return self.copy(3, part, part, device(self.z, self.y, self.x, 1 - self.c))

    def keep(self):
        return pltpu.make_async_copy(self.src, self.slot(self.z, self.y, self.x), self.own)

    def all_of(self, at, count):
        span = self.span(count)
        return self.copy(at, span, span, device(self.z, self.y, self.x, 1 - self.c))

    def start(self):
        self.keep().start()
        for k in range(1, LINE):
            self.to_z(k).start()
        self.to_first(0).start()
        self.to_second(0).start()
        if self.direct:
            self.to_both(0).start()

    def first(self):
        self.all_of(0, LINE - 1).wait_recv()
        for k in range(1, LINE):
            self.to_first(k).start()
            self.to_second(k).start()
            if self.direct:
                self.to_both(k).start()

    def second(self):
        self.all_of(1, LINE).wait_recv()
        for k in range(LINE):
            if not self.direct:
                self.on_to_second(k).start()

    def core(self):
        self.all_of(2, 2 * LINE).wait_recv()
        self.keep().wait()
        for j in range(len(self.halves(self.c))):
            self.to_core(j).start()

    def finish(self):
        held = len(self.halves(self.c)) > 0
        if held:
            self.all_of(3, 4 * LINE).wait_recv()
        self.all_of(0, LINE - 1).wait_send()
        self.all_of(1, LINE).wait_send()
        self.all_of(2, 2 * LINE).wait_send()
        if held:
            self.all_of(3, 4 * LINE).wait_send()


class Sum:
    COPIES = 4

    def __init__(self, take, own, theirs, ways, line, boxes, send, recv, near):
        self.take, self.own, self.theirs, self.ways, self.line, self.boxes = take, own, theirs, ways, line, boxes
        self.send, self.recv, self.near = send, recv, near
        self.z, self.y, self.x, self.c = place()

    def copy(self, at, src, dst, peer):
        return remote(src, dst, self.send.at[at], self.recv.at[at], device(*peer))

    def loads(self):
        return [pltpu.make_async_copy(src, dst, self.near.at[0]) for src, dst in self.take(self.c, self.own)]

    def to_core(self):
        peer = (self.z, self.y, self.x, 1 - self.c)
        return [self.copy(3, src, dst, peer) for src, dst in self.take(1 - self.c, self.theirs)]

    def out(self, turn):
        goes, _, x_way = self.ways[turn]
        peer = (self.z, self.y, 1 - self.x, self.c) if x_way else (self.z, 1 - self.y, self.x, self.c)
        return self.copy(turn, goes, self.boxes[turn], peer)

    def to_z(self, k):
        to = (self.z + k) & (LINE - 1)
        return self.copy(2, self.line(to), self.boxes[2].at[k - 1], (to, self.y, self.x, self.c))

    def all_loads(self):
        return pltpu.make_async_copy(self.own, self.own, self.near.at[0])

    def all_core(self):
        return self.copy(3, self.theirs, self.theirs, (self.z, self.y, self.x, 1 - self.c))

    def all_z(self):
        return self.copy(2, self.boxes[2], self.boxes[2], (self.z, self.y, self.x, 1 - self.c))

    def load(self):
        for one in self.loads() + self.to_core():
            one.start()

    def first(self):
        self.all_loads().wait()
        self.all_core().wait_recv()
        self.own[...] = self.own[...] + self.theirs[...]
        self.out(0).start()

    def second(self):
        self.out(0).wait_recv()
        stays = self.ways[0][1]
        stays[...] = stays[...] + self.boxes[0][...]
        self.out(1).start()

    def settle(self):
        self.out(1).wait_recv()
        stays = self.ways[1][1]
        stays[...] = stays[...] + self.boxes[1][...]

    def third(self):
        self.settle()
        for k in range(1, LINE):
            self.to_z(k).start()

    def total(self):
        self.all_z().wait_recv()
        out = self.line(self.z)[...].astype(F32)
        for k in range(LINE - 1):
            out = out + self.boxes[2][k].astype(F32)
        self.all_z().wait_send()
        self.left()
        return out

    def left(self):
        for one in (self.all_core(), self.out(0), self.out(1)):
            one.wait_send()


class DepthFirstSum(Sum):
    def to_z(self, k):
        to = (self.z + k) & (LINE - 1)
        return self.copy(2, self.own.at[to], self.boxes[0].at[k - 1], (to, self.y, self.x, self.c))

    def all_z(self):
        return self.copy(2, self.boxes[0], self.boxes[0], (self.z, self.y, self.x, 1 - self.c))

    def to_y(self):
        return self.copy(0, self.own.at[self.z, 1 - self.y], self.boxes[1], (self.z, 1 - self.y, self.x, self.c))

    def to_x(self):
        return self.copy(1, self.own.at[self.z, self.y, 1 - self.x], self.boxes[2], (self.z, self.y, 1 - self.x, self.c))

    def first(self):
        self.all_loads().wait()
        self.all_core().wait_recv()
        self.own[...] = self.own[...] + self.theirs[...]
        for k in range(1, LINE):
            self.to_z(k).start()

    def second(self):
        self.all_z().wait_recv()
        total = self.own[self.z].astype(F32)
        for k in range(LINE - 1):
            total = total + self.boxes[0][k].astype(F32)
        self.own[self.z] = total.astype(BF16)
        self.to_y().start()

    def third(self):
        self.to_y().wait_recv()
        self.own[self.z, self.y] = self.own[self.z, self.y] + self.boxes[1][...]
        self.to_x().start()

    def total(self):
        self.to_x().wait_recv()
        for one in (self.all_z(), self.all_core(), self.to_y(), self.to_x()):
            one.wait_send()
        return self.own[self.z, self.y, self.x].astype(F32) + self.boxes[2][...].astype(F32)


class LineSum(Sum):
    def load(self):
        self.loads()[0].start()

    def third(self):
        self.loads()[0].wait()
        for k in range(1, LINE):
            self.to_z(k).start()

    def left(self):
        pass


def rows_of(start, size, extent=None):
    return pl.ds(pl.multiple_of(start, size), size if extent is None else extent)


PICK_PARTS = 2
PICK_ROWS = PATCHES // PICK_PARTS


def pick_step(part, order_ref, patches_ref, out_ref, at, wide_ref):
    values = patches_ref[...].astype(F32).reshape(PICK_ROWS * TOGETHER, D)
    store_wide(wide_ref, slice(0, PICK_ROWS * TOGETHER), values)
    for j in range(TOGETHER):
        hot = picked(order_ref[j : j + 1, :PAD], part * PICK_ROWS, PICK_ROWS)
        own = load_wide(wide_ref, pl.ds(j, PICK_ROWS, stride=TOGETHER)).astype(BF16)
        rows = pl.ds(pl.multiple_of(at + j * PAD, PAD), PAD)
        value = t_mm(hot, own)
        out_ref[rows, :] = jnp.where(part == 0, value, value + out_ref[rows, :].astype(F32)).astype(BF16)


def pick_in(images):
    blocks = images // TOGETHER
    last = PICK_PARTS * blocks - 1
    index = lambda i: (lax.shift_right_logical(jnp.minimum(i, last), 1), 0)
    place_of = lambda i: (jnp.minimum(i, last) & 1, index(i)[0], 0)
    return [pl.BlockSpec((TOGETHER, PATCHES), index), pl.BlockSpec((PICK_ROWS, TOGETHER, D), place_of)]


def pick_kernel(order_ref, patches_ref, out_ref, wide_ref):
    pick_step(pl.program_id(0) % PICK_PARTS, order_ref, patches_ref, out_ref, 0, wide_ref)


def pick(order, patches):
    images = order.shape[0]
    return pl.pallas_call(
        pick_kernel,
        grid=(images // TOGETHER * PICK_PARTS,),
        in_specs=pick_in(images),
        out_specs=pl.BlockSpec((TOGETHER * PAD, D), lambda i: (i // PICK_PARTS, 0)),
        out_shape=jax.ShapeDtypeStruct((images * PAD, D), BF16),
        scratch_shapes=[pltpu.VMEM((D // 128, PICK_ROWS * TOGETHER, 128), F32)],
        compiler_params=params(),
        name="pick",
    )(order, patches)


HALF = 384
OWN = 24
PIECES = 3
SHARE = 4 * HALF + BLOCK


def parts_of_groups(block, g):
    return [block[:, k * D + g * WIDTH : k * D + (g + 1) * WIDTH] for k in range(3)]


def chip_row(z, y, x):
    return rows_of(((2 * z + y) * 2 + x) * 2 * OWN, 2 * OWN)


def share_out(in_ref, out_ref, vector_refs, share_ref):
    lines = [ref[...].astype(F32) for ref in vector_refs]
    lines = lines[:8] + [lines[8][:, k * OWN : (k + 1) * OWN] for k in range(4)]
    vectors = jnp.concatenate(lines, axis=0).astype(BF16)
    row = lax.broadcasted_iota(jnp.int32, (vectors.shape[0], BLOCK), 0)
    lane = lax.broadcasted_iota(jnp.int32, (vectors.shape[0], BLOCK), 1)
    columns = t_mm(vectors, jnp.where(row == lane, 1.0, 0.0).astype(BF16)).astype(BF16)
    share_ref[...] = jnp.zeros_like(share_ref)
    for g in range(GROUPS):
        both = jnp.concatenate(parts_of_groups(in_ref, g), axis=1)
        for h in range(2):
            share_ref[h, :OWN, g * HALF : (g + 1) * HALF] = both[:, h * HALF : (h + 1) * HALF]
    for h in range(2):
        share_ref[h, :OWN, 3 * HALF : 4 * HALF] = out_ref[:, h * HALF : (h + 1) * HALF]
        share_ref[h, :OWN, 4 * HALF :] = columns


def both_rows(mine, theirs):
    c = place()[3]
    mine, theirs = mine.astype(F32)[:OWN], theirs.astype(F32)[:OWN]
    top, low = jnp.where(c == 0, mine, theirs), jnp.where(c == 0, theirs, mine)
    return jnp.concatenate([top, low], axis=0).astype(BF16)


def hidden_bias(columns, out_ref):
    rows = 4 * OWN
    row = lax.broadcasted_iota(jnp.int32, (rows, 4 * rows * 4), 0)
    lane = lax.broadcasted_iota(jnp.int32, (rows, 4 * rows * 4), 1)
    which, hidden = lane // (4 * rows), lane % (4 * rows)
    hot = jnp.where(hidden == (row // OWN) * (4 * OWN) + which * OWN + row % OWN, 1.0, 0.0).astype(BF16)
    take = lax.broadcasted_iota(jnp.int32, (16, 4 * rows * 4), 0) == 8 + lane[:1] // (4 * rows)
    for w in range(2 * LINE):
        spread = t_mm(columns[w * rows : (w + 1) * rows, :16], hot)
        line = sum_rows(jnp.where(take, spread, 0.0))
        own = sum(line[:, k * 4 * rows : (k + 1) * 4 * rows] for k in range(4))
        for s in range(CHUNKS):
            at = s * CHUNK + (w % 2) * HIDDEN + (w // 2) * BLOCK
            out_ref[:, at : at + BLOCK] = own[:, s * BLOCK : (s + 1) * BLOCK]


def scores_of(k4, q_apart):
    return mm_t(k4, q_apart) * SCALE


BLOCKS = 3


def low_one(x, vec_ref):
    normed, _ = norm_parts(x.astype(F32))
    return (normed * vec_ref[G1 : G1 + 1, :] + vec_ref[B1 : B1 + 1, :]).astype(BF16)


def attend_step(g, low, wi, vec_ref, mixed_ref, total_ref, att, at):
    cols = rows_of(g * WIDTH, WIDTH)
    product = mm(low, wi[...])
    mixed_ref[:, :WIDTH] = (product[:, :WIDTH] + vec_ref[QB : QB + 1, cols]).astype(BF16)
    mixed_ref[:, WIDTH : 2 * WIDTH] = product[:, WIDTH : 2 * WIDTH].astype(BF16)
    mixed_ref[:, 2 * WIDTH :] = (product[:, 2 * WIDTH :] + vec_ref[VB : VB + 1, cols]).astype(BF16)
    images = range(TOGETHER)
    rows = [slice(img * PAD, (img + 1) * PAD) for img in images]
    real = lax.broadcasted_iota(jnp.int32, (PAD, WIDTH), 0) < VIS
    scores = [
        scores_of(mixed_ref[r, WIDTH : 2 * WIDTH], heads_apart(mixed_ref[r, :WIDTH])) for r in rows
    ]
    weights = []
    for img in images:
        own = jnp.where(real, scores[img], -1e30)
        top = jnp.max(own, axis=0, keepdims=True)
        raised = jnp.exp(own - top)
        total = sum_rows(raised)
        weights.append((raised * (1.0 / total)).astype(BF16))
        total_ref[0, img // SIDE, img % SIDE : img % SIDE + 1, :] = top + jnp.log(total)
    for img in images:
        value = heads_together(t_mm(weights[img], mixed_ref[rows[img], 2 * WIDTH :]))
        att[pl.ds(pl.multiple_of(at + img * PAD, PAD), PAD), cols] = value.astype(BF16)


def attend_kernel(x_ref, wi_ref, vec_ref, mixed_ref, att_ref, total_ref, low):
    step = pl.program_id(0)
    g, b = step // BLOCKS, step % BLOCKS
    at = b * (TOGETHER * PAD)
    rows = rows_of(at, TOGETHER * PAD)

    @pl.when(g == 0)
    def _():
        low[rows, :] = low_one(x_ref[rows, :], vec_ref)

    attend_step(g, low[rows, :], wi_ref.at[0], vec_ref, mixed_ref, total_ref, att_ref, at)


def full(*shape):
    return pl.BlockSpec(shape, lambda i: (0,) * len(shape))


def whole(a):
    return full(*a.shape)


def by_group(*block, lead=0, blocks=BLOCKS):
    def index(i):
        g, b = of_three(jnp.minimum(jnp.maximum(i - lead, 0), GROUPS * blocks - 1), blocks)
        return (g, b, 0, 0) if len(block) == 4 else (b, g)

    return pl.BlockSpec(block, index)


def TOTALS(lead):
    return by_group(1, TOGETHER // SIDE, 8, WIDTH, lead=lead)


def totals_shape(rows):
    return jax.ShapeDtypeStruct((GROUPS, rows // (SIDE * PAD), 8, WIDTH), F32)


def attend(x, wi, vec):
    rows = x.shape[0]
    block = TOGETHER * PAD
    shape = jax.ShapeDtypeStruct
    return pl.pallas_call(
        attend_kernel,
        grid=(GROUPS * BLOCKS,),
        in_specs=[whole(x), pl.BlockSpec((1, D, D), lambda i: (i // BLOCKS, 0, 0)), whole(vec)],
        out_specs=[by_group(block, D), full(rows, D), TOTALS(0)],
        out_shape=[
            shape((rows, 3 * D), BF16), shape((rows, D), BF16), totals_shape(rows),
        ],
        scratch_shapes=[pltpu.VMEM((rows, D), BF16)],
        compiler_params=params(),
        name="attend",
    )(x, wi, vec)


def gelu_both(x):
    bell = jnp.exp(-0.5 * x * x) * 0.3989422804014327
    below = 0.5 * (1.0 + lax.erf(x * 0.7071067811865476))
    return x * below, below + x * bell


def feed_early(cot_ref, sums_ref, middle, low, grad, low_t, grad_t, feed, back, act, inner):
    rows, held = cot_ref.shape[0], grad.shape[0]
    grad[:rows, :] = cot_ref[...]
    grad[rows:, :] = jnp.zeros((held - rows, D), BF16)
    sums_ref[DB : DB + 1, :] = sum_rows(cot_ref[...].astype(F32))
    grad_t[:, held:] = jnp.zeros((D, grad_t.shape[1] - held), BF16)
    grad_t[:, :held] = grad[...].T


def feed_start(x_ref, att_ref, cot_ref, wo_ref, vec_ref, sums_ref, middle, low, grad, low_t, grad_t, feed, back, act, inner):
    rows = cot_ref.shape[0]
    images = rows // VIS
    held = middle.shape[1]
    feed[...] = jnp.zeros_like(feed)
    back[...] = jnp.zeros_like(back)
    act[held:, :] = jnp.zeros((act.shape[0] - held, HIDDEN), BF16)
    inner[held:, :] = jnp.zeros((act.shape[0] - held, HIDDEN), BF16)
    middle[:, rows:, :] = jnp.zeros((D // 128, held - rows, 128), F32)
    for g in range(images // TOGETHER):
        at = slice(g * TOGETHER * PAD, (g + 1) * TOGETHER * PAD)
        branch = mm(att_ref[at, :], wo_ref[...]) + vec_ref[OB : OB + 1, :]
        mid = x_ref[at, :].astype(F32) + branch
        for j in range(TOGETHER):
            token = pl.ds(g * TOGETHER + j, VIS, stride=images)
            store_wide(middle, token, mid[j * PAD : j * PAD + VIS])
    normed, _ = norm_parts(load_wide(middle))
    low[...] = (normed * vec_ref[G2 : G2 + 1, :] + vec_ref[B2 : B2 + 1, :]).astype(BF16)
    low_t[:, held:] = jnp.zeros((D, low_t.shape[1] - held), BF16)
    low_t[:, :held] = low[...].T


def feed_step(up, upb, down, upbg_ref, middle, low, grad, low_t, grad_t, feed, back, act, inner):
    held = low.shape[0]
    before = mm(low[...], up[...]) + upb
    hidden_grad = mm(grad[...], down[...])
    value, slope = gelu_both(before)
    act[:held, :] = value.astype(BF16)
    before_grad = (hidden_grad * slope).astype(BF16)
    inner[:held, :] = before_grad
    upbg_ref[...] = sum_rows(before_grad.astype(F32))
    feed[...] += mm_t(act[:held, :], down[...])
    back[...] += mm_t(inner[:held, :], up[...])


def feed_grads(upg_ref, downg_ref, middle, low, grad, low_t, grad_t, feed, back, act, inner):
    downg_ref[...] = mm(grad_t[...], act[...]).astype(BF16)
    upg_ref[...] = mm(low_t[...], inner[...]).astype(BF16)


def feed_end(
    vec_ref, result_ref, mg_ref, sums_ref, middle, low, grad, low_t, grad_t, feed, back, act, inner, ready=lambda k: None
):
    rows = result_ref.shape[0]
    images = rows // VIS
    held = low.shape[0]
    mid = load_wide(middle)
    result = feed[...] + mid + vec_ref[DB : DB + 1, :]
    result_ref[...] = result[:rows].astype(BF16)
    ready(0)
    normed, scale = norm_parts(mid)
    pull = back[...]
    sums_ref[G2 : G2 + 1, :] = sum_rows(pull * normed)
    sums_ref[B2 : B2 + 1, :] = sum_rows(pull)
    mid_grad = grad[...].astype(F32) + norm_back(pull, vec_ref[G2 : G2 + 1, :], normed, scale)
    real = lax.broadcasted_iota(jnp.int32, (held, 1), 0) < rows
    mid_grad = jnp.where(real, mid_grad, 0.0)
    sums_ref[OB : OB + 1, :] = sum_rows(mid_grad.astype(BF16).astype(F32))
    store_wide(middle, slice(None), mid_grad)
    for j in range(images):
        out = j * PAD
        token = pl.ds(j, VIS, stride=images)
        own = jnp.concatenate([load_wide(middle, token), jnp.zeros((PAD - VIS, D), F32)], axis=0)
        mg_ref[out : out + PAD, :] = own.astype(BF16)
        if j % TOGETHER == TOGETHER - 1:
            ready(1 + j // TOGETHER)


def feed_scratch(rows):
    held = -(-rows // 32) * 32
    deep = -(-rows // 256) * 256
    return [
        pltpu.VMEM((D // 128, held, 128), F32),
        pltpu.VMEM((held, D), BF16),
        pltpu.VMEM((held, D), BF16),
        pltpu.VMEM((D, deep), BF16),
        pltpu.VMEM((D, deep), BF16),
        pltpu.VMEM((held, D), F32),
        pltpu.VMEM((held, D), F32),
        pltpu.VMEM((deep, HIDDEN), BF16),
        pltpu.VMEM((deep, HIDDEN), BF16),
    ]


def feed_kernel(
    x_ref, att_ref, cot_ref, wo_ref, vec_ref, up_ref, upb_ref, down_ref,
    result_ref, mg_ref, upg_ref, downg_ref, upbg_ref, sums_ref, *scratch,
):
    step = pl.program_id(0)

    @pl.when(step == 0)
    def _():
        feed_early(cot_ref, sums_ref, *scratch)
        feed_start(x_ref, att_ref, cot_ref, wo_ref, vec_ref, sums_ref, *scratch)

    feed_step(up_ref, upb_ref[...], down_ref, upbg_ref, *scratch)
    feed_grads(upg_ref, downg_ref, *scratch)

    @pl.when(step == pl.num_programs(0) - 1)
    def _():
        feed_end(vec_ref, result_ref, mg_ref, sums_ref, *scratch)


def feed_forward(x, att, cot, wo, vec, up, upb, down):
    rows = cot.shape[0]
    ff = up.shape[1]
    hid = lambda r: pl.BlockSpec((r, HIDDEN), lambda i: (0, i))
    return pl.pallas_call(
        feed_kernel,
        grid=(ff // HIDDEN,),
        in_specs=[whole(x), whole(att), whole(cot), whole(wo), whole(vec), hid(D), hid(1), hid(D)],
        out_specs=[whole(cot), full(x.shape[0], D), hid(D), hid(D), hid(1), full(8, D)],
        out_shape=[
            jax.ShapeDtypeStruct(cot.shape, BF16),
            jax.ShapeDtypeStruct((x.shape[0], D), BF16),
            jax.ShapeDtypeStruct((D, ff), BF16),
            jax.ShapeDtypeStruct((D, ff), BF16),
            jax.ShapeDtypeStruct((1, ff), F32),
            jax.ShapeDtypeStruct((8, D), F32),
        ],
        scratch_shapes=feed_scratch(rows),
        compiler_params=params(),
        name="feed_forward",
    )(x, att, cot, wo, vec, up, upb, down)


FORWARD = {
    0: [("start", "v"), ("start", "g0"), ("start", "g1"), ("start", "g2"), ("start", "out")],
    3: [("first", "v")],
    4: [("first", "g0"), ("start", "d0"), ("start", "u0")],
    5: [("second", "v")],
    6: [("core", "v"), ("finish", "v")],
    7: [("first", "g2")],
    8: [("first", "out")],
    9: [("second", "g1"), ("core", "g1"), ("finish", "g1"), ("second", "g2"), ("first", "d0"), ("first", "u0")],
    10: [("start", "u1"), ("start", "d1")],
    11: [("second", "out"), ("core", "g2")],
    12: [("finish", "g2"), ("start", "u2")],
    14: [("second", "d0"), ("second", "u0"), ("start", "d2")],
    15: [("core", "out"), ("first", "u1"), ("first", "d1"), ("finish", "out")],
    16: [("first", "d2")],
    17: [("load", "su"), ("load", "sd"), ("finish", "u1"), ("finish", "d1"), ("second", "u2")],
    19: [("finish", "u2"), ("finish", "d2")],
}
MIDDLE = {
    15: [("second", "u1"), ("second", "d1"), ("first", "u2")],
    16: [("core", "u1"), ("core", "d1")],
    17: [("second", "d2"), ("first", "su"), ("first", "sd")],
    18: [("core", "u2"), ("core", "d2")],
    19: [("second", "su"), ("second", "sd")],
}
BEFORE_ATTENTION = [("first", "g1"), ("second", "g0"), ("core", "g0"), ("finish", "g0")]
BEFORE_FEED = [("core", "d0"), ("core", "u0"), ("finish", "d0"), ("finish", "u0")]
LAST_FORWARD = [("settle", "su"), ("settle", "sd")]


def forward_kernel(
    order_ref, patches_ref, in_ref, out_ref, cot_in, up_own, down_own, *refs,
):
    vector_refs, refs = refs[:9], refs[9:]
    (
    x_out, mixed_ref, total_ref, att_out, result_out, mg_out, upg_ref, downg_ref, upbg_ref, sums_ref, vec_ref, wi_ref, wo_ref,
    upf_ref, downf_ref, result_ref, mg_ref, cot_ref, x_ref, att_ref, share_ref, other, piece, columns, upb, wi_all, wo_all, up_all, down_all, send, recv, own, near, *scratch,
    ) = refs
    step = pl.program_id(0)
    picks = x_ref.shape[0] // (TOGETHER * PAD) * PICK_PARTS
    early = picks + GROUPS * BLOCKS
    last = pl.num_programs(0) - 1
    z, y, x, c = place()
    features = D // 4
    feed_parts, sum_parts = scratch[:9], scratch[9:]
    middle = feed_parts[0]
    low_all = mg_ref
    swap = remote(share_ref.at[1 - c], other, near.at[0], near.at[1], device(z, y, x, 1 - c))

    def weight(j, src, dst, s, x_first):
        def slot(z, y, x):
            rows = rows_of((2 * x + c) * features, features)
            return dst.at[rows, rows_of(s * CHUNK + y * HIDDEN + z * BLOCK, BLOCK)]

        def halves(c):
            return [dst.at[rows_of((2 * k + c) * features, features), pl.ds(s * CHUNK, CHUNK)] for k in range(2)]

        block = src.at[:, pl.ds(s * BLOCK, BLOCK)]
        def span(count):
            rows, count = (features, count) if count <= 8 else (2 * features, count // 2)
            return dst.at[pl.ds(0, rows), pl.ds(0, count * BLOCK)]

        return Gather(block, slot, x_first, halves, span, send.at[j], recv.at[j], own.at[j])

    def square(j, k, dst, x_first, start=0, width=HALF, direct=False):
        lanes = lambda c: rows_of(c * HALF + start, BLOCK, width)
        slot = lambda z, y, x: dst.at[chip_row(z, y, x), lanes(c)]
        halves = lambda c: [dst.at[:, lanes(c)]]
        block = piece.at[:, pl.ds(k * HALF + start, width)]
        span = lambda count: dst.at[pl.ds(0, count * 2 * OWN), pl.ds(0, width)]
        return Gather(block, slot, x_first, halves, span, send.at[j], recv.at[j], own.at[j], direct)

    items = {}
    for s in range(CHUNKS):
        items[f"u{s}"] = [weight(2 * s, up_own, up_all, s, True)]
        items[f"d{s}"] = [weight(2 * s + 1, down_own, down_all, s, False)]
    j = 2 * CHUNKS
    slot = lambda z, y, x: columns.at[chip_row(z, y, x)]
    span = lambda count: columns.at[pl.ds(0, count * 2 * OWN)]
    items["v"] = [Gather(piece.at[:, pl.ds(4 * HALF, BLOCK)], slot, True, lambda c: [], span, send.at[j], recv.at[j], own.at[j], True)]
    items["g0"] = [square(j + 1, 0, wi_all.at[0], True, direct=True)]
    items["g1"] = [square(j + 3, 1, wi_all.at[1], True, direct=True)]
    items["g2"] = [square(j + 4, 2, wi_all.at[2], False)]
    items["out"] = [square(j + 5, 3, wo_all, True)]
    for name, one in zip(("su", "sd"), feed_sums((up_all, down_all), [0], *sum_parts)[0]):
        items[name] = [one]
    copies = [
        pltpu.make_async_copy(wi_all, wi_ref, near.at[2]),
        pltpu.make_async_copy(wo_all, wo_ref, near.at[3]),
        pltpu.make_async_copy(x_ref, x_out, near.at[2 + 2 * CHUNKS]),
        pltpu.make_async_copy(att_ref, att_out, near.at[3 + 2 * CHUNKS]),
    ]
    moves = []
    kept = CHUNK // HIDDEN
    for k in range(kept, CHUNKS * kept):
        lanes, dst = pl.ds(k * HIDDEN, HIDDEN), pl.ds((k - kept) * HIDDEN, HIDDEN)
        moves.append(pltpu.make_async_copy(up_all.at[:, lanes], upg_ref.at[:, dst], near.at[10 + 2 * (k - kept)]))
        moves.append(pltpu.make_async_copy(down_all.at[:, lanes], downg_ref.at[:, dst], near.at[11 + 2 * (k - kept)]))

    bring = pltpu.make_async_copy(cot_in, cot_ref, near.at[2])

    @pl.when(step == 0)
    def _():
        bring.start()
        share_out(in_ref, out_ref, vector_refs, share_ref)
        greet()
        swap.start()
        swap.wait()
        piece[...] = both_rows(share_ref[c], other[...])

    def run(acts):
        for act, which in acts:
            for one in items[which]:
                getattr(one, act)()

    at_step(step, FORWARD, run)

    lines = rows_of(y * HIDDEN, HIDDEN)
    for j, ref in enumerate((upf_ref, downf_ref)):
        copies.append(pltpu.make_async_copy(sum_parts[0].at[j, x, :, lines], ref, near.at[18 + j]))


    @pl.when(step < picks)
    def _():
        block = lax.shift_right_logical(step, 1)
        pick_step(step & 1, order_ref, patches_ref, x_ref, block * (TOGETHER * PAD), middle)

    @pl.when(step == picks - 1)
    def _():
        bring.wait()
        feed_early(cot_ref, sums_ref, *feed_parts)

    @pl.when(step == picks)
    def _():
        copies[2].start()
        vec_ref[...] = columns[...].astype(F32).T[:16]
        hidden_bias(columns[...], upb)
        for k in range(BLOCKS):
            block = slice(k * TOGETHER * PAD, (k + 1) * TOGETHER * PAD)
            low_all[block, :] = low_one(x_ref[block, :], vec_ref)
        run(BEFORE_ATTENTION)

    g, b = of_three(jnp.minimum(jnp.maximum(step - picks, 0), GROUPS * BLOCKS - 1), BLOCKS)
    at = b * (TOGETHER * PAD)
    rows = rows_of(at, TOGETHER * PAD)

    @pl.when((step >= picks) & (step < early))
    def _():
        attend_step(g, low_all[rows, :], wi_all.at[g], vec_ref, mixed_ref, total_ref, att_ref, at)

    @pl.when(step == early)
    def _():
        for k in (0, 1, 3):
            copies[k].start()
        feed_start(x_ref, att_ref, cot_ref, wo_all, vec_ref, sums_ref, *feed_parts)

    late = jnp.maximum(step - early, 0)
    lanes = rows_of(late * HIDDEN, HIDDEN)

    @pl.when(step == early)
    def _():
        run(BEFORE_FEED)

    @pl.when(step >= early)
    def _():
        feed_step(up_all.at[:, lanes], upb[:, lanes], down_all.at[:, lanes], upbg_ref, *feed_parts)
        at_step(step, MIDDLE, run)
        feed_grads(up_all.at[:, lanes], down_all.at[:, lanes], *feed_parts)

    def move(pair):
        for one in pair:
            one.start()

    at_step(step, {early + kept + k: moves[2 * k : 2 * k + 2] for k in range(len(moves) // 2)}, move)

    @pl.when(step == last)
    def _():
        ends = [pltpu.make_async_copy(result_ref, result_out, near.at[20])]
        for k in range(BLOCKS):
            block = pl.ds(k * TOGETHER * PAD, TOGETHER * PAD)
            ends.append(pltpu.make_async_copy(mg_ref.at[block], mg_out.at[block], near.at[21 + k]))
        feed_end(vec_ref, result_ref, mg_ref, sums_ref, *feed_parts, ready=lambda k: ends[k].start())
        run(LAST_FORWARD)
        for one in copies[4:]:
            one.start()
        for name in ("su", "sd"):
            items[name][0].left()
        for one in copies + moves + ends:
            one.wait()


def forward(order, patches, project_in, project_out, cot, up, down, *vectors):
    images = order.shape[0]
    rows = images * PAD
    block = TOGETHER * PAD
    picks = images // TOGETHER * PICK_PARTS
    early = picks + GROUPS * BLOCKS
    ff = CHUNKS * CHUNK
    late = ff // HIDDEN
    here = pl.BlockSpec(memory_space=pl.ANY)
    shape = jax.ShapeDtypeStruct
    count = 2 * CHUNKS + 6
    done = (D // 4, HIDDEN)
    return pl.pallas_call(
        forward_kernel,
        grid=(early + late,),
        in_specs=pick_in(images) + [whole(project_in), whole(project_out), here, here, here] + [whole(v) for v in vectors],
        out_specs=[
            here, by_group(block, D, lead=picks), TOTALS(picks), here,
            here, here, here, here,
            pl.BlockSpec((1, HIDDEN), lambda i: (0, jnp.maximum(i - early, 0))),
            full(8, D), full(16, D), here, here, here, here,
        ],
        out_shape=[
            shape((rows, D), BF16), shape((rows, 3 * D), BF16), totals_shape(rows), shape((rows, D), BF16),
            shape(cot.shape, BF16), shape((rows, D), BF16), shape((D, ff - CHUNK), BF16), shape((D, ff - CHUNK), BF16),
            shape((1, ff), F32), shape((8, D), F32), shape((16, D), F32),
            shape((GROUPS, D, D), BF16), shape((D, D), BF16), shape(done, BF16), shape(done, BF16),
        ],
        scratch_shapes=[
            pltpu.VMEM(cot.shape, BF16),
            pltpu.VMEM((rows, D), BF16),
            pltpu.VMEM(cot.shape, BF16),
            pltpu.VMEM((rows, D), BF16),
            pltpu.VMEM((rows, D), BF16),
            pltpu.VMEM((2, 32, SHARE), BF16),
            pltpu.VMEM((32, SHARE), BF16),
            pltpu.VMEM((2 * OWN, SHARE), BF16),
            pltpu.VMEM((D, BLOCK), BF16),
            pltpu.VMEM((1, ff), F32),
            pltpu.VMEM((GROUPS, D, D), BF16),
            pltpu.VMEM((D, D), BF16),
            pltpu.VMEM((D, ff), BF16),
            pltpu.VMEM((D, ff), BF16),
            pltpu.SemaphoreType.DMA((count, Gather.COPIES)),
            pltpu.SemaphoreType.DMA((count, Gather.COPIES)),
            pltpu.SemaphoreType.DMA((count,)),
            pltpu.SemaphoreType.DMA((13 + BLOCKS + 2 * (CHUNKS - 1) * (CHUNK // HIDDEN),)),
        ] + feed_scratch(cot.shape[0]) + feed_sum_scratch(1),
        compiler_params=params(collective_id=2, has_side_effects=True),
        name="forward",
    )(order, patches, project_in, project_out, cot, up, down, *vectors)


BACKWARD = {
    0: [("load", 1), ("load", 2), ("load", 0)],
    1: [("first", 1), ("third", 0)],
    2: [("first", 2)],
    3: [("load", "out"), ("load", "g0")],
    4: [("second", 1), ("first", "out"), ("first", "g0")],
    6: [("second", 2), ("load", "g1"), ("total", 0)],
    7: [("third", 1)],
    8: [("first", "g1"), ("second", "out")],
    9: [("second", "g0"), ("load", "g2"), ("load", "v")],
    10: [("first", "g2"), ("first", "v"), ("third", 2), ("total", 1)],
    11: [("third", "out")],
    12: [("load", "late"), ("second", "g1"), ("third", "g0"), ("second", "g2")],
    13: [("first", "late"), ("second", "v"), ("third", "g1")],
    14: [("third", "g2"), ("second", "late"), ("third", "v"), ("total", "out")],
}
LAST = [("total", 2), ("third", "late"), ("total", "g0"), ("total", "g1"), ("total", "g2"), ("total", "v")]
BACK = 3


def unattend_step(mixed_ref, att_grad, totals, grads, g, at):
    real = lax.broadcasted_iota(jnp.int32, (PAD, WIDTH), 0) < VIS
    for first in range(0, TOGETHER, SIDE):
        images = range(first, first + SIDE)
        held = []
        for img in images:
            rows = slice(img * PAD, (img + 1) * PAD)
            q4, k4, v4 = [mixed_ref[rows, k * WIDTH : (k + 1) * WIDTH] for k in range(3)]
            q_apart, a_apart = heads_apart(q4), heads_apart(att_grad[rows, :])
            held.append((k4, q_apart, a_apart, scores_of(k4, q_apart), mm_t(v4, a_apart)))
        ready = []
        for img, (k4, q_apart, a_apart, scores, pulled) in zip(images, held):
            exact = jnp.exp(scores - totals[0, img // SIDE, img % SIDE : img % SIDE + 1, :])
            exact = jnp.where(real, exact, 0.0)
            centre = sum_rows(exact * pulled)
            score_grad = (exact * (pulled - centre)).astype(BF16)
            ready.append((k4, q_apart, a_apart, score_grad, exact.astype(BF16)))
        for img, (k4, q_apart, a_apart, score_grad, weights) in zip(images, ready):
            q_grad = heads_together(t_mm(score_grad, k4)) * SCALE
            k_grad = mm(score_grad, q_apart) * SCALE
            v_grad = mm(weights, a_apart)
            out = pl.ds(pl.multiple_of(at + img * PAD, PAD), PAD)
            grads[g, out, :WIDTH] = q_grad.astype(BF16)
            grads[g, out, WIDTH : 2 * WIDTH] = k_grad.astype(BF16)
            grads[g, out, 2 * WIDTH :] = v_grad.astype(BF16)


def pull_step(x, grads, rows, wi_ref, pull_ref, sums_ref):
    normed, _ = norm_parts(x.astype(F32))
    pull = sum(mm_t(grads[g, rows, :], wi_ref[g]) for g in range(GROUPS))
    sums_ref[G1 : G1 + 1, :] += sum_rows(pull * normed)
    sums_ref[B1 : B1 + 1, :] += sum_rows(pull)
    pull_ref[rows, :] = pull


def unnorm_step(x, mg, pull, vec_ref, ig_ref):
    normed, scale = norm_parts(x.astype(F32))
    ig_ref[...] = (mg.astype(F32) + norm_back(pull, vec_ref[G1 : G1 + 1, :], normed, scale)).astype(BF16)


def backward_kernel(x_in, mg_in, mixed_ref, att_ref, total_ref, wi_in, wo_ref, vec_ref, *refs):
    step = pl.program_id(0)
    walk = GROUPS * BACK
    last = pl.num_programs(0) - 1
    g, b = of_three(jnp.minimum(step, walk - 1), BACK)
    b = jnp.where(step >= walk, jnp.where(step >= walk + BACK, step - walk - BACK, step - walk), b)
    at = b * (TOGETHER * PAD)
    rows = rows_of(at, TOGETHER * PAD)
    x_ref, mg_ref, wi_ref, brought = refs[-4:]
    refs = refs[:-4]
    remote_sums = len(refs) > 12
    brings = [pltpu.make_async_copy(wi_in, wi_ref, brought.at[2 * BACK])]
    for k in range(BACK):
        block = pl.ds(k * TOGETHER * PAD, TOGETHER * PAD)
        brings.insert(2 * k, pltpu.make_async_copy(x_in.at[block], x_ref.at[block], brought.at[2 * k]))
        brings.insert(2 * k + 1, pltpu.make_async_copy(mg_in.at[block], mg_ref.at[block], brought.at[2 * k + 1]))

    @pl.when(step == 0)
    def _():
        for one in brings:
            one.start()
    if remote_sums:
        upg_ref, downg_ref, sums_two_ref, upbg_ref, up_first, down_first = refs[:6]
        refs = refs[2:]
        ig_ref, wi_out, wo_out, vec_out, upf_ref, downf_ref = refs[4:10]
        low_t, att_t, grads, pull, sums_ref, wig_ref, wog_ref, end, other_end, end_send, end_recv = refs[10:21]
        feed_parts, square_parts, early_parts, late_parts, line_parts = refs[21:30], refs[30:38], refs[38:46], refs[46:54], refs[54:59]
        depth_parts = refs[59:]
        z, y, x, c = place()
        items = dict(enumerate(feed_sums((upg_ref, downg_ref), range(1, CHUNKS), *feed_parts), 1))
        for j, name in enumerate(("g0", "g1", "out")):
            src = wog_ref if name == "out" else wig_ref.at[j]
            items[name] = [square_sum(j, j, src, slice(0, HALF), j == 0, *square_parts)]
        plain = items["out"][0]
        items["out"] = [DepthFirstSum(plain.take, plain.own, plain.theirs, None, None, depth_parts, plain.send, plain.recv, plain.near)]
        cuts = [slice(0, 2 * BLOCK), slice(2 * BLOCK, HALF)]
        items["g2"] = [square_sum(3, 3 + j, wig_ref.at[2], cut, j == 0, *square_parts) for j, cut in enumerate(cuts)]
        items[0] = [line_sum(j, src, *line_parts) for j, src in enumerate((up_first, down_first))]
        items["v"] = [vector_sum(*early_parts)]
        items["late"] = [vector_sum(*late_parts)]
        places = {"g0": 0, "g1": 1, "g2": 2, "out": 3}

        def swap(j):
            give = end.at[j, pl.ds(pl.multiple_of((1 - c) * OWN, 8), OWN)]
            return remote(give, other_end.at[j], end_send.at[j], end_recv.at[j], device(z, y, x, 1 - c))

        def act(name, which):
            values = [getattr(one, name)() for one in items[which]]
            if name != "total":
                return
            if which in (0, 1, 2):
                lanes = slice(which * BLOCK, (which + 1) * BLOCK)
                upf_ref[:, lanes], downf_ref[:, lanes] = values
            elif which in places:
                end[places[which]] = jnp.concatenate(values, axis=1)
                swap(places[which]).start()
            else:
                early = which == "v"
                value = jnp.where(c == 0, values[0][:, :OWN], values[0][:, OWN : 2 * OWN])
                if early:
                    vec_out[:6, :OWN] = value[:6]
                    vec_out[6:7, :] = jnp.where(c == 0, values[0][6:7], values[0][7:8])
                else:
                    vec_out[8:, :OWN] = value

        def run(acts):
            for name, which in acts:
                if (name, which) == ("load", "v"):
                    own = [sums_ref[k : k + 1, :] for k in (QB, VB)]
                    own += [sums_two_ref[k : k + 1, :] for k in (OB, G2, B2, DB)]
                    items["v"][0].fill(jnp.concatenate(own, axis=0), upbg_ref)
                if (name, which) == ("load", "late"):
                    items["late"][0].fill(sums_ref[G1 : B1 + 1, :])
                act(name, which)

        @pl.when(step == 0)
        def _():
            greet()

        at_step(step, BACKWARD, run)
    else:
        ig_ref, wi_out, wo_out, sums_ref, low_t, att_t, grads, pull, wig_ref, wog_ref = refs

    @pl.when(step == 0)
    def _():
        sums_ref[...] = jnp.zeros_like(sums_ref)
        if remote_sums:
            vec_out[...] = jnp.zeros_like(vec_out)

    for k in range(BACK):

        @pl.when(step == k)
        def _(k=k):
            brings[2 * k].wait()
            brings[2 * k + 1].wait()

    @pl.when(step == walk)
    def _():
        brings[-1].wait()

    @pl.when(step < BACK)
    def _():
        low_t[:, rows] = low_one(x_ref[rows, :], vec_ref).T
        att_t[:, rows] = att_ref[...].T

    @pl.when(step < walk)
    def _():
        cols = rows_of(g * WIDTH, WIDTH)
        att_grad = mm_t(mg_ref[rows, :], wo_ref[cols, :]).astype(BF16)
        unattend_step(mixed_ref, att_grad, total_ref, grads, g, at)
        own = grads[g, rows, :]
        sums_ref[QB : QB + 1, cols] += sum_rows(own[:, :WIDTH].astype(F32))
        sums_ref[VB : VB + 1, cols] += sum_rows(own[:, 2 * WIDTH :].astype(F32))

    @pl.when(step == BACK - 1)
    def _():
        wog_ref[...] = mm(att_t[...], mg_ref[...]).astype(BF16).reshape(wog_ref.shape)

    @pl.when((b == BACK - 1) & (step < walk))
    def _():
        wig_ref[g] = mm(low_t[...], grads[g]).astype(BF16).reshape(wig_ref.shape[1:])

    @pl.when((step >= walk) & (step < walk + BACK))
    def _():
        pull_step(x_ref[rows, :], grads, rows, wi_ref, pull, sums_ref)

    @pl.when(step >= walk + BACK)
    def _():
        unnorm_step(x_ref[rows, :], mg_ref[rows, :], pull[rows, :], vec_ref, ig_ref)

    @pl.when(step == last)
    def _():
        if not remote_sums:
            wi_out[...] = wig_ref[...].reshape(wi_out.shape)
            wo_out[...] = wog_ref[...].reshape(wo_out.shape)
            return
        for name, which in LAST:
            act(name, which)
        for j in range(PIECES + 1):
            swap(j).wait()
            mine, theirs = end[j, pl.ds(pl.multiple_of(c * OWN, 8), OWN), :], other_end[j]
            both = jnp.concatenate([jnp.where(c == 0, mine, theirs), jnp.where(c == 0, theirs, mine)], axis=1)
            if j < GROUPS:
                for k in range(3):
                    wi_out[:, k * D + j * WIDTH : k * D + (j + 1) * WIDTH] = both[:, k * WIDTH : (k + 1) * WIDTH]
            else:
                wo_out[...] = both
        act("total", "late")


CHIPS = (LINE, 2, 2, 2 * OWN)


def ways_of(mine, x_first):
    z, y, x, c = place()
    if x_first:
        return [(mine.at[:, :, 1 - x], mine.at[:, :, x], True), (mine.at[:, 1 - y, x], mine.at[:, y, x], False)]
    return [(mine.at[:, 1 - y], mine.at[:, y], False), (mine.at[:, y, 1 - x], mine.at[:, y, x], True)]


def square_sum(j, at, src, lanes, x_first, own, theirs, box_one, box_two, box_z, send, recv, near):
    z, y, x, c = place()
    width = lanes.stop - lanes.start

    def take(c, into):
        return [(src.at[:, :, :, :, rows_of(c * HALF + lanes.start, BLOCK, width)], into)]

    lanes = pl.ds(lanes.start, width)
    mine = own.at[j, :, :, :, :, lanes]
    line = lambda to: mine.at[to, y, x]
    boxes = (box_one.at[j, :, :, :, lanes], box_two.at[j, :, :, lanes], box_z.at[j, :, :, lanes])
    return Sum(
        take, mine, theirs.at[j, :, :, :, :, lanes], ways_of(mine, x_first), line, boxes, send.at[at], recv.at[at], near.at[at]
    )


class VectorSum(Sum):
    def fill(self, vectors, hidden=None):
        self.own[...] = jnp.zeros(self.own.shape, F32)
        count, width = vectors.shape[0], 4 * OWN
        for k in range(2 * LINE * 2):
            z, y, x = k // 4, k // 2 % 2, k % 2
            self.own[z, y, x, :count, : 2 * OWN] = vectors[:, k * 2 * OWN : (k + 1) * 2 * OWN]
            if hidden is not None:
                at = [s * CHUNK + y * HIDDEN + z * BLOCK for s in range(CHUNKS)]
                line = jnp.concatenate([hidden[:, a : a + BLOCK] for a in at], axis=1)
                for c in range(2):
                    start = (2 * x + c) * width
                    self.own[z, y, x, 6 + c : 7 + c, :width] = line[:, start : start + width]

    def loads(self):
        return []

    def first(self):
        self.all_core().wait_recv()
        self.all_core().wait_send()
        self.own[...] = self.own[...] + self.theirs[...]
        self.out(0).start()

    def total(self):
        self.all_z().wait_recv()
        out = self.line(self.z)[...]
        for k in range(LINE - 1):
            out = out + self.boxes[2][k]
        for one in (self.out(0), self.out(1), self.all_z()):
            one.wait_send()
        return out


def line_sum(j, src, own, box_z, send, recv, near):
    mine = own.at[j]
    line = lambda to: mine.at[:, rows_of(to * BLOCK, BLOCK)]
    take = lambda c, into: [(src, into)]
    return LineSum(take, mine, mine, None, line, (None, None, box_z.at[j]), send.at[j], recv.at[j], near.at[j])


def line_sum_scratch():
    return [
        pltpu.VMEM((2, D // 4, HIDDEN), BF16),
        pltpu.VMEM((2, LINE - 1, D // 4, BLOCK), BF16),
        pltpu.SemaphoreType.DMA((2, Sum.COPIES)),
        pltpu.SemaphoreType.DMA((2, Sum.COPIES)),
        pltpu.SemaphoreType.DMA((2, 1)),
    ]


def vector_sum(own, theirs, box_one, box_two, box_z, send, recv, near):
    z, y, x, c = place()
    mine = own.at[0]
    line = lambda to: mine.at[to, y, x]
    boxes = (box_one.at[0], box_two.at[0], box_z.at[0])
    return VectorSum(
        lambda c, into: [(mine, into)], mine, theirs.at[0], ways_of(mine, False), line, boxes, send.at[0], recv.at[0], near.at[0]
    )


def square_sum_scratch(count, lanes=HALF, dtype=BF16, rows=2 * OWN, copies=None):
    chips = CHIPS[:3] + (rows,)
    copies = count if copies is None else copies
    return [
        pltpu.VMEM((count,) + chips + (lanes,), dtype),
        pltpu.VMEM((count,) + chips + (lanes,), dtype),
        pltpu.VMEM((count, LINE, 2, rows, lanes), dtype),
        pltpu.VMEM((count, LINE, rows, lanes), dtype),
        pltpu.VMEM((count, LINE - 1, rows, lanes), dtype),
        pltpu.SemaphoreType.DMA((copies, Sum.COPIES)),
        pltpu.SemaphoreType.DMA((copies, Sum.COPIES)),
        pltpu.SemaphoreType.DMA((copies, 1)),
    ]


def feed_sums(grads_refs, which_chunks, own, theirs, box_y, box_x, box_two, box_z, send, recv, near):
    z, y, x, c = place()
    features = D // 4

    def one(s, which):
        grads = grads_refs[which]
        j = 2 * s + which

        def take(c, into):
            return [
                (grads.at[rows_of((2 * k + c) * features, features), pl.ds(s * CHUNK, CHUNK)], into.at[k])
                for k in range(2)
            ]

        mine = own.at[j]
        keep, give = rows_of(y * HIDDEN, HIDDEN), rows_of((1 - y) * HIDDEN, HIDDEN)
        if which == 0:
            ways = [
                (mine.at[:, :, give], mine.at[:, :, keep], False),
                (mine.at[1 - x, :, keep], mine.at[x, :, keep], True),
            ]
            box_one = box_y.at[s]
        else:
            ways = [(mine.at[1 - x], mine.at[x], True), (mine.at[x, :, give], mine.at[x, :, keep], False)]
            box_one = box_x.at[s]
        line = lambda to: mine.at[x, :, rows_of(y * HIDDEN + to * BLOCK, BLOCK)]
        boxes = (box_one, box_two.at[j], box_z.at[j])
        return Sum(lambda c, into: take(c, into), mine, theirs.at[j], ways, line, boxes, send.at[j], recv.at[j], near.at[j])

    return [[one(s, 0), one(s, 1)] for s in range(len(which_chunks))]


def feed_sum_scratch(chunks):
    features = D // 4
    count = 2 * chunks
    return [
        pltpu.VMEM((count, 2, features, CHUNK), BF16),
        pltpu.VMEM((count, 2, features, CHUNK), BF16),
        pltpu.VMEM((chunks, 2, features, HIDDEN), BF16),
        pltpu.VMEM((chunks, features, CHUNK), BF16),
        pltpu.VMEM((count, features, HIDDEN), BF16),
        pltpu.VMEM((count, LINE - 1, features, BLOCK), BF16),
        pltpu.SemaphoreType.DMA((count, Sum.COPIES)),
        pltpu.SemaphoreType.DMA((count, Sum.COPIES)),
        pltpu.SemaphoreType.DMA((count, 1)),
    ]


def backward(x, mg, mixed, att, totals, wi, wo, vec, *more):
    rows = x.shape[0]
    block = TOGETHER * PAD
    walk = GROUPS * BACK
    here = pl.BlockSpec(memory_space=pl.ANY)
    shape = jax.ShapeDtypeStruct
    scratch = [pltpu.VMEM((D, rows), BF16), pltpu.VMEM((D, rows), BF16), pltpu.VMEM((GROUPS, rows, D), BF16)]
    scratch += [pltpu.VMEM((rows, D), F32)]
    sums = [pltpu.VMEM((8, D), F32)]
    weights = [pltpu.VMEM((GROUPS,) + CHIPS + (D,), BF16), pltpu.VMEM(CHIPS + (D,), BF16)]
    specs = []
    if more:
        specs = [here, here] + [whole(a) for a in more[2:4]] + [here, here]
        own = (D // 4, CHUNKS * BLOCK)
        out = [(OWN, 3 * D), (OWN, D), (16, BLOCK), own, own]
        scratch += sums + weights + [
            pltpu.VMEM((PIECES + 1, 2 * OWN, HALF), F32),
            pltpu.VMEM((PIECES + 1, OWN, HALF), F32),
            pltpu.SemaphoreType.DMA((PIECES + 1,)),
            pltpu.SemaphoreType.DMA((PIECES + 1,)),
        ] + feed_sum_scratch(CHUNKS - 1) + square_sum_scratch(PIECES + 1, copies=PIECES + 2)
        scratch += square_sum_scratch(1, BLOCK, F32, 8) + square_sum_scratch(1, BLOCK, F32, 8) + line_sum_scratch()
        scratch += [pltpu.VMEM(shape, BF16) for shape in ((LINE - 1, 2, 2, 2 * OWN, HALF), (2, 2 * OWN, HALF), (2 * OWN, HALF))]
        out_shape = [shape(s, F32) for s in out]
    else:
        out = [(GROUPS, D, D), (D, D), (8, D)]
        out_shape = [shape(s, F32 if s[0] == 8 else BF16) for s in out]
        scratch += weights
    return pl.pallas_call(
        backward_kernel,
        grid=(walk + BACK + BLOCKS,),
        in_specs=[
            here, here, by_group(block, D, blocks=BACK),
            pl.BlockSpec((block, D), lambda i: (jnp.minimum(i, BACK - 1), 0)),
            TOTALS(0), here, whole(wo), whole(vec),
        ] + specs,
        out_specs=[pl.BlockSpec((block, D), lambda i: (jnp.maximum(i - walk - BACK, 0), 0))] + [full(*s) for s in out],
        out_shape=[shape((rows, D), BF16)] + out_shape,
        scratch_shapes=scratch + [
            pltpu.VMEM((rows, D), BF16),
            pltpu.VMEM((rows, D), BF16),
            pltpu.VMEM((GROUPS, D, D), BF16),
            pltpu.SemaphoreType.DMA((2 * BACK + 1,)),
        ],
        compiler_params=params(collective_id=3, has_side_effects=True) if more else params(),
        name="backward",
    )(x, mg, mixed, att, totals, wi, wo, vec, *more)


def spread_kernel(lines, order_ref, ig_ref, *refs):
    near, refs = refs[-1], refs[:-1]
    count = (len(refs) - 1 - len(lines)) // 3
    given, out_ref, refs = refs[:count], refs[count], refs[count + 1 :]
    outs, ones, held = refs[:count], refs[count : count + len(lines)], refs[count + len(lines) :]
    step = pl.program_id(0)
    ins = [pltpu.make_async_copy(src, dst, near.at[j]) for j, (src, dst) in enumerate(zip(given, held))]
    outs = [pltpu.make_async_copy(src, dst, near.at[j]) for j, (src, dst) in enumerate(zip(held, outs))]

    @pl.when(step == 0)
    def _():
        for one in ins:
            one.start()

    @pl.when(step == 1)
    def _():
        for one in ins:
            one.wait()
        for one in outs:
            one.start()
        for (row, lanes), one in zip(lines, ones):
            one[...] = held[-1][row, :lanes]

    @pl.when(step == pl.num_programs(0) - 1)
    def _():
        for one in outs:
            one.wait()

    blocks = D // 128
    rows = out_ref.reshape(PATCHES * blocks * TOGETHER, 128)
    own = [mm(picked(order_ref[j : j + 1, :PAD]), ig_ref[j * PAD : (j + 1) * PAD, :]) for j in range(TOGETHER)]
    for j in range(TOGETHER):
        for k in range(blocks):
            at = pl.ds(k * TOGETHER + j, PATCHES, stride=blocks * TOGETHER)
            rows[at, :] = own[j][:, k * 128 : (k + 1) * 128]


def spread(order, ig, result, *more, lines=()):
    images = order.shape[0]
    steps = images // TOGETHER
    passed = [pl.BlockSpec(memory_space=pl.ANY)] * (1 + len(more))
    shape = jax.ShapeDtypeStruct
    return pl.pallas_call(
        functools.partial(spread_kernel, lines),
        grid=(steps,),
        in_specs=[
            pl.BlockSpec((TOGETHER, PATCHES), lambda i: (i, 0)),
            pl.BlockSpec((TOGETHER * PAD, D), lambda i: (i, 0)),
        ] + passed,
        out_specs=[pl.BlockSpec((PATCHES, 1, D // 128, TOGETHER, 128), lambda i: (0, i, 0, 0, 0))] + passed
        + [full(lanes) for _, lanes in lines],
        out_shape=[shape((PATCHES, steps, D // 128, TOGETHER, 128), F32)] + [shape(a.shape, a.dtype) for a in (result,) + more]
        + [shape((lanes,), F32) for _, lanes in lines],
        scratch_shapes=[pltpu.VMEM(a.shape, a.dtype) for a in (result,) + more] + [pltpu.SemaphoreType.DMA((1 + len(more),))],
        compiler_params=params(),
        name="spread",
    )(order, ig, result, *more)


def local(
    patches, keep_order, cotangent, first_gain, first_shift, project_in, query_bias, value_bias,
    project_out, output_bias, second_gain, second_shift, up_weight, up_bias, down_weight, down_bias,
):
    rows_own = project_in.shape[0]
    hidden_own = up_bias.shape[0]
    images = patches.shape[0]
    wide, narrow = lax.axis_size("wide"), lax.axis_size("narrow")
    vectors = [first_gain, first_shift, query_bias, value_bias, output_bias, second_gain, second_shift, down_bias]
    order = keep_order
    patches = patches.transpose(1, 0, 2)
    cot = cotangent.transpose(1, 0, 2).reshape(VIS * images, D)
    if (wide, narrow) == (8, 4):
        x, mixed, totals, att, result, mg, upg, downg, upbg, sums_two, vec, wi, wo, up_zero, down_zero = forward(
            order, patches, project_in, project_out, cot, up_weight.T, down_weight.T,
            *[v.reshape(1, -1) for v in vectors + [up_bias]],
        )
        ig, wig, wog, s, upf, downf = backward(
            x, mg, mixed, att, totals, wi, wo, vec, upg, downg, sums_two, upbg, up_zero, down_zero
        )
        lines = [(k, rows_own) for k in (8, 9, 0, 1, 2, 3, 4, 5)] + [(6, 4 * rows_own)]
        patch_grad, result, wig, wog, upf, downf, _, *s, upbf = spread(
            order, ig, result, wig, wog, upf, downf, s, lines=lines
        )
        upf, downf = upf.T, downf.T
    else:
        share = jnp.concatenate([jnp.stack(vectors).reshape(1, -1), up_bias.reshape(1, -1)], axis=1)
        shares = lax.all_gather(share, AXES, axis=0, tiled=True)
        vec = shares[:, : 8 * rows_own].reshape(-1, 8, rows_own).transpose(1, 0, 2).reshape(8, D)
        vec = jnp.pad(vec.astype(F32), ((0, 8), (0, 0)))
        upb = shares[:, 8 * rows_own :].reshape(1, -1).astype(F32)
        wi = lax.all_gather(project_in, AXES, axis=0, tiled=True)
        wo = lax.all_gather(project_out, AXES, axis=0, tiled=True)
        ffw = jnp.stack([up_weight.T, down_weight.T])
        ffw = lax.all_gather(ffw, "narrow", axis=1, tiled=True)
        ffw = lax.all_gather(ffw, "wide", axis=2, tiled=True)
        wi = wi.reshape(D, 3, GROUPS, WIDTH).transpose(2, 0, 1, 3).reshape(GROUPS, D, D)
        x = pick(order, patches)
        mixed, att, totals = attend(x, wi, vec)
        result, mg, upg, downg, upbg, sums_two = feed_forward(x, att, cot, wo, vec, ffw[0], upb, ffw[1])
        ig, wig, wog, sums_one = backward(x, mg, mixed, att, totals, wi, wo, vec)
        wig = wig.reshape(GROUPS, D, 3, WIDTH).transpose(1, 2, 0, 3).reshape(D, 3 * D)
        ffg = jnp.stack([upg, downg])
        ffg = lax.psum_scatter(ffg, "wide", scatter_dimension=2, tiled=True)
        ffg = lax.psum_scatter(ffg, "narrow", scatter_dimension=1, tiled=True).astype(F32)
        wig = lax.psum_scatter(wig, AXES, scatter_dimension=0, tiled=True).astype(F32)
        wog = lax.psum_scatter(wog, AXES, scatter_dimension=0, tiled=True).astype(F32)
        picks = [sums_one[G1], sums_one[B1], sums_one[QB], sums_one[VB]]
        picks += [sums_two[OB], sums_two[G2], sums_two[B2], sums_two[DB]]
        parts = jnp.stack(picks).reshape(8, -1, rows_own).transpose(1, 0, 2).reshape(-1, 8 * rows_own)
        parts = jnp.concatenate([parts, upbg.reshape(-1, hidden_own)], axis=1)
        own = lax.psum_scatter(parts, AXES, scatter_dimension=0, tiled=True)[0]
        s = [own[k * rows_own : (k + 1) * rows_own] for k in range(8)]
        upf, downf, upbf = ffg[0].T, ffg[1].T, own[8 * rows_own :]
        patch_grad, result = spread(order, ig, result)
    patch_grad = patch_grad.transpose(1, 3, 0, 2, 4).reshape(images, PATCHES, D)
    result = result.reshape(VIS, images, D).transpose(1, 0, 2)
    return (
        result, patch_grad, s[0], s[1], wig, s[2], s[3], wog, s[4], s[5], s[6], upf, upbf, downf, s[7],
    )


def solution(mesh):
    both = P(AXES)
    rows = P(AXES, None)
    cube = P(AXES, None, None)
    tile = P("wide", "narrow")
    return jax.shard_map(
        local,
        mesh=mesh,
        in_specs=(
            cube, rows, cube, both, both, rows, both, both, rows, both, both, both, tile, both, tile, both,
        ),
        out_specs=(
            cube, cube, both, both, rows, both, both, rows, both, both, both, tile, both, tile, both,
        ),
        check_vma=False,
    )
```
